32 devices in a mesh: groups: 2 (over x), band: 16 (over z, y, core).
Axes of the slice: x: 2, y: 2, z: 4, core: 2. Of those that a mesh axis runs over, the one named last changes fastest.
Arguments:
- node_latent: bfloat16 [10240, 512], P(('groups', 'band')), parts along dimension 0, may hold values from -6 to 6
- edge_latent: bfloat16 [32, 11, 128, 512], P(('groups', 'band')), parts along dimension 0, may hold values from -6 to 6
- recv_slot: int32 [32, 11, 128], P(('groups', 'band')), parts along dimension 0, may hold values from 0 to 319
- send_slot: int32 [32, 11, 128], P(('groups', 'band')), parts along dimension 0, may hold values from 0 to 319
- edge_count: int32 [32, 11], P(('groups', 'band')), parts along dimension 0, may hold values from 42 to 128, as said below
- edge_first: bfloat16 [1536, 512], replicated, may hold values from -0.15625 to 0.15625
- edge_second: bfloat16 [512, 512], replicated, may hold values from -0.25 to 0.25
- node_first: bfloat16 [1024, 512], replicated, may hold values from -0.1875 to 0.1875
- node_second: bfloat16 [512, 512], replicated, may hold values from -0.25 to 0.25
- node_cotan: bfloat16 [10240, 512], P(('groups', 'band')), parts along dimension 0, may hold values from -6 to 6
- edge_cotan: bfloat16 [32, 11, 128, 512], P(('groups', 'band')), parts along dimension 0, may hold values from -6 to 6
Outputs:
- node_new: bfloat16 [10240, 512], P(('groups', 'band')), parts along dimension 0
- edge_new: bfloat16 [32, 11, 128, 512], P(('groups', 'band')), parts along dimension 0
- grad_nodes: bfloat16 [10240, 512], P(('groups', 'band')), parts along dimension 0
- grad_edges: bfloat16 [32, 11, 128, 512], P(('groups', 'band')), parts along dimension 0
- grad_edge_first: bfloat16 [3072, 512], P('groups'), parts along dimension 0
- grad_edge_second: bfloat16 [1024, 512], P('groups'), parts along dimension 0
- grad_node_first: bfloat16 [2048, 512], P('groups'), parts along dimension 0
- grad_node_second: bfloat16 [1024, 512], P('groups'), parts along dimension 0
The draws below stay inside these ranges and needn't reach their ends.
There are 2 independent parts, one for each index of `groups`. The reference program is written for one: setup_inputs(seed, part) draws one part's arguments, and reference() takes and returns one part's arrays. A program takes and returns all parts, laid end to end along the dimension named above; an argument that names none is the same for every part. Nothing has to cross between parts.
Inputs may be any that keep to these rules, and one draw needn't show every extreme that they name: Slots from edge_count on are padding; every edge set is full (128 live slots) on some band. `recv_slot`: indices within the receiver band. `send_slot`: indices within the sender band, the band o_k below the receiver round the loop.
All inputs are finite; a program needn't handle non-finite values.
Results may differ from the reference program's by a relative error of at most 0.0085.
Values may be sent and summed in bfloat16 or wider, within the bound.
No kernel may reach another device: no remote copies, remote signals or barrier semaphores. Data moves between devices by JAX's collectives and lax.ppermute only.
A program may use at most 128 MiB of HBM per device.

```python
import jax
import jax.numpy as jnp
from jax import lax

D = 512
NODE_DEV = 320
CAP = 128
EDGE_SETS = 11
NODES = 5120
N_BAND = 16


def draw_edge_count(key, part):
    key = jax.random.fold_in(key, 3)
    counts = jax.random.randint(key, (N_BAND, EDGE_SETS), CAP // 3, CAP + 1)
    full_band = jax.random.randint(jax.random.fold_in(key, 1), (EDGE_SETS,), 0, N_BAND)
    chosen = jnp.arange(N_BAND, dtype=jnp.int32)[:, None] == full_band[None, :]
    return jnp.where(chosen, CAP, counts).astype(jnp.int32)


def with_ends(values, key, smallest, high):
    longest = values.shape.index(max(values.shape))
    spots = []
    for shift in (0, 1):
        where = [jax.random.randint(jax.random.fold_in(key, axis), (), 0, length) for axis, length in enumerate(values.shape)]
        where[longest] = (where[longest] + shift) % values.shape[longest]
        spots.append(tuple(where))
    return values.at[spots[0]].set(smallest).at[spots[1]].set(high)


def level_of(key, shape, cuts, low, top_value):
    gain, own = 1.0, jax.random.fold_in(key, 6)
    for axis_at, parts in cuts:
        draws = jnp.exp(jax.random.uniform(jax.random.fold_in(own, axis_at), (parts,), jnp.float32, low / len(cuts), top_value / len(cuts)))
        gain = gain * jnp.repeat(draws, shape[axis_at] // parts).reshape([-1 if axis == axis_at else 1 for axis in range(len(shape))])
    return gain


def scatter_about(key, dims, scale, limit, cuts=(), kind=jnp.bfloat16):
    entries = scale * jax.random.normal(key, dims, jnp.float32)
    if cuts:
        entries = entries * level_of(key, dims, cuts, -0.22, 0.18)
    return jnp.clip(entries, -limit, limit).astype(kind)


def setup_inputs(seed: int = 0, part: int = 0) -> dict:
    arg_keys = jax.random.split(jax.random.key(seed), 12)
    part_splits = jax.random.split(jax.random.fold_in(arg_keys[11], part), 12)
    node_latent = scatter_about(part_splits[0], (NODES, D), 1.0, 6.0, ((0, 16),))
    edge_latent = scatter_about(part_splits[1], (N_BAND, EDGE_SETS, CAP, D), 1.0, 6.0, ((0, 16),))
    recv_slot = with_ends(jax.random.randint(part_splits[2], (N_BAND, EDGE_SETS, CAP), 0, NODE_DEV), jax.random.fold_in(part_splits[2], 1), 0, NODE_DEV - 1).astype(jnp.int32)
    send_slot = with_ends(jax.random.randint(part_splits[3], (N_BAND, EDGE_SETS, CAP), 0, NODE_DEV), jax.random.fold_in(part_splits[3], 1), 0, NODE_DEV - 1).astype(jnp.int32)
    edge_count = draw_edge_count(jax.random.fold_in(jax.random.fold_in(arg_keys[11], part), 71), part)
    edge_first = scatter_about(arg_keys[5], (3 * D, D), (3 * D) ** -0.5, 0.15625)
    edge_second = scatter_about(arg_keys[6], (D, D), D ** -0.5, 0.25)
    node_first = scatter_about(arg_keys[7], (2 * D, D), (2 * D) ** -0.5, 0.1875)
    node_second = scatter_about(arg_keys[8], (D, D), D ** -0.5, 0.25)
    node_cotan = scatter_about(part_splits[9], (NODES, D), 1.0, 6.0, ((0, 16),))
    edge_cotan = scatter_about(part_splits[10], (N_BAND, EDGE_SETS, CAP, D), 1.0, 6.0, ((0, 16),))
    return dict(node_latent=node_latent, edge_latent=edge_latent, recv_slot=recv_slot, send_slot=send_slot, edge_count=edge_count, edge_first=edge_first, edge_second=edge_second, node_first=node_first, node_second=node_second, node_cotan=node_cotan, edge_cotan=edge_cotan)


band_offsets = (0, 1, -1, 2, -2, 4, -4, 8, -8, 16, -16)
norm_eps = 1e-05

def swish_act(inputs):
    return inputs * jax.nn.sigmoid(inputs)

def swish_slope(inputs):
    squashed = jax.nn.sigmoid(inputs)
    return squashed * (1.0 + inputs * (1.0 - squashed))

def layer_norm(inputs):
    average = lax.optimization_barrier(jnp.mean(inputs, axis=-1, keepdims=True))
    centred = inputs - average
    inverse = lax.rsqrt(lax.optimization_barrier(jnp.mean(centred * centred, axis=-1, keepdims=True)) + norm_eps)
    return (centred * inverse, inverse)

def norm_back(normed, inverse, upstream):
    return inverse * (upstream - lax.optimization_barrier(jnp.mean(upstream, axis=-1, keepdims=True)) - normed * lax.optimization_barrier(jnp.mean(upstream * normed, axis=-1, keepdims=True)))

def plain_dot(left_side, right_side):
    return jnp.dot(left_side, right_side, preferred_element_type=jnp.float32)

def dot_right_t(left_side, right_side):
    return lax.dot_general(left_side, right_side, (((1,), (1,)), ((), ())), preferred_element_type=jnp.float32)

def dot_left_t(left_side, right_side):
    return lax.dot_general(left_side, right_side, (((0,), (0,)), ((), ())), preferred_element_type=jnp.float32)

def reference(node_latent, edge_latent, recv_slot, send_slot, edge_count, edge_first, edge_second, node_first, node_second, node_cotan, edge_cotan):
    width = node_latent.shape[1]
    node_total = node_latent.shape[0]
    band_ids = jnp.arange(N_BAND, dtype=jnp.int32)
    offsets = jnp.array(band_offsets, dtype=jnp.int32)
    sender_band = (band_ids[:, None] - offsets[None, :]) % N_BAND
    sender_rows = (sender_band[:, :, None] * NODE_DEV + send_slot).reshape(-1).astype(jnp.int32)
    receiver_rows = (band_ids[:, None, None] * NODE_DEV + recv_slot).reshape(-1).astype(jnp.int32)
    live = jnp.arange(CAP, dtype=jnp.int32)[None, None, :] < edge_count[:, :, None]
    live = live.reshape(-1, 1).astype(jnp.float32)
    w_edge = edge_first[:width]
    w_send = edge_first[width:2 * width]
    w_recv = edge_first[2 * width:]
    edge_flat = edge_latent.reshape(-1, width)
    cotan_flat = edge_cotan.reshape(-1, width)
    sender_x = node_latent[sender_rows]
    receiver_x = node_latent[receiver_rows]
    sender_term = plain_dot(sender_x, w_send).astype(jnp.bfloat16)
    pre_edge = plain_dot(edge_flat, w_edge) + sender_term.astype(jnp.float32) + plain_dot(receiver_x, w_recv)
    act_edge = swish_act(pre_edge).astype(jnp.bfloat16)
    out_edge = plain_dot(act_edge, edge_second)
    normed_edge, inverse_edge = layer_norm(out_edge)
    message_f = live * normed_edge
    message = message_f.astype(jnp.bfloat16)
    edge_new = (edge_flat.astype(jnp.float32) + message_f).astype(jnp.bfloat16)
    gathered = jax.ops.segment_sum(message.astype(jnp.float32), receiver_rows, num_segments=node_total)
    gathered = gathered.astype(jnp.bfloat16)
    pre_node = plain_dot(node_latent, node_first[:width]) + plain_dot(gathered, node_first[width:])
    act_node = swish_act(pre_node).astype(jnp.bfloat16)
    out_node = plain_dot(act_node, node_second)
    normed_node, inverse_node = layer_norm(out_node)
    node_new = (node_latent.astype(jnp.float32) + normed_node).astype(jnp.bfloat16)
    grad_out_node = norm_back(normed_node, inverse_node, node_cotan.astype(jnp.float32)).astype(jnp.bfloat16)
    grad_node_second = dot_left_t(act_node, grad_out_node)
    grad_pre_node = (dot_right_t(grad_out_node, node_second) * swish_slope(pre_node)).astype(jnp.bfloat16)
    grad_node_first = jnp.concatenate([dot_left_t(node_latent, grad_pre_node), dot_left_t(gathered, grad_pre_node)], axis=0)
    grad_gathered = dot_right_t(grad_pre_node, node_first[width:]).astype(jnp.bfloat16)
    grad_nodes = node_cotan.astype(jnp.float32) + dot_right_t(grad_pre_node, node_first[:width])
    grad_message = live * (cotan_flat.astype(jnp.float32) + grad_gathered[receiver_rows].astype(jnp.float32))
    grad_out_edge = norm_back(normed_edge, inverse_edge, grad_message).astype(jnp.bfloat16)
    grad_edge_second = dot_left_t(act_edge, grad_out_edge)
    grad_pre_edge = (dot_right_t(grad_out_edge, edge_second) * swish_slope(pre_edge)).astype(jnp.bfloat16)
    grad_edge_first = jnp.concatenate([dot_left_t(edge_flat, grad_pre_edge), dot_left_t(sender_x, grad_pre_edge), dot_left_t(receiver_x, grad_pre_edge)], axis=0)
    grad_edges = (cotan_flat.astype(jnp.float32) + dot_right_t(grad_pre_edge, w_edge)).astype(jnp.bfloat16)
    grad_nodes = grad_nodes + jax.ops.segment_sum(dot_right_t(grad_pre_edge, w_recv), receiver_rows, num_segments=node_total)
    grad_nodes = grad_nodes + jax.ops.segment_sum(dot_right_t(grad_pre_edge, w_send), sender_rows, num_segments=node_total)
    edge_shape = edge_latent.shape
    return (node_new, edge_new.reshape(edge_shape), grad_nodes.astype(jnp.bfloat16), grad_edges.reshape(edge_shape), grad_edge_first.astype(jnp.bfloat16), grad_edge_second.astype(jnp.bfloat16), grad_node_first.astype(jnp.bfloat16), grad_node_second.astype(jnp.bfloat16))
```

```python
import jax
import jax.numpy as jnp
from jax import lax
from jax.sharding import PartitionSpec as P

band_offsets = (0, 1, -1, 2, -2, 4, -4, 8, -8, 16, -16)
norm_eps = 1e-05


def passed_along(block, axis, distance):
    devices = range(lax.axis_size(axis))
    route = [((i - distance) % len(devices), i) for i in devices]
    return lax.ppermute(block, axis, route)


def swish_slope(inputs):
    squashed = jax.nn.sigmoid(inputs)
    return squashed * (1.0 + inputs * (1.0 - squashed))


def layer_norm(inputs):
    average = jnp.mean(inputs, axis=-1, keepdims=True)
    centred = inputs - average
    inverse = lax.rsqrt(jnp.mean(centred * centred, axis=-1, keepdims=True) + norm_eps)
    return (centred * inverse, inverse)


def norm_back(normed, inverse, upstream):
    return inverse * (
        upstream
        - jnp.mean(upstream, axis=-1, keepdims=True)
        - normed * jnp.mean(upstream * normed, axis=-1, keepdims=True)
    )


def one_hot(slot_ids, node_count):
    return (slot_ids[:, None] == jnp.arange(node_count, dtype=jnp.int32)).astype(jnp.bfloat16)


def dot(left_side, right_side):
    return jnp.dot(left_side, right_side, preferred_element_type=jnp.float32)


def dot_rt(left_side, right_side):
    return lax.dot_general(
        left_side, right_side, (((1,), (1,)), ((), ())), preferred_element_type=jnp.float32
    )


def dot_lt(left_side, right_side):
    return lax.dot_general(
        left_side, right_side, (((0,), (0,)), ((), ())), preferred_element_type=jnp.float32
    )


def local(
    node_latent,
    edge_latent,
    recv_slot,
    send_slot,
    edge_count,
    edge_first,
    edge_second,
    node_first,
    node_second,
    node_cotan,
    edge_cotan,
):
    bf16 = jnp.bfloat16
    f32 = jnp.float32
    bands = lax.axis_size("band")
    me = lax.axis_index("band")
    nodes, width = node_latent.shape
    sets, cap = edge_latent.shape[1:3]
    by_distance = {}
    for k, offset in enumerate(band_offsets):
        by_distance.setdefault(offset % bands, []).append(k)
    order = sorted(by_distance, key=lambda d: -min(d, bands - d))

    w_edge = edge_first[:width]
    w_send = edge_first[width : 2 * width]
    w_recv = edge_first[2 * width :]
    edges = edge_latent[0].reshape(sets * cap, width)
    cotan = edge_cotan[0].reshape(sets * cap, width)
    recv_hot = one_hot(recv_slot[0].reshape(-1), nodes)
    live = (jnp.arange(cap, dtype=jnp.int32)[None, :] < edge_count[0][:, None]).astype(f32)
    live = live.reshape(sets * cap, 1)

    all_ids = lax.all_gather(send_slot[0], "band")
    send_hot = {}
    rows = [None] * sets
    for d in order:
        ids = lax.dynamic_index_in_dim(all_ids, (me + d) % bands, 0, keepdims=False)
        ids = jnp.concatenate([ids[k] for k in by_distance[d]])
        send_hot[d] = one_hot(ids, nodes)
        picked = dot(send_hot[d], node_latent).astype(bf16)
        if d:
            picked = passed_along(picked, "band", d)
        for i, k in enumerate(by_distance[d]):
            rows[k] = picked[i * cap : (i + 1) * cap]
    sender_x = jnp.concatenate(rows)
    receiver_x = dot(recv_hot, node_latent).astype(bf16)

    pre_edge = dot(edges, w_edge) + dot(sender_x, w_send) + dot(receiver_x, w_recv)
    squashed = jax.nn.sigmoid(pre_edge)
    act_edge = (pre_edge * squashed).astype(bf16)
    out_edge = dot(act_edge, edge_second)
    normed_edge, inverse_edge = layer_norm(out_edge)
    message_f = live * normed_edge
    message = message_f.astype(bf16)
    edge_new = (edges.astype(f32) + message_f).astype(bf16)
    gathered = dot_lt(recv_hot, message).astype(bf16)

    pre_node = dot(node_latent, node_first[:width]) + dot(gathered, node_first[width:])
    act_node = (pre_node * jax.nn.sigmoid(pre_node)).astype(bf16)
    normed_node, inverse_node = layer_norm(dot(act_node, node_second))
    node_new = (node_latent.astype(f32) + normed_node).astype(bf16)
    grad_out_node = norm_back(normed_node, inverse_node, node_cotan.astype(f32)).astype(bf16)
    grad_pre_node = (dot_rt(grad_out_node, node_second) * swish_slope(pre_node)).astype(bf16)
    grad_gathered = dot_rt(grad_pre_node, node_first[width:]).astype(bf16)

    grad_message = live * (cotan.astype(f32) + dot(recv_hot, grad_gathered))
    grad_out_edge = norm_back(normed_edge, inverse_edge, grad_message).astype(bf16)
    grad_pre_edge = (dot_rt(grad_out_edge, edge_second) * swish_slope(pre_edge)).astype(bf16)

    arrived = {}
    for d in order:
        block = jnp.concatenate([grad_pre_edge[k * cap : (k + 1) * cap] for k in by_distance[d]])
        arrived[d] = passed_along(block, "band", -d) if d else block

    recv_sum = dot_lt(recv_hot, grad_pre_edge).astype(bf16)
    weight_grads = jnp.concatenate(
        [
            dot_lt(edges, grad_pre_edge),
            dot_lt(sender_x, grad_pre_edge),
            dot_lt(node_latent, recv_sum),
            dot_lt(act_edge, grad_out_edge),
            dot_lt(node_latent, grad_pre_node),
            dot_lt(gathered, grad_pre_node),
            dot_lt(act_node, grad_out_node),
        ]
    ).astype(bf16)
    share = lax.psum_scatter(weight_grads, "band", scatter_dimension=0, tiled=True)
    weight_grads = lax.all_gather(share, "band", axis=0, tiled=True)

    grad_edges = (cotan.astype(f32) + dot_rt(grad_pre_edge, w_edge)).astype(bf16)
    send_sum = dot_lt(
        jnp.concatenate([send_hot[d] for d in order]),
        jnp.concatenate([arrived[d] for d in order]),
    ).astype(bf16)
    grad_nodes = (
        node_cotan.astype(f32)
        + dot_rt(grad_pre_node, node_first[:width])
        + dot_rt(recv_sum, w_recv)
        + dot_rt(send_sum, w_send)
    )
    first = 3 * width
    return (
        node_new,
        edge_new.reshape(edge_latent.shape),
        grad_nodes.astype(bf16),
        grad_edges.reshape(edge_latent.shape),
        weight_grads[:first],
        weight_grads[first : first + width],
        weight_grads[first + width : first + 3 * width],
        weight_grads[first + 3 * width :],
    )


def solution(mesh):
    return jax.shard_map(
        local,
        mesh=mesh,
        in_specs=(
            P(("groups", "band"), None),
            P(("groups", "band"), None, None, None),
            P(("groups", "band"), None, None),
            P(("groups", "band"), None, None),
            P(("groups", "band"), None),
            P(),
            P(),
            P(),
            P(),
            P(("groups", "band"), None),
            P(("groups", "band"), None, None, None),
        ),
        out_specs=(
            P(("groups", "band"), None),
            P(("groups", "band"), None, None, None),
            P(("groups", "band"), None),
            P(("groups", "band"), None, None, None),
            P("groups", None),
            P("groups", None),
            P("groups", None),
            P("groups", None),
        ),
        check_vma=False,
    )
```

```python
import functools

import jax
import jax.numpy as jnp
from jax import lax
from jax.experimental import pallas as pl
from jax.experimental.pallas import tpu as pltpu
from jax.sharding import PartitionSpec as P

band_offsets = (0, 1, -1, 2, -2, 4, -4, 8, -8, 16, -16)
norm_eps = 1e-05
near_sets = 7
id_rows = 16
bf16 = jnp.bfloat16
f32 = jnp.float32
params = pltpu.CompilerParams(vmem_limit_bytes=48 * 1024 * 1024)


def passed_along(block, axis, distance):
    devices = range(lax.axis_size(axis))
    route = [((i - distance) % len(devices), i) for i in devices]
    return lax.ppermute(block, axis, route)


def swapped(block, axis):
    return lax.ppermute(block, axis, [(i, i ^ 1) for i in range(lax.axis_size(axis))])


def layer_norm(inputs):
    average = jnp.mean(inputs, axis=-1, keepdims=True)
    centred = inputs - average
    inverse = lax.rsqrt(jnp.mean(centred * centred, axis=-1, keepdims=True) + norm_eps)
    return (centred * inverse, inverse)


def norm_back(normed, inverse, upstream):
    return inverse * (
        upstream
        - jnp.mean(upstream, axis=-1, keepdims=True)
        - normed * jnp.mean(upstream * normed, axis=-1, keepdims=True)
    )


def slope_of(inputs, squashed):
    return squashed * (1.0 + inputs * (1.0 - squashed))


def dot(left_side, right_side):
    return jnp.dot(left_side, right_side, preferred_element_type=f32)


def dot_rt(left_side, right_side):
    return lax.dot_general(
        left_side, right_side, (((1,), (1,)), ((), ())), preferred_element_type=f32
    )


def dot_lt(left_side, right_side):
    return lax.dot_general(
        left_side, right_side, (((0,), (0,)), ((), ())), preferred_element_type=f32
    )


def pick_table(ids, nodes):
    cap = ids.shape[1]
    down = jnp.transpose(jnp.broadcast_to(ids, (cap, cap)))
    parts = []
    for first in range(0, nodes, cap):
        wide = min(cap, nodes - first)
        lanes = lax.broadcasted_iota(jnp.int32, (cap, wide), 1) + first
        parts.append(jnp.where(down[:, :wide] == lanes, 1.0, 0.0).astype(bf16))
    return jnp.concatenate(parts, axis=1)


def sum_table(ids, nodes):
    down = lax.broadcasted_iota(jnp.int32, (nodes, ids.shape[1]), 0)
    return jnp.where(down == ids, 1.0, 0.0).astype(bf16)


def live_rows(count, cap):
    return (lax.broadcasted_iota(jnp.int32, (cap, 128), 0) < count).astype(f32)


def call(body, outs, scratch, *args, smem=()):
    spaces = [
        pl.BlockSpec(memory_space=pltpu.SMEM if i in smem else pltpu.VMEM) for i in range(len(args))
    ]
    return pl.pallas_call(
        body,
        out_shape=[jax.ShapeDtypeStruct(shape, kind) for shape, kind in outs],
        in_specs=spaces,
        out_specs=[pl.BlockSpec(memory_space=pltpu.VMEM)] * len(outs),
        scratch_shapes=[pltpu.VMEM(shape, kind) for shape, kind in scratch],
        compiler_params=params,
    )(*args)


def pick_kernel(count, *refs):
    node_ref, id_refs, out_refs = refs[0], refs[1 : 1 + count], refs[1 + count :]
    nodes = node_ref.shape[0]
    for id_ref, out_ref in zip(id_refs, out_refs):
        cap = id_ref.shape[1]
        for i in range(id_ref.shape[0]):
            hot = pick_table(id_ref[i : i + 1, :], nodes)
            out_ref[i * cap : (i + 1) * cap, :] = dot(hot, node_ref[...]).astype(bf16)


def forward_rows(rows, x_ref, w1_ref, w2_ref, live_ref, pre_ref, normed_ref, inv_ref, msg_ref):
    pre = dot(x_ref[rows, :], w1_ref[...])
    pre_ref[rows, :] = pre
    act = (pre * jax.nn.sigmoid(pre)).astype(bf16)
    normed, inverse = layer_norm(dot(act, w2_ref[...]))
    normed_ref[rows, :] = normed
    inv_ref[rows, :] = jnp.broadcast_to(inverse, (inverse.shape[0], 128))
    msg_ref[rows, :] = (live_ref[rows, :1] * normed).astype(bf16)
    return act


def near_kernel(plan, *refs):
    sets, sources, count = plan
    (edge_ref, recv_ref, send_ref, count_ref, w1_ref, w2_ref) = refs[:6]
    node_refs = refs[6 : 6 + count]
    (sx_ref, pre_ref, normed_ref, inv_ref, live_ref, sum_ref, x_ref, msg_ref, hot_ref) = refs[6 + count :]
    nodes, width = node_refs[0].shape
    cap = recv_ref.shape[1]
    for i, k in enumerate(sets):
        rows = slice(i * cap, (i + 1) * cap)
        x_ref[rows, :width] = edge_ref[k]
        picked = dot(pick_table(send_ref[k : k + 1, :], nodes), node_refs[sources[i]][...])
        sx_ref[rows, :] = picked.astype(bf16)
        x_ref[rows, width : 2 * width] = picked.astype(bf16)
        picked = dot(pick_table(recv_ref[k : k + 1, :], nodes), node_refs[0][...])
        x_ref[rows, 2 * width :] = picked.astype(bf16)
        live_ref[rows, :] = live_rows(count_ref[0, k], cap)
        hot_ref[:, rows] = sum_table(recv_ref[k : k + 1, :], nodes)
    half = len(sets) * cap // 2

    def step(j, carry):
        rows = pl.ds(pl.multiple_of(j * half, 16), half)
        forward_rows(rows, x_ref, w1_ref, w2_ref, live_ref, pre_ref, normed_ref, inv_ref, msg_ref)
        return carry

    lax.fori_loop(0, 2, step, 0)
    sum_ref[...] = dot(hot_ref[...], msg_ref[...])


def far_kernel(plan, *refs):
    sets, pieces = plan
    count = len(pieces)
    (
        edge_ref,
        cotan_ref,
        recv_ref,
        count_ref,
        w1_ref,
        w2_ref,
        node_ref,
        ncot_ref,
        sum_ref,
        n1_ref,
        n2_ref,
    ) = refs[:11]
    sx_refs = refs[11 : 11 + count]
    gpe_refs = refs[11 + count : 11 + 2 * count]
    (
        act_ref,
        goe_ref,
        new_ref,
        node_new_ref,
        gathered_ref,
        gpn_ref,
        act_node_ref,
        gon_ref,
        gg_ref,
        x_ref,
        live_ref,
        pre_ref,
        normed_ref,
        inv_ref,
        msg_ref,
        hot_ref,
        pick_ref,
        cot_ref,
    ) = refs[11 + 2 * count :]
    nodes, width = node_ref.shape
    cap = recv_ref.shape[1]
    total = len(sets) * cap
    first = 0
    for sx_ref in sx_refs:
        x_ref[first : first + sx_ref.shape[0], width : 2 * width] = sx_ref[...]
        first += sx_ref.shape[0]
    for i, k in enumerate(sets):
        rows = slice(i * cap, (i + 1) * cap)
        x_ref[rows, :width] = edge_ref[k]
        cot_ref[rows, :] = cotan_ref[k]
        hot = pick_table(recv_ref[k : k + 1, :], nodes)
        pick_ref[rows, :] = hot
        x_ref[rows, 2 * width :] = dot(hot, node_ref[...]).astype(bf16)
        live_ref[rows, :] = live_rows(count_ref[0, k], cap)
        hot_ref[:, rows] = sum_table(recv_ref[k : k + 1, :], nodes)
    half = total // 2

    def ahead(j, carry):
        rows = pl.ds(pl.multiple_of(j * half, 16), half)
        act = forward_rows(
            rows, x_ref, w1_ref, w2_ref, live_ref, pre_ref, normed_ref, inv_ref, msg_ref
        )
        act_ref[rows, :] = act
        message = live_ref[rows, :1] * normed_ref[rows, :]
        new_ref[rows, :] = (x_ref[rows, :width].astype(f32) + message).astype(bf16)
        return carry

    lax.fori_loop(0, 2, ahead, 0)
    gathered = (sum_ref[...] + dot(hot_ref[...], msg_ref[...])).astype(bf16)
    gathered_ref[...] = gathered

    pre = dot(node_ref[...], n1_ref[:width, :]) + dot(gathered, n1_ref[width:, :])
    squashed = jax.nn.sigmoid(pre)
    act_node = (pre * squashed).astype(bf16)
    act_node_ref[...] = act_node
    normed, inverse = layer_norm(dot(act_node, n2_ref[...]))
    node_new_ref[...] = (node_ref[...].astype(f32) + normed).astype(bf16)
    gon = norm_back(normed, inverse, ncot_ref[...].astype(f32)).astype(bf16)
    gon_ref[...] = gon
    gpn = (dot_rt(gon, n2_ref[...]) * slope_of(pre, squashed)).astype(bf16)
    gpn_ref[...] = gpn
    gg_ref[...] = dot_rt(gpn, n1_ref[width:, :]).astype(bf16)

    first = 0
    for gpe_ref in gpe_refs:
        size = gpe_ref.shape[0]
        rows = slice(first, first + size)
        upstream = cot_ref[rows, :].astype(f32) + dot(pick_ref[rows, :], gg_ref[...])
        upstream = live_ref[rows, :1] * upstream
        goe = norm_back(normed_ref[rows, :], inv_ref[rows, :1], upstream).astype(bf16)
        goe_ref[rows, :] = goe
        pre = pre_ref[rows, :]
        slope = slope_of(pre, jax.nn.sigmoid(pre))
        gpe_ref[...] = (dot_rt(goe, w2_ref[...]) * slope).astype(bf16)
        first += size


def back_kernel(plan, *refs):
    near, far, local_count, near_count, far_count = plan
    (
        edge_ref,
        cotan_ref,
        recv_ref,
        send_ref,
        core_ref,
        w1_ref,
        w2_ref,
        wx_ref,
        live_ref,
        pre_ref,
        normed_ref,
        inv_ref,
        sx_ref,
        act_far_ref,
        goe_far_ref,
        new_far_ref,
        node_ref,
        ncot_ref,
        gathered_ref,
        gpn_ref,
        act_node_ref,
        gon_ref,
        gg_ref,
    ) = refs[:23]
    sx_far = refs[23 : 23 + far_count]
    gpe_far = refs[23 + far_count : 23 + 2 * far_count]
    outs = refs[23 + 2 * far_count :]
    new_ref, gedge_ref, base_ref, keep_ref, send_out_ref, gpe_local_ref = outs[:6]
    gpe_out = outs[6 : 6 + near_count]
    xe_ref, sxs_ref, acts_ref, goes_ref, gpes_ref, pick_ref, hot_ref, block_ref = outs[6 + near_count :]
    nodes, width = node_ref.shape
    cap = recv_ref.shape[1]
    near_rows = len(near) * cap
    order = near + far
    for i, k in enumerate(order):
        rows = slice(i * cap, (i + 1) * cap)
        xe_ref[rows, :] = edge_ref[k]
        hot_ref[:, rows] = sum_table(recv_ref[k : k + 1, :], nodes)
        if i < len(near):
            pick_ref[rows, :] = pick_table(recv_ref[k : k + 1, :], nodes)
    half = near_rows // 2
    for j in range(2):
        rows = slice(j * half, (j + 1) * half)
        cot = jnp.concatenate([cotan_ref[k] for k in near]).astype(f32)[rows, :]
        upstream = live_ref[rows, :1] * (cot + dot(pick_ref[rows, :], gg_ref[...]))
        goe = norm_back(normed_ref[rows, :], inv_ref[rows, :1], upstream).astype(bf16)
        goes_ref[rows, :] = goe
        pre = pre_ref[rows, :]
        squashed = jax.nn.sigmoid(pre)
        acts_ref[rows, :] = (pre * squashed).astype(bf16)
        gpes_ref[rows, :] = (dot_rt(goe, w2_ref[...]) * slope_of(pre, squashed)).astype(bf16)
    gpe_local_ref[...] = gpes_ref[: local_count * cap, :]
    for j, out_ref in enumerate(gpe_out):
        i = local_count + j
        out_ref[:cap, :] = gpes_ref[i * cap : (i + 1) * cap, :]
        ids = send_ref[near[i] : near[i] + 1, :]
        high, low = ids // 16, ids % 16
        blank = jnp.zeros((1, width - 2 * cap), f32)
        coded = jnp.concatenate([high.astype(f32), low.astype(f32), blank], axis=1)
        out_ref[cap:, :] = jnp.broadcast_to(coded, (id_rows, width)).astype(bf16)
    acts_ref[near_rows:, :] = act_far_ref[...]
    goes_ref[near_rows:, :] = goe_far_ref[...]
    sxs_ref[:near_rows, :] = sx_ref[...]
    first = near_rows
    for one_x, one_g in zip(sx_far, gpe_far):
        rows = slice(first, first + one_x.shape[0])
        sxs_ref[rows, :] = one_x[...]
        gpes_ref[rows, :] = one_g[...]
        first += one_x.shape[0]

    core = core_ref[0]
    half_rows = width // 2

    def put(index, left_side, right_side):
        block_ref[...] = dot_lt(left_side, right_side)
        mine = pl.ds(pl.multiple_of(core * half_rows, half_rows), half_rows)
        other = pl.ds(pl.multiple_of((1 - core) * half_rows, half_rows), half_rows)
        keep_ref[index] = block_ref[mine, :].astype(bf16)
        send_out_ref[index] = block_ref[other, :].astype(bf16)

    recv_sum = dot(hot_ref[...], gpes_ref[...]).astype(bf16)
    put(0, xe_ref[...], gpes_ref[...])
    put(1, sxs_ref[...], gpes_ref[...])
    put(2, node_ref[...], recv_sum)
    put(3, acts_ref[...], goes_ref[...])
    put(4, node_ref[...], gpn_ref[...])
    put(5, gathered_ref[...], gpn_ref[...])
    put(6, act_node_ref[...], gon_ref[...])

    base_ref[...] = (
        ncot_ref[...].astype(f32)
        + dot_rt(gpn_ref[...], wx_ref[...])
        + dot_rt(recv_sum, w1_ref[2 * width :, :])
    )
    for i, k in enumerate(order):
        rows = slice(i * cap, (i + 1) * cap)
        grad = cotan_ref[k].astype(f32) + dot_rt(gpes_ref[rows, :], w1_ref[:width, :])
        gedge_ref[k] = grad.astype(bf16)
        if i < len(near):
            message = live_ref[rows, :1] * normed_ref[rows, :]
            new_ref[k] = (edge_ref[k].astype(f32) + message).astype(bf16)
        else:
            new_ref[k] = new_far_ref[(i - len(near)) * cap : (i - len(near) + 1) * cap, :]


def final_kernel(plan, *refs):
    local_sets, near_count, far_count = plan
    base_ref, ws_ref, send_ref, gpe_local_ref = refs[:4]
    near_refs = refs[4 : 4 + near_count]
    far_refs = refs[4 + near_count : 4 + near_count + far_count]
    id_refs = refs[4 + near_count + far_count : 4 + near_count + 2 * far_count]
    out_ref, hot_ref, rows_ref = refs[4 + near_count + 2 * far_count :]
    nodes = base_ref.shape[0]
    cap = send_ref.shape[1]
    at = 0
    for k in local_sets:
        hot_ref[:, at : at + cap] = sum_table(send_ref[k : k + 1, :], nodes)
        at += cap
    rows_ref[:at, :] = gpe_local_ref[...]
    for near_ref in near_refs:
        coded = near_ref[cap : cap + 8, :].astype(f32)
        ids = (coded[:1, :cap] * 16.0 + coded[:1, cap : 2 * cap]).astype(jnp.int32)
        hot_ref[:, at : at + cap] = sum_table(ids, nodes)
        rows_ref[at : at + cap, :] = near_ref[:cap, :]
        at += cap
    for far_ref, id_ref in zip(far_refs, id_refs):
        rows_ref[at : at + far_ref.shape[0], :] = far_ref[...]
        for i in range(id_ref.shape[0]):
            hot_ref[:, at : at + cap] = sum_table(id_ref[i : i + 1, :], nodes)
            at += cap
    send_sum = dot(hot_ref[...], rows_ref[...]).astype(bf16)
    out_ref[...] = (base_ref[...] + dot_rt(send_sum, ws_ref[...])).astype(bf16)


def join_kernel(core_ref, mine_ref, other_ref, e1_ref, e2_ref, n1_ref, n2_ref):
    core = core_ref[0]
    half_rows = mine_ref.shape[1]
    places = [(e1_ref, 0), (e1_ref, 1), (e1_ref, 2), (e2_ref, 0), (n1_ref, 0), (n1_ref, 1), (n2_ref, 0)]
    for index, (out_ref, block) in enumerate(places):
        first = 2 * block * half_rows
        at = pl.multiple_of(first + core * half_rows, half_rows)
        out_ref[pl.ds(at, half_rows), :] = mine_ref[index]
        at = pl.multiple_of(first + (1 - core) * half_rows, half_rows)
        out_ref[pl.ds(at, half_rows), :] = other_ref[index]


def local(
    node_latent,
    edge_latent,
    recv_slot,
    send_slot,
    edge_count,
    edge_first,
    edge_second,
    node_first,
    node_second,
    node_cotan,
    edge_cotan,
):
    bands = lax.axis_size("band")
    nodes, width = node_latent.shape
    sets, cap = edge_latent.shape[1:3]
    edges, cotan = edge_latent[0], edge_cotan[0]
    recv_ids, send_ids = recv_slot[0], send_slot[0]
    core = (lax.axis_index("band") % 2).reshape(1)

    def reach(d):
        return min(d, bands - d)

    ordered = sorted(range(sets), key=lambda k: (reach(band_offsets[k] % bands), band_offsets[k] % bands))
    near, far = tuple(ordered[:near_sets]), tuple(ordered[near_sets:])
    near_steps = [band_offsets[k] % bands for k in near]
    far_steps = sorted({band_offsets[k] % bands for k in far}, key=lambda d: -reach(d))
    pieces = tuple(tuple(k for k in far if band_offsets[k] % bands == d) for d in far_steps)
    far = sum(pieces, ())
    local_count = sum(d == 0 for d in near_steps)
    local_sets = near[:local_count]
    near_count = len(near) - local_count
    sources = tuple(max(0, i + 1 - local_count) for i in range(len(near)))

    far_ids = [
        passed_along(send_ids[piece[0] : piece[-1] + 1], "band", -d)
        for piece, d in zip(pieces, far_steps)
    ]
    node_blocks = [node_latent] + [passed_along(node_latent, "band", d) for d in near_steps[local_count:]]
    picked = call(
        functools.partial(pick_kernel, len(far_ids)),
        [((len(piece) * cap, width), bf16) for piece in pieces],
        [],
        node_latent,
        *far_ids,
    )
    sx_far = [passed_along(block, "band", d) for block, d in zip(picked, far_steps)]

    near_rows, far_rows = len(near) * cap, len(far) * cap
    sx, pre, normed, inverse, live, part_sum = call(
        functools.partial(near_kernel, (near, sources, len(node_blocks))),
        [
            ((near_rows, width), bf16),
            ((near_rows, width), f32),
            ((near_rows, width), f32),
            ((near_rows, 128), f32),
            ((near_rows, 128), f32),
            ((nodes, width), f32),
        ],
        [
            ((near_rows, 3 * width), bf16),
            ((near_rows, width), bf16),
            ((nodes, near_rows), bf16),
        ],
        edges,
        recv_ids,
        send_ids,
        edge_count,
        edge_first,
        edge_second,
        *node_blocks,
        smem=(3,),
    )

    outs = call(
        functools.partial(far_kernel, (far, pieces)),
        [((len(piece) * cap, width), bf16) for piece in pieces]
        + [((far_rows, width), bf16)] * 3
        + [((nodes, width), bf16)] * 6,
        [
            ((far_rows, 3 * width), bf16),
            ((far_rows, 128), f32),
            ((far_rows, width), f32),
            ((far_rows, width), f32),
            ((far_rows, 128), f32),
            ((far_rows, width), bf16),
            ((nodes, far_rows), bf16),
            ((far_rows, nodes), bf16),
            ((far_rows, width), bf16),
        ],
        edges,
        cotan,
        recv_ids,
        edge_count,
        edge_first,
        edge_second,
        node_latent,
        node_cotan,
        part_sum,
        node_first,
        node_second,
        *sx_far,
        smem=(3,),
    )
    gpe_far, outs = outs[: len(pieces)], outs[len(pieces) :]
    act_far, goe_far, new_far, node_new, gathered, gpn, act_node, gon, gg = outs
    back_far = [passed_along(block, "band", -d) for block, d in zip(gpe_far, far_steps)]

    outs = call(
        functools.partial(back_kernel, (near, far, local_count, near_count, len(pieces))),
        [
            ((sets, cap, width), bf16),
            ((sets, cap, width), bf16),
            ((nodes, width), f32),
            ((7, width // 2, width), bf16),
            ((7, width // 2, width), bf16),
            ((local_count * cap, width), bf16),
        ]
        + [((cap + id_rows, width), bf16)] * near_count,
        [
            ((sets * cap, width), bf16),
            ((sets * cap, width), bf16),
            ((sets * cap, width), bf16),
            ((sets * cap, width), bf16),
            ((sets * cap, width), bf16),
            ((near_rows, nodes), bf16),
            ((nodes, sets * cap), bf16),
            ((width, width), f32),
        ],
        edges,
        cotan,
        recv_ids,
        send_ids,
        core,
        edge_first,
        edge_second,
        node_first[:width],
        live,
        pre,
        normed,
        inverse,
        sx,
        act_far,
        goe_far,
        new_far,
        node_latent,
        node_cotan,
        gathered,
        gpn,
        act_node,
        gon,
        gg,
        *sx_far,
        *gpe_far,
        smem=(4,),
    )
    edge_new, grad_edges, base, keep, sent, gpe_local = outs[:6]
    back_near = [
        passed_along(block, "band", -d) for block, d in zip(outs[6:], near_steps[local_count:])
    ]
    arrived = swapped(sent, "band")
    share = (keep.astype(f32) + arrived.astype(f32)).astype(bf16)
    chips = [[i for i in range(bands) if i % 2 == c] for c in range(2)]
    total = lax.psum((share[:3], share[3:]), "band", axis_index_groups=chips)
    total = jnp.concatenate(total)
    other = swapped(total, "band")

    (grad_nodes,) = call(
        functools.partial(final_kernel, (local_sets, near_count, len(pieces))),
        [((nodes, width), bf16)],
        [((nodes, sets * cap), bf16), ((sets * cap, width), bf16)],
        base,
        edge_first[width : 2 * width],
        send_ids,
        gpe_local,
        *back_near,
        *back_far,
        *far_ids,
    )
    grad_e1, grad_e2, grad_n1, grad_n2 = call(
        join_kernel,
        [
            ((3 * width, width), bf16),
            ((width, width), bf16),
            ((2 * width, width), bf16),
            ((width, width), bf16),
        ],
        [],
        core,
        total,
        other,
        smem=(0,),
    )
    return (
        node_new,
        edge_new[None],
        grad_nodes,
        grad_edges[None],
        grad_e1,
        grad_e2,
        grad_n1,
        grad_n2,
    )


def solution(mesh):
    return jax.shard_map(
        local,
        mesh=mesh,
        in_specs=(
            P(("groups", "band"), None),
            P(("groups", "band"), None, None, None),
            P(("groups", "band"), None, None),
            P(("groups", "band"), None, None),
            P(("groups", "band"), None),
            P(),
            P(),
            P(),
            P(),
            P(("groups", "band"), None),
            P(("groups", "band"), None, None, None),
        ),
        out_specs=(
            P(("groups", "band"), None),
            P(("groups", "band"), None, None, None),
            P(("groups", "band"), None),
            P(("groups", "band"), None, None, None),
            P("groups", None),
            P("groups", None),
            P("groups", None),
            P("groups", None),
        ),
        check_vma=False,
    )
```

```python
import functools

import jax
import jax.numpy as jnp
from jax import lax
from jax.experimental import pallas as pl
from jax.experimental.pallas import tpu as pltpu
from jax.sharding import PartitionSpec as P

band_offsets = (0, 1, -1, 2, -2, 4, -4, 8, -8, 16, -16)
norm_eps = 1e-05
near_sets = 7
bf16 = jnp.bfloat16
f32 = jnp.float32
params = pltpu.CompilerParams(vmem_limit_bytes=48 * 1024 * 1024)


def passed_along(block, axis, distance):
    devices = range(lax.axis_size(axis))
    route = [((i - distance) % len(devices), i) for i in devices]
    return lax.ppermute(block, axis, route)


def layer_norm(inputs):
    average = jnp.mean(inputs, axis=-1, keepdims=True)
    centred = inputs - average
    inverse = lax.rsqrt(jnp.mean(centred * centred, axis=-1, keepdims=True) + norm_eps)
    return (centred * inverse, inverse)


def norm_back(normed, inverse, upstream):
    return inverse * (
        upstream
        - jnp.mean(upstream, axis=-1, keepdims=True)
        - normed * jnp.mean(upstream * normed, axis=-1, keepdims=True)
    )


def slope_of(inputs, squashed):
    return squashed * (1.0 + inputs * (1.0 - squashed))


def dot(left_side, right_side):
    return jnp.dot(left_side, right_side, preferred_element_type=f32)


def dot_rt(left_side, right_side):
    return lax.dot_general(
        left_side, right_side, (((1,), (1,)), ((), ())), preferred_element_type=f32
    )


def dot_lt(left_side, right_side):
    return lax.dot_general(
        left_side, right_side, (((0,), (0,)), ((), ())), preferred_element_type=f32
    )


def pick_table(ids, nodes):
    cap = ids.shape[1]
    down = jnp.transpose(jnp.broadcast_to(ids, (cap, cap)))
    parts = []
    for first in range(0, nodes, cap):
        wide = min(cap, nodes - first)
        lanes = lax.broadcasted_iota(jnp.int32, (cap, wide), 1) + first
        parts.append(jnp.where(down[:, :wide] == lanes, 1.0, 0.0).astype(bf16))
    return jnp.concatenate(parts, axis=1)


def sum_table(ids, nodes):
    down = lax.broadcasted_iota(jnp.int32, (nodes, ids.shape[1]), 0)
    return jnp.where(down == ids, 1.0, 0.0).astype(bf16)


def live_rows(count, cap):
    return (lax.broadcasted_iota(jnp.int32, (cap, 128), 0) < count).astype(f32)


def call(body, outs, scratch, *args, smem=()):
    spaces = [
        pl.BlockSpec(memory_space=pltpu.SMEM if i in smem else pltpu.VMEM) for i in range(len(args))
    ]
    return pl.pallas_call(
        body,
        out_shape=[jax.ShapeDtypeStruct(shape, kind) for shape, kind in outs],
        in_specs=spaces,
        out_specs=[pl.BlockSpec(memory_space=pltpu.VMEM)] * len(outs),
        scratch_shapes=[pltpu.VMEM(shape, kind) for shape, kind in scratch],
        compiler_params=params,
    )(*args)


def pick_kernel(plan, *refs):
    node_ref = refs[0]
    nodes = node_ref.shape[0]
    for id_ref, out_ref, sets in zip(refs[1 : 1 + len(plan)], refs[1 + len(plan) :], plan):
        cap = id_ref.shape[2]
        for i, k in enumerate(sets):
            hot = pick_table(id_ref[k], nodes)
            out_ref[i * cap : (i + 1) * cap, :] = dot(hot, node_ref[...]).astype(bf16)


def forward_rows(rows, x_ref, w1_ref, w2_ref, live_ref, pre_ref, normed_ref, inv_ref, msg_ref):
    pre = dot(x_ref[rows, :], w1_ref[...])
    pre_ref[rows, :] = pre
    act = (pre * jax.nn.sigmoid(pre)).astype(bf16)
    normed, inverse = layer_norm(dot(act, w2_ref[...]))
    normed_ref[rows, :] = normed
    inv_ref[rows, :] = jnp.broadcast_to(inverse, (inverse.shape[0], 128))
    msg_ref[rows, :] = (live_ref[rows, :1] * normed).astype(bf16)
    return act


def near_kernel(plan, *refs):
    sets, local_count = plan
    (edge_ref, recv_ref, send_ref, count_ref, w1_ref, w2_ref, node_ref) = refs[:7]
    remote = len(sets) - local_count
    in_refs = refs[7 : 7 + remote]
    (
        sx_ref,
        act_ref,
        pre_ref,
        normed_ref,
        inv_ref,
        live_ref,
        sum_ref,
        x_ref,
        msg_ref,
        hot_ref,
    ) = refs[7 + remote :]
    nodes, width = node_ref.shape
    cap = recv_ref.shape[2]
    for i, k in enumerate(sets):
        rows = slice(i * cap, (i + 1) * cap)
        x_ref[rows, :width] = edge_ref[k]
        if i < local_count:
            picked = dot(pick_table(send_ref[k], nodes), node_ref[...]).astype(bf16)
            sx_ref[rows, :] = picked
        else:
            picked = in_refs[i - local_count][...]
        x_ref[rows, width : 2 * width] = picked
        picked = dot(pick_table(recv_ref[k], nodes), node_ref[...])
        x_ref[rows, 2 * width :] = picked.astype(bf16)
        live_ref[rows, :] = live_rows(count_ref[0, k], cap)
        hot_ref[:, rows] = sum_table(recv_ref[k], nodes)
    half = len(sets) * cap // 2

    def step(j, carry):
        rows = pl.ds(pl.multiple_of(j * half, 16), half)
        act_ref[rows, :] = forward_rows(
            rows, x_ref, w1_ref, w2_ref, live_ref, pre_ref, normed_ref, inv_ref, msg_ref
        )
        return carry

    lax.fori_loop(0, 2, step, 0)
    sum_ref[...] = dot(hot_ref[...], msg_ref[...])


def far_kernel(plan, *refs):
    sets, pieces = plan
    count = len(pieces)
    (
        edge_ref,
        cotan_ref,
        recv_ref,
        count_ref,
        w1_ref,
        w2_ref,
        node_ref,
        ncot_ref,
        sum_ref,
        n1_ref,
        n2_ref,
    ) = refs[:11]
    sx_refs = refs[11 : 11 + count]
    gpe_refs = refs[11 + count : 11 + 2 * count]
    (
        act_ref,
        goe_ref,
        new_ref,
        node_new_ref,
        gathered_ref,
        gpn_ref,
        act_node_ref,
        gon_ref,
        gg_ref,
        x_ref,
        live_ref,
        pre_ref,
        normed_ref,
        inv_ref,
        msg_ref,
        hot_ref,
        pick_ref,
        cot_ref,
    ) = refs[11 + 2 * count :]
    nodes, width = node_ref.shape
    cap = recv_ref.shape[2]
    total = len(sets) * cap
    first = 0
    for sx_ref in sx_refs:
        x_ref[first : first + sx_ref.shape[0], width : 2 * width] = sx_ref[...]
        first += sx_ref.shape[0]
    for i, k in enumerate(sets):
        rows = slice(i * cap, (i + 1) * cap)
        x_ref[rows, :width] = edge_ref[k]
        cot_ref[rows, :] = cotan_ref[k]
        hot = pick_table(recv_ref[k], nodes)
        pick_ref[rows, :] = hot
        x_ref[rows, 2 * width :] = dot(hot, node_ref[...]).astype(bf16)
        live_ref[rows, :] = live_rows(count_ref[0, k], cap)
        hot_ref[:, rows] = sum_table(recv_ref[k], nodes)
    half = total // 2

    def ahead(j, carry):
        rows = pl.ds(pl.multiple_of(j * half, 16), half)
        act = forward_rows(
            rows, x_ref, w1_ref, w2_ref, live_ref, pre_ref, normed_ref, inv_ref, msg_ref
        )
        act_ref[rows, :] = act
        message = live_ref[rows, :1] * normed_ref[rows, :]
        new_ref[rows, :] = (x_ref[rows, :width].astype(f32) + message).astype(bf16)
        return carry

    lax.fori_loop(0, 2, ahead, 0)
    gathered = (sum_ref[...] + dot(hot_ref[...], msg_ref[...])).astype(bf16)
    gathered_ref[...] = gathered

    pre = dot(node_ref[...], n1_ref[:width, :]) + dot(gathered, n1_ref[width:, :])
    squashed = jax.nn.sigmoid(pre)
    act_node = (pre * squashed).astype(bf16)
    act_node_ref[...] = act_node
    normed, inverse = layer_norm(dot(act_node, n2_ref[...]))
    node_new_ref[...] = (node_ref[...].astype(f32) + normed).astype(bf16)
    gon = norm_back(normed, inverse, ncot_ref[...].astype(f32)).astype(bf16)
    gon_ref[...] = gon
    gpn = (dot_rt(gon, n2_ref[...]) * slope_of(pre, squashed)).astype(bf16)
    gpn_ref[...] = gpn
    gg_ref[...] = dot_rt(gpn, n1_ref[width:, :]).astype(bf16)

    first = 0
    for gpe_ref in gpe_refs:
        size = gpe_ref.shape[0]
        rows = slice(first, first + size)
        upstream = cot_ref[rows, :].astype(f32) + dot(pick_ref[rows, :], gg_ref[...])
        upstream = live_ref[rows, :1] * upstream
        goe = norm_back(normed_ref[rows, :], inv_ref[rows, :1], upstream).astype(bf16)
        goe_ref[rows, :] = goe
        pre = pre_ref[rows, :]
        slope = slope_of(pre, jax.nn.sigmoid(pre))
        gpe_ref[...] = (dot_rt(goe, w2_ref[...]) * slope).astype(bf16)
        first += size


def back_kernel(plan, *refs):
    near, local_count = plan
    (
        cotan_ref,
        recv_ref,
        me_ref,
        w2_ref,
        live_ref,
        pre_ref,
        normed_ref,
        inv_ref,
        node_ref,
        gathered_ref,
        gpn_ref,
        act_node_ref,
        gon_ref,
        gg_ref,
        keep_ref,
        sent_ref,
        goe_ref,
        local_ref,
    ) = refs[:18]
    gpe_refs, (gpe_ref, pick_ref, block_ref) = refs[18:-3], refs[-3:]
    nodes, width = node_ref.shape
    cap = recv_ref.shape[2]
    for i, k in enumerate(near):
        pick_ref[i * cap : (i + 1) * cap, :] = pick_table(recv_ref[k], nodes)
    half = len(near) * cap // 2
    for j in range(2):
        rows = slice(j * half, (j + 1) * half)
        cot = jnp.concatenate([cotan_ref[k] for k in near])[rows, :].astype(f32)
        upstream = live_ref[rows, :1] * (cot + dot(pick_ref[rows, :], gg_ref[...]))
        goe = norm_back(normed_ref[rows, :], inv_ref[rows, :1], upstream).astype(bf16)
        goe_ref[rows, :] = goe
        pre = pre_ref[rows, :]
        slope = slope_of(pre, jax.nn.sigmoid(pre))
        gpe_ref[rows, :] = (dot_rt(goe, w2_ref[...]) * slope).astype(bf16)
    local_ref[...] = gpe_ref[: local_count * cap, :]
    for j, out_ref in enumerate(gpe_refs):
        i = local_count + j
        out_ref[...] = gpe_ref[i * cap : (i + 1) * cap, :]
    put = functools.partial(put_block, me_ref, block_ref, keep_ref, sent_ref)
    put(0, node_ref[...], gpn_ref[...])
    put(1, gathered_ref[...], gpn_ref[...])
    put(2, act_node_ref[...], gon_ref[...])


def put_block(me_ref, block_ref, keep_ref, sent_ref, index, left_side, right_side):
    core = lax.rem(me_ref[0], 2)
    half = block_ref.shape[0] // 2
    block_ref[...] = dot_lt(left_side, right_side)
    keep_ref[index] = block_ref[pl.ds(pl.multiple_of(core * half, half), half), :]
    other = block_ref[pl.ds(pl.multiple_of((1 - core) * half, half), half), :]
    sent_ref[index] = other.astype(bf16)


def stack_into(out_ref, refs):
    first = 0
    for ref in refs:
        out_ref[first : first + ref.shape[0], :] = ref[...]
        first += ref.shape[0]


def weight_kernel(plan, *refs):
    order, sx_count, gpe_count, act_count = plan
    edge_ref, recv_ref, me_ref, node_ref = refs[:4]
    refs = refs[4:]
    sx_refs, refs = refs[:sx_count], refs[sx_count:]
    gpe_refs, refs = refs[:gpe_count], refs[gpe_count:]
    act_refs, refs = refs[:act_count], refs[act_count:]
    goe_refs, refs = refs[:act_count], refs[act_count:]
    keep_ref, sent_ref, rsum_ref, x_ref, sx_ref, gpe_ref, act_ref, goe_ref, hot_ref, block_ref = refs
    nodes = node_ref.shape[0]
    cap = recv_ref.shape[2]
    for i, k in enumerate(order):
        rows = slice(i * cap, (i + 1) * cap)
        x_ref[rows, :] = edge_ref[k]
        hot_ref[:, rows] = sum_table(recv_ref[k], nodes)
    stack_into(sx_ref, sx_refs)
    stack_into(gpe_ref, gpe_refs)
    stack_into(act_ref, act_refs)
    stack_into(goe_ref, goe_refs)
    recv_sum = dot(hot_ref[...], gpe_ref[...]).astype(bf16)
    rsum_ref[...] = recv_sum
    put = functools.partial(put_block, me_ref, block_ref, keep_ref, sent_ref)
    put(0, x_ref[...], gpe_ref[...])
    put(1, sx_ref[...], gpe_ref[...])
    put(2, node_ref[...], recv_sum)
    put(3, act_ref[...], goe_ref[...])


def edge_kernel(plan, *refs):
    near, far, gpe_count = plan
    (edge_ref, cotan_ref, w1_ref, wn_ref, live_ref, normed_ref, new_far_ref, ncot_ref, gpn_ref, rsum_ref) = refs[:10]
    gpe_refs = refs[10 : 10 + gpe_count]
    new_ref, gedge_ref, base_ref, gpe_ref = refs[10 + gpe_count :]
    width = w1_ref.shape[1]
    cap = edge_ref.shape[1]
    stack_into(gpe_ref, gpe_refs)
    base_ref[...] = (
        ncot_ref[...].astype(f32)
        + dot_rt(gpn_ref[...], wn_ref[:width, :])
        + dot_rt(rsum_ref[...], w1_ref[2 * width :, :])
    )
    for i, k in enumerate(near + far):
        rows = slice(i * cap, (i + 1) * cap)
        grad = cotan_ref[k].astype(f32) + dot_rt(gpe_ref[rows, :], w1_ref[:width, :])
        gedge_ref[k] = grad.astype(bf16)
        if i < len(near):
            message = live_ref[rows, :1] * normed_ref[rows, :]
            new_ref[k] = (edge_ref[k].astype(f32) + message).astype(bf16)
        else:
            first = (i - len(near)) * cap
            new_ref[k] = new_far_ref[first : first + cap, :]


def final_kernel(plan, *refs):
    base_ref, w1_ref = refs[:2]
    id_refs = refs[2 : 2 + len(plan)]
    row_refs = refs[2 + len(plan) : 2 + 2 * len(plan)]
    out_ref, hot_ref, rows_ref = refs[2 + 2 * len(plan) :]
    nodes, width = base_ref.shape
    cap = id_refs[0].shape[2]
    at = 0
    for id_ref, sets in zip(id_refs, plan):
        for k in sets:
            hot_ref[:, at : at + cap] = sum_table(id_ref[k], nodes)
            at += cap
    stack_into(rows_ref, row_refs)
    send_sum = dot(hot_ref[...], rows_ref[...]).astype(bf16)
    grad = base_ref[...] + dot_rt(send_sum, w1_ref[width : 2 * width, :])
    out_ref[...] = grad.astype(bf16)


def place(me_ref, stride, members):
    return lax.rem(lax.div(me_ref[0], stride), members)


def add_kernel(plan, *refs):
    came, stride, members = plan
    me_ref, keep_ref = refs[:2]
    arr_refs, out_refs = refs[2 : 2 + came], refs[2 + came :]
    size = keep_ref.shape[1] // members
    here = place(me_ref, stride, members)
    for j, out_ref in enumerate(out_refs):
        at = lax.rem(here + j, members) * size
        rows = pl.ds(pl.multiple_of(at, size), size)
        piece = keep_ref[:, rows, :]
        for arr_ref in arr_refs:
            piece += arr_ref[:, rows, :].astype(f32)
        out_ref[...] = piece.astype(out_ref.dtype)


def gather_kernel(plan, *refs):
    stride, members = plan
    me_ref, piece_refs, out_ref = refs[0], refs[1:-1], refs[-1]
    size = piece_refs[0].shape[1]
    here = place(me_ref, stride, members)
    for j, piece_ref in enumerate(piece_refs):
        at = lax.rem(here + members - j, members) * size
        out_ref[:, pl.ds(pl.multiple_of(at, size), size), :] = piece_ref[...]


def join_kernel(plan, *refs):
    members, blocks = plan
    me_ref = refs[0]
    piece_refs, other_refs = refs[1 : 1 + members], refs[1 + members : 1 + 2 * members]
    out_refs = refs[1 + 2 * members :]
    size = piece_refs[0].shape[1]
    core = lax.rem(me_ref[0], 2)
    here = place(me_ref, 2, members)
    for index, (which, block) in enumerate(blocks):
        first = 2 * block * members * size
        for side, side_refs in ((core, piece_refs), (1 - core, other_refs)):
            for j, piece_ref in enumerate(side_refs):
                at = first + (side * members + lax.rem(here + members - j, members)) * size
                rows = pl.ds(pl.multiple_of(at, size), size)
                out_refs[which][rows, :] = piece_ref[index]


def in_group(block, axis, stride, members, step):
    route = []
    for i in range(lax.axis_size(axis)):
        at = (i // stride) % members
        route.append((i, i + ((at + step) % members - at) * stride))
    return lax.ppermute(block, axis, route)


def split_of(bands):
    chips = bands // 2
    first = 1
    while first * first * 4 <= chips:
        first *= 2
    return first, chips // first


def reduce_over_chips(me, keep, sent):
    bands = lax.axis_size("band")
    first, second = split_of(bands)
    count, rows, width = keep.shape
    arrived = [in_group(sent, "band", 1, 2, 1)]
    for stride, members in ((2, first), (2 * first, second)):
        rows //= members
        outs = call(
            functools.partial(add_kernel, (len(arrived), stride, members)),
            [((count, rows, width), f32)] + [((count, rows, width), bf16)] * (members - 1),
            [],
            me,
            keep,
            *arrived,
            smem=(0,),
        )
        keep = outs[0]
        arrived = [
            in_group(out, "band", stride, members, j + 1) for j, out in enumerate(outs[1:])
        ]
    (piece,) = call(
        functools.partial(add_kernel, (len(arrived), 1, 1)),
        [((count, rows, width), bf16)],
        [],
        me,
        keep,
        *arrived,
        smem=(0,),
    )
    return piece


def gather_over_chips(me, piece, blocks, shapes):
    bands = lax.axis_size("band")
    first, second = split_of(bands)
    count, rows, width = piece.shape
    pieces = [piece] + [
        in_group(piece, "band", 2 * first, second, j) for j in range(1, second)
    ]
    (mine,) = call(
        functools.partial(gather_kernel, (2 * first, second)),
        [((count, rows * second, width), bf16)],
        [],
        me,
        *pieces,
        smem=(0,),
    )
    pieces = [mine] + [in_group(mine, "band", 2, first, j) for j in range(1, first)]
    others = [in_group(one, "band", 1, 2, 1) for one in pieces]
    return call(
        functools.partial(join_kernel, (first, blocks)),
        [(shape, bf16) for shape in shapes],
        [],
        me,
        *pieces,
        *others,
        smem=(0,),
    )


def reduce_whole(keep, sent):
    bands = lax.axis_size("band")
    chips = [[i for i in range(bands) if i % 2 == c] for c in range(2)]
    total = keep + in_group(sent, "band", 1, 2, 1).astype(f32)
    total = lax.psum(total.astype(bf16), "band", axis_index_groups=chips)
    other = in_group(total, "band", 1, 2, 1)
    core = lax.axis_index("band") % 2
    low, high = jnp.where(core == 0, total, other), jnp.where(core == 0, other, total)
    return jnp.concatenate([low, high], axis=1)


def local(
    node_latent,
    edge_latent,
    recv_slot,
    send_slot,
    edge_count,
    edge_first,
    edge_second,
    node_first,
    node_second,
    node_cotan,
    edge_cotan,
):
    bands = lax.axis_size("band")
    nodes, width = node_latent.shape
    sets, cap = edge_latent.shape[1:3]
    edges, cotan = edge_latent[0], edge_cotan[0]
    recv_ids, send_ids = recv_slot.reshape(sets, 1, cap), send_slot.reshape(sets, 1, cap)
    me = lax.axis_index("band").astype(jnp.int32).reshape(1)

    def step_of(k):
        return band_offsets[k] % bands

    def reach(k):
        return min(step_of(k), bands - step_of(k))

    ordered = sorted(range(sets), key=lambda k: (reach(k), step_of(k)))
    near, far = tuple(ordered[:near_sets]), tuple(ordered[near_sets:])
    local_count = sum(step_of(k) == 0 for k in near)
    near_steps = [step_of(k) for k in near[local_count:]]
    far_steps = list(dict.fromkeys(step_of(k) for k in far))
    steps = near_steps + far_steps
    near_plan = tuple((k,) for k in near[local_count:])
    far_plan = tuple(tuple(k for k in far if step_of(k) == d) for d in far_steps)
    far = sum(far_plan, ())

    ids = [passed_along(send_ids, "band", -d) for d in steps]
    picked = call(
        functools.partial(pick_kernel, near_plan + far_plan),
        [((len(piece) * cap, width), bf16) for piece in near_plan + far_plan],
        [],
        node_latent,
        *ids,
    )
    sx = [passed_along(block, "band", d) for block, d in zip(picked, steps)]
    sx_near, sx_far = sx[: len(near_plan)], sx[len(near_plan) :]

    local_rows, near_rows, far_rows = local_count * cap, len(near) * cap, len(far) * cap
    sx_local, act_near, pre, normed, inverse, live, part_sum = call(
        functools.partial(near_kernel, (near, local_count)),
        [
            ((local_rows, width), bf16),
            ((near_rows, width), bf16),
            ((near_rows, width), f32),
            ((near_rows, width), f32),
            ((near_rows, 128), f32),
            ((near_rows, 128), f32),
            ((nodes, width), f32),
        ],
        [
            ((near_rows, 3 * width), bf16),
            ((near_rows, width), bf16),
            ((nodes, near_rows), bf16),
        ],
        edges,
        recv_ids,
        send_ids,
        edge_count,
        edge_first,
        edge_second,
        node_latent,
        *sx_near,
        smem=(3,),
    )

    outs = call(
        functools.partial(far_kernel, (far, far_plan)),
        [((len(piece) * cap, width), bf16) for piece in far_plan]
        + [((far_rows, width), bf16)] * 3
        + [((nodes, width), bf16)] * 6,
        [
            ((far_rows, 3 * width), bf16),
            ((far_rows, 128), f32),
            ((far_rows, width), f32),
            ((far_rows, width), f32),
            ((far_rows, 128), f32),
            ((far_rows, width), bf16),
            ((nodes, far_rows), bf16),
            ((far_rows, nodes), bf16),
            ((far_rows, width), bf16),
        ],
        edges,
        cotan,
        recv_ids,
        edge_count,
        edge_first,
        edge_second,
        node_latent,
        node_cotan,
        part_sum,
        node_first,
        node_second,
        *sx_far,
        smem=(3,),
    )
    gpe_far, outs = list(outs[: len(far_plan)]), outs[len(far_plan) :]
    act_far, goe_far, new_far, node_new, gathered, gpn, act_node, gon, gg = outs
    back_far = [passed_along(block, "band", -d) for block, d in zip(gpe_far, far_steps)]

    half = (width // 2, width)
    outs = call(
        functools.partial(back_kernel, (near, local_count)),
        [
            ((3, *half), f32),
            ((3, *half), bf16),
            ((near_rows, width), bf16),
            ((local_rows, width), bf16),
        ]
        + [((cap, width), bf16)] * len(near_steps),
        [((near_rows, width), bf16), ((near_rows, nodes), bf16), ((width, width), f32)],
        cotan,
        recv_ids,
        me,
        edge_second,
        live,
        pre,
        normed,
        inverse,
        node_latent,
        gathered,
        gpn,
        act_node,
        gon,
        gg,
        smem=(2,),
    )
    keep_node, sent_node, goe_near, gpe_local = outs[:4]
    gpe_near = list(outs[4:])
    back_near = [passed_along(block, "band", -d) for block, d in zip(gpe_near, near_steps)]

    order = near + far
    gpe = [gpe_local] + gpe_near + gpe_far
    sx_all = [sx_local] + sx_near + sx_far
    total = sets * cap
    keep_edge, sent_edge, recv_sum = call(
        functools.partial(weight_kernel, (order, len(sx_all), len(gpe), 2)),
        [((4, *half), f32), ((4, *half), bf16), ((nodes, width), bf16)],
        [((total, width), bf16)] * 5 + [((nodes, total), bf16), ((width, width), f32)],
        edges,
        recv_ids,
        me,
        node_latent,
        *sx_all,
        *gpe,
        act_near,
        act_far,
        goe_near,
        goe_far,
        smem=(2,),
    )

    first, second = split_of(bands)
    if width // 2 % (16 * first * second) == 0:
        piece_node = reduce_over_chips(me, keep_node, sent_node)
        piece_edge = reduce_over_chips(me, keep_edge, sent_edge)
        grad_n1, grad_n2 = gather_over_chips(
            me, piece_node, ((0, 0), (0, 1), (1, 0)), [(2 * width, width), (width, width)]
        )
        grad_e1, grad_e2 = gather_over_chips(
            me, piece_edge, ((0, 0), (0, 1), (0, 2), (1, 0)), [(3 * width, width), (width, width)]
        )
    else:
        whole = reduce_whole(keep_node, sent_node)
        grad_n1, grad_n2 = whole[:2].reshape(2 * width, width), whole[2]
        whole = reduce_whole(keep_edge, sent_edge)
        grad_e1, grad_e2 = whole[:3].reshape(3 * width, width), whole[3]

    edge_new, grad_edges, base = call(
        functools.partial(edge_kernel, (near, far, len(gpe))),
        [((sets, cap, width), bf16), ((sets, cap, width), bf16), ((nodes, width), f32)],
        [((total, width), bf16)],
        edges,
        cotan,
        edge_first,
        node_first,
        live,
        normed,
        new_far,
        node_cotan,
        gpn,
        recv_sum,
        *gpe,
    )
    (grad_nodes,) = call(
        functools.partial(final_kernel, (near[:local_count],) + near_plan + far_plan),
        [((nodes, width), bf16)],
        [((nodes, total), bf16), ((total, width), bf16)],
        base,
        edge_first,
        send_ids,
        *ids,
        gpe_local,
        *back_near,
        *back_far,
    )
    return (
        node_new,
        edge_new[None],
        grad_nodes,
        grad_edges[None],
        grad_e1,
        grad_e2,
        grad_n1,
        grad_n2,
    )


def solution(mesh):
    return jax.shard_map(
        local,
        mesh=mesh,
        in_specs=(
            P(("groups", "band"), None),
            P(("groups", "band"), None, None, None),
            P(("groups", "band"), None, None),
            P(("groups", "band"), None, None),
            P(("groups", "band"), None),
            P(),
            P(),
            P(),
            P(),
            P(("groups", "band"), None),
            P(("groups", "band"), None, None, None),
        ),
        out_specs=(
            P(("groups", "band"), None),
            P(("groups", "band"), None, None, None),
            P(("groups", "band"), None),
            P(("groups", "band"), None, None, None),
            P("groups", None),
            P("groups", None),
            P("groups", None),
            P("groups", None),
        ),
        check_vma=False,
    )
```

```python
import functools

import jax
import jax.numpy as jnp
from jax import lax
from jax.experimental import pallas as pl
from jax.experimental.pallas import tpu as pltpu
from jax.sharding import PartitionSpec as P

band_offsets = (0, 1, -1, 2, -2, 4, -4, 8, -8, 16, -16)
norm_eps = 1e-05
near_sets = 7
bf16 = jnp.bfloat16
f32 = jnp.float32
small, large = 24 * 1024 * 1024, 24 * 1024 * 1024


def passed_along(block, axis, distance):
    devices = range(lax.axis_size(axis))
    route = [((i - distance) % len(devices), i) for i in devices]
    return lax.ppermute(block, axis, route)


def layer_norm(inputs):
    average = jnp.mean(inputs, axis=-1, keepdims=True)
    centred = inputs - average
    inverse = lax.rsqrt(jnp.mean(centred * centred, axis=-1, keepdims=True) + norm_eps)
    return (centred * inverse, inverse)


def norm_back(normed, inverse, upstream):
    return inverse * (
        upstream
        - jnp.mean(upstream, axis=-1, keepdims=True)
        - normed * jnp.mean(upstream * normed, axis=-1, keepdims=True)
    )


def slope_of(inputs, squashed):
    return squashed * (1.0 + inputs * (1.0 - squashed))


def dot(left_side, right_side):
    return jnp.dot(left_side, right_side, preferred_element_type=f32)


def dot_rt(left_side, right_side):
    return lax.dot_general(
        left_side, right_side, (((1,), (1,)), ((), ())), preferred_element_type=f32
    )


def dot_lt(left_side, right_side):
    return lax.dot_general(
        left_side, right_side, (((0,), (0,)), ((), ())), preferred_element_type=f32
    )


def pick_table(ids, nodes):
    cap = ids.shape[1]
    down = jnp.transpose(jnp.broadcast_to(ids, (cap, cap)))
    parts = []
    for first in range(0, nodes, cap):
        wide = min(cap, nodes - first)
        lanes = lax.broadcasted_iota(jnp.int32, (cap, wide), 1) + first
        parts.append(jnp.where(down[:, :wide] == lanes, 1.0, 0.0).astype(bf16))
    return jnp.concatenate(parts, axis=1)


def sum_table(ids, nodes):
    down = lax.broadcasted_iota(jnp.int32, (nodes, ids.shape[1]), 0)
    return jnp.where(down == ids, 1.0, 0.0).astype(bf16)


def live_rows(count, cap):
    return (lax.broadcasted_iota(jnp.int32, (cap, 128), 0) < count).astype(f32)


def call(body, outs, scratch, *args, smem=(), after=(), vmem=small):
    spaces = [
        pl.BlockSpec(memory_space=pltpu.SMEM if i in smem else pltpu.VMEM) for i in range(len(args))
    ]
    spaces += [pl.BlockSpec(memory_space=pl.ANY)] * len(after)

    def kernel(*refs):
        body(*refs[: len(args)], *refs[len(args) + len(after) :])

    return pl.pallas_call(
        kernel,
        out_shape=[jax.ShapeDtypeStruct(shape, kind) for shape, kind in outs],
        in_specs=spaces,
        out_specs=[pl.BlockSpec(memory_space=pltpu.VMEM)] * len(outs),
        scratch_shapes=[pltpu.VMEM(shape, kind) for shape, kind in scratch],
        compiler_params=pltpu.CompilerParams(vmem_limit_bytes=vmem),
        cost_estimate=pl.CostEstimate(flops=1, bytes_accessed=1, transcendentals=0),
    )(*args, *after)


def pick_kernel(plan, *refs):
    node_ref = refs[0]
    nodes = node_ref.shape[0]
    for id_ref, out_ref, sets in zip(refs[1 : 1 + len(plan)], refs[1 + len(plan) :], plan):
        cap = id_ref.shape[2]
        for i, k in enumerate(sets):
            hot = pick_table(id_ref[k], nodes)
            out_ref[i * cap : (i + 1) * cap, :] = dot(hot, node_ref[...]).astype(bf16)


def forward_rows(rows, x_ref, w1_ref, w2_ref, live_ref, pre_ref, normed_ref, inv_ref, msg_ref):
    pre = dot(x_ref[rows, :], w1_ref[...])
    pre_ref[rows, :] = pre
    act = (pre * jax.nn.sigmoid(pre)).astype(bf16)
    normed, inverse = layer_norm(dot(act, w2_ref[...]))
    normed_ref[rows, :] = normed
    inv_ref[rows, :] = jnp.broadcast_to(inverse, (inverse.shape[0], 128))
    msg_ref[rows, :] = (live_ref[rows, :1] * normed).astype(bf16)
    return act


def near_kernel(plan, *refs):
    sets, local_count = plan
    (edge_ref, recv_ref, send_ref, count_ref, w1_ref, w2_ref, node_ref) = refs[:7]
    remote = len(sets) - local_count
    in_refs = refs[7 : 7 + remote]
    (
        sx_ref,
        act_ref,
        pre_ref,
        normed_ref,
        inv_ref,
        live_ref,
        sum_ref,
        x_ref,
        msg_ref,
        hot_ref,
    ) = refs[7 + remote :]
    nodes, width = node_ref.shape
    cap = recv_ref.shape[2]
    for i, k in enumerate(sets):
        rows = slice(i * cap, (i + 1) * cap)
        x_ref[rows, :width] = edge_ref[k]
        if i < local_count:
            picked = dot(pick_table(send_ref[k], nodes), node_ref[...]).astype(bf16)
            sx_ref[rows, :] = picked
        else:
            picked = in_refs[i - local_count][...]
        x_ref[rows, width : 2 * width] = picked
        picked = dot(pick_table(recv_ref[k], nodes), node_ref[...])
        x_ref[rows, 2 * width :] = picked.astype(bf16)
        live_ref[rows, :] = live_rows(count_ref[0, k], cap)
        hot_ref[:, rows] = sum_table(recv_ref[k], nodes)
    half = len(sets) * cap // 2

    def step(j, carry):
        rows = pl.ds(pl.multiple_of(j * half, 16), half)
        act_ref[rows, :] = forward_rows(
            rows, x_ref, w1_ref, w2_ref, live_ref, pre_ref, normed_ref, inv_ref, msg_ref
        )
        return carry

    lax.fori_loop(0, 2, step, 0)
    sum_ref[...] = dot(hot_ref[...], msg_ref[...])


def far_kernel(plan, *refs):
    sets, pieces = plan
    count = len(pieces)
    (
        edge_ref,
        cotan_ref,
        recv_ref,
        count_ref,
        w1_ref,
        w2_ref,
        node_ref,
        ncot_ref,
        sum_ref,
        n1_ref,
        n2_ref,
    ) = refs[:11]
    sx_refs = refs[11 : 11 + count]
    gpe_refs = refs[11 + count : 11 + 2 * count]
    (
        act_ref,
        goe_ref,
        new_ref,
        node_new_ref,
        gathered_ref,
        gpn_ref,
        act_node_ref,
        gon_ref,
        gg_ref,
        x_ref,
        live_ref,
        pre_ref,
        normed_ref,
        inv_ref,
        msg_ref,
        hot_ref,
        pick_ref,
        cot_ref,
    ) = refs[11 + 2 * count :]
    nodes, width = node_ref.shape
    cap = recv_ref.shape[2]
    total = len(sets) * cap
    first = 0
    for sx_ref in sx_refs:
        x_ref[first : first + sx_ref.shape[0], width : 2 * width] = sx_ref[...]
        first += sx_ref.shape[0]
    for i, k in enumerate(sets):
        rows = slice(i * cap, (i + 1) * cap)
        x_ref[rows, :width] = edge_ref[k]
        cot_ref[rows, :] = cotan_ref[k]
        hot = pick_table(recv_ref[k], nodes)
        pick_ref[rows, :] = hot
        x_ref[rows, 2 * width :] = dot(hot, node_ref[...]).astype(bf16)
        live_ref[rows, :] = live_rows(count_ref[0, k], cap)
        hot_ref[:, rows] = sum_table(recv_ref[k], nodes)
    half = total // 2

    def ahead(j, carry):
        rows = pl.ds(pl.multiple_of(j * half, 16), half)
        act = forward_rows(
            rows, x_ref, w1_ref, w2_ref, live_ref, pre_ref, normed_ref, inv_ref, msg_ref
        )
        act_ref[rows, :] = act
        message = live_ref[rows, :1] * normed_ref[rows, :]
        new_ref[rows, :] = (x_ref[rows, :width].astype(f32) + message).astype(bf16)
        return carry

    lax.fori_loop(0, 2, ahead, 0)
    gathered = (sum_ref[...] + dot(hot_ref[...], msg_ref[...])).astype(bf16)
    gathered_ref[...] = gathered

    pre = dot(node_ref[...], n1_ref[:width, :]) + dot(gathered, n1_ref[width:, :])
    squashed = jax.nn.sigmoid(pre)
    act_node = (pre * squashed).astype(bf16)
    act_node_ref[...] = act_node
    normed, inverse = layer_norm(dot(act_node, n2_ref[...]))
    node_new_ref[...] = (node_ref[...].astype(f32) + normed).astype(bf16)
    gon = norm_back(normed, inverse, ncot_ref[...].astype(f32)).astype(bf16)
    gon_ref[...] = gon
    gpn = (dot_rt(gon, n2_ref[...]) * slope_of(pre, squashed)).astype(bf16)
    gpn_ref[...] = gpn
    gg_ref[...] = dot_rt(gpn, n1_ref[width:, :]).astype(bf16)

    first = 0
    for gpe_ref in gpe_refs:
        size = gpe_ref.shape[0]
        rows = slice(first, first + size)
        upstream = cot_ref[rows, :].astype(f32) + dot(pick_ref[rows, :], gg_ref[...])
        upstream = live_ref[rows, :1] * upstream
        goe = norm_back(normed_ref[rows, :], inv_ref[rows, :1], upstream).astype(bf16)
        goe_ref[rows, :] = goe
        pre = pre_ref[rows, :]
        slope = slope_of(pre, jax.nn.sigmoid(pre))
        gpe_ref[...] = (dot_rt(goe, w2_ref[...]) * slope).astype(bf16)
        first += size


def back_kernel(plan, *refs):
    near, local_count = plan
    (
        cotan_ref,
        recv_ref,
        w2_ref,
        live_ref,
        pre_ref,
        normed_ref,
        inv_ref,
        gg_ref,
        goe_ref,
        local_ref,
    ) = refs[:10]
    gpe_refs, (gpe_ref, pick_ref) = refs[10:-2], refs[-2:]
    nodes = gg_ref.shape[0]
    cap = recv_ref.shape[2]
    for i, k in enumerate(near):
        pick_ref[i * cap : (i + 1) * cap, :] = pick_table(recv_ref[k], nodes)
    half = len(near) * cap // 2
    for j in range(2):
        rows = slice(j * half, (j + 1) * half)
        cot = jnp.concatenate([cotan_ref[k] for k in near])[rows, :].astype(f32)
        upstream = live_ref[rows, :1] * (cot + dot(pick_ref[rows, :], gg_ref[...]))
        goe = norm_back(normed_ref[rows, :], inv_ref[rows, :1], upstream).astype(bf16)
        goe_ref[rows, :] = goe
        pre = pre_ref[rows, :]
        slope = slope_of(pre, jax.nn.sigmoid(pre))
        gpe_ref[rows, :] = (dot_rt(goe, w2_ref[...]) * slope).astype(bf16)
    local_ref[...] = gpe_ref[: local_count * cap, :]
    for j, out_ref in enumerate(gpe_refs):
        i = local_count + j
        out_ref[...] = gpe_ref[i * cap : (i + 1) * cap, :]


def node_weight_kernel(me_ref, node_ref, gathered_ref, gpn_ref, act_node_ref, gon_ref, keep_ref, sent_ref, block_ref):
    put = functools.partial(put_block, me_ref, block_ref, keep_ref, sent_ref)
    put(0, node_ref[...], gpn_ref[...])
    put(1, gathered_ref[...], gpn_ref[...])
    put(2, act_node_ref[...], gon_ref[...])


def put_block(me_ref, block_ref, keep_ref, sent_ref, index, left_side, right_side):
    core = lax.rem(me_ref[0], 2)
    half = block_ref.shape[0] // 2
    block_ref[...] = dot_lt(left_side, right_side)
    keep_ref[index] = block_ref[pl.ds(pl.multiple_of(core * half, half), half), :]
    other = block_ref[pl.ds(pl.multiple_of((1 - core) * half, half), half), :]
    sent_ref[index] = other.astype(bf16)


def stack_into(out_ref, refs):
    first = 0
    for ref in refs:
        out_ref[first : first + ref.shape[0], :] = ref[...]
        first += ref.shape[0]


def weight_kernel(plan, *refs):
    order, sx_count, gpe_count, act_count = plan
    edge_ref, recv_ref, me_ref, node_ref = refs[:4]
    refs = refs[4:]
    sx_refs, refs = refs[:sx_count], refs[sx_count:]
    gpe_refs, refs = refs[:gpe_count], refs[gpe_count:]
    act_refs, refs = refs[:act_count], refs[act_count:]
    goe_refs, refs = refs[:act_count], refs[act_count:]
    keep_ref, sent_ref, rsum_ref, x_ref, sx_ref, gpe_ref, act_ref, goe_ref, hot_ref, block_ref = refs
    nodes = node_ref.shape[0]
    cap = recv_ref.shape[2]
    for i, k in enumerate(order):
        rows = slice(i * cap, (i + 1) * cap)
        x_ref[rows, :] = edge_ref[k]
        hot_ref[:, rows] = sum_table(recv_ref[k], nodes)
    stack_into(sx_ref, sx_refs)
    stack_into(gpe_ref, gpe_refs)
    stack_into(act_ref, act_refs)
    stack_into(goe_ref, goe_refs)
    recv_sum = dot(hot_ref[...], gpe_ref[...]).astype(bf16)
    rsum_ref[...] = recv_sum
    put = functools.partial(put_block, me_ref, block_ref, keep_ref, sent_ref)
    put(0, x_ref[...], gpe_ref[...])
    put(1, sx_ref[...], gpe_ref[...])
    put(2, node_ref[...], recv_sum)
    put(3, act_ref[...], goe_ref[...])


def edge_kernel(plan, *refs):
    near, far, gpe_count = plan
    (edge_ref, cotan_ref, w1_ref, wn_ref, live_ref, normed_ref, new_far_ref, ncot_ref, gpn_ref, rsum_ref) = refs[:10]
    gpe_refs = refs[10 : 10 + gpe_count]
    new_ref, gedge_ref, base_ref, gpe_ref = refs[10 + gpe_count :]
    width = w1_ref.shape[1]
    cap = edge_ref.shape[1]
    stack_into(gpe_ref, gpe_refs)
    base_ref[...] = (
        ncot_ref[...].astype(f32)
        + dot_rt(gpn_ref[...], wn_ref[:width, :])
        + dot_rt(rsum_ref[...], w1_ref[2 * width :, :])
    )
    for i, k in enumerate(near + far):
        rows = slice(i * cap, (i + 1) * cap)
        grad = cotan_ref[k].astype(f32) + dot_rt(gpe_ref[rows, :], w1_ref[:width, :])
        gedge_ref[k] = grad.astype(bf16)
        if i < len(near):
            message = live_ref[rows, :1] * normed_ref[rows, :]
            new_ref[k] = (edge_ref[k].astype(f32) + message).astype(bf16)
        else:
            first = (i - len(near)) * cap
            new_ref[k] = new_far_ref[first : first + cap, :]


def final_kernel(plan, *refs):
    base_ref, w1_ref = refs[:2]
    id_refs = refs[2 : 2 + len(plan)]
    row_refs = refs[2 + len(plan) : 2 + 2 * len(plan)]
    out_ref, hot_ref, rows_ref = refs[2 + 2 * len(plan) :]
    nodes, width = base_ref.shape
    cap = id_refs[0].shape[2]
    at = 0
    for id_ref, sets in zip(id_refs, plan):
        for k in sets:
            hot_ref[:, at : at + cap] = sum_table(id_ref[k], nodes)
            at += cap
    stack_into(rows_ref, row_refs)
    send_sum = dot(hot_ref[...], rows_ref[...]).astype(bf16)
    grad = base_ref[...] + dot_rt(send_sum, w1_ref[width : 2 * width, :])
    out_ref[...] = grad.astype(bf16)


def place(me_ref, stride, members):
    return lax.rem(lax.div(me_ref[0], stride), members)


def add_kernel(plan, *refs):
    came, stride, members = plan
    me_ref, keep_ref = refs[:2]
    arr_refs, out_refs = refs[2 : 2 + came], refs[2 + came :]
    size = keep_ref.shape[1] // members
    here = place(me_ref, stride, members)
    for j, out_ref in enumerate(out_refs):
        at = lax.rem(here + j, members) * size
        rows = pl.ds(pl.multiple_of(at, size), size)
        piece = keep_ref[:, rows, :]
        for arr_ref in arr_refs:
            piece += arr_ref[:, rows, :].astype(f32)
        out_ref[...] = piece.astype(out_ref.dtype)


def gather_kernel(plan, *refs):
    stride, members = plan
    me_ref, piece_refs, out_ref = refs[0], refs[1:-1], refs[-1]
    size = piece_refs[0].shape[1]
    here = place(me_ref, stride, members)
    for j, piece_ref in enumerate(piece_refs):
        at = lax.rem(here + members - j, members) * size
        out_ref[:, pl.ds(pl.multiple_of(at, size), size), :] = piece_ref[...]


def join_kernel(plan, *refs):
    members, blocks = plan
    me_ref = refs[0]
    piece_refs, other_refs = refs[1 : 1 + members], refs[1 + members : 1 + 2 * members]
    out_refs = refs[1 + 2 * members :]
    size = piece_refs[0].shape[1]
    core = lax.rem(me_ref[0], 2)
    here = place(me_ref, 2, members)
    for index, (which, block) in enumerate(blocks):
        first = 2 * block * members * size
        for side, side_refs in ((core, piece_refs), (1 - core, other_refs)):
            for j, piece_ref in enumerate(side_refs):
                at = first + (side * members + lax.rem(here + members - j, members)) * size
                rows = pl.ds(pl.multiple_of(at, size), size)
                out_refs[which][rows, :] = piece_ref[index]


def in_group(block, axis, stride, members, step):
    route = []
    for i in range(lax.axis_size(axis)):
        at = (i // stride) % members
        route.append((i, i + ((at + step) % members - at) * stride))
    return lax.ppermute(block, axis, route)


def split_of(bands):
    chips = bands // 2
    first = 1
    while first * first * 4 <= chips:
        first *= 2
    return first, chips // first


def add_stage(me, keep, arrived, stride, members, kind, after):
    count, rows, width = keep.shape
    shape = (count, rows // members, width)
    outs = call(
        functools.partial(add_kernel, (len(arrived), stride, members)),
        [(shape, kind)] + [(shape, bf16)] * (members - 1),
        [],
        me,
        keep,
        *arrived,
        smem=(0,),
        after=after,
    )
    return outs[0], [in_group(out, "band", stride, members, j + 1) for j, out in enumerate(outs[1:])]


def held_until(array, after):
    return pl.pallas_call(
        lambda *refs: None,
        out_shape=jax.ShapeDtypeStruct(array.shape, array.dtype),
        in_specs=[pl.BlockSpec(memory_space=pl.ANY)] * (1 + len(after)),
        out_specs=pl.BlockSpec(memory_space=pl.ANY),
        input_output_aliases={0: 0},
        cost_estimate=pl.CostEstimate(flops=1, bytes_accessed=1, transcendentals=0),
    )(array, *after)


def gather_stage(me, piece, stride, members, after):
    count, rows, width = piece.shape
    pieces = [piece] + [in_group(piece, "band", stride, members, j) for j in range(1, members)]
    (mine,) = call(
        functools.partial(gather_kernel, (stride, members)),
        [((count, rows * members, width), bf16)],
        [],
        me,
        *pieces,
        smem=(0,),
        after=after,
    )
    return mine


def join_stage(me, mine, members, blocks, shapes, after):
    pieces = [mine] + [in_group(mine, "band", 2, members, j) for j in range(1, members)]
    others = [in_group(one, "band", 1, 2, 1) for one in pieces]
    return call(
        functools.partial(join_kernel, (members, blocks)),
        [(shape, bf16) for shape in shapes],
        [],
        me,
        *pieces,
        *others,
        smem=(0,),
        after=after,
    )


def reduce_whole(keep, sent):
    bands = lax.axis_size("band")
    chips = [[i for i in range(bands) if i % 2 == c] for c in range(2)]
    total = keep + in_group(sent, "band", 1, 2, 1).astype(f32)
    total = lax.psum(total.astype(bf16), "band", axis_index_groups=chips)
    other = in_group(total, "band", 1, 2, 1)
    core = lax.axis_index("band") % 2
    low, high = jnp.where(core == 0, total, other), jnp.where(core == 0, other, total)
    return jnp.concatenate([low, high], axis=1)


def local(
    node_latent,
    edge_latent,
    recv_slot,
    send_slot,
    edge_count,
    edge_first,
    edge_second,
    node_first,
    node_second,
    node_cotan,
    edge_cotan,
):
    bands = lax.axis_size("band")
    nodes, width = node_latent.shape
    sets, cap = edge_latent.shape[1:3]
    edges, cotan = edge_latent[0], edge_cotan[0]
    recv_ids, send_ids = recv_slot.reshape(sets, 1, cap), send_slot.reshape(sets, 1, cap)
    me = lax.axis_index("band").astype(jnp.int32).reshape(1)

    def step_of(k):
        return band_offsets[k] % bands

    def reach(k):
        return min(step_of(k), bands - step_of(k))

    ordered = sorted(range(sets), key=lambda k: (reach(k), step_of(k)))
    near, far = tuple(ordered[:near_sets]), tuple(ordered[near_sets:])
    local_count = sum(step_of(k) == 0 for k in near)
    near_steps = [step_of(k) for k in near[local_count:]]
    far_steps = list(dict.fromkeys(step_of(k) for k in far))
    steps = near_steps + far_steps
    near_plan = tuple((k,) for k in near[local_count:])
    far_plan = tuple(tuple(k for k in far if step_of(k) == d) for d in far_steps)
    far = sum(far_plan, ())

    ids = [passed_along(send_ids, "band", -d) for d in steps]
    picked = call(
        functools.partial(pick_kernel, near_plan + far_plan),
        [((len(piece) * cap, width), bf16) for piece in near_plan + far_plan],
        [],
        node_latent,
        *ids,
    )
    sx = [passed_along(block, "band", d) for block, d in zip(picked, steps)]
    sx_near, sx_far = sx[: len(near_plan)], sx[len(near_plan) :]

    local_rows, near_rows, far_rows = local_count * cap, len(near) * cap, len(far) * cap
    sx_local, act_near, pre, normed, inverse, live, part_sum = call(
        functools.partial(near_kernel, (near, local_count)),
        [
            ((local_rows, width), bf16),
            ((near_rows, width), bf16),
            ((near_rows, width), f32),
            ((near_rows, width), f32),
            ((near_rows, 128), f32),
            ((near_rows, 128), f32),
            ((nodes, width), f32),
        ],
        [
            ((near_rows, 3 * width), bf16),
            ((near_rows, width), bf16),
            ((nodes, near_rows), bf16),
        ],
        edges,
        recv_ids,
        send_ids,
        edge_count,
        edge_first,
        edge_second,
        node_latent,
        *sx_near,
        smem=(3,),
        vmem=large,
    )

    outs = call(
        functools.partial(far_kernel, (far, far_plan)),
        [((len(piece) * cap, width), bf16) for piece in far_plan]
        + [((far_rows, width), bf16)] * 3
        + [((nodes, width), bf16)] * 6,
        [
            ((far_rows, 3 * width), bf16),
            ((far_rows, 128), f32),
            ((far_rows, width), f32),
            ((far_rows, width), f32),
            ((far_rows, 128), f32),
            ((far_rows, width), bf16),
            ((nodes, far_rows), bf16),
            ((far_rows, nodes), bf16),
            ((far_rows, width), bf16),
        ],
        edges,
        cotan,
        recv_ids,
        edge_count,
        edge_first,
        edge_second,
        node_latent,
        node_cotan,
        part_sum,
        node_first,
        node_second,
        *sx_far,
        smem=(3,),
        vmem=large,
    )
    gpe_far, outs = list(outs[: len(far_plan)]), outs[len(far_plan) :]
    act_far, goe_far, new_far, node_new, gathered, gpn, act_node, gon, gg = outs
    back_far = [passed_along(block, "band", -d) for block, d in zip(gpe_far, far_steps)]

    half = (width // 2, width)
    outs = call(
        functools.partial(back_kernel, (near, local_count)),
        [((near_rows, width), bf16), ((local_rows, width), bf16)]
        + [((cap, width), bf16)] * len(near_steps),
        [((near_rows, width), bf16), ((near_rows, nodes), bf16)],
        cotan,
        recv_ids,
        edge_second,
        live,
        pre,
        normed,
        inverse,
        gg,
    )
    goe_near, gpe_local = outs[:2]
    gpe_near = list(outs[2:])
    back_near = [passed_along(block, "band", -d) for block, d in zip(gpe_near, near_steps)]

    order = near + far
    gpe = [gpe_local] + gpe_near + gpe_far
    sx_all = [sx_local] + sx_near + sx_far
    total = sets * cap
    keep_edge, sent_edge, recv_sum = call(
        functools.partial(weight_kernel, (order, len(sx_all), len(gpe), 2)),
        [((4, *half), f32), ((4, *half), bf16), ((nodes, width), bf16)],
        [((total, width), bf16)] * 5 + [((nodes, total), bf16), ((width, width), f32)],
        edges,
        recv_ids,
        me,
        node_latent,
        *sx_all,
        *gpe,
        act_near,
        act_far,
        goe_near,
        goe_far,
        smem=(2,),
        vmem=large,
    )

    def edge_outputs(after):
        return call(
            functools.partial(edge_kernel, (near, far, len(gpe))),
            [((sets, cap, width), bf16), ((sets, cap, width), bf16), ((nodes, width), f32)],
            [((total, width), bf16)],
            edges,
            cotan,
            edge_first,
            node_first,
            live,
            normed,
            new_far,
            node_cotan,
            gpn,
            recv_sum,
            *gpe,
            after=after,
            vmem=large,
        )

    def node_output(base, after):
        (grad_nodes,) = call(
            functools.partial(final_kernel, (near[:local_count],) + near_plan + far_plan),
            [((nodes, width), bf16)],
            [((nodes, total), bf16), ((total, width), bf16)],
            base,
            edge_first,
            send_ids,
            *ids,
            gpe_local,
            *back_near,
            *back_far,
            after=after,
            vmem=large,
        )
        return grad_nodes

    def node_weights(after):
        return call(
            node_weight_kernel,
            [((3, *half), f32), ((3, *half), bf16)],
            [((width, width), f32)],
            me,
            node_latent,
            gathered,
            gpn,
            act_node,
            gon,
            smem=(0,),
            after=after,
        )

    first, second = split_of(bands)
    node_blocks, node_shapes = ((0, 0), (0, 1), (1, 0)), [(2 * width, width), (width, width)]
    edge_blocks = ((0, 0), (0, 1), (0, 2), (1, 0))
    edge_shapes = [(3 * width, width), (width, width)]
    if width // 2 % (16 * first * second) == 0:
        along_y, along_z = (2, first), (2 * first, second)
        sent_edge = held_until(sent_edge, back_far)
        came_edge = [in_group(sent_edge, "band", 1, 2, 1)]
        keep_node, sent_node = node_weights([sent_edge])
        came_node = [in_group(sent_node, "band", 1, 2, 1)]
        keep_edge, came_edge = add_stage(me, keep_edge, came_edge, *along_y, f32, [keep_node])
        keep_node, came_node = add_stage(me, keep_node, came_node, *along_y, f32, [keep_edge])
        edge_new, grad_edges, base = edge_outputs([keep_node])
        keep_edge, came_edge = add_stage(me, keep_edge, came_edge, *along_z, f32, [base])
        grad_nodes = node_output(base, [keep_edge])
        keep_node, came_node = add_stage(me, keep_node, came_node, *along_z, f32, [grad_nodes])
        piece_edge, _ = add_stage(me, keep_edge, came_edge, 1, 1, bf16, [keep_node])
        piece_node, _ = add_stage(me, keep_node, came_node, 1, 1, bf16, [piece_edge])
        mine_edge = gather_stage(me, piece_edge, *along_z, [piece_node])
        mine_node = gather_stage(me, piece_node, *along_z, [mine_edge])
        grad_e1, grad_e2 = join_stage(me, mine_edge, first, edge_blocks, edge_shapes, [mine_node])
        grad_n1, grad_n2 = join_stage(me, mine_node, first, node_blocks, node_shapes, [grad_e2])
    else:
        whole = reduce_whole(*node_weights([]))
        grad_n1, grad_n2 = whole[:2].reshape(2 * width, width), whole[2]
        whole = reduce_whole(keep_edge, sent_edge)
        grad_e1, grad_e2 = whole[:3].reshape(3 * width, width), whole[3]
        edge_new, grad_edges, base = edge_outputs([])
        grad_nodes = node_output(base, [])
    return (
        node_new,
        edge_new[None],
        grad_nodes,
        grad_edges[None],
        grad_e1,
        grad_e2,
        grad_n1,
        grad_n2,
    )


def solution(mesh):
    return jax.shard_map(
        local,
        mesh=mesh,
        in_specs=(
            P(("groups", "band"), None),
            P(("groups", "band"), None, None, None),
            P(("groups", "band"), None, None),
            P(("groups", "band"), None, None),
            P(("groups", "band"), None),
            P(),
            P(),
            P(),
            P(),
            P(("groups", "band"), None),
            P(("groups", "band"), None, None, None),
        ),
        out_specs=(
            P(("groups", "band"), None),
            P(("groups", "band"), None, None, None),
            P(("groups", "band"), None),
            P(("groups", "band"), None, None, None),
            P("groups", None),
            P("groups", None),
            P("groups", None),
            P("groups", None),
        ),
        check_vma=False,
    )
```

```python
import functools

import jax
import jax.numpy as jnp
from jax import lax
from jax.experimental import pallas as pl
from jax.experimental.pallas import tpu as pltpu
from jax.sharding import PartitionSpec as P

band_offsets = (0, 1, -1, 2, -2, 4, -4, 8, -8, 16, -16)
norm_eps = 1e-05
near_sets = 7
bf16 = jnp.bfloat16
f32 = jnp.float32
vmem_limit = 24 * 1024 * 1024


def passed_along(block, axis, distance):
    devices = range(lax.axis_size(axis))
    route = [((i - distance) % len(devices), i) for i in devices]
    return lax.ppermute(block, axis, route)


def layer_norm(inputs):
    average = jnp.mean(inputs, axis=-1, keepdims=True)
    centred = inputs - average
    inverse = lax.rsqrt(jnp.mean(centred * centred, axis=-1, keepdims=True) + norm_eps)
    return (centred * inverse, inverse)


def norm_back(normed, inverse, upstream):
    return inverse * (
        upstream
        - jnp.mean(upstream, axis=-1, keepdims=True)
        - normed * jnp.mean(upstream * normed, axis=-1, keepdims=True)
    )


def slope_of(inputs, squashed):
    return squashed * (1.0 + inputs * (1.0 - squashed))


def dot(left_side, right_side):
    return jnp.dot(left_side, right_side, preferred_element_type=f32)


def dot_rt(left_side, right_side):
    return lax.dot_general(
        left_side, right_side, (((1,), (1,)), ((), ())), preferred_element_type=f32
    )


def dot_lt(left_side, right_side):
    return lax.dot_general(
        left_side, right_side, (((0,), (0,)), ((), ())), preferred_element_type=f32
    )


def pick_table(ids, nodes):
    cap = ids.shape[1]
    down = jnp.transpose(jnp.broadcast_to(ids, (cap, cap)))
    parts = []
    for first in range(0, nodes, cap):
        wide = min(cap, nodes - first)
        lanes = lax.broadcasted_iota(jnp.int32, (cap, wide), 1) + first
        parts.append(jnp.where(down[:, :wide] == lanes, 1.0, 0.0).astype(bf16))
    return jnp.concatenate(parts, axis=1)


def sum_table(ids, nodes):
    down = lax.broadcasted_iota(jnp.int32, (nodes, ids.shape[1]), 0)
    return jnp.where(down == ids, 1.0, 0.0).astype(bf16)


def live_rows(count, cap):
    return (lax.broadcasted_iota(jnp.int32, (cap, 128), 0) < count).astype(f32)


def call(body, outs, scratch, *args, smem=(), after=(), last=()):
    spaces, given = [], []
    for i, arg in enumerate(args):
        spaces.append(pl.BlockSpec(memory_space=pltpu.SMEM if i in smem else pltpu.VMEM))
        given.append(arg if i in smem else pltpu.with_memory_space_constraint(arg, pltpu.VMEM))
    spaces += [pl.BlockSpec(memory_space=pl.ANY)] * len(after)

    def kernel(*refs):
        body(*refs[: len(args)], *refs[len(args) + len(after) :])

    return pl.pallas_call(
        kernel,
        out_shape=[
            (pltpu.HBM if i in last else pltpu.VMEM)(shape, kind)
            for i, (shape, kind) in enumerate(outs)
        ],
        in_specs=spaces,
        out_specs=[pl.BlockSpec(memory_space=pltpu.VMEM)] * len(outs),
        scratch_shapes=[pltpu.VMEM(shape, kind) for shape, kind in scratch],
        compiler_params=pltpu.CompilerParams(vmem_limit_bytes=vmem_limit),
        cost_estimate=pl.CostEstimate(flops=1, bytes_accessed=1, transcendentals=0),
    )(*given, *after)


def in_hbm(array):
    return pltpu.with_memory_space_constraint(array, pltpu.HBM)


def load_kernel(count, *refs):
    sems = refs[-1]
    copies = [
        pltpu.make_async_copy(refs[i], refs[count + i], sems.at[i]) for i in range(count)
    ]
    for copy in copies:
        copy.start()
    for copy in copies:
        copy.wait()


def loaded(*args):
    count = len(args)
    return pl.pallas_call(
        functools.partial(load_kernel, count),
        out_shape=[pltpu.VMEM(arg.shape, arg.dtype) for arg in args],
        in_specs=[pl.BlockSpec(memory_space=pltpu.HBM)] * count,
        out_specs=[pl.BlockSpec(memory_space=pltpu.VMEM)] * count,
        scratch_shapes=[pltpu.SemaphoreType.DMA((count,))],
        compiler_params=pltpu.CompilerParams(vmem_limit_bytes=1024 * 1024),
        cost_estimate=pl.CostEstimate(flops=1, bytes_accessed=1, transcendentals=0),
    )(*[in_hbm(arg) for arg in args])


def pick_kernel(plan, *refs):
    node_ref = refs[0]
    nodes = node_ref.shape[0]
    for id_ref, out_ref, sets in zip(refs[1 : 1 + len(plan)], refs[1 + len(plan) :], plan):
        cap = id_ref.shape[2]
        for i, k in enumerate(sets):
            hot = pick_table(id_ref[k], nodes)
            out_ref[i * cap : (i + 1) * cap, :] = dot(hot, node_ref[...]).astype(bf16)


def forward_rows(pre, live, w2, act_ref, slope_ref, normed_ref, inv_ref, msg_ref, rows):
    squashed = jax.nn.sigmoid(pre)
    slope_ref[rows, :] = slope_of(pre, squashed)
    act = (pre * squashed).astype(bf16)
    act_ref[rows, :] = act
    normed, inverse = layer_norm(dot(act, w2))
    normed_ref[rows, :] = normed
    inv_ref[rows, :] = jnp.broadcast_to(inverse, (inverse.shape[0], 128))
    msg_ref[rows, :] = (live * normed).astype(bf16)


def backward_rows(cotan, picked, live, normed, inverse, slope, w2):
    upstream = live * (cotan.astype(f32) + picked)
    goe = norm_back(normed, inverse, upstream).astype(bf16)
    return goe, (dot_rt(goe, w2) * slope).astype(bf16)


def stack_into(out_ref, refs):
    first = 0
    for ref in refs:
        out_ref[first : first + ref.shape[0], :] = ref[...]
        first += ref.shape[0]


def start_kernel(plan, *refs):
    order, local_count = plan
    (
        edge_ref,
        recv_ref,
        send_ref,
        count_ref,
        w1_ref,
        w2_ref,
        node_ref,
        pick_ref,
        hot_ref,
        live_ref,
        part_ref,
        sx_ref,
        act_ref,
        slope_ref,
        normed_ref,
        inv_ref,
        sum_ref,
        x_ref,
        msg_ref,
    ) = refs
    nodes, width = node_ref.shape
    cap = recv_ref.shape[2]
    split = local_count * cap
    for i, k in enumerate(order):
        rows = slice(i * cap, (i + 1) * cap)
        x_ref[rows, :width] = edge_ref[k]
        pick_ref[rows, :] = pick_table(recv_ref[k], nodes)
        hot_ref[:, rows] = sum_table(recv_ref[k], nodes)
        live_ref[rows, :] = live_rows(count_ref[0, k], cap)
        if i < local_count:
            sx_ref[rows, :] = dot(pick_table(send_ref[k], nodes), node_ref[...]).astype(bf16)
    x_ref[:, width:] = dot(pick_ref[...], node_ref[...]).astype(bf16)
    part = dot(x_ref[:split, :width], w1_ref[:width, :])
    part += dot(x_ref[:split, width:], w1_ref[2 * width :, :])
    pre = part + dot(sx_ref[...], w1_ref[width : 2 * width, :])
    rows = slice(0, split)
    live = live_ref[rows, :1]
    forward_rows(pre, live, w2_ref[...], act_ref, slope_ref, normed_ref, inv_ref, msg_ref, rows)
    sum_ref[...] = dot(hot_ref[:, :split], msg_ref[...])
    part = dot(x_ref[split:, :width], w1_ref[:width, :])
    part_ref[...] = part + dot(x_ref[split:, width:], w1_ref[2 * width :, :])


def near_kernel(plan, *refs):
    first, count = plan
    part_ref, live_ref, hot_ref, sum_in_ref, w1_ref, w2_ref = refs[:6]
    sx_refs = refs[6 : 6 + count]
    act_ref, slope_ref, normed_ref, inv_ref, sum_ref, sx_ref, msg_ref = refs[6 + count :]
    total, width = sx_ref.shape
    stack_into(sx_ref, sx_refs)
    for j in range(2):
        rows = slice(j * total // 2, (j + 1) * total // 2)
        pre = part_ref[rows, :] + dot(sx_ref[rows, :], w1_ref[width : 2 * width, :])
        live = live_ref[first + rows.start : first + rows.stop, :1]
        forward_rows(pre, live, w2_ref[...], act_ref, slope_ref, normed_ref, inv_ref, msg_ref, rows)
    sum_ref[...] = sum_in_ref[...] + dot(hot_ref[:, first : first + total], msg_ref[...])


def far_kernel(plan, *refs):
    sets, sizes, first, part_first = plan
    count = len(sizes)
    (
        cotan_ref,
        part_ref,
        live_ref,
        pick_ref,
        hot_ref,
        sum_ref,
        w1_ref,
        w2_ref,
        node_ref,
        ncot_ref,
        n1_ref,
        n2_ref,
    ) = refs[:12]
    sx_refs, refs = refs[12 : 12 + count], refs[12 + count :]
    gpe_refs, refs = refs[:count], refs[count:]
    (
        act_ref,
        goe_ref,
        normed_ref,
        gathered_ref,
        gpn_ref,
        act_node_ref,
        gon_ref,
        gg_ref,
        node_new_ref,
        sx_ref,
        slope_ref,
        inv_ref,
        msg_ref,
        cot_ref,
        gpe_ref,
    ) = refs
    total, width = sx_ref.shape
    cap = cotan_ref.shape[1]
    stack_into(sx_ref, sx_refs)
    for i, k in enumerate(sets):
        cot_ref[i * cap : (i + 1) * cap, :] = cotan_ref[k]
    halves = [slice(j * total // 2, (j + 1) * total // 2) for j in range(2)]
    for rows in halves:
        pre = part_ref[part_first + rows.start : part_first + rows.stop, :]
        pre = pre + dot(sx_ref[rows, :], w1_ref[width : 2 * width, :])
        live = live_ref[first + rows.start : first + rows.stop, :1]
        forward_rows(pre, live, w2_ref[...], act_ref, slope_ref, normed_ref, inv_ref, msg_ref, rows)
    gathered = sum_ref[...] + dot(hot_ref[:, first : first + total], msg_ref[...])
    gathered = gathered.astype(bf16)
    gathered_ref[...] = gathered

    pre = dot(node_ref[...], n1_ref[:width, :]) + dot(gathered, n1_ref[width:, :])
    squashed = jax.nn.sigmoid(pre)
    act_node = (pre * squashed).astype(bf16)
    act_node_ref[...] = act_node
    normed, inverse = layer_norm(dot(act_node, n2_ref[...]))
    node_new_ref[...] = (node_ref[...].astype(f32) + normed).astype(bf16)
    gon = norm_back(normed, inverse, ncot_ref[...].astype(f32)).astype(bf16)
    gon_ref[...] = gon
    gpn = (dot_rt(gon, n2_ref[...]) * slope_of(pre, squashed)).astype(bf16)
    gpn_ref[...] = gpn
    gg_ref[...] = dot_rt(gpn, n1_ref[width:, :]).astype(bf16)

    for rows in halves:
        whole = slice(first + rows.start, first + rows.stop)
        goe, gpe = backward_rows(
            cot_ref[rows, :],
            dot(pick_ref[whole, :], gg_ref[...]),
            live_ref[whole, :1],
            normed_ref[rows, :],
            inv_ref[rows, :1],
            slope_ref[rows, :],
            w2_ref[...],
        )
        goe_ref[rows, :] = goe
        gpe_ref[rows, :] = gpe
    at = 0
    for out_ref, size in zip(gpe_refs, sizes):
        out_ref[...] = gpe_ref[at : at + size, :]
        at += size


def back_kernel(plan, *refs):
    sets, local_count = plan
    cotan_ref, live_ref, pick_ref, gg_ref, w2_ref = refs[:5]
    groups = (refs[5:8], refs[8:11])
    goe_ref, local_ref = refs[11:13]
    gpe_refs, (cot_ref, gpe_ref) = refs[13:-2], refs[-2:]
    cap = cotan_ref.shape[1]
    for i, k in enumerate(sets):
        cot_ref[i * cap : (i + 1) * cap, :] = cotan_ref[k]
    first = 0
    for slope_ref, normed_ref, inv_ref in groups:
        rows = slice(first, first + slope_ref.shape[0])
        goe, gpe = backward_rows(
            cot_ref[rows, :],
            dot(pick_ref[rows, :], gg_ref[...]),
            live_ref[rows, :1],
            normed_ref[...],
            inv_ref[:, :1],
            slope_ref[...],
            w2_ref[...],
        )
        goe_ref[rows, :] = goe
        gpe_ref[rows, :] = gpe
        first = rows.stop
    local_ref[...] = gpe_ref[: local_count * cap, :]
    for j, out_ref in enumerate(gpe_refs):
        i = local_count + j
        out_ref[...] = gpe_ref[i * cap : (i + 1) * cap, :]


def node_weight_kernel(me_ref, node_ref, gathered_ref, gpn_ref, act_node_ref, gon_ref, keep_ref, sent_ref, block_ref):
    put = functools.partial(put_block, me_ref, block_ref, keep_ref, sent_ref)
    put(0, node_ref[...], gpn_ref[...])
    put(1, gathered_ref[...], gpn_ref[...])
    put(2, act_node_ref[...], gon_ref[...])


def put_block(me_ref, block_ref, keep_ref, sent_ref, index, left_side, right_side):
    core = lax.rem(me_ref[0], 2)
    half = block_ref.shape[0] // 2
    block_ref[...] = dot_lt(left_side, right_side)
    keep_ref[index] = block_ref[pl.ds(pl.multiple_of(core * half, half), half), :]
    other = block_ref[pl.ds(pl.multiple_of((1 - core) * half, half), half), :]
    sent_ref[index] = other.astype(bf16)


def weight_kernel(plan, *refs):
    order, sx_count, gpe_count, act_count, goe_count = plan
    edge_ref, hot_ref, me_ref, node_ref = refs[:4]
    refs = refs[4:]
    sx_refs, refs = refs[:sx_count], refs[sx_count:]
    gpe_refs, refs = refs[:gpe_count], refs[gpe_count:]
    act_refs, refs = refs[:act_count], refs[act_count:]
    goe_refs, refs = refs[:goe_count], refs[goe_count:]
    keep_ref, sent_ref, rsum_ref, x_ref, sx_ref, gpe_ref, act_ref, goe_ref, block_ref = refs
    cap = edge_ref.shape[1]
    for i, k in enumerate(order):
        x_ref[i * cap : (i + 1) * cap, :] = edge_ref[k]
    stack_into(sx_ref, sx_refs)
    stack_into(gpe_ref, gpe_refs)
    stack_into(act_ref, act_refs)
    stack_into(goe_ref, goe_refs)
    recv_sum = dot(hot_ref[...], gpe_ref[...]).astype(bf16)
    rsum_ref[...] = recv_sum
    put = functools.partial(put_block, me_ref, block_ref, keep_ref, sent_ref)
    put(0, x_ref[...], gpe_ref[...])
    put(1, sx_ref[...], gpe_ref[...])
    put(2, node_ref[...], recv_sum)
    put(3, act_ref[...], goe_ref[...])


def base_kernel(ncot_ref, gpn_ref, rsum_ref, w1_ref, n1_ref, base_ref):
    width = w1_ref.shape[1]
    base_ref[...] = (
        ncot_ref[...].astype(f32)
        + dot_rt(gpn_ref[...], n1_ref[:width, :])
        + dot_rt(rsum_ref[...], w1_ref[2 * width :, :])
    )


def edge_kernel(plan, *refs):
    order, normed_count, gpe_count = plan
    edge_ref, cotan_ref, w1_ref, live_ref = refs[:4]
    refs = refs[4:]
    normed_refs, refs = refs[:normed_count], refs[normed_count:]
    gpe_refs, refs = refs[:gpe_count], refs[gpe_count:]
    new_ref, gedge_ref, gpe_ref = refs
    width = w1_ref.shape[1]
    cap = edge_ref.shape[1]
    stack_into(gpe_ref, gpe_refs)
    places = [(ref, at) for ref in normed_refs for at in range(0, ref.shape[0], cap)]
    for i, (k, (normed_ref, at)) in enumerate(zip(order, places)):
        rows = slice(i * cap, (i + 1) * cap)
        grad = cotan_ref[k].astype(f32) + dot_rt(gpe_ref[rows, :], w1_ref[:width, :])
        gedge_ref[k] = grad.astype(bf16)
        message = live_ref[rows, :1] * normed_ref[at : at + cap, :]
        new_ref[k] = (edge_ref[k].astype(f32) + message).astype(bf16)


def final_kernel(plan, *refs):
    base_ref, w1_ref = refs[:2]
    id_refs = refs[2 : 2 + len(plan)]
    row_refs = refs[2 + len(plan) : 2 + 2 * len(plan)]
    out_ref, hot_ref, rows_ref = refs[2 + 2 * len(plan) :]
    nodes, width = base_ref.shape
    cap = id_refs[0].shape[2]
    at = 0
    for id_ref, sets in zip(id_refs, plan):
        for k in sets:
            hot_ref[:, at : at + cap] = sum_table(id_ref[k], nodes)
            at += cap
    stack_into(rows_ref, row_refs)
    send_sum = dot(hot_ref[...], rows_ref[...]).astype(bf16)
    grad = base_ref[...] + dot_rt(send_sum, w1_ref[width : 2 * width, :])
    out_ref[...] = grad.astype(bf16)


def place(me_ref, stride, members):
    return lax.rem(lax.div(me_ref[0], stride), members)


def add_kernel(plan, *refs):
    came, stride, members = plan
    me_ref, keep_ref = refs[:2]
    arr_refs, out_refs = refs[2 : 2 + came], refs[2 + came :]
    size = keep_ref.shape[1] // members
    here = place(me_ref, stride, members)
    for j, out_ref in enumerate(out_refs):
        at = lax.rem(here + j, members) * size
        rows = pl.ds(pl.multiple_of(at, size), size)
        piece = keep_ref[:, rows, :]
        for arr_ref in arr_refs:
            piece += arr_ref[:, rows, :].astype(f32)
        out_ref[...] = piece.astype(out_ref.dtype)


def gather_kernel(plan, *refs):
    stride, members = plan
    me_ref, piece_refs, out_ref = refs[0], refs[1:-1], refs[-1]
    size = piece_refs[0].shape[1]
    here = place(me_ref, stride, members)
    for j, piece_ref in enumerate(piece_refs):
        at = lax.rem(here + members - j, members) * size
        out_ref[:, pl.ds(pl.multiple_of(at, size), size), :] = piece_ref[...]


def join_kernel(plan, *refs):
    members, blocks = plan
    me_ref = refs[0]
    piece_refs, other_refs = refs[1 : 1 + members], refs[1 + members : 1 + 2 * members]
    out_refs = refs[1 + 2 * members :]
    size = piece_refs[0].shape[1]
    core = lax.rem(me_ref[0], 2)
    here = place(me_ref, 2, members)
    for index, (which, block) in enumerate(blocks):
        first = 2 * block * members * size
        for side, side_refs in ((core, piece_refs), (1 - core, other_refs)):
            for j, piece_ref in enumerate(side_refs):
                at = first + (side * members + lax.rem(here + members - j, members)) * size
                rows = pl.ds(pl.multiple_of(at, size), size)
                out_refs[which][rows, :] = piece_ref[index]


def in_group(block, axis, stride, members, step):
    route = []
    for i in range(lax.axis_size(axis)):
        at = (i // stride) % members
        route.append((i, i + ((at + step) % members - at) * stride))
    return lax.ppermute(block, axis, route)


def split_of(bands):
    chips = bands // 2
    first = 1
    while first * first * 4 <= chips:
        first *= 2
    return first, chips // first


def add_stage(me, keep, arrived, stride, members, kind, after):
    count, rows, width = keep.shape
    shape = (count, rows // members, width)
    outs = call(
        functools.partial(add_kernel, (len(arrived), stride, members)),
        [(shape, kind)] + [(shape, bf16)] * (members - 1),
        [],
        me,
        keep,
        *arrived,
        smem=(0,),
        after=after,
    )
    return outs[0], [in_group(out, "band", stride, members, j + 1) for j, out in enumerate(outs[1:])]


def held_until(array, after):
    return pl.pallas_call(
        lambda *refs: None,
        out_shape=pltpu.VMEM(array.shape, array.dtype),
        in_specs=[pl.BlockSpec(memory_space=pltpu.VMEM)]
        + [pl.BlockSpec(memory_space=pl.ANY)] * len(after),
        out_specs=pl.BlockSpec(memory_space=pltpu.VMEM),
        input_output_aliases={0: 0},
        compiler_params=pltpu.CompilerParams(vmem_limit_bytes=1024 * 1024),
        cost_estimate=pl.CostEstimate(flops=1, bytes_accessed=1, transcendentals=0),
    )(pltpu.with_memory_space_constraint(array, pltpu.VMEM), *after)


def gather_stage(me, piece, stride, members, after):
    count, rows, width = piece.shape
    pieces = [piece] + [in_group(piece, "band", stride, members, j) for j in range(1, members)]
    (mine,) = call(
        functools.partial(gather_kernel, (stride, members)),
        [((count, rows * members, width), bf16)],
        [],
        me,
        *pieces,
        smem=(0,),
        after=after,
    )
    return mine


def join_stage(me, mine, members, blocks, shapes, after):
    pieces = [mine] + [in_group(mine, "band", 2, members, j) for j in range(1, members)]
    others = [in_group(one, "band", 1, 2, 1) for one in pieces]
    return call(
        functools.partial(join_kernel, (members, blocks)),
        [(shape, bf16) for shape in shapes],
        [],
        me,
        *pieces,
        *others,
        smem=(0,),
        after=after,
        last=range(len(shapes)),
    )


def reduce_whole(keep, sent):
    bands = lax.axis_size("band")
    chips = [[i for i in range(bands) if i % 2 == c] for c in range(2)]
    total = keep + in_group(sent, "band", 1, 2, 1).astype(f32)
    total = lax.psum(total.astype(bf16), "band", axis_index_groups=chips)
    other = in_group(total, "band", 1, 2, 1)
    core = lax.axis_index("band") % 2
    low, high = jnp.where(core == 0, total, other), jnp.where(core == 0, other, total)
    return jnp.concatenate([low, high], axis=1)


def local(
    node_latent,
    edge_latent,
    recv_slot,
    send_slot,
    edge_count,
    edge_first,
    edge_second,
    node_first,
    node_second,
    node_cotan,
    edge_cotan,
):
    bands = lax.axis_size("band")
    nodes, width = node_latent.shape
    sets, cap = edge_latent.shape[1:3]
    send_ids = send_slot.reshape(sets, 1, cap)
    me = lax.axis_index("band").astype(jnp.int32).reshape(1)

    def step_of(k):
        return band_offsets[k] % bands

    def reach(k):
        return min(step_of(k), bands - step_of(k))

    ordered = sorted(range(sets), key=lambda k: (reach(k), step_of(k)))
    near, far = tuple(ordered[:near_sets]), tuple(ordered[near_sets:])
    local_count = sum(step_of(k) == 0 for k in near)
    near_steps = [step_of(k) for k in near[local_count:]]
    far_steps = list(dict.fromkeys(step_of(k) for k in far))
    steps = near_steps + far_steps
    near_plan = tuple((k,) for k in near[local_count:])
    far_plan = tuple(tuple(k for k in far if step_of(k) == d) for d in far_steps)
    far = sum(far_plan, ())

    order = near + far

    ids = [passed_along(send_ids, "band", -d) for d in steps]
    (
        node_latent,
        send_ids,
        recv_ids,
        edges,
        edge_first,
        edge_second,
        node_first,
        node_second,
        node_cotan,
        cotan,
    ) = loaded(
        node_latent,
        send_ids,
        recv_slot.reshape(sets, 1, cap),
        edge_latent[0],
        edge_first,
        edge_second,
        node_first,
        node_second,
        node_cotan,
        edge_cotan[0],
    )
    picked = call(
        functools.partial(pick_kernel, near_plan + far_plan),
        [((len(piece) * cap, width), bf16) for piece in near_plan + far_plan],
        [],
        node_latent,
        *ids,
    )
    sx = [passed_along(block, "band", d) for block, d in zip(picked, steps)]
    sx_near, sx_far = sx[: len(near_plan)], sx[len(near_plan) :]

    local_rows, near_rows, far_rows = local_count * cap, len(near_plan) * cap, len(far) * cap
    total = sets * cap

    def forward_outs(rows):
        return [
            ((rows, width), bf16),
            ((rows, width), f32),
            ((rows, width), f32),
            ((rows, 128), f32),
            ((nodes, width), f32),
        ]

    pick, hot, live, part, sx_local, act_local, slope_local, normed_local, inv_local, node_sum = call(
        functools.partial(start_kernel, (order, local_count)),
        [
            ((total, nodes), bf16),
            ((nodes, total), bf16),
            ((total, 128), f32),
            ((near_rows + far_rows, width), f32),
            ((local_rows, width), bf16),
        ]
        + forward_outs(local_rows),
        [((total, 2 * width), bf16), ((local_rows, width), bf16)],
        edges,
        recv_ids,
        send_ids,
        in_hbm(edge_count),
        edge_first,
        edge_second,
        node_latent,
        smem=(3,),
        after=[picked[0]],
    )
    act_near, slope_near, normed_near, inv_near, node_sum = call(
        functools.partial(near_kernel, (local_rows, len(near_plan))),
        forward_outs(near_rows),
        [((near_rows, width), bf16), ((near_rows, width), bf16)],
        part,
        live,
        hot,
        node_sum,
        edge_first,
        edge_second,
        *sx_near,
    )
    sizes = [len(piece) * cap for piece in far_plan]
    outs = call(
        functools.partial(far_kernel, (far, sizes, local_rows + near_rows, near_rows)),
        [((size, width), bf16) for size in sizes]
        + [((far_rows, width), bf16), ((far_rows, width), bf16), ((far_rows, width), f32)]
        + [((nodes, width), bf16)] * 6,
        [
            ((far_rows, width), bf16),
            ((far_rows, width), f32),
            ((far_rows, 128), f32),
            ((far_rows, width), bf16),
            ((far_rows, width), bf16),
            ((far_rows, width), bf16),
        ],
        cotan,
        part,
        live,
        pick,
        hot,
        node_sum,
        edge_first,
        edge_second,
        node_latent,
        node_cotan,
        node_first,
        node_second,
        *sx_far,
        last=(len(sizes) + 8,),
    )
    gpe_far, outs = list(outs[: len(far_plan)]), outs[len(far_plan) :]
    act_far, goe_far, normed_far, gathered, gpn, act_node, gon, gg, node_new = outs
    back_far = [passed_along(block, "band", -d) for block, d in zip(gpe_far, far_steps)]

    half = (width // 2, width)
    outs = call(
        functools.partial(back_kernel, (near, local_count)),
        [((local_rows + near_rows, width), bf16), ((local_rows, width), bf16)]
        + [((cap, width), bf16)] * len(near_steps),
        [((local_rows + near_rows, width), bf16)] * 2,
        cotan,
        live,
        pick,
        gg,
        edge_second,
        slope_local,
        normed_local,
        inv_local,
        slope_near,
        normed_near,
        inv_near,
    )
    goe_near, gpe_local = outs[:2]
    gpe_near = list(outs[2:])
    back_near = [passed_along(block, "band", -d) for block, d in zip(gpe_near, near_steps)]

    gpe = [gpe_local] + gpe_near + gpe_far
    sx_all = [sx_local] + sx_near + sx_far
    keep_edge, sent_edge, recv_sum = call(
        functools.partial(weight_kernel, (order, len(sx_all), len(gpe), 3, 2)),
        [((4, *half), f32), ((4, *half), bf16), ((nodes, width), bf16)],
        [((total, width), bf16)] * 5 + [((width, width), f32)],
        edges,
        hot,
        me,
        node_latent,
        *sx_all,
        *gpe,
        act_local,
        act_near,
        act_far,
        goe_near,
        goe_far,
        smem=(2,),
    )

    def edge_outputs(after):
        return call(
            functools.partial(edge_kernel, (order, 3, len(gpe))),
            [((sets, cap, width), bf16), ((sets, cap, width), bf16)],
            [((total, width), bf16)],
            edges,
            cotan,
            edge_first,
            live,
            normed_local,
            normed_near,
            normed_far,
            *gpe,
            after=after,
            last=(0, 1),
        )

    def node_output(after):
        (base,) = call(
            base_kernel,
            [((nodes, width), f32)],
            [],
            node_cotan,
            gpn,
            recv_sum,
            edge_first,
            node_first,
            after=after,
        )
        (grad_nodes,) = call(
            functools.partial(final_kernel, (near[:local_count],) + near_plan + far_plan),
            [((nodes, width), bf16)],
            [((nodes, total), bf16), ((total, width), bf16)],
            base,
            edge_first,
            send_ids,
            *ids,
            gpe_local,
            *back_near,
            *back_far,
            last=(0,),
        )
        return grad_nodes

    def node_weights(after):
        return call(
            node_weight_kernel,
            [((3, *half), f32), ((3, *half), bf16)],
            [((width, width), f32)],
            me,
            node_latent,
            gathered,
            gpn,
            act_node,
            gon,
            smem=(0,),
            after=after,
        )

    first, second = split_of(bands)
    node_blocks, node_shapes = ((0, 0), (0, 1), (1, 0)), [(2 * width, width), (width, width)]
    edge_blocks = ((0, 0), (0, 1), (0, 2), (1, 0))
    edge_shapes = [(3 * width, width), (width, width)]
    if width // 2 % (16 * first * second) == 0:
        along_y, along_z = (2, first), (2 * first, second)
        sent_edge = held_until(sent_edge, back_far)
        came_edge = [in_group(sent_edge, "band", 1, 2, 1)]
        keep_node, sent_node = node_weights([sent_edge])
        came_node = [in_group(sent_node, "band", 1, 2, 1)]
        keep_edge, came_edge = add_stage(me, keep_edge, came_edge, *along_y, f32, [keep_node])
        keep_node, came_node = add_stage(me, keep_node, came_node, *along_y, f32, [keep_edge])
        edge_new, grad_edges = edge_outputs([keep_node])
        keep_edge, came_edge = add_stage(me, keep_edge, came_edge, *along_z, f32, [in_hbm(edge_new)])
        grad_nodes = node_output([keep_edge])
        keep_node, came_node = add_stage(me, keep_node, came_node, *along_z, f32, [in_hbm(grad_nodes)])
        piece_edge, _ = add_stage(me, keep_edge, came_edge, 1, 1, bf16, [keep_node])
        piece_node, _ = add_stage(me, keep_node, came_node, 1, 1, bf16, [piece_edge])
        mine_edge = gather_stage(me, piece_edge, *along_z, [piece_node])
        mine_node = gather_stage(me, piece_node, *along_z, [mine_edge])
        grad_e1, grad_e2 = join_stage(me, mine_edge, first, edge_blocks, edge_shapes, [mine_node])
        grad_n1, grad_n2 = join_stage(me, mine_node, first, node_blocks, node_shapes, [in_hbm(grad_e2)])
    else:
        whole = reduce_whole(*node_weights([]))
        grad_n1, grad_n2 = whole[:2].reshape(2 * width, width), whole[2]
        whole = reduce_whole(keep_edge, sent_edge)
        grad_e1, grad_e2 = whole[:3].reshape(3 * width, width), whole[3]
        edge_new, grad_edges = edge_outputs([])
        grad_nodes = node_output([])
    return (
        node_new,
        edge_new[None],
        grad_nodes,
        grad_edges[None],
        grad_e1,
        grad_e2,
        grad_n1,
        grad_n2,
    )


def solution(mesh):
    return jax.shard_map(
        local,
        mesh=mesh,
        in_specs=(
            P(("groups", "band"), None),
            P(("groups", "band"), None, None, None),
            P(("groups", "band"), None, None),
            P(("groups", "band"), None, None),
            P(("groups", "band"), None),
            P(),
            P(),
            P(),
            P(),
            P(("groups", "band"), None),
            P(("groups", "band"), None, None, None),
        ),
        out_specs=(
            P(("groups", "band"), None),
            P(("groups", "band"), None, None, None),
            P(("groups", "band"), None),
            P(("groups", "band"), None, None, None),
            P("groups", None),
            P("groups", None),
            P("groups", None),
            P("groups", None),
        ),
        check_vma=False,
    )
```

```python
import functools

import jax
import jax.numpy as jnp
from jax import lax
from jax.experimental import pallas as pl
from jax.experimental.pallas import tpu as pltpu
from jax.sharding import PartitionSpec as P

band_offsets = (0, 1, -1, 2, -2, 4, -4, 8, -8, 16, -16)
norm_eps = 1e-05
near_sets = 7
bf16 = jnp.bfloat16
f32 = jnp.float32
vmem_limit = 20 * 1024 * 1024


def passed_along(block, axis, distance):
    devices = range(lax.axis_size(axis))
    route = [((i - distance) % len(devices), i) for i in devices]
    return lax.ppermute(block, axis, route)


def layer_norm(inputs):
    average = jnp.mean(inputs, axis=-1, keepdims=True)
    centred = inputs - average
    inverse = lax.rsqrt(jnp.mean(centred * centred, axis=-1, keepdims=True) + norm_eps)
    return (centred * inverse, inverse)


def norm_back(normed, inverse, upstream):
    return inverse * (
        upstream
        - jnp.mean(upstream, axis=-1, keepdims=True)
        - normed * jnp.mean(upstream * normed, axis=-1, keepdims=True)
    )


def slope_of(inputs, squashed):
    return squashed * (1.0 + inputs * (1.0 - squashed))


def dot(left_side, right_side):
    return jnp.dot(left_side, right_side, preferred_element_type=f32)


def dot_rt(left_side, right_side):
    return lax.dot_general(
        left_side, right_side, (((1,), (1,)), ((), ())), preferred_element_type=f32
    )


def dot_lt(left_side, right_side):
    return lax.dot_general(
        left_side, right_side, (((0,), (0,)), ((), ())), preferred_element_type=f32
    )


def pick_table(ids, nodes):
    cap = ids.shape[1]
    down = jnp.transpose(jnp.broadcast_to(ids, (cap, cap)))
    parts = []
    for first in range(0, nodes, cap):
        wide = min(cap, nodes - first)
        lanes = lax.broadcasted_iota(jnp.int32, (cap, wide), 1) + first
        parts.append(jnp.where(down[:, :wide] == lanes, 1.0, 0.0).astype(bf16))
    return jnp.concatenate(parts, axis=1)


def sum_table(ids, nodes):
    down = lax.broadcasted_iota(jnp.int32, (nodes, ids.shape[1]), 0)
    return jnp.where(down == ids, 1.0, 0.0).astype(bf16)


def live_rows(count, cap):
    return (lax.broadcasted_iota(jnp.int32, (cap, 128), 0) < count).astype(f32)


def call(body, outs, scratch, *args, smem=(), after=(), last=()):
    spaces, given = [], []
    for i, arg in enumerate(args):
        spaces.append(pl.BlockSpec(memory_space=pltpu.SMEM if i in smem else pltpu.VMEM))
        given.append(arg if i in smem else pltpu.with_memory_space_constraint(arg, pltpu.VMEM))
    spaces += [pl.BlockSpec(memory_space=pl.ANY)] * len(after)

    def kernel(*refs):
        body(*refs[: len(args)], *refs[len(args) + len(after) :])

    return pl.pallas_call(
        kernel,
        out_shape=[
            (pltpu.HBM if i in last else pltpu.VMEM)(shape, kind)
            for i, (shape, kind) in enumerate(outs)
        ],
        in_specs=spaces,
        out_specs=[pl.BlockSpec(memory_space=pltpu.VMEM)] * len(outs),
        scratch_shapes=[pltpu.VMEM(shape, kind) for shape, kind in scratch],
        compiler_params=pltpu.CompilerParams(vmem_limit_bytes=vmem_limit),
        cost_estimate=pl.CostEstimate(flops=1, bytes_accessed=1, transcendentals=0),
    )(*given, *after)


def in_hbm(array):
    return pltpu.with_memory_space_constraint(array, pltpu.HBM)


def load_kernel(count, *refs):
    sems, refs = refs[-1], refs[1:]
    copies = [
        pltpu.make_async_copy(refs[i], refs[count + i], sems.at[i]) for i in range(count)
    ]
    for copy in copies:
        copy.start()
    for copy in copies:
        copy.wait()


def loaded(me, *args):
    count = len(args)
    return pl.pallas_call(
        functools.partial(load_kernel, count),
        out_shape=[pltpu.VMEM(arg.shape, arg.dtype) for arg in args],
        in_specs=[pl.BlockSpec(memory_space=pltpu.SMEM)]
        + [pl.BlockSpec(memory_space=pltpu.HBM)] * count,
        out_specs=[pl.BlockSpec(memory_space=pltpu.VMEM)] * count,
        scratch_shapes=[pltpu.SemaphoreType.DMA((count,))],
        compiler_params=pltpu.CompilerParams(vmem_limit_bytes=1024 * 1024),
        cost_estimate=pl.CostEstimate(flops=1, bytes_accessed=1, transcendentals=0),
    )(me, *[in_hbm(arg) for arg in args])


def pick_kernel(plan, *refs):
    node_ref = refs[0]
    nodes = node_ref.shape[0]
    for id_ref, out_ref, sets in zip(refs[1 : 1 + len(plan)], refs[1 + len(plan) :], plan):
        cap = id_ref.shape[2]
        for i, k in enumerate(sets):
            hot = pick_table(id_ref[k], nodes)
            out_ref[i * cap : (i + 1) * cap, :] = dot(hot, node_ref[...]).astype(bf16)


def forward_rows(pre, live, w2, act_ref, slope_ref, normed_ref, inv_ref, msg_ref, rows):
    squashed = jax.nn.sigmoid(pre)
    slope_ref[rows, :] = slope_of(pre, squashed)
    act = (pre * squashed).astype(bf16)
    act_ref[rows, :] = act
    normed, inverse = layer_norm(dot(act, w2))
    normed_ref[rows, :] = normed
    inv_ref[rows, :] = jnp.broadcast_to(inverse, (inverse.shape[0], 128))
    msg_ref[rows, :] = (live * normed).astype(bf16)


def backward_rows(cotan, picked, live, normed, inverse, slope, w2):
    upstream = live * (cotan.astype(f32) + picked)
    goe = norm_back(normed, inverse, upstream).astype(bf16)
    return goe, (dot_rt(goe, w2) * slope).astype(bf16)


def stack_into(out_ref, refs):
    first = 0
    for ref in refs:
        out_ref[first : first + ref.shape[0], :] = ref[...]
        first += ref.shape[0]


def start_kernel(plan, *refs):
    order, local_count = plan
    (
        edge_ref,
        recv_ref,
        send_ref,
        count_ref,
        w1_ref,
        w2_ref,
        node_ref,
        pick_ref,
        hot_ref,
        live_ref,
        part_ref,
        sx_ref,
        act_ref,
        slope_ref,
        normed_ref,
        inv_ref,
        sum_ref,
        x_ref,
        msg_ref,
    ) = refs
    nodes, width = node_ref.shape
    cap = recv_ref.shape[2]
    split = local_count * cap
    for i, k in enumerate(order):
        rows = slice(i * cap, (i + 1) * cap)
        x_ref[rows, :width] = edge_ref[k]
        pick_ref[rows, :] = pick_table(recv_ref[k], nodes)
        hot_ref[:, rows] = sum_table(recv_ref[k], nodes)
        live_ref[rows, :] = live_rows(count_ref[0, k], cap)
        if i < local_count:
            sx_ref[rows, :] = dot(pick_table(send_ref[k], nodes), node_ref[...]).astype(bf16)
    x_ref[:, width:] = dot(pick_ref[...], node_ref[...]).astype(bf16)
    part = dot(x_ref[:split, :width], w1_ref[:width, :])
    part += dot(x_ref[:split, width:], w1_ref[2 * width :, :])
    pre = part + dot(sx_ref[...], w1_ref[width : 2 * width, :])
    rows = slice(0, split)
    live = live_ref[rows, :1]
    forward_rows(pre, live, w2_ref[...], act_ref, slope_ref, normed_ref, inv_ref, msg_ref, rows)
    sum_ref[...] = dot(hot_ref[:, :split], msg_ref[...])
    part = dot(x_ref[split:, :width], w1_ref[:width, :])
    part_ref[...] = part + dot(x_ref[split:, width:], w1_ref[2 * width :, :])


def near_kernel(plan, *refs):
    first, count = plan
    part_ref, live_ref, hot_ref, sum_in_ref, w1_ref, w2_ref = refs[:6]
    sx_refs = refs[6 : 6 + count]
    act_ref, slope_ref, normed_ref, inv_ref, sum_ref, sx_ref, msg_ref = refs[6 + count :]
    total, width = sx_ref.shape
    stack_into(sx_ref, sx_refs)
    for j in range(2):
        rows = slice(j * total // 2, (j + 1) * total // 2)
        pre = part_ref[rows, :] + dot(sx_ref[rows, :], w1_ref[width : 2 * width, :])
        live = live_ref[first + rows.start : first + rows.stop, :1]
        forward_rows(pre, live, w2_ref[...], act_ref, slope_ref, normed_ref, inv_ref, msg_ref, rows)
    sum_ref[...] = sum_in_ref[...] + dot(hot_ref[:, first : first + total], msg_ref[...])


def far_kernel(plan, *refs):
    sets, sizes, first, part_first = plan
    count = len(sizes)
    (
        cotan_ref,
        part_ref,
        live_ref,
        pick_ref,
        hot_ref,
        sum_ref,
        w1_ref,
        w2_ref,
        node_ref,
        ncot_ref,
        n1_ref,
        n2_ref,
    ) = refs[:12]
    sx_refs, refs = refs[12 : 12 + count], refs[12 + count :]
    gpe_refs, refs = refs[:count], refs[count:]
    (
        act_ref,
        goe_ref,
        normed_ref,
        gathered_ref,
        gpn_ref,
        act_node_ref,
        gon_ref,
        gg_ref,
        node_new_ref,
        sx_ref,
        slope_ref,
        inv_ref,
        msg_ref,
        cot_ref,
        gpe_ref,
    ) = refs
    total, width = sx_ref.shape
    cap = cotan_ref.shape[1]
    stack_into(sx_ref, sx_refs)
    for i, k in enumerate(sets):
        cot_ref[i * cap : (i + 1) * cap, :] = cotan_ref[k]
    halves = [slice(j * total // 2, (j + 1) * total // 2) for j in range(2)]
    for rows in halves:
        pre = part_ref[part_first + rows.start : part_first + rows.stop, :]
        pre = pre + dot(sx_ref[rows, :], w1_ref[width : 2 * width, :])
        live = live_ref[first + rows.start : first + rows.stop, :1]
        forward_rows(pre, live, w2_ref[...], act_ref, slope_ref, normed_ref, inv_ref, msg_ref, rows)
    gathered = sum_ref[...] + dot(hot_ref[:, first : first + total], msg_ref[...])
    gathered = gathered.astype(bf16)
    gathered_ref[...] = gathered

    pre = dot(node_ref[...], n1_ref[:width, :]) + dot(gathered, n1_ref[width:, :])
    squashed = jax.nn.sigmoid(pre)
    act_node = (pre * squashed).astype(bf16)
    act_node_ref[...] = act_node
    normed, inverse = layer_norm(dot(act_node, n2_ref[...]))
    node_new_ref[...] = (node_ref[...].astype(f32) + normed).astype(bf16)
    gon = norm_back(normed, inverse, ncot_ref[...].astype(f32)).astype(bf16)
    gon_ref[...] = gon
    gpn = (dot_rt(gon, n2_ref[...]) * slope_of(pre, squashed)).astype(bf16)
    gpn_ref[...] = gpn
    gg_ref[...] = dot_rt(gpn, n1_ref[width:, :]).astype(bf16)

    for rows in halves:
        whole = slice(first + rows.start, first + rows.stop)
        goe, gpe = backward_rows(
            cot_ref[rows, :],
            dot(pick_ref[whole, :], gg_ref[...]),
            live_ref[whole, :1],
            normed_ref[rows, :],
            inv_ref[rows, :1],
            slope_ref[rows, :],
            w2_ref[...],
        )
        goe_ref[rows, :] = goe
        gpe_ref[rows, :] = gpe
    at = 0
    for out_ref, size in zip(gpe_refs, sizes):
        out_ref[...] = gpe_ref[at : at + size, :]
        at += size


def back_kernel(plan, *refs):
    sets, local_count = plan
    cotan_ref, live_ref, pick_ref, gg_ref, w2_ref = refs[:5]
    groups = (refs[5:8], refs[8:11])
    goe_ref, local_ref = refs[11:13]
    gpe_refs, (cot_ref, gpe_ref) = refs[13:-2], refs[-2:]
    cap = cotan_ref.shape[1]
    for i, k in enumerate(sets):
        cot_ref[i * cap : (i + 1) * cap, :] = cotan_ref[k]
    first = 0
    for slope_ref, normed_ref, inv_ref in groups:
        rows = slice(first, first + slope_ref.shape[0])
        goe, gpe = backward_rows(
            cot_ref[rows, :],
            dot(pick_ref[rows, :], gg_ref[...]),
            live_ref[rows, :1],
            normed_ref[...],
            inv_ref[:, :1],
            slope_ref[...],
            w2_ref[...],
        )
        goe_ref[rows, :] = goe
        gpe_ref[rows, :] = gpe
        first = rows.stop
    local_ref[...] = gpe_ref[: local_count * cap, :]
    for j, out_ref in enumerate(gpe_refs):
        i = local_count + j
        out_ref[...] = gpe_ref[i * cap : (i + 1) * cap, :]


def node_weight_kernel(me_ref, node_ref, gathered_ref, gpn_ref, act_node_ref, gon_ref, keep_ref, sent_ref, block_ref):
    put = functools.partial(put_block, me_ref, block_ref, keep_ref, sent_ref)
    put(0, node_ref[...], gpn_ref[...])
    put(1, gathered_ref[...], gpn_ref[...])
    put(2, act_node_ref[...], gon_ref[...])


def put_block(me_ref, block_ref, keep_ref, sent_ref, index, left_side, right_side):
    core = lax.rem(me_ref[0], 2)
    half = block_ref.shape[0] // 2
    block_ref[...] = dot_lt(left_side, right_side)
    keep_ref[index] = block_ref[pl.ds(pl.multiple_of(core * half, half), half), :]
    other = block_ref[pl.ds(pl.multiple_of((1 - core) * half, half), half), :]
    sent_ref[index] = other.astype(bf16)


def weight_kernel(plan, *refs):
    order, sx_count, gpe_count, act_count, goe_count = plan
    edge_ref, hot_ref, me_ref, node_ref = refs[:4]
    refs = refs[4:]
    sx_refs, refs = refs[:sx_count], refs[sx_count:]
    gpe_refs, refs = refs[:gpe_count], refs[gpe_count:]
    act_refs, refs = refs[:act_count], refs[act_count:]
    goe_refs, refs = refs[:goe_count], refs[goe_count:]
    keep_ref, sent_ref, rsum_ref, x_ref, sx_ref, gpe_ref, act_ref, goe_ref, block_ref = refs
    cap = edge_ref.shape[1]
    for i, k in enumerate(order):
        x_ref[i * cap : (i + 1) * cap, :] = edge_ref[k]
    stack_into(sx_ref, sx_refs)
    stack_into(gpe_ref, gpe_refs)
    stack_into(act_ref, act_refs)
    stack_into(goe_ref, goe_refs)
    recv_sum = dot(hot_ref[...], gpe_ref[...]).astype(bf16)
    rsum_ref[...] = recv_sum
    put = functools.partial(put_block, me_ref, block_ref, keep_ref, sent_ref)
    put(0, x_ref[...], gpe_ref[...])
    put(1, sx_ref[...], gpe_ref[...])
    put(2, node_ref[...], recv_sum)
    put(3, act_ref[...], goe_ref[...])


def base_kernel(ncot_ref, gpn_ref, rsum_ref, w1_ref, n1_ref, base_ref):
    width = w1_ref.shape[1]
    base_ref[...] = (
        ncot_ref[...].astype(f32)
        + dot_rt(gpn_ref[...], n1_ref[:width, :])
        + dot_rt(rsum_ref[...], w1_ref[2 * width :, :])
    )


def edge_kernel(plan, *refs):
    order, normed_count, gpe_count = plan
    edge_ref, cotan_ref, w1_ref, live_ref = refs[:4]
    refs = refs[4:]
    normed_refs, refs = refs[:normed_count], refs[normed_count:]
    gpe_refs, refs = refs[:gpe_count], refs[gpe_count:]
    new_ref, gedge_ref, gpe_ref = refs
    width = w1_ref.shape[1]
    cap = edge_ref.shape[1]
    stack_into(gpe_ref, gpe_refs)
    places = [(ref, at) for ref in normed_refs for at in range(0, ref.shape[0], cap)]
    for i, (k, (normed_ref, at)) in enumerate(zip(order, places)):
        rows = slice(i * cap, (i + 1) * cap)
        grad = cotan_ref[k].astype(f32) + dot_rt(gpe_ref[rows, :], w1_ref[:width, :])
        gedge_ref[k] = grad.astype(bf16)
        message = live_ref[rows, :1] * normed_ref[at : at + cap, :]
        new_ref[k] = (edge_ref[k].astype(f32) + message).astype(bf16)


def final_kernel(plan, *refs):
    base_ref, w1_ref = refs[:2]
    id_refs = refs[2 : 2 + len(plan)]
    row_refs = refs[2 + len(plan) : 2 + 2 * len(plan)]
    out_ref, hot_ref, rows_ref = refs[2 + 2 * len(plan) :]
    nodes, width = base_ref.shape
    cap = id_refs[0].shape[2]
    at = 0
    for id_ref, sets in zip(id_refs, plan):
        for k in sets:
            hot_ref[:, at : at + cap] = sum_table(id_ref[k], nodes)
            at += cap
    stack_into(rows_ref, row_refs)
    send_sum = dot(hot_ref[...], rows_ref[...]).astype(bf16)
    grad = base_ref[...] + dot_rt(send_sum, w1_ref[width : 2 * width, :])
    out_ref[...] = grad.astype(bf16)


def place(me_ref, stride, members):
    return lax.rem(lax.div(me_ref[0], stride), members)


def add_kernel(plan, *refs):
    came, stride, members = plan
    me_ref, keep_ref = refs[:2]
    arr_refs, out_refs = refs[2 : 2 + came], refs[2 + came :]
    size = keep_ref.shape[1] // members
    here = place(me_ref, stride, members)
    for j, out_ref in enumerate(out_refs):
        at = lax.rem(here + j, members) * size
        rows = pl.ds(pl.multiple_of(at, size), size)
        piece = keep_ref[:, rows, :]
        for arr_ref in arr_refs:
            piece += arr_ref[:, rows, :].astype(f32)
        out_ref[...] = piece.astype(out_ref.dtype)


def gather_kernel(plan, *refs):
    stride, members = plan
    me_ref, piece_refs, out_ref = refs[0], refs[1:-1], refs[-1]
    size = piece_refs[0].shape[1]
    here = place(me_ref, stride, members)
    for j, piece_ref in enumerate(piece_refs):
        at = lax.rem(here + members - j, members) * size
        out_ref[:, pl.ds(pl.multiple_of(at, size), size), :] = piece_ref[...]


def join_kernel(plan, *refs):
    members, blocks = plan
    me_ref = refs[0]
    piece_refs, other_refs = refs[1 : 1 + members], refs[1 + members : 1 + 2 * members]
    out_refs = refs[1 + 2 * members :]
    size = piece_refs[0].shape[1]
    core = lax.rem(me_ref[0], 2)
    here = place(me_ref, 2, members)
    for index, (which, block) in enumerate(blocks):
        first = 2 * block * members * size
        for side, side_refs in ((core, piece_refs), (1 - core, other_refs)):
            for j, piece_ref in enumerate(side_refs):
                at = first + (side * members + lax.rem(here + members - j, members)) * size
                rows = pl.ds(pl.multiple_of(at, size), size)
                out_refs[which][rows, :] = piece_ref[index]


def in_group(block, axis, stride, members, step):
    route = []
    for i in range(lax.axis_size(axis)):
        at = (i // stride) % members
        route.append((i, i + ((at + step) % members - at) * stride))
    return lax.ppermute(block, axis, route)


def split_of(bands):
    chips = bands // 2
    first = 1
    while first * first * 4 <= chips:
        first *= 2
    return first, chips // first


def add_stage(me, keep, arrived, stride, members, kind, after):
    count, rows, width = keep.shape
    shape = (count, rows // members, width)
    outs = call(
        functools.partial(add_kernel, (len(arrived), stride, members)),
        [(shape, kind)] + [(shape, bf16)] * (members - 1),
        [],
        me,
        keep,
        *arrived,
        smem=(0,),
        after=after,
    )
    return outs[0], [in_group(out, "band", stride, members, j + 1) for j, out in enumerate(outs[1:])]


def held_until(array, after):
    return pl.pallas_call(
        lambda *refs: None,
        out_shape=pltpu.VMEM(array.shape, array.dtype),
        in_specs=[pl.BlockSpec(memory_space=pltpu.VMEM)]
        + [pl.BlockSpec(memory_space=pl.ANY)] * len(after),
        out_specs=pl.BlockSpec(memory_space=pltpu.VMEM),
        input_output_aliases={0: 0},
        compiler_params=pltpu.CompilerParams(vmem_limit_bytes=1024 * 1024),
        cost_estimate=pl.CostEstimate(flops=1, bytes_accessed=1, transcendentals=0),
    )(pltpu.with_memory_space_constraint(array, pltpu.VMEM), *after)


def gather_stage(me, piece, stride, members, after):
    count, rows, width = piece.shape
    pieces = [piece] + [in_group(piece, "band", stride, members, j) for j in range(1, members)]
    (mine,) = call(
        functools.partial(gather_kernel, (stride, members)),
        [((count, rows * members, width), bf16)],
        [],
        me,
        *pieces,
        smem=(0,),
        after=after,
    )
    return mine


def join_stage(me, mine, members, blocks, shapes, after):
    pieces = [mine] + [in_group(mine, "band", 2, members, j) for j in range(1, members)]
    others = [in_group(one, "band", 1, 2, 1) for one in pieces]
    return call(
        functools.partial(join_kernel, (members, blocks)),
        [(shape, bf16) for shape in shapes],
        [],
        me,
        *pieces,
        *others,
        smem=(0,),
        after=after,
        last=range(len(shapes)),
    )


def reduce_whole(keep, sent):
    bands = lax.axis_size("band")
    chips = [[i for i in range(bands) if i % 2 == c] for c in range(2)]
    total = keep + in_group(sent, "band", 1, 2, 1).astype(f32)
    total = lax.psum(total.astype(bf16), "band", axis_index_groups=chips)
    other = in_group(total, "band", 1, 2, 1)
    core = lax.axis_index("band") % 2
    low, high = jnp.where(core == 0, total, other), jnp.where(core == 0, other, total)
    return jnp.concatenate([low, high], axis=1)


def local(
    node_latent,
    edge_latent,
    recv_slot,
    send_slot,
    edge_count,
    edge_first,
    edge_second,
    node_first,
    node_second,
    node_cotan,
    edge_cotan,
):
    bands = lax.axis_size("band")
    nodes, width = node_latent.shape
    sets, cap = edge_latent.shape[1:3]
    send_ids = send_slot.reshape(sets, 1, cap)
    me = lax.axis_index("band").astype(jnp.int32).reshape(1)

    def step_of(k):
        return band_offsets[k] % bands

    def reach(k):
        return min(step_of(k), bands - step_of(k))

    ordered = sorted(range(sets), key=lambda k: (reach(k), step_of(k)))
    near, far = tuple(ordered[:near_sets]), tuple(ordered[near_sets:])
    local_count = sum(step_of(k) == 0 for k in near)
    near_steps = [step_of(k) for k in near[local_count:]]
    far_steps = list(dict.fromkeys(step_of(k) for k in far))
    steps = near_steps + far_steps
    near_plan = tuple((k,) for k in near[local_count:])
    far_plan = tuple(tuple(k for k in far if step_of(k) == d) for d in far_steps)
    far = sum(far_plan, ())

    order = near + far

    ids = [passed_along(send_ids, "band", -d) for d in steps]
    (
        node_latent,
        send_ids,
        recv_ids,
        edges,
        edge_first,
        edge_second,
        node_first,
        node_second,
        node_cotan,
        cotan,
    ) = loaded(
        me,
        node_latent,
        send_ids,
        recv_slot.reshape(sets, 1, cap),
        edge_latent[0],
        edge_first,
        edge_second,
        node_first,
        node_second,
        node_cotan,
        edge_cotan[0],
    )
    picked = call(
        functools.partial(pick_kernel, near_plan + far_plan),
        [((len(piece) * cap, width), bf16) for piece in near_plan + far_plan],
        [],
        node_latent,
        *ids,
    )
    sx = [passed_along(block, "band", d) for block, d in zip(picked, steps)]
    sx_near, sx_far = sx[: len(near_plan)], sx[len(near_plan) :]

    local_rows, near_rows, far_rows = local_count * cap, len(near_plan) * cap, len(far) * cap
    total = sets * cap

    def forward_outs(rows):
        return [
            ((rows, width), bf16),
            ((rows, width), f32),
            ((rows, width), f32),
            ((rows, 128), f32),
            ((nodes, width), f32),
        ]

    pick, hot, live, part, sx_local, act_local, slope_local, normed_local, inv_local, node_sum = call(
        functools.partial(start_kernel, (order, local_count)),
        [
            ((total, nodes), bf16),
            ((nodes, total), bf16),
            ((total, 128), f32),
            ((near_rows + far_rows, width), f32),
            ((local_rows, width), bf16),
        ]
        + forward_outs(local_rows),
        [((total, 2 * width), bf16), ((local_rows, width), bf16)],
        edges,
        recv_ids,
        send_ids,
        in_hbm(edge_count),
        edge_first,
        edge_second,
        node_latent,
        smem=(3,),
        after=[picked[0]],
    )
    act_near, slope_near, normed_near, inv_near, node_sum = call(
        functools.partial(near_kernel, (local_rows, len(near_plan))),
        forward_outs(near_rows),
        [((near_rows, width), bf16), ((near_rows, width), bf16)],
        part,
        live,
        hot,
        node_sum,
        edge_first,
        edge_second,
        *sx_near,
    )
    sizes = [len(piece) * cap for piece in far_plan]
    outs = call(
        functools.partial(far_kernel, (far, sizes, local_rows + near_rows, near_rows)),
        [((size, width), bf16) for size in sizes]
        + [((far_rows, width), bf16), ((far_rows, width), bf16), ((far_rows, width), f32)]
        + [((nodes, width), bf16)] * 6,
        [
            ((far_rows, width), bf16),
            ((far_rows, width), f32),
            ((far_rows, 128), f32),
            ((far_rows, width), bf16),
            ((far_rows, width), bf16),
            ((far_rows, width), bf16),
        ],
        cotan,
        part,
        live,
        pick,
        hot,
        node_sum,
        edge_first,
        edge_second,
        node_latent,
        node_cotan,
        node_first,
        node_second,
        *sx_far,
        last=(len(sizes) + 8,),
    )
    gpe_far, outs = list(outs[: len(far_plan)]), outs[len(far_plan) :]
    act_far, goe_far, normed_far, gathered, gpn, act_node, gon, gg, node_new = outs
    back_far = [passed_along(block, "band", -d) for block, d in zip(gpe_far, far_steps)]

    half = (width // 2, width)
    outs = call(
        functools.partial(back_kernel, (near, local_count)),
        [((local_rows + near_rows, width), bf16), ((local_rows, width), bf16)]
        + [((cap, width), bf16)] * len(near_steps),
        [((local_rows + near_rows, width), bf16)] * 2,
        cotan,
        live,
        pick,
        gg,
        edge_second,
        slope_local,
        normed_local,
        inv_local,
        slope_near,
        normed_near,
        inv_near,
    )
    goe_near, gpe_local = outs[:2]
    gpe_near = list(outs[2:])
    back_near = [passed_along(block, "band", -d) for block, d in zip(gpe_near, near_steps)]

    gpe = [gpe_local] + gpe_near + gpe_far
    sx_all = [sx_local] + sx_near + sx_far
    keep_edge, sent_edge, recv_sum = call(
        functools.partial(weight_kernel, (order, len(sx_all), len(gpe), 3, 2)),
        [((4, *half), f32), ((4, *half), bf16), ((nodes, width), bf16)],
        [((total, width), bf16)] * 5 + [((width, width), f32)],
        edges,
        hot,
        me,
        node_latent,
        *sx_all,
        *gpe,
        act_local,
        act_near,
        act_far,
        goe_near,
        goe_far,
        smem=(2,),
    )

    def edge_outputs(after):
        return call(
            functools.partial(edge_kernel, (order, 3, len(gpe))),
            [((sets, cap, width), bf16), ((sets, cap, width), bf16)],
            [((total, width), bf16)],
            edges,
            cotan,
            edge_first,
            live,
            normed_local,
            normed_near,
            normed_far,
            *gpe,
            after=after,
            last=(0, 1),
        )

    def node_output(after):
        (base,) = call(
            base_kernel,
            [((nodes, width), f32)],
            [],
            node_cotan,
            gpn,
            recv_sum,
            edge_first,
            node_first,
            after=after,
        )
        (grad_nodes,) = call(
            functools.partial(final_kernel, (near[:local_count],) + near_plan + far_plan),
            [((nodes, width), bf16)],
            [((nodes, total), bf16), ((total, width), bf16)],
            base,
            edge_first,
            send_ids,
            *ids,
            gpe_local,
            *back_near,
            *back_far,
            last=(0,),
        )
        return grad_nodes

    def node_weights(after):
        return call(
            node_weight_kernel,
            [((3, *half), f32), ((3, *half), bf16)],
            [((width, width), f32)],
            me,
            node_latent,
            gathered,
            gpn,
            act_node,
            gon,
            smem=(0,),
            after=after,
        )

    first, second = split_of(bands)
    node_blocks, node_shapes = ((0, 0), (0, 1), (1, 0)), [(2 * width, width), (width, width)]
    edge_blocks = ((0, 0), (0, 1), (0, 2), (1, 0))
    edge_shapes = [(3 * width, width), (width, width)]
    if width // 2 % (16 * first * second) == 0:
        along_y, along_z = (2, first), (2 * first, second)
        sent_edge = held_until(sent_edge, back_far)
        came_edge = [in_group(sent_edge, "band", 1, 2, 1)]
        keep_node, sent_node = node_weights([sent_edge])
        came_node = [in_group(sent_node, "band", 1, 2, 1)]
        keep_edge, came_edge = add_stage(me, keep_edge, came_edge, *along_y, f32, [keep_node])
        keep_node, came_node = add_stage(me, keep_node, came_node, *along_y, f32, [keep_edge])
        edge_new, grad_edges = edge_outputs([keep_node])
        keep_edge, came_edge = add_stage(me, keep_edge, came_edge, *along_z, f32, [in_hbm(edge_new)])
        grad_nodes = node_output([keep_edge])
        keep_node, came_node = add_stage(me, keep_node, came_node, *along_z, f32, [in_hbm(grad_nodes)])
        piece_edge, _ = add_stage(me, keep_edge, came_edge, 1, 1, bf16, [keep_node])
        piece_node, _ = add_stage(me, keep_node, came_node, 1, 1, bf16, [piece_edge])
        mine_edge = gather_stage(me, piece_edge, *along_z, [piece_node])
        mine_node = gather_stage(me, piece_node, *along_z, [mine_edge])
        grad_e1, grad_e2 = join_stage(me, mine_edge, first, edge_blocks, edge_shapes, [mine_node])
        grad_n1, grad_n2 = join_stage(me, mine_node, first, node_blocks, node_shapes, [in_hbm(grad_e2)])
    else:
        whole = reduce_whole(*node_weights([]))
        grad_n1, grad_n2 = whole[:2].reshape(2 * width, width), whole[2]
        whole = reduce_whole(keep_edge, sent_edge)
        grad_e1, grad_e2 = whole[:3].reshape(3 * width, width), whole[3]
        edge_new, grad_edges = edge_outputs([])
        grad_nodes = node_output([])
    return (
        node_new,
        edge_new[None],
        grad_nodes,
        grad_edges[None],
        grad_e1,
        grad_e2,
        grad_n1,
        grad_n2,
    )


def solution(mesh):
    return jax.shard_map(
        local,
        mesh=mesh,
        in_specs=(
            P(("groups", "band"), None),
            P(("groups", "band"), None, None, None),
            P(("groups", "band"), None, None),
            P(("groups", "band"), None, None),
            P(("groups", "band"), None),
            P(),
            P(),
            P(),
            P(),
            P(("groups", "band"), None),
            P(("groups", "band"), None, None, None),
        ),
        out_specs=(
            P(("groups", "band"), None),
            P(("groups", "band"), None, None, None),
            P(("groups", "band"), None),
            P(("groups", "band"), None, None, None),
            P("groups", None),
            P("groups", None),
            P("groups", None),
            P("groups", None),
        ),
        check_vma=False,
    )
```

```python
import functools

import jax
import jax.numpy as jnp
from jax import lax
from jax.experimental import pallas as pl
from jax.experimental.pallas import tpu as pltpu
from jax.sharding import PartitionSpec as P

band_offsets = (0, 1, -1, 2, -2, 4, -4, 8, -8, 16, -16)
norm_eps = 1e-05
near_sets = 7
bf16 = jnp.bfloat16
f32 = jnp.float32
vmem_limit = 20 * 1024 * 1024


def passed_along(block, axis, distance):
    devices = range(lax.axis_size(axis))
    route = [((i - distance) % len(devices), i) for i in devices]
    return lax.ppermute(block, axis, route)


def layer_norm(inputs):
    average = jnp.mean(inputs, axis=-1, keepdims=True)
    centred = inputs - average
    inverse = lax.rsqrt(jnp.mean(centred * centred, axis=-1, keepdims=True) + norm_eps)
    return (centred * inverse, inverse)


def norm_back(normed, inverse, upstream):
    return inverse * (
        upstream
        - jnp.mean(upstream, axis=-1, keepdims=True)
        - normed * jnp.mean(upstream * normed, axis=-1, keepdims=True)
    )


def slope_of(inputs, squashed):
    return squashed * (1.0 + inputs * (1.0 - squashed))


def dot(left_side, right_side):
    return jnp.dot(left_side, right_side, preferred_element_type=f32)


def dot_rt(left_side, right_side):
    return lax.dot_general(
        left_side, right_side, (((1,), (1,)), ((), ())), preferred_element_type=f32
    )


def dot_lt(left_side, right_side):
    return lax.dot_general(
        left_side, right_side, (((0,), (0,)), ((), ())), preferred_element_type=f32
    )


def pick_table(ids, nodes):
    cap = ids.shape[1]
    down = jnp.transpose(jnp.broadcast_to(ids, (cap, cap)))
    parts = []
    for first in range(0, nodes, cap):
        wide = min(cap, nodes - first)
        lanes = lax.broadcasted_iota(jnp.int32, (cap, wide), 1) + first
        parts.append(jnp.where(down[:, :wide] == lanes, 1.0, 0.0).astype(bf16))
    return jnp.concatenate(parts, axis=1)


def sum_table(ids, nodes):
    down = lax.broadcasted_iota(jnp.int32, (nodes, ids.shape[1]), 0)
    return jnp.where(down == ids, 1.0, 0.0).astype(bf16)


def live_rows(count, cap):
    return (lax.broadcasted_iota(jnp.int32, (cap, 128), 0) < count).astype(f32)


def call(body, outs, scratch, *args, smem=(), after=(), last=()):
    spaces, given = [], []
    for i, arg in enumerate(args):
        spaces.append(pl.BlockSpec(memory_space=pltpu.SMEM if i in smem else pltpu.VMEM))
        given.append(arg if i in smem else pltpu.with_memory_space_constraint(arg, pltpu.VMEM))
    spaces += [pl.BlockSpec(memory_space=pl.ANY)] * len(after)

    def kernel(*refs):
        body(*refs[: len(args)], *refs[len(args) + len(after) :])

    return pl.pallas_call(
        kernel,
        out_shape=[
            (pltpu.HBM if i in last else pltpu.VMEM)(shape, kind)
            for i, (shape, kind) in enumerate(outs)
        ],
        in_specs=spaces,
        out_specs=[pl.BlockSpec(memory_space=pltpu.VMEM)] * len(outs),
        scratch_shapes=[pltpu.VMEM(shape, kind) for shape, kind in scratch],
        compiler_params=pltpu.CompilerParams(vmem_limit_bytes=vmem_limit),
        cost_estimate=pl.CostEstimate(flops=1, bytes_accessed=1, transcendentals=0),
    )(*given, *after)


def in_hbm(array):
    return pltpu.with_memory_space_constraint(array, pltpu.HBM)


def load_kernel(count, *refs):
    sems, refs = refs[-1], refs[1:]
    copies = [
        pltpu.make_async_copy(refs[i], refs[count + i], sems.at[i]) for i in range(count)
    ]
    for copy in copies:
        copy.start()
    for copy in copies:
        copy.wait()


def loaded(me, *args):
    count = len(args)
    return pl.pallas_call(
        functools.partial(load_kernel, count),
        out_shape=[pltpu.VMEM(arg.shape, arg.dtype) for arg in args],
        in_specs=[pl.BlockSpec(memory_space=pltpu.SMEM)]
        + [pl.BlockSpec(memory_space=pltpu.HBM)] * count,
        out_specs=[pl.BlockSpec(memory_space=pltpu.VMEM)] * count,
        scratch_shapes=[pltpu.SemaphoreType.DMA((count,))],
        compiler_params=pltpu.CompilerParams(vmem_limit_bytes=1024 * 1024),
        cost_estimate=pl.CostEstimate(flops=1, bytes_accessed=1, transcendentals=0),
    )(me, *[in_hbm(arg) for arg in args])


def pick_kernel(plan, *refs):
    node_ref = refs[0]
    nodes = node_ref.shape[0]
    for id_ref, out_ref, sets in zip(refs[1 : 1 + len(plan)], refs[1 + len(plan) :], plan):
        cap = id_ref.shape[2]
        for i, k in enumerate(sets):
            hot = pick_table(id_ref[k], nodes)
            out_ref[i * cap : (i + 1) * cap, :] = dot(hot, node_ref[...]).astype(bf16)


def forward_rows(pre, live, w2, act_ref, slope_ref, normed_ref, inv_ref, msg_ref, rows):
    squashed = jax.nn.sigmoid(pre)
    slope_ref[rows, :] = slope_of(pre, squashed)
    act = (pre * squashed).astype(bf16)
    act_ref[rows, :] = act
    normed, inverse = layer_norm(dot(act, w2))
    normed_ref[rows, :] = normed
    inv_ref[rows, :] = jnp.broadcast_to(inverse, (inverse.shape[0], 128))
    msg_ref[rows, :] = (live * normed).astype(bf16)


def backward_rows(cotan, picked, live, normed, inverse, slope, w2):
    upstream = live * (cotan.astype(f32) + picked)
    goe = norm_back(normed, inverse, upstream).astype(bf16)
    return goe, (dot_rt(goe, w2) * slope).astype(bf16)


def stack_into(out_ref, refs):
    first = 0
    for ref in refs:
        out_ref[first : first + ref.shape[0], :] = ref[...]
        first += ref.shape[0]


def start_kernel(plan, *refs):
    order, local_count = plan
    (
        edge_ref,
        recv_ref,
        send_ref,
        count_ref,
        w1_ref,
        w2_ref,
        node_ref,
        pick_ref,
        hot_ref,
        live_ref,
        part_ref,
        sx_ref,
        act_ref,
        slope_ref,
        normed_ref,
        inv_ref,
        sum_ref,
        x_ref,
        msg_ref,
    ) = refs
    nodes, width = node_ref.shape
    cap = recv_ref.shape[2]
    split = local_count * cap
    for i, k in enumerate(order):
        rows = slice(i * cap, (i + 1) * cap)
        x_ref[rows, :width] = edge_ref[k]
        pick_ref[rows, :] = pick_table(recv_ref[k], nodes)
        hot_ref[:, rows] = sum_table(recv_ref[k], nodes)
        live_ref[rows, :] = live_rows(count_ref[0, k], cap)
        if i < local_count:
            sx_ref[rows, :] = dot(pick_table(send_ref[k], nodes), node_ref[...]).astype(bf16)
    x_ref[:, width:] = dot(pick_ref[...], node_ref[...]).astype(bf16)
    part = dot(x_ref[:split, :width], w1_ref[:width, :])
    part += dot(x_ref[:split, width:], w1_ref[2 * width :, :])
    pre = part + dot(sx_ref[...], w1_ref[width : 2 * width, :])
    rows = slice(0, split)
    live = live_ref[rows, :1]
    forward_rows(pre, live, w2_ref[...], act_ref, slope_ref, normed_ref, inv_ref, msg_ref, rows)
    sum_ref[...] = dot(hot_ref[:, :split], msg_ref[...])
    part = dot(x_ref[split:, :width], w1_ref[:width, :])
    part_ref[...] = part + dot(x_ref[split:, width:], w1_ref[2 * width :, :])


def near_kernel(plan, *refs):
    first, count = plan
    part_ref, live_ref, hot_ref, sum_in_ref, w1_ref, w2_ref = refs[:6]
    sx_refs = refs[6 : 6 + count]
    act_ref, slope_ref, normed_ref, inv_ref, sum_ref, sx_ref, msg_ref = refs[6 + count :]
    total, width = sx_ref.shape
    stack_into(sx_ref, sx_refs)
    for j in range(2):
        rows = slice(j * total // 2, (j + 1) * total // 2)
        pre = part_ref[rows, :] + dot(sx_ref[rows, :], w1_ref[width : 2 * width, :])
        live = live_ref[first + rows.start : first + rows.stop, :1]
        forward_rows(pre, live, w2_ref[...], act_ref, slope_ref, normed_ref, inv_ref, msg_ref, rows)
    sum_ref[...] = sum_in_ref[...] + dot(hot_ref[:, first : first + total], msg_ref[...])


def far_kernel(plan, *refs):
    sets, sizes, first, part_first = plan
    count = len(sizes)
    (
        cotan_ref,
        part_ref,
        live_ref,
        pick_ref,
        hot_ref,
        sum_ref,
        w1_ref,
        w2_ref,
        node_ref,
        ncot_ref,
        n1_ref,
        n2_ref,
    ) = refs[:12]
    sx_refs, refs = refs[12 : 12 + count], refs[12 + count :]
    gpe_refs, refs = refs[:count], refs[count:]
    (
        act_ref,
        goe_ref,
        normed_ref,
        gathered_ref,
        gpn_ref,
        act_node_ref,
        gon_ref,
        gg_ref,
        node_new_ref,
        sx_ref,
        slope_ref,
        inv_ref,
        msg_ref,
        cot_ref,
        gpe_ref,
    ) = refs
    total, width = sx_ref.shape
    cap = cotan_ref.shape[1]
    stack_into(sx_ref, sx_refs)
    for i, k in enumerate(sets):
        cot_ref[i * cap : (i + 1) * cap, :] = cotan_ref[k]
    halves = [slice(j * total // 2, (j + 1) * total // 2) for j in range(2)]
    for rows in halves:
        pre = part_ref[part_first + rows.start : part_first + rows.stop, :]
        pre = pre + dot(sx_ref[rows, :], w1_ref[width : 2 * width, :])
        live = live_ref[first + rows.start : first + rows.stop, :1]
        forward_rows(pre, live, w2_ref[...], act_ref, slope_ref, normed_ref, inv_ref, msg_ref, rows)
    gathered = sum_ref[...] + dot(hot_ref[:, first : first + total], msg_ref[...])
    gathered = gathered.astype(bf16)
    gathered_ref[...] = gathered

    pre = dot(node_ref[...], n1_ref[:width, :]) + dot(gathered, n1_ref[width:, :])
    squashed = jax.nn.sigmoid(pre)
    act_node = (pre * squashed).astype(bf16)
    act_node_ref[...] = act_node
    normed, inverse = layer_norm(dot(act_node, n2_ref[...]))
    node_new_ref[...] = (node_ref[...].astype(f32) + normed).astype(bf16)
    gon = norm_back(normed, inverse, ncot_ref[...].astype(f32)).astype(bf16)
    gon_ref[...] = gon
    gpn = (dot_rt(gon, n2_ref[...]) * slope_of(pre, squashed)).astype(bf16)
    gpn_ref[...] = gpn
    gg_ref[...] = dot_rt(gpn, n1_ref[width:, :]).astype(bf16)

    for rows in halves:
        whole = slice(first + rows.start, first + rows.stop)
        goe, gpe = backward_rows(
            cot_ref[rows, :],
            dot(pick_ref[whole, :], gg_ref[...]),
            live_ref[whole, :1],
            normed_ref[rows, :],
            inv_ref[rows, :1],
            slope_ref[rows, :],
            w2_ref[...],
        )
        goe_ref[rows, :] = goe
        gpe_ref[rows, :] = gpe
    at = 0
    for out_ref, size in zip(gpe_refs, sizes):
        out_ref[...] = gpe_ref[at : at + size, :]
        at += size


def back_kernel(plan, *refs):
    sets, local_count = plan
    cotan_ref, live_ref, pick_ref, gg_ref, w2_ref = refs[:5]
    groups = (refs[5:8], refs[8:11])
    goe_ref, local_ref = refs[11:13]
    gpe_refs, (cot_ref, gpe_ref) = refs[13:-2], refs[-2:]
    cap = cotan_ref.shape[1]
    for i, k in enumerate(sets):
        cot_ref[i * cap : (i + 1) * cap, :] = cotan_ref[k]
    first = 0
    for slope_ref, normed_ref, inv_ref in groups:
        rows = slice(first, first + slope_ref.shape[0])
        goe, gpe = backward_rows(
            cot_ref[rows, :],
            dot(pick_ref[rows, :], gg_ref[...]),
            live_ref[rows, :1],
            normed_ref[...],
            inv_ref[:, :1],
            slope_ref[...],
            w2_ref[...],
        )
        goe_ref[rows, :] = goe
        gpe_ref[rows, :] = gpe
        first = rows.stop
    local_ref[...] = gpe_ref[: local_count * cap, :]
    for j, out_ref in enumerate(gpe_refs):
        i = local_count + j
        out_ref[...] = gpe_ref[i * cap : (i + 1) * cap, :]


def node_weight_kernel(me_ref, node_ref, gathered_ref, gpn_ref, act_node_ref, gon_ref, keep_ref, sent_ref, block_ref):
    put = functools.partial(put_block, me_ref, block_ref, keep_ref, sent_ref)
    put(0, node_ref[...], gpn_ref[...])
    put(1, gathered_ref[...], gpn_ref[...])
    put(2, act_node_ref[...], gon_ref[...])


def put_block(me_ref, block_ref, keep_ref, sent_ref, index, left_side, right_side):
    core = lax.rem(me_ref[0], 2)
    half = block_ref.shape[0] // 2
    block_ref[...] = dot_lt(left_side, right_side)
    keep_ref[index] = block_ref[pl.ds(pl.multiple_of(core * half, half), half), :]
    other = block_ref[pl.ds(pl.multiple_of((1 - core) * half, half), half), :]
    sent_ref[index] = other.astype(bf16)


def weight_kernel(plan, *refs):
    order, sx_count, gpe_count, act_count, goe_count = plan
    edge_ref, hot_ref, me_ref, node_ref = refs[:4]
    refs = refs[4:]
    sx_refs, refs = refs[:sx_count], refs[sx_count:]
    gpe_refs, refs = refs[:gpe_count], refs[gpe_count:]
    act_refs, refs = refs[:act_count], refs[act_count:]
    goe_refs, refs = refs[:goe_count], refs[goe_count:]
    keep_ref, sent_ref, rsum_ref, x_ref, sx_ref, gpe_ref, act_ref, goe_ref, block_ref = refs
    cap = edge_ref.shape[1]
    for i, k in enumerate(order):
        x_ref[i * cap : (i + 1) * cap, :] = edge_ref[k]
    stack_into(sx_ref, sx_refs)
    stack_into(gpe_ref, gpe_refs)
    stack_into(act_ref, act_refs)
    stack_into(goe_ref, goe_refs)
    recv_sum = dot(hot_ref[...], gpe_ref[...]).astype(bf16)
    rsum_ref[...] = recv_sum
    put = functools.partial(put_block, me_ref, block_ref, keep_ref, sent_ref)
    put(0, x_ref[...], gpe_ref[...])
    put(1, sx_ref[...], gpe_ref[...])
    put(2, node_ref[...], recv_sum)
    put(3, act_ref[...], goe_ref[...])


def base_kernel(ncot_ref, gpn_ref, rsum_ref, w1_ref, n1_ref, base_ref):
    width = w1_ref.shape[1]
    base_ref[...] = (
        ncot_ref[...].astype(f32)
        + dot_rt(gpn_ref[...], n1_ref[:width, :])
        + dot_rt(rsum_ref[...], w1_ref[2 * width :, :])
    )


def edge_kernel(plan, *refs):
    order, normed_count, gpe_count = plan
    edge_ref, cotan_ref, w1_ref, live_ref = refs[:4]
    refs = refs[4:]
    normed_refs, refs = refs[:normed_count], refs[normed_count:]
    gpe_refs, refs = refs[:gpe_count], refs[gpe_count:]
    new_ref, gedge_ref, gpe_ref = refs
    width = w1_ref.shape[1]
    cap = edge_ref.shape[1]
    stack_into(gpe_ref, gpe_refs)
    places = [(ref, at) for ref in normed_refs for at in range(0, ref.shape[0], cap)]
    for i, (k, (normed_ref, at)) in enumerate(zip(order, places)):
        rows = slice(i * cap, (i + 1) * cap)
        grad = cotan_ref[k].astype(f32) + dot_rt(gpe_ref[rows, :], w1_ref[:width, :])
        gedge_ref[k] = grad.astype(bf16)
        message = live_ref[rows, :1] * normed_ref[at : at + cap, :]
        new_ref[k] = (edge_ref[k].astype(f32) + message).astype(bf16)


def final_kernel(plan, *refs):
    base_ref, w1_ref = refs[:2]
    id_refs = refs[2 : 2 + len(plan)]
    row_refs = refs[2 + len(plan) : 2 + 2 * len(plan)]
    out_ref, hot_ref, rows_ref = refs[2 + 2 * len(plan) :]
    nodes, width = base_ref.shape
    cap = id_refs[0].shape[2]
    at = 0
    for id_ref, sets in zip(id_refs, plan):
        for k in sets:
            hot_ref[:, at : at + cap] = sum_table(id_ref[k], nodes)
            at += cap
    stack_into(rows_ref, row_refs)
    send_sum = dot(hot_ref[...], rows_ref[...]).astype(bf16)
    grad = base_ref[...] + dot_rt(send_sum, w1_ref[width : 2 * width, :])
    out_ref[...] = grad.astype(bf16)


def place(me_ref, stride, members):
    return lax.rem(lax.div(me_ref[0], stride), members)


def add_kernel(plan, *refs):
    came, stride, members = plan
    me_ref, keep_ref = refs[:2]
    arr_refs, out_refs = refs[2 : 2 + came], refs[2 + came :]
    size = keep_ref.shape[1] // members
    here = place(me_ref, stride, members)
    for j, out_ref in enumerate(out_refs):
        at = lax.rem(here + j, members) * size
        rows = pl.ds(pl.multiple_of(at, size), size)
        piece = keep_ref[:, rows, :]
        for arr_ref in arr_refs:
            piece += arr_ref[:, rows, :].astype(f32)
        out_ref[...] = piece.astype(out_ref.dtype)


def gather_kernel(plan, *refs):
    stride, members = plan
    me_ref, piece_refs, out_ref = refs[0], refs[1:-1], refs[-1]
    size = piece_refs[0].shape[1]
    here = place(me_ref, stride, members)
    for j, piece_ref in enumerate(piece_refs):
        at = lax.rem(here + members - j, members) * size
        out_ref[:, pl.ds(pl.multiple_of(at, size), size), :] = piece_ref[...]


def join_kernel(plan, *refs):
    members, blocks = plan
    me_ref = refs[0]
    piece_refs, other_refs = refs[1 : 1 + members], refs[1 + members : 1 + 2 * members]
    out_refs = refs[1 + 2 * members :]
    size = piece_refs[0].shape[1]
    core = lax.rem(me_ref[0], 2)
    here = place(me_ref, 2, members)
    for index, (which, block) in enumerate(blocks):
        first = 2 * block * members * size
        for side, side_refs in ((core, piece_refs), (1 - core, other_refs)):
            for j, piece_ref in enumerate(side_refs):
                at = first + (side * members + lax.rem(here + members - j, members)) * size
                rows = pl.ds(pl.multiple_of(at, size), size)
                out_refs[which][rows, :] = piece_ref[index]


def in_group(block, axis, stride, members, step):
    route = []
    for i in range(lax.axis_size(axis)):
        at = (i // stride) % members
        route.append((i, i + ((at + step) % members - at) * stride))
    return lax.ppermute(block, axis, route)


def split_of(bands):
    chips = bands // 2
    first = 1
    while first * first * 4 <= chips:
        first *= 2
    return first, chips // first


def add_stage(me, keep, arrived, stride, members, kind, after):
    count, rows, width = keep.shape
    shape = (count, rows // members, width)
    outs = call(
        functools.partial(add_kernel, (len(arrived), stride, members)),
        [(shape, kind)] + [(shape, bf16)] * (members - 1),
        [],
        me,
        keep,
        *arrived,
        smem=(0,),
        after=after,
    )
    return outs[0], [in_group(out, "band", stride, members, j + 1) for j, out in enumerate(outs[1:])]


def held_until(array, after):
    return pl.pallas_call(
        lambda *refs: None,
        out_shape=pltpu.VMEM(array.shape, array.dtype),
        in_specs=[pl.BlockSpec(memory_space=pltpu.VMEM)]
        + [pl.BlockSpec(memory_space=pl.ANY)] * len(after),
        out_specs=pl.BlockSpec(memory_space=pltpu.VMEM),
        input_output_aliases={0: 0},
        compiler_params=pltpu.CompilerParams(vmem_limit_bytes=1024 * 1024),
        cost_estimate=pl.CostEstimate(flops=1, bytes_accessed=1, transcendentals=0),
    )(pltpu.with_memory_space_constraint(array, pltpu.VMEM), *after)


def gather_stage(me, piece, stride, members, after):
    count, rows, width = piece.shape
    pieces = [piece] + [in_group(piece, "band", stride, members, j) for j in range(1, members)]
    (mine,) = call(
        functools.partial(gather_kernel, (stride, members)),
        [((count, rows * members, width), bf16)],
        [],
        me,
        *pieces,
        smem=(0,),
        after=after,
    )
    return mine


def join_stage(me, mine, members, blocks, shapes, after):
    pieces = [in_group(mine, "band", 2, members, j) for j in range(1, members)]
    pieces = [mine] + [held_until(piece, after) if after else piece for piece in pieces]
    others = [in_group(one, "band", 1, 2, 1) for one in pieces]
    return call(
        functools.partial(join_kernel, (members, blocks)),
        [(shape, bf16) for shape in shapes],
        [],
        me,
        *pieces,
        *others,
        smem=(0,),
        last=range(len(shapes)),
    )


def reduce_whole(keep, sent):
    bands = lax.axis_size("band")
    chips = [[i for i in range(bands) if i % 2 == c] for c in range(2)]
    total = keep + in_group(sent, "band", 1, 2, 1).astype(f32)
    total = lax.psum(total.astype(bf16), "band", axis_index_groups=chips)
    other = in_group(total, "band", 1, 2, 1)
    core = lax.axis_index("band") % 2
    low, high = jnp.where(core == 0, total, other), jnp.where(core == 0, other, total)
    return jnp.concatenate([low, high], axis=1)


def local(
    node_latent,
    edge_latent,
    recv_slot,
    send_slot,
    edge_count,
    edge_first,
    edge_second,
    node_first,
    node_second,
    node_cotan,
    edge_cotan,
):
    bands = lax.axis_size("band")
    nodes, width = node_latent.shape
    sets, cap = edge_latent.shape[1:3]
    send_ids = send_slot.reshape(sets, 1, cap)
    me = lax.axis_index("band").astype(jnp.int32).reshape(1)

    def step_of(k):
        return band_offsets[k] % bands

    def reach(k):
        return min(step_of(k), bands - step_of(k))

    ordered = sorted(range(sets), key=lambda k: (reach(k), step_of(k)))
    near, far = tuple(ordered[:near_sets]), tuple(ordered[near_sets:])
    local_count = sum(step_of(k) == 0 for k in near)
    near_steps = [step_of(k) for k in near[local_count:]]
    far_steps = list(dict.fromkeys(step_of(k) for k in far))
    steps = near_steps + far_steps
    near_plan = tuple((k,) for k in near[local_count:])
    far_plan = tuple(tuple(k for k in far if step_of(k) == d) for d in far_steps)
    far = sum(far_plan, ())

    order = near + far

    ids = [passed_along(send_ids, "band", -d) for d in steps]
    (
        node_latent,
        send_ids,
        recv_ids,
        edges,
        edge_first,
        edge_second,
        node_first,
        node_second,
        node_cotan,
        cotan,
    ) = loaded(
        me,
        node_latent,
        send_ids,
        recv_slot.reshape(sets, 1, cap),
        edge_latent[0],
        edge_first,
        edge_second,
        node_first,
        node_second,
        node_cotan,
        edge_cotan[0],
    )
    picked = call(
        functools.partial(pick_kernel, near_plan + far_plan),
        [((len(piece) * cap, width), bf16) for piece in near_plan + far_plan],
        [],
        node_latent,
        *ids,
    )
    sx = [passed_along(block, "band", d) for block, d in zip(picked, steps)]
    sx_near, sx_far = sx[: len(near_plan)], sx[len(near_plan) :]

    local_rows, near_rows, far_rows = local_count * cap, len(near_plan) * cap, len(far) * cap
    total = sets * cap

    def forward_outs(rows):
        return [
            ((rows, width), bf16),
            ((rows, width), f32),
            ((rows, width), f32),
            ((rows, 128), f32),
            ((nodes, width), f32),
        ]

    pick, hot, live, part, sx_local, act_local, slope_local, normed_local, inv_local, node_sum = call(
        functools.partial(start_kernel, (order, local_count)),
        [
            ((total, nodes), bf16),
            ((nodes, total), bf16),
            ((total, 128), f32),
            ((near_rows + far_rows, width), f32),
            ((local_rows, width), bf16),
        ]
        + forward_outs(local_rows),
        [((total, 2 * width), bf16), ((local_rows, width), bf16)],
        edges,
        recv_ids,
        send_ids,
        in_hbm(edge_count),
        edge_first,
        edge_second,
        node_latent,
        smem=(3,),
        after=[picked[0]],
    )
    act_near, slope_near, normed_near, inv_near, node_sum = call(
        functools.partial(near_kernel, (local_rows, len(near_plan))),
        forward_outs(near_rows),
        [((near_rows, width), bf16), ((near_rows, width), bf16)],
        part,
        live,
        hot,
        node_sum,
        edge_first,
        edge_second,
        *sx_near,
    )
    sizes = [len(piece) * cap for piece in far_plan]
    outs = call(
        functools.partial(far_kernel, (far, sizes, local_rows + near_rows, near_rows)),
        [((size, width), bf16) for size in sizes]
        + [((far_rows, width), bf16), ((far_rows, width), bf16), ((far_rows, width), f32)]
        + [((nodes, width), bf16)] * 6,
        [
            ((far_rows, width), bf16),
            ((far_rows, width), f32),
            ((far_rows, 128), f32),
            ((far_rows, width), bf16),
            ((far_rows, width), bf16),
            ((far_rows, width), bf16),
        ],
        cotan,
        part,
        live,
        pick,
        hot,
        node_sum,
        edge_first,
        edge_second,
        node_latent,
        node_cotan,
        node_first,
        node_second,
        *sx_far,
        last=(len(sizes) + 8,),
    )
    gpe_far, outs = list(outs[: len(far_plan)]), outs[len(far_plan) :]
    act_far, goe_far, normed_far, gathered, gpn, act_node, gon, gg, node_new = outs
    back_far = [passed_along(block, "band", -d) for block, d in zip(gpe_far, far_steps)]

    half = (width // 2, width)
    outs = call(
        functools.partial(back_kernel, (near, local_count)),
        [((local_rows + near_rows, width), bf16), ((local_rows, width), bf16)]
        + [((cap, width), bf16)] * len(near_steps),
        [((local_rows + near_rows, width), bf16)] * 2,
        cotan,
        live,
        pick,
        gg,
        edge_second,
        slope_local,
        normed_local,
        inv_local,
        slope_near,
        normed_near,
        inv_near,
    )
    goe_near, gpe_local = outs[:2]
    gpe_near = list(outs[2:])
    back_near = [passed_along(block, "band", -d) for block, d in zip(gpe_near, near_steps)]

    gpe = [gpe_local] + gpe_near + gpe_far
    sx_all = [sx_local] + sx_near + sx_far
    keep_edge, sent_edge, recv_sum = call(
        functools.partial(weight_kernel, (order, len(sx_all), len(gpe), 3, 2)),
        [((4, *half), f32), ((4, *half), bf16), ((nodes, width), bf16)],
        [((total, width), bf16)] * 5 + [((width, width), f32)],
        edges,
        hot,
        me,
        node_latent,
        *sx_all,
        *gpe,
        act_local,
        act_near,
        act_far,
        goe_near,
        goe_far,
        smem=(2,),
    )

    def edge_outputs(after):
        return call(
            functools.partial(edge_kernel, (order, 3, len(gpe))),
            [((sets, cap, width), bf16), ((sets, cap, width), bf16)],
            [((total, width), bf16)],
            edges,
            cotan,
            edge_first,
            live,
            normed_local,
            normed_near,
            normed_far,
            *gpe,
            after=after,
            last=(0, 1),
        )

    def node_output(after):
        (base,) = call(
            base_kernel,
            [((nodes, width), f32)],
            [],
            node_cotan,
            gpn,
            recv_sum,
            edge_first,
            node_first,
            after=after,
        )
        (grad_nodes,) = call(
            functools.partial(final_kernel, (near[:local_count],) + near_plan + far_plan),
            [((nodes, width), bf16)],
            [((nodes, total), bf16), ((total, width), bf16)],
            base,
            edge_first,
            send_ids,
            *ids,
            gpe_local,
            *back_near,
            *back_far,
            last=(0,),
        )
        return grad_nodes

    def node_weights(after):
        return call(
            node_weight_kernel,
            [((3, *half), f32), ((3, *half), bf16)],
            [((width, width), f32)],
            me,
            node_latent,
            gathered,
            gpn,
            act_node,
            gon,
            smem=(0,),
            after=after,
        )

    first, second = split_of(bands)
    node_blocks, node_shapes = ((0, 0), (0, 1), (1, 0)), [(2 * width, width), (width, width)]
    edge_blocks = ((0, 0), (0, 1), (0, 2), (1, 0))
    edge_shapes = [(3 * width, width), (width, width)]
    if width // 2 % (16 * first * second) == 0:
        along_y, along_z = (2, first), (2 * first, second)
        sent_edge = held_until(sent_edge, back_far[-1:])
        came_edge = [in_group(sent_edge, "band", 1, 2, 1)]
        keep_node, sent_node = node_weights([sent_edge])
        came_node = [in_group(sent_node, "band", 1, 2, 1)]
        keep_edge, came_edge = add_stage(me, keep_edge, came_edge, *along_y, f32, [keep_node])
        edge_new, grad_edges = edge_outputs([keep_edge])
        keep_edge, came_edge = add_stage(
            me, keep_edge, came_edge, *along_z, f32, [in_hbm(edge_new)] + back_near + back_far[:-1]
        )
        keep_node, came_node = add_stage(me, keep_node, came_node, *along_y, f32, [keep_edge])
        grad_nodes = node_output([keep_node])
        piece_edge, _ = add_stage(me, keep_edge, came_edge, 1, 1, bf16, [in_hbm(grad_nodes)])
        keep_node, came_node = add_stage(me, keep_node, came_node, *along_z, f32, [piece_edge])
        mine_edge = gather_stage(me, piece_edge, *along_z, [keep_node])
        piece_node, _ = add_stage(me, keep_node, came_node, 1, 1, bf16, [mine_edge])
        grad_e1, grad_e2 = join_stage(me, mine_edge, first, edge_blocks, edge_shapes, [piece_node])
        mine_node = gather_stage(me, piece_node, *along_z, [in_hbm(grad_e2)])
        grad_n1, grad_n2 = join_stage(me, mine_node, first, node_blocks, node_shapes, [])
    else:
        whole = reduce_whole(*node_weights([]))
        grad_n1, grad_n2 = whole[:2].reshape(2 * width, width), whole[2]
        whole = reduce_whole(keep_edge, sent_edge)
        grad_e1, grad_e2 = whole[:3].reshape(3 * width, width), whole[3]
        edge_new, grad_edges = edge_outputs([])
        grad_nodes = node_output([])
    return (
        node_new,
        edge_new[None],
        grad_nodes,
        grad_edges[None],
        grad_e1,
        grad_e2,
        grad_n1,
        grad_n2,
    )


def solution(mesh):
    return jax.shard_map(
        local,
        mesh=mesh,
        in_specs=(
            P(("groups", "band"), None),
            P(("groups", "band"), None, None, None),
            P(("groups", "band"), None, None),
            P(("groups", "band"), None, None),
            P(("groups", "band"), None),
            P(),
            P(),
            P(),
            P(),
            P(("groups", "band"), None),
            P(("groups", "band"), None, None, None),
        ),
        out_specs=(
            P(("groups", "band"), None),
            P(("groups", "band"), None, None, None),
            P(("groups", "band"), None),
            P(("groups", "band"), None, None, None),
            P("groups", None),
            P("groups", None),
            P("groups", None),
            P("groups", None),
        ),
        check_vma=False,
    )
```

```python
import functools

import jax
import jax.numpy as jnp
from jax import lax
from jax.experimental import pallas as pl
from jax.experimental.pallas import tpu as pltpu
from jax.sharding import PartitionSpec as P

band_offsets = (0, 1, -1, 2, -2, 4, -4, 8, -8, 16, -16)
norm_eps = 1e-05
near_sets = 7
bf16 = jnp.bfloat16
f32 = jnp.float32
vmem_limit = 20 * 1024 * 1024


def passed_along(block, axis, distance):
    devices = range(lax.axis_size(axis))
    route = [((i - distance) % len(devices), i) for i in devices]
    return lax.ppermute(block, axis, route)


def layer_norm(inputs):
    average = jnp.mean(inputs, axis=-1, keepdims=True)
    centred = inputs - average
    inverse = lax.rsqrt(jnp.mean(centred * centred, axis=-1, keepdims=True) + norm_eps)
    return (centred * inverse, inverse)


def norm_back(normed, inverse, upstream):
    return inverse * (
        upstream
        - jnp.mean(upstream, axis=-1, keepdims=True)
        - normed * jnp.mean(upstream * normed, axis=-1, keepdims=True)
    )


def slope_of(inputs, squashed):
    return squashed * (1.0 + inputs * (1.0 - squashed))


def dot(left_side, right_side):
    return jnp.dot(left_side, right_side, preferred_element_type=f32)


def dot_rt(left_side, right_side):
    return lax.dot_general(
        left_side, right_side, (((1,), (1,)), ((), ())), preferred_element_type=f32
    )


def dot_lt(left_side, right_side):
    return lax.dot_general(
        left_side, right_side, (((0,), (0,)), ((), ())), preferred_element_type=f32
    )


def pick_table(ids, nodes):
    cap = ids.shape[1]
    down = jnp.transpose(jnp.broadcast_to(ids, (cap, cap)))
    parts = []
    for first in range(0, nodes, cap):
        wide = min(cap, nodes - first)
        lanes = lax.broadcasted_iota(jnp.int32, (cap, wide), 1) + first
        parts.append(jnp.where(down[:, :wide] == lanes, 1.0, 0.0).astype(bf16))
    return jnp.concatenate(parts, axis=1)


def sum_table(ids, nodes):
    down = lax.broadcasted_iota(jnp.int32, (nodes, ids.shape[1]), 0)
    return jnp.where(down == ids, 1.0, 0.0).astype(bf16)


def live_rows(count, cap):
    return (lax.broadcasted_iota(jnp.int32, (cap, 128), 0) < count).astype(f32)


def call(body, outs, scratch, *args, smem=(), after=(), last=()):
    spaces, given = [], []
    for i, arg in enumerate(args):
        spaces.append(pl.BlockSpec(memory_space=pltpu.SMEM if i in smem else pltpu.VMEM))
        given.append(arg if i in smem else pltpu.with_memory_space_constraint(arg, pltpu.VMEM))
    spaces += [pl.BlockSpec(memory_space=pl.ANY)] * len(after)

    def kernel(*refs):
        body(*refs[: len(args)], *refs[len(args) + len(after) :])

    return pl.pallas_call(
        kernel,
        out_shape=[
            (pltpu.HBM if i in last else pltpu.VMEM)(shape, kind)
            for i, (shape, kind) in enumerate(outs)
        ],
        in_specs=spaces,
        out_specs=[pl.BlockSpec(memory_space=pltpu.VMEM)] * len(outs),
        scratch_shapes=[pltpu.VMEM(shape, kind) for shape, kind in scratch],
        compiler_params=pltpu.CompilerParams(vmem_limit_bytes=vmem_limit),
        cost_estimate=pl.CostEstimate(flops=1, bytes_accessed=1, transcendentals=0),
    )(*given, *after)


def in_hbm(array):
    return pltpu.with_memory_space_constraint(array, pltpu.HBM)


def load_kernel(count, *refs):
    sems, refs = refs[-1], refs[1:]
    copies = [
        pltpu.make_async_copy(refs[i], refs[count + i], sems.at[i]) for i in range(count)
    ]
    for copy in copies:
        copy.start()
    for copy in copies:
        copy.wait()


def loaded(me, *args):
    count = len(args)
    return pl.pallas_call(
        functools.partial(load_kernel, count),
        out_shape=[pltpu.VMEM(arg.shape, arg.dtype) for arg in args],
        in_specs=[pl.BlockSpec(memory_space=pltpu.SMEM)]
        + [pl.BlockSpec(memory_space=pltpu.HBM)] * count,
        out_specs=[pl.BlockSpec(memory_space=pltpu.VMEM)] * count,
        scratch_shapes=[pltpu.SemaphoreType.DMA((count,))],
        compiler_params=pltpu.CompilerParams(vmem_limit_bytes=1024 * 1024),
        cost_estimate=pl.CostEstimate(flops=1, bytes_accessed=1, transcendentals=0),
    )(me, *[in_hbm(arg) for arg in args])


def ask_kernel(plan, me_ref, send_ref, out_ref):
    bands = out_ref.shape[0]
    out_ref[...] = jnp.zeros_like(out_ref)
    for step, sets in plan:
        ids = [send_ref[k] for k in sets]
        blank = out_ref.shape[2] - len(sets) * send_ref.shape[2]
        if blank:
            ids.append(jnp.zeros((1, blank), jnp.int32))
        out_ref[lax.rem(me_ref[0] + bands - step, bands)] = jnp.concatenate(ids, axis=1)


def asked(me_ref, id_ref, step, index, cap):
    row = lax.rem(me_ref[0] + step, id_ref.shape[0])
    return id_ref[row][:, index * cap : (index + 1) * cap]


def pick_kernel(plan, me_ref, node_ref, id_ref, *out_refs):
    nodes = node_ref.shape[0]
    for out_ref, (step, sets) in zip(out_refs, plan):
        cap = out_ref.shape[0] // len(sets)
        for i in range(len(sets)):
            hot = pick_table(asked(me_ref, id_ref, step, i, cap), nodes)
            out_ref[i * cap : (i + 1) * cap, :] = dot(hot, node_ref[...]).astype(bf16)


def forward_rows(pre, live, w2, act_ref, slope_ref, normed_ref, inv_ref, msg_ref, rows):
    squashed = jax.nn.sigmoid(pre)
    slope_ref[rows, :] = slope_of(pre, squashed)
    act = (pre * squashed).astype(bf16)
    act_ref[rows, :] = act
    normed, inverse = layer_norm(dot(act, w2))
    normed_ref[rows, :] = normed
    inv_ref[rows, :] = jnp.broadcast_to(inverse, (inverse.shape[0], 128))
    msg_ref[rows, :] = (live * normed).astype(bf16)


def backward_rows(cotan, picked, live, normed, inverse, slope, w2):
    upstream = live * (cotan.astype(f32) + picked)
    goe = norm_back(normed, inverse, upstream).astype(bf16)
    return goe, (dot_rt(goe, w2) * slope).astype(bf16)


def stack_into(out_ref, refs):
    first = 0
    for ref in refs:
        out_ref[first : first + ref.shape[0], :] = ref[...]
        first += ref.shape[0]


def start_kernel(plan, *refs):
    order, local_count = plan
    (
        edge_ref,
        recv_ref,
        send_ref,
        count_ref,
        w1_ref,
        w2_ref,
        node_ref,
        pick_ref,
        hot_ref,
        live_ref,
        part_ref,
        sx_ref,
        act_ref,
        slope_ref,
        normed_ref,
        inv_ref,
        sum_ref,
        x_ref,
        msg_ref,
    ) = refs
    nodes, width = node_ref.shape
    cap = recv_ref.shape[2]
    split = local_count * cap
    for i, k in enumerate(order):
        rows = slice(i * cap, (i + 1) * cap)
        x_ref[rows, :width] = edge_ref[k]
        pick_ref[rows, :] = pick_table(recv_ref[k], nodes)
        hot_ref[:, rows] = sum_table(recv_ref[k], nodes)
        live_ref[rows, :] = live_rows(count_ref[0, k], cap)
        if i < local_count:
            sx_ref[rows, :] = dot(pick_table(send_ref[k], nodes), node_ref[...]).astype(bf16)
    x_ref[:, width:] = dot(pick_ref[...], node_ref[...]).astype(bf16)
    part = dot(x_ref[:split, :width], w1_ref[:width, :])
    part += dot(x_ref[:split, width:], w1_ref[2 * width :, :])
    pre = part + dot(sx_ref[...], w1_ref[width : 2 * width, :])
    rows = slice(0, split)
    live = live_ref[rows, :1]
    forward_rows(pre, live, w2_ref[...], act_ref, slope_ref, normed_ref, inv_ref, msg_ref, rows)
    sum_ref[...] = dot(hot_ref[:, :split], msg_ref[...])
    part = dot(x_ref[split:, :width], w1_ref[:width, :])
    part_ref[...] = part + dot(x_ref[split:, width:], w1_ref[2 * width :, :])


def near_kernel(plan, *refs):
    first, count = plan
    part_ref, live_ref, hot_ref, sum_in_ref, w1_ref, w2_ref = refs[:6]
    sx_refs = refs[6 : 6 + count]
    act_ref, slope_ref, normed_ref, inv_ref, sum_ref, sx_ref, msg_ref = refs[6 + count :]
    total, width = sx_ref.shape
    stack_into(sx_ref, sx_refs)
    for j in range(2):
        rows = slice(j * total // 2, (j + 1) * total // 2)
        pre = part_ref[rows, :] + dot(sx_ref[rows, :], w1_ref[width : 2 * width, :])
        live = live_ref[first + rows.start : first + rows.stop, :1]
        forward_rows(pre, live, w2_ref[...], act_ref, slope_ref, normed_ref, inv_ref, msg_ref, rows)
    sum_ref[...] = sum_in_ref[...] + dot(hot_ref[:, first : first + total], msg_ref[...])


def far_kernel(plan, *refs):
    sets, sizes, first, part_first = plan
    count = len(sizes)
    (
        cotan_ref,
        part_ref,
        live_ref,
        pick_ref,
        hot_ref,
        sum_ref,
        w1_ref,
        w2_ref,
        node_ref,
        ncot_ref,
        n1_ref,
        n2_ref,
    ) = refs[:12]
    sx_refs, refs = refs[12 : 12 + count], refs[12 + count :]
    gpe_refs, refs = refs[:count], refs[count:]
    (
        act_ref,
        goe_ref,
        normed_ref,
        gathered_ref,
        gpn_ref,
        act_node_ref,
        gon_ref,
        gg_ref,
        node_new_ref,
        sx_ref,
        slope_ref,
        inv_ref,
        msg_ref,
        cot_ref,
        gpe_ref,
    ) = refs
    total, width = sx_ref.shape
    cap = cotan_ref.shape[1]
    stack_into(sx_ref, sx_refs)
    for i, k in enumerate(sets):
        cot_ref[i * cap : (i + 1) * cap, :] = cotan_ref[k]
    halves = [slice(j * total // 2, (j + 1) * total // 2) for j in range(2)]
    for rows in halves:
        pre = part_ref[part_first + rows.start : part_first + rows.stop, :]
        pre = pre + dot(sx_ref[rows, :], w1_ref[width : 2 * width, :])
        live = live_ref[first + rows.start : first + rows.stop, :1]
        forward_rows(pre, live, w2_ref[...], act_ref, slope_ref, normed_ref, inv_ref, msg_ref, rows)
    gathered = sum_ref[...] + dot(hot_ref[:, first : first + total], msg_ref[...])
    gathered = gathered.astype(bf16)
    gathered_ref[...] = gathered

    pre = dot(node_ref[...], n1_ref[:width, :]) + dot(gathered, n1_ref[width:, :])
    squashed = jax.nn.sigmoid(pre)
    act_node = (pre * squashed).astype(bf16)
    act_node_ref[...] = act_node
    normed, inverse = layer_norm(dot(act_node, n2_ref[...]))
    node_new_ref[...] = (node_ref[...].astype(f32) + normed).astype(bf16)
    gon = norm_back(normed, inverse, ncot_ref[...].astype(f32)).astype(bf16)
    gon_ref[...] = gon
    gpn = (dot_rt(gon, n2_ref[...]) * slope_of(pre, squashed)).astype(bf16)
    gpn_ref[...] = gpn
    gg_ref[...] = dot_rt(gpn, n1_ref[width:, :]).astype(bf16)

    for rows in halves:
        whole = slice(first + rows.start, first + rows.stop)
        goe, gpe = backward_rows(
            cot_ref[rows, :],
            dot(pick_ref[whole, :], gg_ref[...]),
            live_ref[whole, :1],
            normed_ref[rows, :],
            inv_ref[rows, :1],
            slope_ref[rows, :],
            w2_ref[...],
        )
        goe_ref[rows, :] = goe
        gpe_ref[rows, :] = gpe
    at = 0
    for out_ref, size in zip(gpe_refs, sizes):
        out_ref[...] = gpe_ref[at : at + size, :]
        at += size


def back_kernel(plan, *refs):
    sets, local_count = plan
    cotan_ref, live_ref, pick_ref, gg_ref, w2_ref = refs[:5]
    groups = (refs[5:8], refs[8:11])
    goe_ref, local_ref = refs[11:13]
    gpe_refs, (cot_ref, gpe_ref) = refs[13:-2], refs[-2:]
    cap = cotan_ref.shape[1]
    for i, k in enumerate(sets):
        cot_ref[i * cap : (i + 1) * cap, :] = cotan_ref[k]
    first = 0
    for slope_ref, normed_ref, inv_ref in groups:
        rows = slice(first, first + slope_ref.shape[0])
        goe, gpe = backward_rows(
            cot_ref[rows, :],
            dot(pick_ref[rows, :], gg_ref[...]),
            live_ref[rows, :1],
            normed_ref[...],
            inv_ref[:, :1],
            slope_ref[...],
            w2_ref[...],
        )
        goe_ref[rows, :] = goe
        gpe_ref[rows, :] = gpe
        first = rows.stop
    local_ref[...] = gpe_ref[: local_count * cap, :]
    for j, out_ref in enumerate(gpe_refs):
        i = local_count + j
        out_ref[...] = gpe_ref[i * cap : (i + 1) * cap, :]


def node_weight_kernel(me_ref, node_ref, gathered_ref, gpn_ref, act_node_ref, gon_ref, keep_ref, sent_ref, block_ref):
    put = functools.partial(put_block, me_ref, block_ref, keep_ref, sent_ref)
    put(0, node_ref[...], gpn_ref[...])
    put(1, gathered_ref[...], gpn_ref[...])
    put(2, act_node_ref[...], gon_ref[...])


def put_block(me_ref, block_ref, keep_ref, sent_ref, index, left_side, right_side):
    core = lax.rem(me_ref[0], 2)
    half = block_ref.shape[0] // 2
    block_ref[...] = dot_lt(left_side, right_side)
    keep_ref[index] = block_ref[pl.ds(pl.multiple_of(core * half, half), half), :]
    other = block_ref[pl.ds(pl.multiple_of((1 - core) * half, half), half), :]
    sent_ref[index] = other.astype(bf16)


def weight_kernel(plan, *refs):
    order, sx_count, gpe_count, act_count, goe_count = plan
    edge_ref, hot_ref, me_ref, node_ref = refs[:4]
    refs = refs[4:]
    sx_refs, refs = refs[:sx_count], refs[sx_count:]
    gpe_refs, refs = refs[:gpe_count], refs[gpe_count:]
    act_refs, refs = refs[:act_count], refs[act_count:]
    goe_refs, refs = refs[:goe_count], refs[goe_count:]
    keep_ref, sent_ref, rsum_ref, x_ref, sx_ref, gpe_ref, act_ref, goe_ref, block_ref = refs
    cap = edge_ref.shape[1]
    for i, k in enumerate(order):
        x_ref[i * cap : (i + 1) * cap, :] = edge_ref[k]
    stack_into(sx_ref, sx_refs)
    stack_into(gpe_ref, gpe_refs)
    stack_into(act_ref, act_refs)
    stack_into(goe_ref, goe_refs)
    recv_sum = dot(hot_ref[...], gpe_ref[...]).astype(bf16)
    rsum_ref[...] = recv_sum
    put = functools.partial(put_block, me_ref, block_ref, keep_ref, sent_ref)
    put(0, x_ref[...], gpe_ref[...])
    put(1, sx_ref[...], gpe_ref[...])
    put(2, node_ref[...], recv_sum)
    put(3, act_ref[...], goe_ref[...])


def base_kernel(ncot_ref, gpn_ref, rsum_ref, w1_ref, n1_ref, base_ref):
    width = w1_ref.shape[1]
    base_ref[...] = (
        ncot_ref[...].astype(f32)
        + dot_rt(gpn_ref[...], n1_ref[:width, :])
        + dot_rt(rsum_ref[...], w1_ref[2 * width :, :])
    )


def edge_kernel(plan, *refs):
    order, normed_count, gpe_count = plan
    edge_ref, cotan_ref, w1_ref, live_ref = refs[:4]
    refs = refs[4:]
    normed_refs, refs = refs[:normed_count], refs[normed_count:]
    gpe_refs, refs = refs[:gpe_count], refs[gpe_count:]
    new_ref, gedge_ref, gpe_ref = refs
    width = w1_ref.shape[1]
    cap = edge_ref.shape[1]
    stack_into(gpe_ref, gpe_refs)
    places = [(ref, at) for ref in normed_refs for at in range(0, ref.shape[0], cap)]
    for i, (k, (normed_ref, at)) in enumerate(zip(order, places)):
        rows = slice(i * cap, (i + 1) * cap)
        grad = cotan_ref[k].astype(f32) + dot_rt(gpe_ref[rows, :], w1_ref[:width, :])
        gedge_ref[k] = grad.astype(bf16)
        message = live_ref[rows, :1] * normed_ref[at : at + cap, :]
        new_ref[k] = (edge_ref[k].astype(f32) + message).astype(bf16)


def final_kernel(plan, *refs):
    local_sets, remote = plan
    me_ref, base_ref, w1_ref, send_ref, id_ref = refs[:5]
    row_refs, (out_ref, hot_ref, rows_ref) = refs[5:-3], refs[-3:]
    nodes, width = base_ref.shape
    cap = send_ref.shape[2]
    ids = [send_ref[k] for k in local_sets]
    ids += [
        asked(me_ref, id_ref, step, i, cap) for step, sets in remote for i in range(len(sets))
    ]
    for i, one in enumerate(ids):
        hot_ref[:, i * cap : (i + 1) * cap] = sum_table(one, nodes)
    stack_into(rows_ref, row_refs)
    send_sum = dot(hot_ref[...], rows_ref[...]).astype(bf16)
    grad = base_ref[...] + dot_rt(send_sum, w1_ref[width : 2 * width, :])
    out_ref[...] = grad.astype(bf16)


def place(me_ref, stride, members):
    return lax.rem(lax.div(me_ref[0], stride), members)


def add_kernel(plan, *refs):
    came, stride, members = plan
    me_ref, keep_ref = refs[:2]
    arr_refs, out_refs = refs[2 : 2 + came], refs[2 + came :]
    size = keep_ref.shape[1] // members
    here = place(me_ref, stride, members)
    for j, out_ref in enumerate(out_refs):
        at = lax.rem(here + j, members) * size
        rows = pl.ds(pl.multiple_of(at, size), size)
        piece = keep_ref[:, rows, :]
        for arr_ref in arr_refs:
            piece += arr_ref[:, rows, :].astype(f32)
        out_ref[...] = piece.astype(out_ref.dtype)


def gather_kernel(plan, *refs):
    stride, members = plan
    me_ref, piece_refs, out_ref = refs[0], refs[1:-1], refs[-1]
    size = piece_refs[0].shape[1]
    here = place(me_ref, stride, members)
    for j, piece_ref in enumerate(piece_refs):
        at = lax.rem(here + members - j, members) * size
        out_ref[:, pl.ds(pl.multiple_of(at, size), size), :] = piece_ref[...]


def join_kernel(plan, *refs):
    members, blocks = plan
    me_ref = refs[0]
    piece_refs, other_refs = refs[1 : 1 + members], refs[1 + members : 1 + 2 * members]
    out_refs = refs[1 + 2 * members :]
    size = piece_refs[0].shape[1]
    core = lax.rem(me_ref[0], 2)
    here = place(me_ref, 2, members)
    for index, (which, block) in enumerate(blocks):
        first = 2 * block * members * size
        for side, side_refs in ((core, piece_refs), (1 - core, other_refs)):
            for j, piece_ref in enumerate(side_refs):
                at = first + (side * members + lax.rem(here + members - j, members)) * size
                rows = pl.ds(pl.multiple_of(at, size), size)
                out_refs[which][rows, :] = piece_ref[index]


def in_group(block, axis, stride, members, step):
    route = []
    for i in range(lax.axis_size(axis)):
        at = (i // stride) % members
        route.append((i, i + ((at + step) % members - at) * stride))
    return lax.ppermute(block, axis, route)


def split_of(bands):
    chips = bands // 2
    first = 1
    while first * first * 4 <= chips:
        first *= 2
    return first, chips // first


def add_stage(me, keep, arrived, stride, members, kind, after):
    count, rows, width = keep.shape
    shape = (count, rows // members, width)
    outs = call(
        functools.partial(add_kernel, (len(arrived), stride, members)),
        [(shape, kind)] + [(shape, bf16)] * (members - 1),
        [],
        me,
        keep,
        *arrived,
        smem=(0,),
        after=after,
    )
    return outs[0], [in_group(out, "band", stride, members, j + 1) for j, out in enumerate(outs[1:])]


def held_until(array, after):
    return pl.pallas_call(
        lambda *refs: None,
        out_shape=pltpu.VMEM(array.shape, array.dtype),
        in_specs=[pl.BlockSpec(memory_space=pltpu.VMEM)]
        + [pl.BlockSpec(memory_space=pl.ANY)] * len(after),
        out_specs=pl.BlockSpec(memory_space=pltpu.VMEM),
        input_output_aliases={0: 0},
        compiler_params=pltpu.CompilerParams(vmem_limit_bytes=1024 * 1024),
        cost_estimate=pl.CostEstimate(flops=1, bytes_accessed=1, transcendentals=0),
    )(pltpu.with_memory_space_constraint(array, pltpu.VMEM), *after)


def gather_stage(me, piece, stride, members, after):
    count, rows, width = piece.shape
    pieces = [piece] + [in_group(piece, "band", stride, members, j) for j in range(1, members)]
    (mine,) = call(
        functools.partial(gather_kernel, (stride, members)),
        [((count, rows * members, width), bf16)],
        [],
        me,
        *pieces,
        smem=(0,),
        after=after,
    )
    return mine


def join_stage(me, mine, members, blocks, shapes, after):
    pieces = [in_group(mine, "band", 2, members, j) for j in range(1, members)]
    pieces = [mine] + [held_until(piece, after) if after else piece for piece in pieces]
    others = [in_group(one, "band", 1, 2, 1) for one in pieces]
    return call(
        functools.partial(join_kernel, (members, blocks)),
        [(shape, bf16) for shape in shapes],
        [],
        me,
        *pieces,
        *others,
        smem=(0,),
        last=range(len(shapes)),
    )


def reduce_whole(keep, sent):
    bands = lax.axis_size("band")
    chips = [[i for i in range(bands) if i % 2 == c] for c in range(2)]
    total = keep + in_group(sent, "band", 1, 2, 1).astype(f32)
    total = lax.psum(total.astype(bf16), "band", axis_index_groups=chips)
    other = in_group(total, "band", 1, 2, 1)
    core = lax.axis_index("band") % 2
    low, high = jnp.where(core == 0, total, other), jnp.where(core == 0, other, total)
    return jnp.concatenate([low, high], axis=1)


def local(
    node_latent,
    edge_latent,
    recv_slot,
    send_slot,
    edge_count,
    edge_first,
    edge_second,
    node_first,
    node_second,
    node_cotan,
    edge_cotan,
):
    bands = lax.axis_size("band")
    nodes, width = node_latent.shape
    sets, cap = edge_latent.shape[1:3]
    send_ids = send_slot.reshape(sets, 1, cap)
    me = lax.axis_index("band").astype(jnp.int32).reshape(1)

    def step_of(k):
        return band_offsets[k] % bands

    def reach(k):
        return min(step_of(k), bands - step_of(k))

    ordered = sorted(range(sets), key=lambda k: (reach(k), step_of(k)))
    near, far = tuple(ordered[:near_sets]), tuple(ordered[near_sets:])
    local_count = sum(step_of(k) == 0 for k in near)
    near_steps = [step_of(k) for k in near[local_count:]]
    far_steps = list(dict.fromkeys(step_of(k) for k in far))
    steps = near_steps + far_steps
    near_plan = tuple((k,) for k in near[local_count:])
    far_plan = tuple(tuple(k for k in far if step_of(k) == d) for d in far_steps)
    far = sum(far_plan, ())

    order = near + far

    (
        node_latent,
        send_ids,
        recv_ids,
        edges,
        edge_first,
        edge_second,
        node_first,
        node_second,
        node_cotan,
        cotan,
    ) = loaded(
        me,
        node_latent,
        send_ids,
        recv_slot.reshape(sets, 1, cap),
        edge_latent[0],
        edge_first,
        edge_second,
        node_first,
        node_second,
        node_cotan,
        edge_cotan[0],
    )
    remote_plan = tuple(zip(steps, near_plan + far_plan))
    widest = max(len(piece) for piece in near_plan + far_plan)
    (ids,) = call(
        functools.partial(ask_kernel, remote_plan),
        [((bands, 1, widest * cap), jnp.int32)],
        [],
        me,
        send_ids,
        smem=(0,),
    )
    ids = lax.all_to_all(ids, "band", 0, 0, tiled=True)
    picked = call(
        functools.partial(pick_kernel, remote_plan),
        [((len(piece) * cap, width), bf16) for piece in near_plan + far_plan],
        [],
        me,
        node_latent,
        ids,
        smem=(0,),
    )
    sx = [passed_along(block, "band", d) for block, d in zip(picked, steps)]
    sx_near, sx_far = sx[: len(near_plan)], sx[len(near_plan) :]

    local_rows, near_rows, far_rows = local_count * cap, len(near_plan) * cap, len(far) * cap
    total = sets * cap

    def forward_outs(rows):
        return [
            ((rows, width), bf16),
            ((rows, width), f32),
            ((rows, width), f32),
            ((rows, 128), f32),
            ((nodes, width), f32),
        ]

    pick, hot, live, part, sx_local, act_local, slope_local, normed_local, inv_local, node_sum = call(
        functools.partial(start_kernel, (order, local_count)),
        [
            ((total, nodes), bf16),
            ((nodes, total), bf16),
            ((total, 128), f32),
            ((near_rows + far_rows, width), f32),
            ((local_rows, width), bf16),
        ]
        + forward_outs(local_rows),
        [((total, 2 * width), bf16), ((local_rows, width), bf16)],
        edges,
        recv_ids,
        send_ids,
        in_hbm(edge_count),
        edge_first,
        edge_second,
        node_latent,
        smem=(3,),
        after=[picked[0]],
    )
    act_near, slope_near, normed_near, inv_near, node_sum = call(
        functools.partial(near_kernel, (local_rows, len(near_plan))),
        forward_outs(near_rows),
        [((near_rows, width), bf16), ((near_rows, width), bf16)],
        part,
        live,
        hot,
        node_sum,
        edge_first,
        edge_second,
        *sx_near,
    )
    sizes = [len(piece) * cap for piece in far_plan]
    outs = call(
        functools.partial(far_kernel, (far, sizes, local_rows + near_rows, near_rows)),
        [((size, width), bf16) for size in sizes]
        + [((far_rows, width), bf16), ((far_rows, width), bf16), ((far_rows, width), f32)]
        + [((nodes, width), bf16)] * 6,
        [
            ((far_rows, width), bf16),
            ((far_rows, width), f32),
            ((far_rows, 128), f32),
            ((far_rows, width), bf16),
            ((far_rows, width), bf16),
            ((far_rows, width), bf16),
        ],
        cotan,
        part,
        live,
        pick,
        hot,
        node_sum,
        edge_first,
        edge_second,
        node_latent,
        node_cotan,
        node_first,
        node_second,
        *sx_far,
        last=(len(sizes) + 8,),
    )
    gpe_far, outs = list(outs[: len(far_plan)]), outs[len(far_plan) :]
    act_far, goe_far, normed_far, gathered, gpn, act_node, gon, gg, node_new = outs
    back_far = [passed_along(block, "band", -d) for block, d in zip(gpe_far, far_steps)]

    half = (width // 2, width)
    outs = call(
        functools.partial(back_kernel, (near, local_count)),
        [((local_rows + near_rows, width), bf16), ((local_rows, width), bf16)]
        + [((cap, width), bf16)] * len(near_steps),
        [((local_rows + near_rows, width), bf16)] * 2,
        cotan,
        live,
        pick,
        gg,
        edge_second,
        slope_local,
        normed_local,
        inv_local,
        slope_near,
        normed_near,
        inv_near,
    )
    goe_near, gpe_local = outs[:2]
    gpe_near = list(outs[2:])
    back_near = [passed_along(block, "band", -d) for block, d in zip(gpe_near, near_steps)]

    gpe = [gpe_local] + gpe_near + gpe_far
    sx_all = [sx_local] + sx_near + sx_far
    keep_edge, sent_edge, recv_sum = call(
        functools.partial(weight_kernel, (order, len(sx_all), len(gpe), 3, 2)),
        [((4, *half), f32), ((4, *half), bf16), ((nodes, width), bf16)],
        [((total, width), bf16)] * 5 + [((width, width), f32)],
        edges,
        hot,
        me,
        node_latent,
        *sx_all,
        *gpe,
        act_local,
        act_near,
        act_far,
        goe_near,
        goe_far,
        smem=(2,),
    )

    def edge_outputs(after):
        return call(
            functools.partial(edge_kernel, (order, 3, len(gpe))),
            [((sets, cap, width), bf16), ((sets, cap, width), bf16)],
            [((total, width), bf16)],
            edges,
            cotan,
            edge_first,
            live,
            normed_local,
            normed_near,
            normed_far,
            *gpe,
            after=after,
            last=(0, 1),
        )

    def node_output(after):
        (base,) = call(
            base_kernel,
            [((nodes, width), f32)],
            [],
            node_cotan,
            gpn,
            recv_sum,
            edge_first,
            node_first,
            after=after,
        )
        (grad_nodes,) = call(
            functools.partial(final_kernel, (near[:local_count], remote_plan)),
            [((nodes, width), bf16)],
            [((nodes, total), bf16), ((total, width), bf16)],
            me,
            base,
            edge_first,
            send_ids,
            ids,
            gpe_local,
            *back_near,
            *back_far,
            smem=(0,),
            last=(0,),
        )
        return grad_nodes

    def node_weights(after):
        return call(
            node_weight_kernel,
            [((3, *half), f32), ((3, *half), bf16)],
            [((width, width), f32)],
            me,
            node_latent,
            gathered,
            gpn,
            act_node,
            gon,
            smem=(0,),
            after=after,
        )

    first, second = split_of(bands)
    node_blocks, node_shapes = ((0, 0), (0, 1), (1, 0)), [(2 * width, width), (width, width)]
    edge_blocks = ((0, 0), (0, 1), (0, 2), (1, 0))
    edge_shapes = [(3 * width, width), (width, width)]
    if width // 2 % (16 * first * second) == 0:
        along_y, along_z = (2, first), (2 * first, second)
        sent_edge = held_until(sent_edge, back_far[-1:])
        came_edge = [in_group(sent_edge, "band", 1, 2, 1)]
        keep_edge, came_edge = add_stage(me, keep_edge, came_edge, *along_y, f32, back_near)
        edge_new, grad_edges = edge_outputs([keep_edge])
        keep_node, sent_node = node_weights([in_hbm(edge_new)])
        came_node = [in_group(sent_node, "band", 1, 2, 1)]
        keep_edge, came_edge = add_stage(
            me, keep_edge, came_edge, *along_z, f32, [keep_node] + back_far[:-1]
        )
        keep_node, came_node = add_stage(me, keep_node, came_node, *along_y, f32, [keep_edge])
        grad_nodes = node_output([keep_node])
        piece_edge, _ = add_stage(me, keep_edge, came_edge, 1, 1, bf16, [in_hbm(grad_nodes)])
        keep_node, came_node = add_stage(me, keep_node, came_node, *along_z, f32, [piece_edge])
        mine_edge = gather_stage(me, piece_edge, *along_z, [keep_node])
        piece_node, _ = add_stage(me, keep_node, came_node, 1, 1, bf16, [mine_edge])
        grad_e1, grad_e2 = join_stage(me, mine_edge, first, edge_blocks, edge_shapes, [piece_node])
        mine_node = gather_stage(me, piece_node, *along_z, [in_hbm(grad_e2)])
        grad_n1, grad_n2 = join_stage(me, mine_node, first, node_blocks, node_shapes, [])
    else:
        whole = reduce_whole(*node_weights([]))
        grad_n1, grad_n2 = whole[:2].reshape(2 * width, width), whole[2]
        whole = reduce_whole(keep_edge, sent_edge)
        grad_e1, grad_e2 = whole[:3].reshape(3 * width, width), whole[3]
        edge_new, grad_edges = edge_outputs([])
        grad_nodes = node_output([])
    return (
        node_new,
        edge_new[None],
        grad_nodes,
        grad_edges[None],
        grad_e1,
        grad_e2,
        grad_n1,
        grad_n2,
    )


def solution(mesh):
    return jax.shard_map(
        local,
        mesh=mesh,
        in_specs=(
            P(("groups", "band"), None),
            P(("groups", "band"), None, None, None),
            P(("groups", "band"), None, None),
            P(("groups", "band"), None, None),
            P(("groups", "band"), None),
            P(),
            P(),
            P(),
            P(),
            P(("groups", "band"), None),
            P(("groups", "band"), None, None, None),
        ),
        out_specs=(
            P(("groups", "band"), None),
            P(("groups", "band"), None, None, None),
            P(("groups", "band"), None),
            P(("groups", "band"), None, None, None),
            P("groups", None),
            P("groups", None),
            P("groups", None),
            P("groups", None),
        ),
        check_vma=False,
    )
```

```python
import functools

import jax
import jax.numpy as jnp
from jax import lax
from jax.experimental import pallas as pl
from jax.experimental.pallas import tpu as pltpu
from jax.sharding import PartitionSpec as P

band_offsets = (0, 1, -1, 2, -2, 4, -4, 8, -8, 16, -16)
norm_eps = 1e-05
near_sets = 7
bf16 = jnp.bfloat16
f32 = jnp.float32
vmem_limit = 20 * 1024 * 1024


def passed_along(block, axis, distance):
    devices = range(lax.axis_size(axis))
    route = [((i - distance) % len(devices), i) for i in devices]
    return lax.ppermute(block, axis, route)


def layer_norm(inputs):
    average = jnp.mean(inputs, axis=-1, keepdims=True)
    centred = inputs - average
    inverse = lax.rsqrt(jnp.mean(centred * centred, axis=-1, keepdims=True) + norm_eps)
    return (centred * inverse, inverse)


def norm_back(normed, inverse, upstream):
    return inverse * (
        upstream
        - jnp.mean(upstream, axis=-1, keepdims=True)
        - normed * jnp.mean(upstream * normed, axis=-1, keepdims=True)
    )


def slope_of(inputs, squashed):
    return squashed * (1.0 + inputs * (1.0 - squashed))


def dot(left_side, right_side):
    return jnp.dot(left_side, right_side, preferred_element_type=f32)


def dot_rt(left_side, right_side):
    return lax.dot_general(
        left_side, right_side, (((1,), (1,)), ((), ())), preferred_element_type=f32
    )


def dot_lt(left_side, right_side):
    return lax.dot_general(
        left_side, right_side, (((0,), (0,)), ((), ())), preferred_element_type=f32
    )


def pick_table(ids, nodes):
    cap = ids.shape[1]
    down = jnp.transpose(jnp.broadcast_to(ids, (cap, cap)))
    parts = []
    for first in range(0, nodes, cap):
        wide = min(cap, nodes - first)
        lanes = lax.broadcasted_iota(jnp.int32, (cap, wide), 1) + first
        parts.append(jnp.where(down[:, :wide] == lanes, 1.0, 0.0).astype(bf16))
    return jnp.concatenate(parts, axis=1)


def sum_table(ids, nodes):
    down = lax.broadcasted_iota(jnp.int32, (nodes, ids.shape[1]), 0)
    return jnp.where(down == ids, 1.0, 0.0).astype(bf16)


def live_rows(count, cap):
    return (lax.broadcasted_iota(jnp.int32, (cap, 128), 0) < count).astype(f32)


def call(body, outs, scratch, *args, smem=(), after=(), last=()):
    spaces, given = [], []
    for i, arg in enumerate(args):
        spaces.append(pl.BlockSpec(memory_space=pltpu.SMEM if i in smem else pltpu.VMEM))
        given.append(arg if i in smem else pltpu.with_memory_space_constraint(arg, pltpu.VMEM))
    spaces += [pl.BlockSpec(memory_space=pl.ANY)] * len(after)

    def kernel(*refs):
        body(*refs[: len(args)], *refs[len(args) + len(after) :])

    return pl.pallas_call(
        kernel,
        out_shape=[
            (pltpu.HBM if i in last else pltpu.VMEM)(shape, kind)
            for i, (shape, kind) in enumerate(outs)
        ],
        in_specs=spaces,
        out_specs=[pl.BlockSpec(memory_space=pltpu.VMEM)] * len(outs),
        scratch_shapes=[pltpu.VMEM(shape, kind) for shape, kind in scratch],
        compiler_params=pltpu.CompilerParams(vmem_limit_bytes=vmem_limit),
        cost_estimate=pl.CostEstimate(flops=1, bytes_accessed=1, transcendentals=0),
    )(*given, *after)


def in_hbm(array):
    return pltpu.with_memory_space_constraint(array, pltpu.HBM)


def load_kernel(count, *refs):
    sems, refs = refs[-1], refs[1:]
    copies = [
        pltpu.make_async_copy(refs[i], refs[count + i], sems.at[i]) for i in range(count)
    ]
    for copy in copies:
        copy.start()
    for copy in copies:
        copy.wait()


def loaded(me, *args):
    count = len(args)
    return pl.pallas_call(
        functools.partial(load_kernel, count),
        out_shape=[pltpu.VMEM(arg.shape, arg.dtype) for arg in args],
        in_specs=[pl.BlockSpec(memory_space=pltpu.SMEM)]
        + [pl.BlockSpec(memory_space=pltpu.HBM)] * count,
        out_specs=[pl.BlockSpec(memory_space=pltpu.VMEM)] * count,
        scratch_shapes=[pltpu.SemaphoreType.DMA((count,))],
        compiler_params=pltpu.CompilerParams(vmem_limit_bytes=1024 * 1024),
        cost_estimate=pl.CostEstimate(flops=1, bytes_accessed=1, transcendentals=0),
    )(me, *[in_hbm(arg) for arg in args])


def ask_kernel(plan, me_ref, send_ref, out_ref):
    bands = out_ref.shape[0]
    out_ref[...] = jnp.zeros_like(out_ref)
    for step, sets in plan:
        ids = [send_ref[k] for k in sets]
        blank = out_ref.shape[2] - len(sets) * send_ref.shape[2]
        if blank:
            ids.append(jnp.zeros((1, blank), jnp.int32))
        out_ref[lax.rem(me_ref[0] + bands - step, bands)] = jnp.concatenate(ids, axis=1)


def asked(me_ref, id_ref, step, index, cap):
    row = lax.rem(me_ref[0] + step, id_ref.shape[0])
    return id_ref[row][:, index * cap : (index + 1) * cap]


def pick_kernel(plan, me_ref, node_ref, id_ref, *out_refs):
    nodes = node_ref.shape[0]
    for out_ref, (step, sets) in zip(out_refs, plan):
        cap = out_ref.shape[0] // len(sets)
        for i in range(len(sets)):
            hot = pick_table(asked(me_ref, id_ref, step, i, cap), nodes)
            out_ref[i * cap : (i + 1) * cap, :] = dot(hot, node_ref[...]).astype(bf16)


def forward_rows(pre, live, w2, act_ref, slope_ref, normed_ref, inv_ref, msg_ref, rows):
    squashed = jax.nn.sigmoid(pre)
    slope_ref[rows, :] = slope_of(pre, squashed)
    act = (pre * squashed).astype(bf16)
    act_ref[rows, :] = act
    normed, inverse = layer_norm(dot(act, w2))
    normed_ref[rows, :] = normed
    inv_ref[rows, :] = jnp.broadcast_to(inverse, (inverse.shape[0], 128))
    msg_ref[rows, :] = (live * normed).astype(bf16)


def backward_rows(cotan, picked, live, normed, inverse, slope, w2):
    upstream = live * (cotan.astype(f32) + picked)
    goe = norm_back(normed, inverse, upstream).astype(bf16)
    return goe, (dot_rt(goe, w2) * slope).astype(bf16)


def stack_into(out_ref, refs):
    first = 0
    for ref in refs:
        out_ref[first : first + ref.shape[0], :] = ref[...]
        first += ref.shape[0]


def start_kernel(plan, *refs):
    order, local_count = plan
    (
        edge_ref,
        recv_ref,
        send_ref,
        count_ref,
        w1_ref,
        w2_ref,
        node_ref,
        pick_ref,
        hot_ref,
        live_ref,
        part_ref,
        sx_ref,
        act_ref,
        slope_ref,
        normed_ref,
        inv_ref,
        sum_ref,
        x_ref,
        msg_ref,
    ) = refs
    nodes, width = node_ref.shape
    cap = recv_ref.shape[2]
    split = local_count * cap
    for i, k in enumerate(order):
        rows = slice(i * cap, (i + 1) * cap)
        x_ref[rows, :width] = edge_ref[k]
        pick_ref[rows, :] = pick_table(recv_ref[k], nodes)
        hot_ref[:, rows] = sum_table(recv_ref[k], nodes)
        live_ref[rows, :] = live_rows(count_ref[0, k], cap)
        if i < local_count:
            sx_ref[rows, :] = dot(pick_table(send_ref[k], nodes), node_ref[...]).astype(bf16)
    x_ref[:, width:] = dot(pick_ref[...], node_ref[...]).astype(bf16)
    part = dot(x_ref[:split, :width], w1_ref[:width, :])
    part += dot(x_ref[:split, width:], w1_ref[2 * width :, :])
    pre = part + dot(sx_ref[...], w1_ref[width : 2 * width, :])
    rows = slice(0, split)
    live = live_ref[rows, :1]
    forward_rows(pre, live, w2_ref[...], act_ref, slope_ref, normed_ref, inv_ref, msg_ref, rows)
    sum_ref[...] = dot(hot_ref[:, :split], msg_ref[...])
    part = dot(x_ref[split:, :width], w1_ref[:width, :])
    part_ref[...] = part + dot(x_ref[split:, width:], w1_ref[2 * width :, :])


def near_kernel(plan, *refs):
    first, count = plan
    part_ref, live_ref, hot_ref, sum_in_ref, w1_ref, w2_ref = refs[:6]
    sx_refs = refs[6 : 6 + count]
    act_ref, slope_ref, normed_ref, inv_ref, sum_ref, sx_ref, msg_ref = refs[6 + count :]
    total, width = sx_ref.shape
    stack_into(sx_ref, sx_refs)
    for j in range(2):
        rows = slice(j * total // 2, (j + 1) * total // 2)
        pre = part_ref[rows, :] + dot(sx_ref[rows, :], w1_ref[width : 2 * width, :])
        live = live_ref[first + rows.start : first + rows.stop, :1]
        forward_rows(pre, live, w2_ref[...], act_ref, slope_ref, normed_ref, inv_ref, msg_ref, rows)
    sum_ref[...] = sum_in_ref[...] + dot(hot_ref[:, first : first + total], msg_ref[...])


def far_kernel(plan, *refs):
    sets, sizes, first, part_first = plan
    count = len(sizes)
    (
        cotan_ref,
        part_ref,
        live_ref,
        pick_ref,
        hot_ref,
        sum_ref,
        w1_ref,
        w2_ref,
        node_ref,
        ncot_ref,
        n1_ref,
        n2_ref,
    ) = refs[:12]
    sx_refs, refs = refs[12 : 12 + count], refs[12 + count :]
    gpe_refs, refs = refs[:count], refs[count:]
    (
        act_ref,
        goe_ref,
        normed_ref,
        gathered_ref,
        gpn_ref,
        act_node_ref,
        gon_ref,
        gg_ref,
        node_new_ref,
        sx_ref,
        slope_ref,
        inv_ref,
        msg_ref,
        cot_ref,
        gpe_ref,
    ) = refs
    total, width = sx_ref.shape
    cap = cotan_ref.shape[1]
    stack_into(sx_ref, sx_refs)
    for i, k in enumerate(sets):
        cot_ref[i * cap : (i + 1) * cap, :] = cotan_ref[k]
    halves = [slice(j * total // 2, (j + 1) * total // 2) for j in range(2)]
    for rows in halves:
        pre = part_ref[part_first + rows.start : part_first + rows.stop, :]
        pre = pre + dot(sx_ref[rows, :], w1_ref[width : 2 * width, :])
        live = live_ref[first + rows.start : first + rows.stop, :1]
        forward_rows(pre, live, w2_ref[...], act_ref, slope_ref, normed_ref, inv_ref, msg_ref, rows)
    gathered = sum_ref[...] + dot(hot_ref[:, first : first + total], msg_ref[...])
    gathered = gathered.astype(bf16)
    gathered_ref[...] = gathered

    pre = dot(node_ref[...], n1_ref[:width, :]) + dot(gathered, n1_ref[width:, :])
    squashed = jax.nn.sigmoid(pre)
    act_node = (pre * squashed).astype(bf16)
    act_node_ref[...] = act_node
    normed, inverse = layer_norm(dot(act_node, n2_ref[...]))
    node_new_ref[...] = (node_ref[...].astype(f32) + normed).astype(bf16)
    gon = norm_back(normed, inverse, ncot_ref[...].astype(f32)).astype(bf16)
    gon_ref[...] = gon
    gpn = (dot_rt(gon, n2_ref[...]) * slope_of(pre, squashed)).astype(bf16)
    gpn_ref[...] = gpn
    gg_ref[...] = dot_rt(gpn, n1_ref[width:, :]).astype(bf16)

    for rows in halves:
        whole = slice(first + rows.start, first + rows.stop)
        goe, gpe = backward_rows(
            cot_ref[rows, :],
            dot(pick_ref[whole, :], gg_ref[...]),
            live_ref[whole, :1],
            normed_ref[rows, :],
            inv_ref[rows, :1],
            slope_ref[rows, :],
            w2_ref[...],
        )
        goe_ref[rows, :] = goe
        gpe_ref[rows, :] = gpe
    at = 0
    for out_ref, size in zip(gpe_refs, sizes):
        out_ref[...] = gpe_ref[at : at + size, :]
        at += size


def back_kernel(plan, *refs):
    sets, local_count = plan
    cotan_ref, live_ref, pick_ref, gg_ref, w2_ref = refs[:5]
    groups = (refs[5:8], refs[8:11])
    goe_ref, local_ref = refs[11:13]
    gpe_refs, (cot_ref, gpe_ref) = refs[13:-2], refs[-2:]
    cap = cotan_ref.shape[1]
    for i, k in enumerate(sets):
        cot_ref[i * cap : (i + 1) * cap, :] = cotan_ref[k]
    first = 0
    for slope_ref, normed_ref, inv_ref in groups:
        rows = slice(first, first + slope_ref.shape[0])
        goe, gpe = backward_rows(
            cot_ref[rows, :],
            dot(pick_ref[rows, :], gg_ref[...]),
            live_ref[rows, :1],
            normed_ref[...],
            inv_ref[:, :1],
            slope_ref[...],
            w2_ref[...],
        )
        goe_ref[rows, :] = goe
        gpe_ref[rows, :] = gpe
        first = rows.stop
    local_ref[...] = gpe_ref[: local_count * cap, :]
    for j, out_ref in enumerate(gpe_refs):
        i = local_count + j
        out_ref[...] = gpe_ref[i * cap : (i + 1) * cap, :]


def node_weight_kernel(me_ref, node_ref, gathered_ref, gpn_ref, act_node_ref, gon_ref, keep_ref, sent_ref, block_ref):
    put = functools.partial(put_block, me_ref, block_ref, keep_ref, sent_ref)
    put(0, node_ref[...], gpn_ref[...])
    put(1, gathered_ref[...], gpn_ref[...])
    put(2, act_node_ref[...], gon_ref[...])


def put_block(me_ref, block_ref, keep_ref, sent_ref, index, left_side, right_side):
    core = lax.rem(me_ref[0], 2)
    half = block_ref.shape[0] // 2
    block_ref[...] = dot_lt(left_side, right_side)
    keep_ref[index] = block_ref[pl.ds(pl.multiple_of(core * half, half), half), :]
    other = block_ref[pl.ds(pl.multiple_of((1 - core) * half, half), half), :]
    sent_ref[index] = other.astype(bf16)


def weight_kernel(plan, *refs):
    order, sx_count, gpe_count, act_count, goe_count = plan
    edge_ref, hot_ref, me_ref, node_ref = refs[:4]
    refs = refs[4:]
    sx_refs, refs = refs[:sx_count], refs[sx_count:]
    gpe_refs, refs = refs[:gpe_count], refs[gpe_count:]
    act_refs, refs = refs[:act_count], refs[act_count:]
    goe_refs, refs = refs[:goe_count], refs[goe_count:]
    keep_ref, sent_ref, rsum_ref, x_ref, sx_ref, gpe_ref, act_ref, goe_ref, block_ref = refs
    cap = edge_ref.shape[1]
    for i, k in enumerate(order):
        x_ref[i * cap : (i + 1) * cap, :] = edge_ref[k]
    stack_into(sx_ref, sx_refs)
    stack_into(gpe_ref, gpe_refs)
    stack_into(act_ref, act_refs)
    stack_into(goe_ref, goe_refs)
    recv_sum = dot(hot_ref[...], gpe_ref[...]).astype(bf16)
    rsum_ref[...] = recv_sum
    put = functools.partial(put_block, me_ref, block_ref, keep_ref, sent_ref)
    put(0, x_ref[...], gpe_ref[...])
    put(1, sx_ref[...], gpe_ref[...])
    put(2, node_ref[...], recv_sum)
    put(3, act_ref[...], goe_ref[...])


def base_kernel(ncot_ref, gpn_ref, rsum_ref, w1_ref, n1_ref, base_ref):
    width = w1_ref.shape[1]
    base_ref[...] = (
        ncot_ref[...].astype(f32)
        + dot_rt(gpn_ref[...], n1_ref[:width, :])
        + dot_rt(rsum_ref[...], w1_ref[2 * width :, :])
    )


def edge_kernel(plan, *refs):
    order, normed_count, gpe_count = plan
    edge_ref, cotan_ref, w1_ref, live_ref = refs[:4]
    refs = refs[4:]
    normed_refs, refs = refs[:normed_count], refs[normed_count:]
    gpe_refs, refs = refs[:gpe_count], refs[gpe_count:]
    new_ref, gedge_ref, gpe_ref = refs
    width = w1_ref.shape[1]
    cap = edge_ref.shape[1]
    stack_into(gpe_ref, gpe_refs)
    places = [(ref, at) for ref in normed_refs for at in range(0, ref.shape[0], cap)]
    for i, (k, (normed_ref, at)) in enumerate(zip(order, places)):
        rows = slice(i * cap, (i + 1) * cap)
        grad = cotan_ref[k].astype(f32) + dot_rt(gpe_ref[rows, :], w1_ref[:width, :])
        gedge_ref[k] = grad.astype(bf16)
        message = live_ref[rows, :1] * normed_ref[at : at + cap, :]
        new_ref[k] = (edge_ref[k].astype(f32) + message).astype(bf16)


def final_kernel(plan, *refs):
    local_sets, remote = plan
    me_ref, base_ref, w1_ref, send_ref, id_ref = refs[:5]
    row_refs, (out_ref, hot_ref, rows_ref) = refs[5:-3], refs[-3:]
    nodes, width = base_ref.shape
    cap = send_ref.shape[2]
    ids = [send_ref[k] for k in local_sets]
    ids += [
        asked(me_ref, id_ref, step, i, cap) for step, sets in remote for i in range(len(sets))
    ]
    for i, one in enumerate(ids):
        hot_ref[:, i * cap : (i + 1) * cap] = sum_table(one, nodes)
    stack_into(rows_ref, row_refs)
    send_sum = dot(hot_ref[...], rows_ref[...]).astype(bf16)
    grad = base_ref[...] + dot_rt(send_sum, w1_ref[width : 2 * width, :])
    out_ref[...] = grad.astype(bf16)


def place(me_ref, stride, members):
    return lax.rem(lax.div(me_ref[0], stride), members)


def add_kernel(plan, *refs):
    came, stride, members = plan
    me_ref, keep_ref = refs[:2]
    arr_refs, out_refs = refs[2 : 2 + came], refs[2 + came :]
    size = keep_ref.shape[1] // members
    here = place(me_ref, stride, members)
    for j, out_ref in enumerate(out_refs):
        at = lax.rem(here + j, members) * size
        rows = pl.ds(pl.multiple_of(at, size), size)
        piece = keep_ref[:, rows, :]
        for arr_ref in arr_refs:
            piece += arr_ref[:, rows, :].astype(f32)
        out_ref[...] = piece.astype(out_ref.dtype)


def gather_kernel(plan, *refs):
    stride, members = plan
    me_ref, piece_refs, out_ref = refs[0], refs[1:-1], refs[-1]
    size = piece_refs[0].shape[1]
    here = place(me_ref, stride, members)
    for j, piece_ref in enumerate(piece_refs):
        at = lax.rem(here + members - j, members) * size
        out_ref[:, pl.ds(pl.multiple_of(at, size), size), :] = piece_ref[...]


def join_kernel(plan, *refs):
    members, blocks = plan
    me_ref = refs[0]
    piece_refs, other_refs = refs[1 : 1 + members], refs[1 + members : 1 + 2 * members]
    out_refs = refs[1 + 2 * members :]
    size = piece_refs[0].shape[1]
    core = lax.rem(me_ref[0], 2)
    here = place(me_ref, 2, members)
    for index, (which, block) in enumerate(blocks):
        first = 2 * block * members * size
        for side, side_refs in ((core, piece_refs), (1 - core, other_refs)):
            for j, piece_ref in enumerate(side_refs):
                at = first + (side * members + lax.rem(here + members - j, members)) * size
                rows = pl.ds(pl.multiple_of(at, size), size)
                out_refs[which][rows, :] = piece_ref[index]


def in_group(block, axis, stride, members, step):
    route = []
    for i in range(lax.axis_size(axis)):
        at = (i // stride) % members
        route.append((i, i + ((at + step) % members - at) * stride))
    return lax.ppermute(block, axis, route)


def split_of(bands):
    chips = bands // 2
    first = 1
    while first * first * 4 <= chips:
        first *= 2
    return first, chips // first


def add_stage(me, keep, arrived, stride, members, kind, after):
    count, rows, width = keep.shape
    shape = (count, rows // members, width)
    outs = call(
        functools.partial(add_kernel, (len(arrived), stride, members)),
        [(shape, kind)] + [(shape, bf16)] * (members - 1),
        [],
        me,
        keep,
        *arrived,
        smem=(0,),
        after=after,
    )
    return outs[0], [in_group(out, "band", stride, members, j + 1) for j, out in enumerate(outs[1:])]


def held_until(array, after):
    return pl.pallas_call(
        lambda *refs: None,
        out_shape=pltpu.VMEM(array.shape, array.dtype),
        in_specs=[pl.BlockSpec(memory_space=pltpu.VMEM)]
        + [pl.BlockSpec(memory_space=pl.ANY)] * len(after),
        out_specs=pl.BlockSpec(memory_space=pltpu.VMEM),
        input_output_aliases={0: 0},
        compiler_params=pltpu.CompilerParams(vmem_limit_bytes=1024 * 1024),
        cost_estimate=pl.CostEstimate(flops=1, bytes_accessed=1, transcendentals=0),
    )(pltpu.with_memory_space_constraint(array, pltpu.VMEM), *after)


def gather_stage(me, piece, stride, members, after):
    count, rows, width = piece.shape
    pieces = [piece] + [in_group(piece, "band", stride, members, j) for j in range(1, members)]
    (mine,) = call(
        functools.partial(gather_kernel, (stride, members)),
        [((count, rows * members, width), bf16)],
        [],
        me,
        *pieces,
        smem=(0,),
        after=after,
    )
    return mine


def join_stage(me, mine, members, blocks, shapes, swap_after, after):
    pieces = [in_group(mine, "band", 2, members, j) for j in range(1, members)]
    pieces = [mine] + [held_until(piece, swap_after) if swap_after else piece for piece in pieces]
    others = [in_group(one, "band", 1, 2, 1) for one in pieces]
    return call(
        functools.partial(join_kernel, (members, blocks)),
        [(shape, bf16) for shape in shapes],
        [],
        me,
        *pieces,
        *others,
        smem=(0,),
        after=after,
        last=range(len(shapes)),
    )


def reduce_whole(keep, sent):
    bands = lax.axis_size("band")
    chips = [[i for i in range(bands) if i % 2 == c] for c in range(2)]
    total = keep + in_group(sent, "band", 1, 2, 1).astype(f32)
    total = lax.psum(total.astype(bf16), "band", axis_index_groups=chips)
    other = in_group(total, "band", 1, 2, 1)
    core = lax.axis_index("band") % 2
    low, high = jnp.where(core == 0, total, other), jnp.where(core == 0, other, total)
    return jnp.concatenate([low, high], axis=1)


def local(
    node_latent,
    edge_latent,
    recv_slot,
    send_slot,
    edge_count,
    edge_first,
    edge_second,
    node_first,
    node_second,
    node_cotan,
    edge_cotan,
):
    bands = lax.axis_size("band")
    nodes, width = node_latent.shape
    sets, cap = edge_latent.shape[1:3]
    send_ids = send_slot.reshape(sets, 1, cap)
    me = lax.axis_index("band").astype(jnp.int32).reshape(1)

    def step_of(k):
        return band_offsets[k] % bands

    def reach(k):
        return min(step_of(k), bands - step_of(k))

    ordered = sorted(range(sets), key=lambda k: (reach(k), step_of(k)))
    near, far = tuple(ordered[:near_sets]), tuple(ordered[near_sets:])
    local_count = sum(step_of(k) == 0 for k in near)
    near_steps = [step_of(k) for k in near[local_count:]]
    far_steps = list(dict.fromkeys(step_of(k) for k in far))
    steps = near_steps + far_steps
    near_plan = tuple((k,) for k in near[local_count:])
    far_plan = tuple(tuple(k for k in far if step_of(k) == d) for d in far_steps)
    far = sum(far_plan, ())

    order = near + far

    (
        node_latent,
        send_ids,
        recv_ids,
        edges,
        edge_first,
        edge_second,
        node_first,
        node_second,
        node_cotan,
        cotan,
    ) = loaded(
        me,
        node_latent,
        send_ids,
        recv_slot.reshape(sets, 1, cap),
        edge_latent[0],
        edge_first,
        edge_second,
        node_first,
        node_second,
        node_cotan,
        edge_cotan[0],
    )
    remote_plan = tuple(zip(steps, near_plan + far_plan))
    widest = max(len(piece) for piece in near_plan + far_plan)
    (ids,) = call(
        functools.partial(ask_kernel, remote_plan),
        [((bands, 1, widest * cap), jnp.int32)],
        [],
        me,
        send_ids,
        smem=(0,),
    )
    ids = lax.all_to_all(ids, "band", 0, 0, tiled=True)
    picked = call(
        functools.partial(pick_kernel, remote_plan),
        [((len(piece) * cap, width), bf16) for piece in near_plan + far_plan],
        [],
        me,
        node_latent,
        ids,
        smem=(0,),
    )
    sx = [passed_along(block, "band", d) for block, d in zip(picked, steps)]
    sx_near, sx_far = sx[: len(near_plan)], sx[len(near_plan) :]

    local_rows, near_rows, far_rows = local_count * cap, len(near_plan) * cap, len(far) * cap
    total = sets * cap

    def forward_outs(rows):
        return [
            ((rows, width), bf16),
            ((rows, width), f32),
            ((rows, width), f32),
            ((rows, 128), f32),
            ((nodes, width), f32),
        ]

    pick, hot, live, part, sx_local, act_local, slope_local, normed_local, inv_local, node_sum = call(
        functools.partial(start_kernel, (order, local_count)),
        [
            ((total, nodes), bf16),
            ((nodes, total), bf16),
            ((total, 128), f32),
            ((near_rows + far_rows, width), f32),
            ((local_rows, width), bf16),
        ]
        + forward_outs(local_rows),
        [((total, 2 * width), bf16), ((local_rows, width), bf16)],
        edges,
        recv_ids,
        send_ids,
        in_hbm(edge_count),
        edge_first,
        edge_second,
        node_latent,
        smem=(3,),
        after=[picked[0]],
    )
    act_near, slope_near, normed_near, inv_near, node_sum = call(
        functools.partial(near_kernel, (local_rows, len(near_plan))),
        forward_outs(near_rows),
        [((near_rows, width), bf16), ((near_rows, width), bf16)],
        part,
        live,
        hot,
        node_sum,
        edge_first,
        edge_second,
        *sx_near,
    )
    sizes = [len(piece) * cap for piece in far_plan]
    outs = call(
        functools.partial(far_kernel, (far, sizes, local_rows + near_rows, near_rows)),
        [((size, width), bf16) for size in sizes]
        + [((far_rows, width), bf16), ((far_rows, width), bf16), ((far_rows, width), f32)]
        + [((nodes, width), bf16)] * 6,
        [
            ((far_rows, width), bf16),
            ((far_rows, width), f32),
            ((far_rows, 128), f32),
            ((far_rows, width), bf16),
            ((far_rows, width), bf16),
            ((far_rows, width), bf16),
        ],
        cotan,
        part,
        live,
        pick,
        hot,
        node_sum,
        edge_first,
        edge_second,
        node_latent,
        node_cotan,
        node_first,
        node_second,
        *sx_far,
        last=(len(sizes) + 8,),
    )
    gpe_far, outs = list(outs[: len(far_plan)]), outs[len(far_plan) :]
    act_far, goe_far, normed_far, gathered, gpn, act_node, gon, gg, node_new = outs
    back_far = [passed_along(block, "band", -d) for block, d in zip(gpe_far, far_steps)]

    half = (width // 2, width)
    outs = call(
        functools.partial(back_kernel, (near, local_count)),
        [((local_rows + near_rows, width), bf16), ((local_rows, width), bf16)]
        + [((cap, width), bf16)] * len(near_steps),
        [((local_rows + near_rows, width), bf16)] * 2,
        cotan,
        live,
        pick,
        gg,
        edge_second,
        slope_local,
        normed_local,
        inv_local,
        slope_near,
        normed_near,
        inv_near,
    )
    goe_near, gpe_local = outs[:2]
    gpe_near = list(outs[2:])
    back_near = [passed_along(block, "band", -d) for block, d in zip(gpe_near, near_steps)]

    gpe = [gpe_local] + gpe_near + gpe_far
    sx_all = [sx_local] + sx_near + sx_far
    keep_edge, sent_edge, recv_sum = call(
        functools.partial(weight_kernel, (order, len(sx_all), len(gpe), 3, 2)),
        [((4, *half), f32), ((4, *half), bf16), ((nodes, width), bf16)],
        [((total, width), bf16)] * 5 + [((width, width), f32)],
        edges,
        hot,
        me,
        node_latent,
        *sx_all,
        *gpe,
        act_local,
        act_near,
        act_far,
        goe_near,
        goe_far,
        smem=(2,),
    )

    def edge_outputs(after):
        return call(
            functools.partial(edge_kernel, (order, 3, len(gpe))),
            [((sets, cap, width), bf16), ((sets, cap, width), bf16)],
            [((total, width), bf16)],
            edges,
            cotan,
            edge_first,
            live,
            normed_local,
            normed_near,
            normed_far,
            *gpe,
            after=after,
            last=(0, 1),
        )

    def node_output(after):
        (base,) = call(
            base_kernel,
            [((nodes, width), f32)],
            [],
            node_cotan,
            gpn,
            recv_sum,
            edge_first,
            node_first,
            after=after,
        )
        (grad_nodes,) = call(
            functools.partial(final_kernel, (near[:local_count], remote_plan)),
            [((nodes, width), bf16)],
            [((nodes, total), bf16), ((total, width), bf16)],
            me,
            base,
            edge_first,
            send_ids,
            ids,
            gpe_local,
            *back_near,
            *back_far,
            smem=(0,),
            last=(0,),
        )
        return grad_nodes

    def node_weights(after):
        return call(
            node_weight_kernel,
            [((3, *half), f32), ((3, *half), bf16)],
            [((width, width), f32)],
            me,
            node_latent,
            gathered,
            gpn,
            act_node,
            gon,
            smem=(0,),
            after=after,
        )

    first, second = split_of(bands)
    node_blocks, node_shapes = ((0, 0), (0, 1), (1, 0)), [(2 * width, width), (width, width)]
    edge_blocks = ((0, 0), (0, 1), (0, 2), (1, 0))
    edge_shapes = [(3 * width, width), (width, width)]
    if width // 2 % (16 * first * second) == 0:
        along_y, along_z = (2, first), (2 * first, second)
        keep_node, sent_node = node_weights([])
        came_node = [in_group(sent_node, "band", 1, 2, 1)]
        keep_node, came_node = add_stage(me, keep_node, came_node, *along_y, f32, [])
        sent_edge = held_until(sent_edge, back_far + came_node)
        came_edge = [in_group(sent_edge, "band", 1, 2, 1)]
        keep_node, came_node = add_stage(me, keep_node, came_node, *along_z, f32, [sent_edge])
        keep_edge, came_edge = add_stage(me, keep_edge, came_edge, *along_y, f32, [keep_node])
        edge_new, grad_edges = edge_outputs([keep_edge])
        piece_node, _ = add_stage(me, keep_node, came_node, 1, 1, bf16, [in_hbm(edge_new)])
        keep_edge, came_edge = add_stage(me, keep_edge, came_edge, *along_z, f32, [piece_node])
        mine_node = gather_stage(me, piece_node, *along_z, [keep_edge])
        piece_edge, _ = add_stage(me, keep_edge, came_edge, 1, 1, bf16, [mine_node])
        grad_n1, grad_n2 = join_stage(
            me, mine_node, first, node_blocks, node_shapes, [piece_edge], []
        )
        mine_edge = gather_stage(me, piece_edge, *along_z, [in_hbm(grad_n2)])
        grad_nodes = node_output([mine_edge])
        grad_e1, grad_e2 = join_stage(
            me, mine_edge, first, edge_blocks, edge_shapes, [in_hbm(grad_nodes)], []
        )
    else:
        whole = reduce_whole(*node_weights([]))
        grad_n1, grad_n2 = whole[:2].reshape(2 * width, width), whole[2]
        whole = reduce_whole(keep_edge, sent_edge)
        grad_e1, grad_e2 = whole[:3].reshape(3 * width, width), whole[3]
        edge_new, grad_edges = edge_outputs([])
        grad_nodes = node_output([])
    return (
        node_new,
        edge_new[None],
        grad_nodes,
        grad_edges[None],
        grad_e1,
        grad_e2,
        grad_n1,
        grad_n2,
    )


def solution(mesh):
    return jax.shard_map(
        local,
        mesh=mesh,
        in_specs=(
            P(("groups", "band"), None),
            P(("groups", "band"), None, None, None),
            P(("groups", "band"), None, None),
            P(("groups", "band"), None, None),
            P(("groups", "band"), None),
            P(),
            P(),
            P(),
            P(),
            P(("groups", "band"), None),
            P(("groups", "band"), None, None, None),
        ),
        out_specs=(
            P(("groups", "band"), None),
            P(("groups", "band"), None, None, None),
            P(("groups", "band"), None),
            P(("groups", "band"), None, None, None),
            P("groups", None),
            P("groups", None),
            P("groups", None),
            P("groups", None),
        ),
        check_vma=False,
    )
```

```python
import functools

import jax
import jax.numpy as jnp
from jax import lax
from jax.experimental import pallas as pl
from jax.experimental.pallas import tpu as pltpu
from jax.sharding import PartitionSpec as P

band_offsets = (0, 1, -1, 2, -2, 4, -4, 8, -8, 16, -16)
norm_eps = 1e-05
near_sets = 7
bf16 = jnp.bfloat16
f32 = jnp.float32
vmem_limit = 20 * 1024 * 1024


def passed_along(block, axis, distance):
    devices = range(lax.axis_size(axis))
    route = [((i - distance) % len(devices), i) for i in devices]
    return lax.ppermute(block, axis, route)


def layer_norm(inputs):
    average = jnp.mean(inputs, axis=-1, keepdims=True)
    centred = inputs - average
    inverse = lax.rsqrt(jnp.mean(centred * centred, axis=-1, keepdims=True) + norm_eps)
    return (centred * inverse, inverse)


def norm_back(normed, inverse, upstream):
    return inverse * (
        upstream
        - jnp.mean(upstream, axis=-1, keepdims=True)
        - normed * jnp.mean(upstream * normed, axis=-1, keepdims=True)
    )


def slope_of(inputs, squashed):
    return squashed * (1.0 + inputs * (1.0 - squashed))


def dot(left_side, right_side):
    return jnp.dot(left_side, right_side, preferred_element_type=f32)


def dot_rt(left_side, right_side):
    return lax.dot_general(
        left_side, right_side, (((1,), (1,)), ((), ())), preferred_element_type=f32
    )


def dot_lt(left_side, right_side):
    return lax.dot_general(
        left_side, right_side, (((0,), (0,)), ((), ())), preferred_element_type=f32
    )


def pick_table(ids, nodes):
    cap = ids.shape[1]
    down = jnp.transpose(jnp.broadcast_to(ids, (cap, cap)))
    parts = []
    for first in range(0, nodes, cap):
        wide = min(cap, nodes - first)
        lanes = lax.broadcasted_iota(jnp.int32, (cap, wide), 1) + first
        parts.append(jnp.where(down[:, :wide] == lanes, 1.0, 0.0).astype(bf16))
    return jnp.concatenate(parts, axis=1)


def sum_table(ids, nodes):
    down = lax.broadcasted_iota(jnp.int32, (nodes, ids.shape[1]), 0)
    return jnp.where(down == ids, 1.0, 0.0).astype(bf16)


def live_rows(count, cap):
    return (lax.broadcasted_iota(jnp.int32, (cap, 128), 0) < count).astype(f32)


def call(body, outs, scratch, *args, smem=(), after=(), last=()):
    spaces, given = [], []
    for i, arg in enumerate(args):
        spaces.append(pl.BlockSpec(memory_space=pltpu.SMEM if i in smem else pltpu.VMEM))
        given.append(arg if i in smem else pltpu.with_memory_space_constraint(arg, pltpu.VMEM))
    spaces += [pl.BlockSpec(memory_space=pl.ANY)] * len(after)

    def kernel(*refs):
        body(*refs[: len(args)], *refs[len(args) + len(after) :])

    return pl.pallas_call(
        kernel,
        out_shape=[
            (pltpu.HBM if i in last else pltpu.VMEM)(shape, kind)
            for i, (shape, kind) in enumerate(outs)
        ],
        in_specs=spaces,
        out_specs=[pl.BlockSpec(memory_space=pltpu.VMEM)] * len(outs),
        scratch_shapes=[pltpu.VMEM(shape, kind) for shape, kind in scratch],
        compiler_params=pltpu.CompilerParams(vmem_limit_bytes=vmem_limit),
        cost_estimate=pl.CostEstimate(flops=1, bytes_accessed=1, transcendentals=0),
    )(*given, *after)


def in_hbm(array):
    return pltpu.with_memory_space_constraint(array, pltpu.HBM)


def load_kernel(count, *refs):
    sems, refs = refs[-1], refs[1:]
    copies = [
        pltpu.make_async_copy(refs[i], refs[count + i], sems.at[i]) for i in range(count)
    ]
    for copy in copies:
        copy.start()
    for copy in copies:
        copy.wait()


def loaded(me, *args):
    count = len(args)
    return pl.pallas_call(
        functools.partial(load_kernel, count),
        out_shape=[pltpu.VMEM(arg.shape, arg.dtype) for arg in args],
        in_specs=[pl.BlockSpec(memory_space=pltpu.SMEM)]
        + [pl.BlockSpec(memory_space=pltpu.HBM)] * count,
        out_specs=[pl.BlockSpec(memory_space=pltpu.VMEM)] * count,
        scratch_shapes=[pltpu.SemaphoreType.DMA((count,))],
        compiler_params=pltpu.CompilerParams(vmem_limit_bytes=1024 * 1024),
        cost_estimate=pl.CostEstimate(flops=1, bytes_accessed=1, transcendentals=0),
    )(me, *[in_hbm(arg) for arg in args])


def ask_kernel(plan, me_ref, send_ref, out_ref):
    bands = out_ref.shape[0]
    out_ref[...] = jnp.zeros_like(out_ref)
    for step, sets in plan:
        ids = [send_ref[k] for k in sets]
        blank = out_ref.shape[2] - len(sets) * send_ref.shape[2]
        if blank:
            ids.append(jnp.zeros((1, blank), jnp.int32))
        out_ref[lax.rem(me_ref[0] + bands - step, bands)] = jnp.concatenate(ids, axis=1)


def asked(me_ref, id_ref, step, index, cap):
    row = lax.rem(me_ref[0] + step, id_ref.shape[0])
    return id_ref[row][:, index * cap : (index + 1) * cap]


def pick_kernel(plan, me_ref, node_ref, id_ref, *out_refs):
    nodes = node_ref.shape[0]
    for out_ref, (step, sets) in zip(out_refs, plan):
        cap = out_ref.shape[0] // len(sets)
        for i in range(len(sets)):
            hot = pick_table(asked(me_ref, id_ref, step, i, cap), nodes)
            out_ref[i * cap : (i + 1) * cap, :] = dot(hot, node_ref[...]).astype(bf16)


def forward_rows(pre, live, w2, act_ref, slope_ref, normed_ref, inv_ref, msg_ref, rows):
    squashed = jax.nn.sigmoid(pre)
    slope_ref[rows, :] = slope_of(pre, squashed)
    act = (pre * squashed).astype(bf16)
    act_ref[rows, :] = act
    normed, inverse = layer_norm(dot(act, w2))
    normed_ref[rows, :] = normed
    inv_ref[rows, :] = jnp.broadcast_to(inverse, (inverse.shape[0], 128))
    msg_ref[rows, :] = (live * normed).astype(bf16)


def backward_rows(cotan, picked, live, normed, inverse, slope, w2):
    upstream = live * (cotan.astype(f32) + picked)
    goe = norm_back(normed, inverse, upstream).astype(bf16)
    return goe, (dot_rt(goe, w2) * slope).astype(bf16)


def stack_into(out_ref, refs):
    first = 0
    for ref in refs:
        out_ref[first : first + ref.shape[0], :] = ref[...]
        first += ref.shape[0]


def start_kernel(plan, *refs):
    order, local_count = plan
    (
        edge_ref,
        recv_ref,
        send_ref,
        count_ref,
        w1_ref,
        w2_ref,
        node_ref,
        pick_ref,
        hot_ref,
        live_ref,
        part_ref,
        sx_ref,
        act_ref,
        slope_ref,
        normed_ref,
        inv_ref,
        sum_ref,
        x_ref,
        msg_ref,
    ) = refs
    nodes, width = node_ref.shape
    cap = recv_ref.shape[2]
    split = local_count * cap
    for i, k in enumerate(order):
        rows = slice(i * cap, (i + 1) * cap)
        x_ref[rows, :width] = edge_ref[k]
        pick_ref[rows, :] = pick_table(recv_ref[k], nodes)
        hot_ref[:, rows] = sum_table(recv_ref[k], nodes)
        live_ref[rows, :] = live_rows(count_ref[0, k], cap)
        if i < local_count:
            sx_ref[rows, :] = dot(pick_table(send_ref[k], nodes), node_ref[...]).astype(bf16)
    x_ref[:, width:] = dot(pick_ref[...], node_ref[...]).astype(bf16)
    part = dot(x_ref[:split, :width], w1_ref[:width, :])
    part += dot(x_ref[:split, width:], w1_ref[2 * width :, :])
    pre = part + dot(sx_ref[...], w1_ref[width : 2 * width, :])
    rows = slice(0, split)
    live = live_ref[rows, :1]
    forward_rows(pre, live, w2_ref[...], act_ref, slope_ref, normed_ref, inv_ref, msg_ref, rows)
    sum_ref[...] = dot(hot_ref[:, :split], msg_ref[...])
    part = dot(x_ref[split:, :width], w1_ref[:width, :])
    part_ref[...] = part + dot(x_ref[split:, width:], w1_ref[2 * width :, :])


def near_kernel(plan, *refs):
    first, count = plan
    part_ref, live_ref, hot_ref, sum_in_ref, w1_ref, w2_ref = refs[:6]
    sx_refs = refs[6 : 6 + count]
    act_ref, slope_ref, normed_ref, inv_ref, sum_ref, sx_ref, msg_ref = refs[6 + count :]
    total, width = sx_ref.shape
    stack_into(sx_ref, sx_refs)
    for j in range(2):
        rows = slice(j * total // 2, (j + 1) * total // 2)
        pre = part_ref[rows, :] + dot(sx_ref[rows, :], w1_ref[width : 2 * width, :])
        live = live_ref[first + rows.start : first + rows.stop, :1]
        forward_rows(pre, live, w2_ref[...], act_ref, slope_ref, normed_ref, inv_ref, msg_ref, rows)
    sum_ref[...] = sum_in_ref[...] + dot(hot_ref[:, first : first + total], msg_ref[...])


def far_kernel(plan, *refs):
    sets, sizes, first, part_first = plan
    count = len(sizes)
    (
        cotan_ref,
        part_ref,
        live_ref,
        pick_ref,
        hot_ref,
        sum_ref,
        w1_ref,
        w2_ref,
        node_ref,
        ncot_ref,
        n1_ref,
        n2_ref,
    ) = refs[:12]
    sx_refs, refs = refs[12 : 12 + count], refs[12 + count :]
    gpe_refs, refs = refs[:count], refs[count:]
    (
        act_ref,
        goe_ref,
        normed_ref,
        gathered_ref,
        gpn_ref,
        act_node_ref,
        gon_ref,
        gg_ref,
        node_new_ref,
        sx_ref,
        slope_ref,
        inv_ref,
        msg_ref,
        cot_ref,
        gpe_ref,
    ) = refs
    total, width = sx_ref.shape
    cap = cotan_ref.shape[1]
    stack_into(sx_ref, sx_refs)
    for i, k in enumerate(sets):
        cot_ref[i * cap : (i + 1) * cap, :] = cotan_ref[k]
    halves = [slice(j * total // 2, (j + 1) * total // 2) for j in range(2)]
    for rows in halves:
        pre = part_ref[part_first + rows.start : part_first + rows.stop, :]
        pre = pre + dot(sx_ref[rows, :], w1_ref[width : 2 * width, :])
        live = live_ref[first + rows.start : first + rows.stop, :1]
        forward_rows(pre, live, w2_ref[...], act_ref, slope_ref, normed_ref, inv_ref, msg_ref, rows)
    gathered = sum_ref[...] + dot(hot_ref[:, first : first + total], msg_ref[...])
    gathered = gathered.astype(bf16)
    gathered_ref[...] = gathered

    pre = dot(node_ref[...], n1_ref[:width, :]) + dot(gathered, n1_ref[width:, :])
    squashed = jax.nn.sigmoid(pre)
    act_node = (pre * squashed).astype(bf16)
    act_node_ref[...] = act_node
    normed, inverse = layer_norm(dot(act_node, n2_ref[...]))
    node_new_ref[...] = (node_ref[...].astype(f32) + normed).astype(bf16)
    gon = norm_back(normed, inverse, ncot_ref[...].astype(f32)).astype(bf16)
    gon_ref[...] = gon
    gpn = (dot_rt(gon, n2_ref[...]) * slope_of(pre, squashed)).astype(bf16)
    gpn_ref[...] = gpn
    gg_ref[...] = dot_rt(gpn, n1_ref[width:, :]).astype(bf16)

    for rows in halves:
        whole = slice(first + rows.start, first + rows.stop)
        goe, gpe = backward_rows(
            cot_ref[rows, :],
            dot(pick_ref[whole, :], gg_ref[...]),
            live_ref[whole, :1],
            normed_ref[rows, :],
            inv_ref[rows, :1],
            slope_ref[rows, :],
            w2_ref[...],
        )
        goe_ref[rows, :] = goe
        gpe_ref[rows, :] = gpe
    at = 0
    for out_ref, size in zip(gpe_refs, sizes):
        out_ref[...] = gpe_ref[at : at + size, :]
        at += size


def back_kernel(plan, *refs):
    sets, local_count = plan
    cotan_ref, live_ref, pick_ref, gg_ref, w2_ref = refs[:5]
    groups = (refs[5:8], refs[8:11])
    goe_ref, local_ref = refs[11:13]
    gpe_refs, (cot_ref, gpe_ref) = refs[13:-2], refs[-2:]
    cap = cotan_ref.shape[1]
    for i, k in enumerate(sets):
        cot_ref[i * cap : (i + 1) * cap, :] = cotan_ref[k]
    first = 0
    for slope_ref, normed_ref, inv_ref in groups:
        rows = slice(first, first + slope_ref.shape[0])
        goe, gpe = backward_rows(
            cot_ref[rows, :],
            dot(pick_ref[rows, :], gg_ref[...]),
            live_ref[rows, :1],
            normed_ref[...],
            inv_ref[:, :1],
            slope_ref[...],
            w2_ref[...],
        )
        goe_ref[rows, :] = goe
        gpe_ref[rows, :] = gpe
        first = rows.stop
    local_ref[...] = gpe_ref[: local_count * cap, :]
    for j, out_ref in enumerate(gpe_refs):
        i = local_count + j
        out_ref[...] = gpe_ref[i * cap : (i + 1) * cap, :]


def deal_out(plan, me_ref, grad_ref, keep_ref, sent_ref):
    core = lax.rem(me_ref[0], 2)
    outer, inner = keep_ref.shape[:2]
    for i in range(outer):
        for j in range(inner):
            pair = (i * inner + j) * 2
            at = 0
            for first, rows in plan:
                for side, out_ref in ((core, keep_ref), (1 - core, sent_ref)):
                    start = pl.multiple_of(first + (pair + side) * rows, rows)
                    piece = grad_ref[pl.ds(start, rows), :]
                    out_ref[i, j, at : at + rows, :] = piece.astype(out_ref.dtype)
                at += rows


def node_weight_kernel(plan, *refs):
    me_ref, node_ref, gathered_ref, gpn_ref, act_node_ref, gon_ref = refs[:6]
    *deal_refs, grad_ref = refs[6:] if plan else (refs[6],)
    width = node_ref.shape[1]
    grad_ref[:width, :] = dot_lt(node_ref[...], gpn_ref[...])
    grad_ref[width : 2 * width, :] = dot_lt(gathered_ref[...], gpn_ref[...])
    grad_ref[2 * width :, :] = dot_lt(act_node_ref[...], gon_ref[...])
    if plan:
        deal_out(plan, me_ref, grad_ref, *deal_refs)


def weight_kernel(plan, *refs):
    order, counts, cuts = plan
    edge_ref, hot_ref, me_ref, node_ref = refs[:4]
    refs = refs[4:]
    groups = []
    for count in counts:
        groups.append(refs[:count])
        refs = refs[count:]
    sx_refs, gpe_refs, act_refs, goe_refs = groups
    rsum_ref, refs = refs[0], refs[1:]
    if cuts:
        deal_refs, refs = refs[:2], refs[2:]
        x_ref, sx_ref, gpe_ref, act_ref, goe_ref, grad_ref = refs
    else:
        grad_ref, x_ref, sx_ref, gpe_ref, act_ref, goe_ref = refs
    width = node_ref.shape[1]
    cap = edge_ref.shape[1]
    for i, k in enumerate(order):
        x_ref[i * cap : (i + 1) * cap, :] = edge_ref[k]
    stack_into(sx_ref, sx_refs)
    stack_into(gpe_ref, gpe_refs)
    stack_into(act_ref, act_refs)
    stack_into(goe_ref, goe_refs)
    recv_sum = dot(hot_ref[...], gpe_ref[...]).astype(bf16)
    rsum_ref[...] = recv_sum
    grad_ref[:width, :] = dot_lt(x_ref[...], gpe_ref[...])
    grad_ref[width : 2 * width, :] = dot_lt(sx_ref[...], gpe_ref[...])
    grad_ref[2 * width : 3 * width, :] = dot_lt(node_ref[...], recv_sum)
    grad_ref[3 * width :, :] = dot_lt(act_ref[...], goe_ref[...])
    if cuts:
        deal_out(cuts, me_ref, grad_ref, *deal_refs)


def base_kernel(ncot_ref, gpn_ref, rsum_ref, w1_ref, n1_ref, base_ref):
    width = w1_ref.shape[1]
    base_ref[...] = (
        ncot_ref[...].astype(f32)
        + dot_rt(gpn_ref[...], n1_ref[:width, :])
        + dot_rt(rsum_ref[...], w1_ref[2 * width :, :])
    )


def edge_kernel(plan, *refs):
    order, normed_count, gpe_count = plan
    edge_ref, cotan_ref, w1_ref, live_ref = refs[:4]
    refs = refs[4:]
    normed_refs, refs = refs[:normed_count], refs[normed_count:]
    gpe_refs, refs = refs[:gpe_count], refs[gpe_count:]
    new_ref, gedge_ref, gpe_ref = refs
    width = w1_ref.shape[1]
    cap = edge_ref.shape[1]
    stack_into(gpe_ref, gpe_refs)
    places = [(ref, at) for ref in normed_refs for at in range(0, ref.shape[0], cap)]
    for i, (k, (normed_ref, at)) in enumerate(zip(order, places)):
        rows = slice(i * cap, (i + 1) * cap)
        grad = cotan_ref[k].astype(f32) + dot_rt(gpe_ref[rows, :], w1_ref[:width, :])
        gedge_ref[k] = grad.astype(bf16)
        message = live_ref[rows, :1] * normed_ref[at : at + cap, :]
        new_ref[k] = (edge_ref[k].astype(f32) + message).astype(bf16)


def final_kernel(plan, *refs):
    local_sets, remote = plan
    me_ref, base_ref, w1_ref, send_ref, id_ref = refs[:5]
    row_refs, (out_ref, hot_ref, rows_ref) = refs[5:-3], refs[-3:]
    nodes, width = base_ref.shape
    cap = send_ref.shape[2]
    ids = [send_ref[k] for k in local_sets]
    ids += [
        asked(me_ref, id_ref, step, i, cap) for step, sets in remote for i in range(len(sets))
    ]
    for i, one in enumerate(ids):
        hot_ref[:, i * cap : (i + 1) * cap] = sum_table(one, nodes)
    stack_into(rows_ref, row_refs)
    send_sum = dot(hot_ref[...], rows_ref[...]).astype(bf16)
    grad = base_ref[...] + dot_rt(send_sum, w1_ref[width : 2 * width, :])
    out_ref[...] = grad.astype(bf16)


def place(me_ref, stride, members):
    return lax.rem(lax.div(me_ref[0], stride), members)


def add_kernel(plan, *refs):
    came, stride, members, axis = plan
    me_ref, keep_ref = refs[:2]
    arr_refs, out_refs = refs[2 : 2 + came], refs[2 + came :]
    here = place(me_ref, stride, members)
    for j, out_ref in enumerate(out_refs):
        at = lax.rem(here + j, members)
        index = (slice(None), at) if axis else (at,)
        piece = keep_ref[index]
        for arr_ref in arr_refs:
            piece += arr_ref[index].astype(f32)
        out_ref[...] = piece.astype(out_ref.dtype)


def last_kernel(counts, *refs):
    refs, out_ref = refs[:-1], refs[-1]
    at = 0
    for count in counts:
        keep_ref, arr_refs, refs = refs[0], refs[1:count], refs[count:]
        piece = keep_ref[...]
        for arr_ref in arr_refs:
            piece += arr_ref[...].astype(f32)
        out_ref[at : at + keep_ref.shape[0], :] = piece.astype(bf16)
        at += keep_ref.shape[0]


def sort_kernel(plan, in_ref, *refs):
    bands, sizes = plan
    out_refs, sems = refs[:-1], refs[-1]
    copies = []
    for band in range(bands):
        at = band * sum(sizes)
        for size, out_ref in zip(sizes, out_refs):
            source, target = in_ref.at[pl.ds(at, size)], out_ref.at[pl.ds(band * size, size)]
            copies.append(pltpu.make_async_copy(source, target, sems.at[len(copies)]))
            at += size
    for copy in copies:
        copy.start()
    for copy in copies:
        copy.wait()


def in_group(block, axis, stride, members, step):
    route = []
    for i in range(lax.axis_size(axis)):
        at = (i // stride) % members
        route.append((i, i + ((at + step) % members - at) * stride))
    return lax.ppermute(block, axis, route)


def split_of(bands):
    chips = bands // 2
    first = 1
    while first * first * 4 <= chips:
        first *= 2
    return first, chips // first


def add_stage(me, keep, arrived, stride, members, axis, after):
    shape = keep.shape[:axis] + keep.shape[axis + 1 :]
    outs = call(
        functools.partial(add_kernel, (len(arrived), stride, members, axis)),
        [(shape, f32)] + [(shape, bf16)] * (members - 1),
        [],
        me,
        keep,
        *arrived,
        smem=(0,),
        after=after,
    )
    return outs[0], [in_group(out, "band", stride, members, j + 1) for j, out in enumerate(outs[1:])]


def last_sum(*chunks):
    rows, width = sum(keep.shape[0] for keep, _ in chunks), chunks[0][0].shape[1]
    (piece,) = call(
        functools.partial(last_kernel, [1 + len(arrived) for _, arrived in chunks]),
        [((rows, width), bf16)],
        [],
        *[array for keep, arrived in chunks for array in [keep, *arrived]],
    )
    return piece


def gathered_from_all(piece, sizes, after):
    width = piece.shape[1]
    bands = lax.axis_size("band")
    whole = lax.all_gather(piece, "band", axis=0, tiled=True)
    count = bands * len(sizes)

    def kernel(in_ref, *refs):
        sort_kernel((bands, sizes), in_ref, *refs[len(after) :])

    return pl.pallas_call(
        kernel,
        out_shape=[pltpu.HBM((bands * size, width), bf16) for size in sizes],
        in_specs=[pl.BlockSpec(memory_space=pltpu.HBM)]
        + [pl.BlockSpec(memory_space=pl.ANY)] * len(after),
        out_specs=[pl.BlockSpec(memory_space=pltpu.HBM)] * len(sizes),
        scratch_shapes=[pltpu.SemaphoreType.DMA((count,))],
        compiler_params=pltpu.CompilerParams(vmem_limit_bytes=1024 * 1024),
        cost_estimate=pl.CostEstimate(flops=1, bytes_accessed=1, transcendentals=0),
    )(in_hbm(whole), *after)


def held_until(array, after):
    return pl.pallas_call(
        lambda *refs: None,
        out_shape=pltpu.VMEM(array.shape, array.dtype),
        in_specs=[pl.BlockSpec(memory_space=pltpu.VMEM)]
        + [pl.BlockSpec(memory_space=pl.ANY)] * len(after),
        out_specs=pl.BlockSpec(memory_space=pltpu.VMEM),
        input_output_aliases={0: 0},
        compiler_params=pltpu.CompilerParams(vmem_limit_bytes=1024 * 1024),
        cost_estimate=pl.CostEstimate(flops=1, bytes_accessed=1, transcendentals=0),
    )(pltpu.with_memory_space_constraint(array, pltpu.VMEM), *after)


def local(
    node_latent,
    edge_latent,
    recv_slot,
    send_slot,
    edge_count,
    edge_first,
    edge_second,
    node_first,
    node_second,
    node_cotan,
    edge_cotan,
):
    bands = lax.axis_size("band")
    nodes, width = node_latent.shape
    sets, cap = edge_latent.shape[1:3]
    send_ids = send_slot.reshape(sets, 1, cap)
    me = lax.axis_index("band").astype(jnp.int32).reshape(1)

    def step_of(k):
        return band_offsets[k] % bands

    def reach(k):
        return min(step_of(k), bands - step_of(k))

    ordered = sorted(range(sets), key=lambda k: (reach(k), step_of(k)))
    near, far = tuple(ordered[:near_sets]), tuple(ordered[near_sets:])
    local_count = sum(step_of(k) == 0 for k in near)
    near_steps = [step_of(k) for k in near[local_count:]]
    far_steps = list(dict.fromkeys(step_of(k) for k in far))
    steps = near_steps + far_steps
    near_plan = tuple((k,) for k in near[local_count:])
    far_plan = tuple(tuple(k for k in far if step_of(k) == d) for d in far_steps)
    far = sum(far_plan, ())

    order = near + far

    given_cotan, given_first = node_cotan, node_first
    (
        node_latent,
        send_ids,
        recv_ids,
        edges,
        edge_first,
        edge_second,
        node_first,
        node_second,
        node_cotan,
        cotan,
    ) = loaded(
        me,
        node_latent,
        send_ids,
        recv_slot.reshape(sets, 1, cap),
        edge_latent[0],
        edge_first,
        edge_second,
        node_first,
        node_second,
        node_cotan,
        edge_cotan[0],
    )
    remote_plan = tuple(zip(steps, near_plan + far_plan))
    widest = max(len(piece) for piece in near_plan + far_plan)
    (ids,) = call(
        functools.partial(ask_kernel, remote_plan),
        [((bands, 1, widest * cap), jnp.int32)],
        [],
        me,
        send_ids,
        smem=(0,),
    )
    ids = lax.all_to_all(ids, "band", 0, 0, tiled=True)
    picked = call(
        functools.partial(pick_kernel, remote_plan),
        [((len(piece) * cap, width), bf16) for piece in near_plan + far_plan],
        [],
        me,
        node_latent,
        ids,
        smem=(0,),
    )
    sx = [passed_along(block, "band", d) for block, d in zip(picked, steps)]
    sx_near, sx_far = sx[: len(near_plan)], sx[len(near_plan) :]

    local_rows, near_rows, far_rows = local_count * cap, len(near_plan) * cap, len(far) * cap
    total = sets * cap

    def forward_outs(rows):
        return [
            ((rows, width), bf16),
            ((rows, width), f32),
            ((rows, width), f32),
            ((rows, 128), f32),
            ((nodes, width), f32),
        ]

    pick, hot, live, part, sx_local, act_local, slope_local, normed_local, inv_local, node_sum = call(
        functools.partial(start_kernel, (order, local_count)),
        [
            ((total, nodes), bf16),
            ((nodes, total), bf16),
            ((total, 128), f32),
            ((near_rows + far_rows, width), f32),
            ((local_rows, width), bf16),
        ]
        + forward_outs(local_rows),
        [((total, 2 * width), bf16), ((local_rows, width), bf16)],
        edges,
        recv_ids,
        send_ids,
        in_hbm(edge_count),
        edge_first,
        edge_second,
        node_latent,
        smem=(3,),
        after=[picked[0]],
    )
    act_near, slope_near, normed_near, inv_near, node_sum = call(
        functools.partial(near_kernel, (local_rows, len(near_plan))),
        forward_outs(near_rows),
        [((near_rows, width), bf16), ((near_rows, width), bf16)],
        part,
        live,
        hot,
        node_sum,
        edge_first,
        edge_second,
        *sx_near,
    )
    sizes = [len(piece) * cap for piece in far_plan]
    outs = call(
        functools.partial(far_kernel, (far, sizes, local_rows + near_rows, near_rows)),
        [((size, width), bf16) for size in sizes]
        + [((far_rows, width), bf16), ((far_rows, width), bf16), ((far_rows, width), f32)]
        + [((nodes, width), bf16)] * 6,
        [
            ((far_rows, width), bf16),
            ((far_rows, width), f32),
            ((far_rows, 128), f32),
            ((far_rows, width), bf16),
            ((far_rows, width), bf16),
            ((far_rows, width), bf16),
        ],
        cotan,
        part,
        live,
        pick,
        hot,
        node_sum,
        edge_first,
        edge_second,
        node_latent,
        node_cotan,
        node_first,
        node_second,
        *sx_far,
        last=(len(sizes) + 8,),
    )
    gpe_far, outs = list(outs[: len(far_plan)]), outs[len(far_plan) :]
    act_far, goe_far, normed_far, gathered, gpn, act_node, gon, gg, node_new = outs
    back_far = [passed_along(block, "band", -d) for block, d in zip(gpe_far, far_steps)]

    first, second = split_of(bands)
    cut = width % (32 * bands) == 0
    edge_sizes, node_sizes = (3 * width // bands, width // bands), (2 * width // bands, width // bands)
    edge_cuts, node_cuts = ((0, edge_sizes[0]), (3 * width, edge_sizes[1])), ((0, node_sizes[0]), (2 * width, node_sizes[1]))

    def weight_outs(sizes, rows):
        if cut:
            shape = (second, first, sum(sizes), width)
            return [(shape, f32), (shape, bf16)]
        return [((rows, width), f32)]

    outs = call(
        functools.partial(back_kernel, (near, local_count)),
        [((local_rows + near_rows, width), bf16), ((local_rows, width), bf16)]
        + [((cap, width), bf16)] * len(near_steps),
        [((local_rows + near_rows, width), bf16)] * 2,
        cotan,
        live,
        pick,
        gg,
        edge_second,
        slope_local,
        normed_local,
        inv_local,
        slope_near,
        normed_near,
        inv_near,
    )
    goe_near, gpe_local = outs[:2]
    gpe_near = list(outs[2:])
    back_near = [passed_along(block, "band", -d) for block, d in zip(gpe_near, near_steps)]

    gpe = [gpe_local] + gpe_near + gpe_far
    sx_all = [sx_local] + sx_near + sx_far
    recv_sum, *edge_weights = call(
        functools.partial(
            weight_kernel, (order, (len(sx_all), len(gpe), 3, 2), edge_cuts if cut else ())
        ),
        [((nodes, width), bf16)] + weight_outs(edge_sizes, 4 * width),
        [((total, width), bf16)] * 5 + [((4 * width, width), f32)] * cut,
        edges,
        hot,
        me,
        node_latent,
        *sx_all,
        *gpe,
        act_local,
        act_near,
        act_far,
        goe_near,
        goe_far,
        smem=(2,),
    )

    def edge_outputs(after):
        return call(
            functools.partial(edge_kernel, (order, 3, len(gpe))),
            [((sets, cap, width), bf16), ((sets, cap, width), bf16)],
            [((total, width), bf16)],
            edges,
            cotan,
            edge_first,
            live,
            normed_local,
            normed_near,
            normed_far,
            *gpe,
            after=after,
            last=(0, 1),
        )

    def node_output(after):
        (base,) = call(
            base_kernel,
            [((nodes, width), f32)],
            [],
            given_cotan,
            gpn,
            recv_sum,
            edge_first,
            given_first,
            after=after,
        )
        (grad_nodes,) = call(
            functools.partial(final_kernel, (near[:local_count], remote_plan)),
            [((nodes, width), bf16)],
            [((nodes, total), bf16), ((total, width), bf16)],
            me,
            base,
            edge_first,
            send_ids,
            ids,
            gpe_local,
            *back_near,
            *back_far,
            smem=(0,),
            last=(0,),
        )
        return grad_nodes

    node_weights = call(
        functools.partial(node_weight_kernel, node_cuts if cut else ()),
        weight_outs(node_sizes, 3 * width),
        [((3 * width, width), f32)] * cut,
        me,
        node_latent,
        gathered,
        gpn,
        act_node,
        gon,
        smem=(0,),
    )
    if cut:
        along_y, along_z = (2, first, 1), (2 * first, second, 0)
        keep_node, sent_node = node_weights
        keep_edge, sent_edge = edge_weights
        came_node = [in_group(sent_node, "band", 1, 2, 1)]
        keep_node, came_node = add_stage(me, keep_node, came_node, *along_y, [])
        sent_edge = held_until(sent_edge, back_far + came_node)
        came_edge = [in_group(sent_edge, "band", 1, 2, 1)]
        keep_node, came_node = add_stage(me, keep_node, came_node, *along_z, [sent_edge])
        keep_edge, came_edge = add_stage(me, keep_edge, came_edge, *along_y, [keep_node])
        edge_new, grad_edges = edge_outputs([keep_edge])
        keep_edge, came_edge = add_stage(me, keep_edge, came_edge, *along_z, [in_hbm(edge_new)] + came_node)
        piece = last_sum((keep_edge, came_edge), (keep_node, came_node))
        grad_nodes = node_output([piece])
        grad_e1, grad_e2, grad_n1, grad_n2 = gathered_from_all(
            piece, edge_sizes + node_sizes, [in_hbm(grad_nodes)]
        )
    else:
        whole = lax.psum(node_weights[0], "band").astype(bf16)
        grad_n1, grad_n2 = whole[: 2 * width], whole[2 * width :]
        whole = lax.psum(edge_weights[0], "band").astype(bf16)
        grad_e1, grad_e2 = whole[: 3 * width], whole[3 * width :]
        edge_new, grad_edges = edge_outputs([])
        grad_nodes = node_output([])
    return (
        node_new,
        edge_new[None],
        grad_nodes,
        grad_edges[None],
        grad_e1,
        grad_e2,
        grad_n1,
        grad_n2,
    )


def solution(mesh):
    return jax.shard_map(
        local,
        mesh=mesh,
        in_specs=(
            P(("groups", "band"), None),
            P(("groups", "band"), None, None, None),
            P(("groups", "band"), None, None),
            P(("groups", "band"), None, None),
            P(("groups", "band"), None),
            P(),
            P(),
            P(),
            P(),
            P(("groups", "band"), None),
            P(("groups", "band"), None, None, None),
        ),
        out_specs=(
            P(("groups", "band"), None),
            P(("groups", "band"), None, None, None),
            P(("groups", "band"), None),
            P(("groups", "band"), None, None, None),
            P("groups", None),
            P("groups", None),
            P("groups", None),
            P("groups", None),
        ),
        check_vma=False,
    )
```

```python
import functools

import jax
import jax.numpy as jnp
from jax import lax
from jax.experimental import pallas as pl
from jax.experimental.pallas import tpu as pltpu
from jax.sharding import PartitionSpec as P

band_offsets = (0, 1, -1, 2, -2, 4, -4, 8, -8, 16, -16)
norm_eps = 1e-05
near_sets = 7
bf16 = jnp.bfloat16
f32 = jnp.float32
vmem_limit = 20 * 1024 * 1024


def passed_along(block, axis, distance):
    devices = range(lax.axis_size(axis))
    route = [((i - distance) % len(devices), i) for i in devices]
    return lax.ppermute(block, axis, route)


def layer_norm(inputs):
    average = jnp.mean(inputs, axis=-1, keepdims=True)
    centred = inputs - average
    inverse = lax.rsqrt(jnp.mean(centred * centred, axis=-1, keepdims=True) + norm_eps)
    return (centred * inverse, inverse)


def norm_back(normed, inverse, upstream):
    return inverse * (
        upstream
        - jnp.mean(upstream, axis=-1, keepdims=True)
        - normed * jnp.mean(upstream * normed, axis=-1, keepdims=True)
    )


def slope_of(inputs, squashed):
    return squashed * (1.0 + inputs * (1.0 - squashed))


def dot(left_side, right_side):
    return jnp.dot(left_side, right_side, preferred_element_type=f32)


def dot_rt(left_side, right_side):
    return lax.dot_general(
        left_side, right_side, (((1,), (1,)), ((), ())), preferred_element_type=f32
    )


def dot_lt(left_side, right_side):
    return lax.dot_general(
        left_side, right_side, (((0,), (0,)), ((), ())), preferred_element_type=f32
    )


def pick_table(ids, nodes):
    cap = ids.shape[1]
    down = jnp.transpose(jnp.broadcast_to(ids, (cap, cap)))
    parts = []
    for first in range(0, nodes, cap):
        wide = min(cap, nodes - first)
        lanes = lax.broadcasted_iota(jnp.int32, (cap, wide), 1) + first
        parts.append(jnp.where(down[:, :wide] == lanes, 1.0, 0.0).astype(bf16))
    return jnp.concatenate(parts, axis=1)


def sum_table(ids, nodes):
    down = lax.broadcasted_iota(jnp.int32, (nodes, ids.shape[1]), 0)
    return jnp.where(down == ids, 1.0, 0.0).astype(bf16)


def live_rows(count, cap):
    return (lax.broadcasted_iota(jnp.int32, (cap, 128), 0) < count).astype(f32)


def call(body, outs, scratch, *args, smem=(), after=(), last=()):
    spaces, given = [], []
    for i, arg in enumerate(args):
        spaces.append(pl.BlockSpec(memory_space=pltpu.SMEM if i in smem else pltpu.VMEM))
        given.append(arg if i in smem else pltpu.with_memory_space_constraint(arg, pltpu.VMEM))
    spaces += [pl.BlockSpec(memory_space=pl.ANY)] * len(after)

    def kernel(*refs):
        body(*refs[: len(args)], *refs[len(args) + len(after) :])

    return pl.pallas_call(
        kernel,
        out_shape=[
            (pltpu.HBM if i in last else pltpu.VMEM)(shape, kind)
            for i, (shape, kind) in enumerate(outs)
        ],
        in_specs=spaces,
        out_specs=[pl.BlockSpec(memory_space=pltpu.VMEM)] * len(outs),
        scratch_shapes=[pltpu.VMEM(shape, kind) for shape, kind in scratch],
        compiler_params=pltpu.CompilerParams(vmem_limit_bytes=vmem_limit),
        cost_estimate=pl.CostEstimate(flops=1, bytes_accessed=1, transcendentals=0),
    )(*given, *after)


def in_hbm(array):
    return pltpu.with_memory_space_constraint(array, pltpu.HBM)


def load_kernel(count, *refs):
    sems, refs = refs[-1], refs[1:]
    copies = [
        pltpu.make_async_copy(refs[i], refs[count + i], sems.at[i]) for i in range(count)
    ]
    for copy in copies:
        copy.start()
    for copy in copies:
        copy.wait()


def loaded(me, *args):
    count = len(args)
    return pl.pallas_call(
        functools.partial(load_kernel, count),
        out_shape=[pltpu.VMEM(arg.shape, arg.dtype) for arg in args],
        in_specs=[pl.BlockSpec(memory_space=pltpu.SMEM)]
        + [pl.BlockSpec(memory_space=pltpu.HBM)] * count,
        out_specs=[pl.BlockSpec(memory_space=pltpu.VMEM)] * count,
        scratch_shapes=[pltpu.SemaphoreType.DMA((count,))],
        compiler_params=pltpu.CompilerParams(vmem_limit_bytes=1024 * 1024),
        cost_estimate=pl.CostEstimate(flops=1, bytes_accessed=1, transcendentals=0),
    )(me, *[in_hbm(arg) for arg in args])


def ask_kernel(plan, me_ref, send_ref, out_ref):
    bands = out_ref.shape[0]
    out_ref[...] = jnp.zeros_like(out_ref)
    for step, sets in plan:
        ids = [send_ref[k] for k in sets]
        blank = out_ref.shape[2] - len(sets) * send_ref.shape[2]
        if blank:
            ids.append(jnp.zeros((1, blank), jnp.int32))
        out_ref[lax.rem(me_ref[0] + bands - step, bands)] = jnp.concatenate(ids, axis=1)


def asked(me_ref, id_ref, step, index, cap):
    row = lax.rem(me_ref[0] + step, id_ref.shape[0])
    return id_ref[row][:, index * cap : (index + 1) * cap]


def pick_kernel(plan, me_ref, node_ref, id_ref, *out_refs):
    nodes = node_ref.shape[0]
    for out_ref, (step, sets) in zip(out_refs, plan):
        cap = out_ref.shape[0] // len(sets)
        for i in range(len(sets)):
            hot = pick_table(asked(me_ref, id_ref, step, i, cap), nodes)
            out_ref[i * cap : (i + 1) * cap, :] = dot(hot, node_ref[...]).astype(bf16)


def forward_rows(pre, live, w2, act_ref, slope_ref, normed_ref, inv_ref, msg_ref, rows):
    squashed = jax.nn.sigmoid(pre)
    slope_ref[rows, :] = slope_of(pre, squashed)
    act = (pre * squashed).astype(bf16)
    act_ref[rows, :] = act
    normed, inverse = layer_norm(dot(act, w2))
    normed_ref[rows, :] = normed
    inv_ref[rows, :] = jnp.broadcast_to(inverse, (inverse.shape[0], 128))
    msg_ref[rows, :] = (live * normed).astype(bf16)


def backward_rows(cotan, picked, live, normed, inverse, slope, w2):
    upstream = live * (cotan.astype(f32) + picked)
    goe = norm_back(normed, inverse, upstream).astype(bf16)
    return goe, (dot_rt(goe, w2) * slope).astype(bf16)


def stack_into(out_ref, refs):
    first = 0
    for ref in refs:
        out_ref[first : first + ref.shape[0], :] = ref[...]
        first += ref.shape[0]


def start_kernel(plan, *refs):
    order, local_count = plan
    (
        edge_ref,
        recv_ref,
        send_ref,
        count_ref,
        w1_ref,
        w2_ref,
        node_ref,
        pick_ref,
        hot_ref,
        live_ref,
        part_ref,
        sx_ref,
        act_ref,
        slope_ref,
        normed_ref,
        inv_ref,
        sum_ref,
        x_ref,
        msg_ref,
    ) = refs
    nodes, width = node_ref.shape
    cap = recv_ref.shape[2]
    split = local_count * cap
    for i, k in enumerate(order):
        rows = slice(i * cap, (i + 1) * cap)
        x_ref[rows, :width] = edge_ref[k]
        pick_ref[rows, :] = pick_table(recv_ref[k], nodes)
        hot_ref[:, rows] = sum_table(recv_ref[k], nodes)
        live_ref[rows, :] = live_rows(count_ref[0, k], cap)
        if i < local_count:
            sx_ref[rows, :] = dot(pick_table(send_ref[k], nodes), node_ref[...]).astype(bf16)
    x_ref[:, width:] = dot(pick_ref[...], node_ref[...]).astype(bf16)
    part = dot(x_ref[:split, :width], w1_ref[:width, :])
    part += dot(x_ref[:split, width:], w1_ref[2 * width :, :])
    pre = part + dot(sx_ref[...], w1_ref[width : 2 * width, :])
    rows = slice(0, split)
    live = live_ref[rows, :1]
    forward_rows(pre, live, w2_ref[...], act_ref, slope_ref, normed_ref, inv_ref, msg_ref, rows)
    sum_ref[...] = dot(hot_ref[:, :split], msg_ref[...])
    part = dot(x_ref[split:, :width], w1_ref[:width, :])
    part_ref[...] = part + dot(x_ref[split:, width:], w1_ref[2 * width :, :])


def near_kernel(plan, *refs):
    first, count = plan
    part_ref, live_ref, hot_ref, sum_in_ref, w1_ref, w2_ref = refs[:6]
    sx_refs = refs[6 : 6 + count]
    act_ref, slope_ref, normed_ref, inv_ref, sum_ref, sx_ref, msg_ref = refs[6 + count :]
    total, width = sx_ref.shape
    stack_into(sx_ref, sx_refs)
    for j in range(2):
        rows = slice(j * total // 2, (j + 1) * total // 2)
        pre = part_ref[rows, :] + dot(sx_ref[rows, :], w1_ref[width : 2 * width, :])
        live = live_ref[first + rows.start : first + rows.stop, :1]
        forward_rows(pre, live, w2_ref[...], act_ref, slope_ref, normed_ref, inv_ref, msg_ref, rows)
    sum_ref[...] = sum_in_ref[...] + dot(hot_ref[:, first : first + total], msg_ref[...])


def far_kernel(plan, *refs):
    sets, sizes, first, part_first = plan
    count = len(sizes)
    (
        cotan_ref,
        part_ref,
        live_ref,
        pick_ref,
        hot_ref,
        sum_ref,
        w1_ref,
        w2_ref,
        node_ref,
        ncot_ref,
        n1_ref,
        n2_ref,
    ) = refs[:12]
    sx_refs, refs = refs[12 : 12 + count], refs[12 + count :]
    gpe_refs, refs = refs[:count], refs[count:]
    (
        act_ref,
        goe_ref,
        normed_ref,
        gathered_ref,
        gpn_ref,
        act_node_ref,
        gon_ref,
        gg_ref,
        node_new_ref,
        sx_ref,
        slope_ref,
        inv_ref,
        msg_ref,
        cot_ref,
        gpe_ref,
    ) = refs
    total, width = sx_ref.shape
    cap = cotan_ref.shape[1]
    stack_into(sx_ref, sx_refs)
    for i, k in enumerate(sets):
        cot_ref[i * cap : (i + 1) * cap, :] = cotan_ref[k]
    halves = [slice(j * total // 2, (j + 1) * total // 2) for j in range(2)]
    for rows in halves:
        pre = part_ref[part_first + rows.start : part_first + rows.stop, :]
        pre = pre + dot(sx_ref[rows, :], w1_ref[width : 2 * width, :])
        live = live_ref[first + rows.start : first + rows.stop, :1]
        forward_rows(pre, live, w2_ref[...], act_ref, slope_ref, normed_ref, inv_ref, msg_ref, rows)
    gathered = sum_ref[...] + dot(hot_ref[:, first : first + total], msg_ref[...])
    gathered = gathered.astype(bf16)
    gathered_ref[...] = gathered

    pre = dot(node_ref[...], n1_ref[:width, :]) + dot(gathered, n1_ref[width:, :])
    squashed = jax.nn.sigmoid(pre)
    act_node = (pre * squashed).astype(bf16)
    act_node_ref[...] = act_node
    normed, inverse = layer_norm(dot(act_node, n2_ref[...]))
    node_new_ref[...] = (node_ref[...].astype(f32) + normed).astype(bf16)
    gon = norm_back(normed, inverse, ncot_ref[...].astype(f32)).astype(bf16)
    gon_ref[...] = gon
    gpn = (dot_rt(gon, n2_ref[...]) * slope_of(pre, squashed)).astype(bf16)
    gpn_ref[...] = gpn
    gg_ref[...] = dot_rt(gpn, n1_ref[width:, :]).astype(bf16)

    for rows in halves:
        whole = slice(first + rows.start, first + rows.stop)
        goe, gpe = backward_rows(
            cot_ref[rows, :],
            dot(pick_ref[whole, :], gg_ref[...]),
            live_ref[whole, :1],
            normed_ref[rows, :],
            inv_ref[rows, :1],
            slope_ref[rows, :],
            w2_ref[...],
        )
        goe_ref[rows, :] = goe
        gpe_ref[rows, :] = gpe
    at = 0
    for out_ref, size in zip(gpe_refs, sizes):
        out_ref[...] = gpe_ref[at : at + size, :]
        at += size


def back_kernel(plan, *refs):
    sets, local_count = plan
    cotan_ref, live_ref, pick_ref, gg_ref, w2_ref = refs[:5]
    groups = (refs[5:8], refs[8:11])
    goe_ref, local_ref = refs[11:13]
    gpe_refs, (cot_ref, gpe_ref) = refs[13:-2], refs[-2:]
    cap = cotan_ref.shape[1]
    for i, k in enumerate(sets):
        cot_ref[i * cap : (i + 1) * cap, :] = cotan_ref[k]
    first = 0
    for slope_ref, normed_ref, inv_ref in groups:
        rows = slice(first, first + slope_ref.shape[0])
        goe, gpe = backward_rows(
            cot_ref[rows, :],
            dot(pick_ref[rows, :], gg_ref[...]),
            live_ref[rows, :1],
            normed_ref[...],
            inv_ref[:, :1],
            slope_ref[...],
            w2_ref[...],
        )
        goe_ref[rows, :] = goe
        gpe_ref[rows, :] = gpe
        first = rows.stop
    local_ref[...] = gpe_ref[: local_count * cap, :]
    for j, out_ref in enumerate(gpe_refs):
        i = local_count + j
        out_ref[...] = gpe_ref[i * cap : (i + 1) * cap, :]


def deal_out(plan, me_ref, grad_ref, keep_ref, sent_ref):
    core = lax.rem(me_ref[0], 2)
    outer, inner = keep_ref.shape[:2]
    for i in range(outer):
        for j in range(inner):
            pair = (i * inner + j) * 2
            at = 0
            for first, rows in plan:
                for side, out_ref in ((core, keep_ref), (1 - core, sent_ref)):
                    start = pl.multiple_of(first + (pair + side) * rows, rows)
                    piece = grad_ref[pl.ds(start, rows), :]
                    out_ref[i, j, at : at + rows, :] = piece.astype(out_ref.dtype)
                at += rows


def node_weight_kernel(plan, *refs):
    me_ref, node_ref, gathered_ref, gpn_ref, act_node_ref, gon_ref = refs[:6]
    *deal_refs, grad_ref = refs[6:] if plan else (refs[6],)
    width = node_ref.shape[1]
    grad_ref[:width, :] = dot_lt(node_ref[...], gpn_ref[...])
    grad_ref[width : 2 * width, :] = dot_lt(gathered_ref[...], gpn_ref[...])
    grad_ref[2 * width :, :] = dot_lt(act_node_ref[...], gon_ref[...])
    if plan:
        deal_out(plan, me_ref, grad_ref, *deal_refs)


def weight_kernel(plan, *refs):
    order, counts, cuts = plan
    edge_ref, hot_ref, me_ref, node_ref = refs[:4]
    refs = refs[4:]
    groups = []
    for count in counts:
        groups.append(refs[:count])
        refs = refs[count:]
    sx_refs, gpe_refs, act_refs, goe_refs = groups
    rsum_ref, refs = refs[0], refs[1:]
    if cuts:
        deal_refs, refs = refs[:2], refs[2:]
        x_ref, sx_ref, gpe_ref, act_ref, goe_ref, grad_ref = refs
    else:
        grad_ref, x_ref, sx_ref, gpe_ref, act_ref, goe_ref = refs
    width = node_ref.shape[1]
    cap = edge_ref.shape[1]
    for i, k in enumerate(order):
        x_ref[i * cap : (i + 1) * cap, :] = edge_ref[k]
    stack_into(sx_ref, sx_refs)
    stack_into(gpe_ref, gpe_refs)
    stack_into(act_ref, act_refs)
    stack_into(goe_ref, goe_refs)
    recv_sum = dot(hot_ref[...], gpe_ref[...]).astype(bf16)
    rsum_ref[...] = recv_sum
    grad_ref[:width, :] = dot_lt(x_ref[...], gpe_ref[...])
    grad_ref[width : 2 * width, :] = dot_lt(sx_ref[...], gpe_ref[...])
    grad_ref[2 * width : 3 * width, :] = dot_lt(node_ref[...], recv_sum)
    grad_ref[3 * width :, :] = dot_lt(act_ref[...], goe_ref[...])
    if cuts:
        deal_out(cuts, me_ref, grad_ref, *deal_refs)


def base_kernel(ncot_ref, gpn_ref, rsum_ref, w1_ref, n1_ref, base_ref):
    width = w1_ref.shape[1]
    base_ref[...] = (
        ncot_ref[...].astype(f32)
        + dot_rt(gpn_ref[...], n1_ref[:width, :])
        + dot_rt(rsum_ref[...], w1_ref[2 * width :, :])
    )


def edge_kernel(plan, *refs):
    order, normed_count, gpe_count = plan
    edge_ref, cotan_ref, w1_ref, live_ref = refs[:4]
    refs = refs[4:]
    normed_refs, refs = refs[:normed_count], refs[normed_count:]
    gpe_refs, refs = refs[:gpe_count], refs[gpe_count:]
    new_ref, gedge_ref, gpe_ref = refs
    width = w1_ref.shape[1]
    cap = edge_ref.shape[1]
    stack_into(gpe_ref, gpe_refs)
    places = [(ref, at) for ref in normed_refs for at in range(0, ref.shape[0], cap)]
    for i, (k, (normed_ref, at)) in enumerate(zip(order, places)):
        rows = slice(i * cap, (i + 1) * cap)
        grad = cotan_ref[k].astype(f32) + dot_rt(gpe_ref[rows, :], w1_ref[:width, :])
        gedge_ref[k] = grad.astype(bf16)
        message = live_ref[rows, :1] * normed_ref[at : at + cap, :]
        new_ref[k] = (edge_ref[k].astype(f32) + message).astype(bf16)


def final_kernel(plan, *refs):
    local_sets, remote = plan
    me_ref, base_ref, w1_ref, send_ref, id_ref = refs[:5]
    row_refs, (out_ref, hot_ref, rows_ref) = refs[5:-3], refs[-3:]
    nodes, width = base_ref.shape
    cap = send_ref.shape[2]
    ids = [send_ref[k] for k in local_sets]
    ids += [
        asked(me_ref, id_ref, step, i, cap) for step, sets in remote for i in range(len(sets))
    ]
    for i, one in enumerate(ids):
        hot_ref[:, i * cap : (i + 1) * cap] = sum_table(one, nodes)
    stack_into(rows_ref, row_refs)
    send_sum = dot(hot_ref[...], rows_ref[...]).astype(bf16)
    grad = base_ref[...] + dot_rt(send_sum, w1_ref[width : 2 * width, :])
    out_ref[...] = grad.astype(bf16)


def place(me_ref, stride, members):
    return lax.rem(lax.div(me_ref[0], stride), members)


def add_kernel(plan, *refs):
    came, stride, members, axis = plan
    me_ref, keep_ref = refs[:2]
    arr_refs, out_refs = refs[2 : 2 + came], refs[2 + came :]
    here = place(me_ref, stride, members)
    for j, out_ref in enumerate(out_refs):
        at = lax.rem(here + j, members)
        index = (slice(None), at) if axis else (at,)
        piece = keep_ref[index]
        for arr_ref in arr_refs:
            piece += arr_ref[index].astype(f32)
        out_ref[...] = piece.astype(out_ref.dtype)


def last_kernel(counts, *refs):
    refs, out_ref = refs[:-1], refs[-1]
    at = 0
    for count in counts:
        keep_ref, arr_refs, refs = refs[0], refs[1:count], refs[count:]
        piece = keep_ref[...]
        for arr_ref in arr_refs:
            piece += arr_ref[...].astype(f32)
        out_ref[at : at + keep_ref.shape[0], :] = piece.astype(bf16)
        at += keep_ref.shape[0]


def sort_kernel(plan, in_ref, *refs):
    bands, sizes = plan
    out_refs, sems = refs[:-1], refs[-1]
    copies = []
    for band in range(bands):
        at = band * sum(sizes)
        for size, out_ref in zip(sizes, out_refs):
            source, target = in_ref.at[pl.ds(at, size)], out_ref.at[pl.ds(band * size, size)]
            copies.append(pltpu.make_async_copy(source, target, sems.at[len(copies)]))
            at += size
    for copy in copies:
        copy.start()
    for copy in copies:
        copy.wait()


def in_group(block, axis, stride, members, step):
    route = []
    for i in range(lax.axis_size(axis)):
        at = (i // stride) % members
        route.append((i, i + ((at + step) % members - at) * stride))
    return lax.ppermute(block, axis, route)


def split_of(bands):
    chips = bands // 2
    first = 1
    while first * first * 4 <= chips:
        first *= 2
    return first, chips // first


def add_stage(me, keep, arrived, stride, members, axis, after):
    shape = keep.shape[:axis] + keep.shape[axis + 1 :]
    outs = call(
        functools.partial(add_kernel, (len(arrived), stride, members, axis)),
        [(shape, f32)] + [(shape, bf16)] * (members - 1),
        [],
        me,
        keep,
        *arrived,
        smem=(0,),
        after=after,
    )
    return outs[0], [in_group(out, "band", stride, members, j + 1) for j, out in enumerate(outs[1:])]


def last_sum(keep, arrived, after):
    (piece,) = call(
        functools.partial(last_kernel, [1 + len(arrived)]),
        [(keep.shape, bf16)],
        [],
        keep,
        *arrived,
        after=after,
    )
    return piece


def gathered_from_all(piece, sizes, after):
    width = piece.shape[1]
    bands = lax.axis_size("band")
    whole = lax.all_gather(piece, "band", axis=0, tiled=True)
    count = bands * len(sizes)

    def kernel(in_ref, *refs):
        sort_kernel((bands, sizes), in_ref, *refs[len(after) :])

    return pl.pallas_call(
        kernel,
        out_shape=[pltpu.HBM((bands * size, width), bf16) for size in sizes],
        in_specs=[pl.BlockSpec(memory_space=pltpu.HBM)]
        + [pl.BlockSpec(memory_space=pl.ANY)] * len(after),
        out_specs=[pl.BlockSpec(memory_space=pltpu.VMEM)] * len(sizes),
        scratch_shapes=[pltpu.SemaphoreType.DMA((count,))],
        compiler_params=pltpu.CompilerParams(vmem_limit_bytes=8 * 1024 * 1024),
        cost_estimate=pl.CostEstimate(flops=1, bytes_accessed=1, transcendentals=0),
    )(in_hbm(whole), *after)


def held_until(array, after):
    return pl.pallas_call(
        lambda *refs: None,
        out_shape=pltpu.VMEM(array.shape, array.dtype),
        in_specs=[pl.BlockSpec(memory_space=pltpu.VMEM)]
        + [pl.BlockSpec(memory_space=pl.ANY)] * len(after),
        out_specs=pl.BlockSpec(memory_space=pltpu.VMEM),
        input_output_aliases={0: 0},
        compiler_params=pltpu.CompilerParams(vmem_limit_bytes=1024 * 1024),
        cost_estimate=pl.CostEstimate(flops=1, bytes_accessed=1, transcendentals=0),
    )(pltpu.with_memory_space_constraint(array, pltpu.VMEM), *after)


def local(
    node_latent,
    edge_latent,
    recv_slot,
    send_slot,
    edge_count,
    edge_first,
    edge_second,
    node_first,
    node_second,
    node_cotan,
    edge_cotan,
):
    bands = lax.axis_size("band")
    nodes, width = node_latent.shape
    sets, cap = edge_latent.shape[1:3]
    send_ids = send_slot.reshape(sets, 1, cap)
    me = lax.axis_index("band").astype(jnp.int32).reshape(1)

    def step_of(k):
        return band_offsets[k] % bands

    def reach(k):
        return min(step_of(k), bands - step_of(k))

    ordered = sorted(range(sets), key=lambda k: (reach(k), step_of(k)))
    near, far = tuple(ordered[:near_sets]), tuple(ordered[near_sets:])
    local_count = sum(step_of(k) == 0 for k in near)
    near_steps = [step_of(k) for k in near[local_count:]]
    far_steps = list(dict.fromkeys(step_of(k) for k in far))
    steps = near_steps + far_steps
    near_plan = tuple((k,) for k in near[local_count:])
    far_plan = tuple(tuple(k for k in far if step_of(k) == d) for d in far_steps)
    far = sum(far_plan, ())

    order = near + far

    given_cotan, given_first = node_cotan, node_first
    (
        node_latent,
        send_ids,
        recv_ids,
        edges,
        edge_first,
        edge_second,
        node_first,
        node_second,
        node_cotan,
        cotan,
    ) = loaded(
        me,
        node_latent,
        send_ids,
        recv_slot.reshape(sets, 1, cap),
        edge_latent[0],
        edge_first,
        edge_second,
        node_first,
        node_second,
        node_cotan,
        edge_cotan[0],
    )
    remote_plan = tuple(zip(steps, near_plan + far_plan))
    widest = max(len(piece) for piece in near_plan + far_plan)
    (ids,) = call(
        functools.partial(ask_kernel, remote_plan),
        [((bands, 1, widest * cap), jnp.int32)],
        [],
        me,
        send_ids,
        smem=(0,),
    )
    ids = lax.all_to_all(ids, "band", 0, 0, tiled=True)
    picked = call(
        functools.partial(pick_kernel, remote_plan),
        [((len(piece) * cap, width), bf16) for piece in near_plan + far_plan],
        [],
        me,
        node_latent,
        ids,
        smem=(0,),
    )
    sx = [passed_along(block, "band", d) for block, d in zip(picked, steps)]
    sx_near, sx_far = sx[: len(near_plan)], sx[len(near_plan) :]

    local_rows, near_rows, far_rows = local_count * cap, len(near_plan) * cap, len(far) * cap
    total = sets * cap

    def forward_outs(rows):
        return [
            ((rows, width), bf16),
            ((rows, width), f32),
            ((rows, width), f32),
            ((rows, 128), f32),
            ((nodes, width), f32),
        ]

    pick, hot, live, part, sx_local, act_local, slope_local, normed_local, inv_local, node_sum = call(
        functools.partial(start_kernel, (order, local_count)),
        [
            ((total, nodes), bf16),
            ((nodes, total), bf16),
            ((total, 128), f32),
            ((near_rows + far_rows, width), f32),
            ((local_rows, width), bf16),
        ]
        + forward_outs(local_rows),
        [((total, 2 * width), bf16), ((local_rows, width), bf16)],
        edges,
        recv_ids,
        send_ids,
        in_hbm(edge_count),
        edge_first,
        edge_second,
        node_latent,
        smem=(3,),
        after=[picked[0]],
    )
    act_near, slope_near, normed_near, inv_near, node_sum = call(
        functools.partial(near_kernel, (local_rows, len(near_plan))),
        forward_outs(near_rows),
        [((near_rows, width), bf16), ((near_rows, width), bf16)],
        part,
        live,
        hot,
        node_sum,
        edge_first,
        edge_second,
        *sx_near,
    )
    sizes = [len(piece) * cap for piece in far_plan]
    outs = call(
        functools.partial(far_kernel, (far, sizes, local_rows + near_rows, near_rows)),
        [((size, width), bf16) for size in sizes]
        + [((far_rows, width), bf16), ((far_rows, width), bf16), ((far_rows, width), f32)]
        + [((nodes, width), bf16)] * 6,
        [
            ((far_rows, width), bf16),
            ((far_rows, width), f32),
            ((far_rows, 128), f32),
            ((far_rows, width), bf16),
            ((far_rows, width), bf16),
            ((far_rows, width), bf16),
        ],
        cotan,
        part,
        live,
        pick,
        hot,
        node_sum,
        edge_first,
        edge_second,
        node_latent,
        node_cotan,
        node_first,
        node_second,
        *sx_far,
        last=(len(sizes) + 8,),
    )
    gpe_far, outs = list(outs[: len(far_plan)]), outs[len(far_plan) :]
    act_far, goe_far, normed_far, gathered, gpn, act_node, gon, gg, node_new = outs
    back_far = [passed_along(block, "band", -d) for block, d in zip(gpe_far, far_steps)]

    first, second = split_of(bands)
    cut = width % (32 * bands) == 0
    edge_sizes, node_sizes = (3 * width // bands, width // bands), (2 * width // bands, width // bands)
    edge_cuts, node_cuts = ((0, edge_sizes[0]), (3 * width, edge_sizes[1])), ((0, node_sizes[0]), (2 * width, node_sizes[1]))

    def weight_outs(sizes, rows):
        if cut:
            shape = (second, first, sum(sizes), width)
            return [(shape, f32), (shape, bf16)]
        return [((rows, width), f32)]

    outs = call(
        functools.partial(back_kernel, (near, local_count)),
        [((local_rows + near_rows, width), bf16), ((local_rows, width), bf16)]
        + [((cap, width), bf16)] * len(near_steps),
        [((local_rows + near_rows, width), bf16)] * 2,
        cotan,
        live,
        pick,
        gg,
        edge_second,
        slope_local,
        normed_local,
        inv_local,
        slope_near,
        normed_near,
        inv_near,
    )
    goe_near, gpe_local = outs[:2]
    gpe_near = list(outs[2:])
    back_near = [passed_along(block, "band", -d) for block, d in zip(gpe_near, near_steps)]

    gpe = [gpe_local] + gpe_near + gpe_far
    sx_all = [sx_local] + sx_near + sx_far
    recv_sum, *edge_weights = call(
        functools.partial(
            weight_kernel, (order, (len(sx_all), len(gpe), 3, 2), edge_cuts if cut else ())
        ),
        [((nodes, width), bf16)] + weight_outs(edge_sizes, 4 * width),
        [((total, width), bf16)] * 5 + [((4 * width, width), f32)] * cut,
        edges,
        hot,
        me,
        node_latent,
        *sx_all,
        *gpe,
        act_local,
        act_near,
        act_far,
        goe_near,
        goe_far,
        smem=(2,),
    )

    def edge_outputs(after):
        return call(
            functools.partial(edge_kernel, (order, 3, len(gpe))),
            [((sets, cap, width), bf16), ((sets, cap, width), bf16)],
            [((total, width), bf16)],
            edges,
            cotan,
            edge_first,
            live,
            normed_local,
            normed_near,
            normed_far,
            *gpe,
            after=after,
            last=(0, 1),
        )

    def node_output(after):
        (base,) = call(
            base_kernel,
            [((nodes, width), f32)],
            [],
            given_cotan,
            gpn,
            recv_sum,
            edge_first,
            given_first,
            after=after,
        )
        (grad_nodes,) = call(
            functools.partial(final_kernel, (near[:local_count], remote_plan)),
            [((nodes, width), bf16)],
            [((nodes, total), bf16), ((total, width), bf16)],
            me,
            base,
            edge_first,
            send_ids,
            ids,
            gpe_local,
            *back_near,
            *back_far,
            smem=(0,),
            last=(0,),
        )
        return grad_nodes

    node_weights = call(
        functools.partial(node_weight_kernel, node_cuts if cut else ()),
        weight_outs(node_sizes, 3 * width),
        [((3 * width, width), f32)] * cut,
        me,
        node_latent,
        gathered,
        gpn,
        act_node,
        gon,
        smem=(0,),
    )
    if cut:
        along_y, along_z = (2, first, 1), (2 * first, second, 0)
        keep_node, sent_node = node_weights
        keep_edge, sent_edge = edge_weights
        came_node = [in_group(sent_node, "band", 1, 2, 1)]
        keep_node, came_node = add_stage(me, keep_node, came_node, *along_y, [])
        sent_edge = held_until(sent_edge, back_far + came_node)
        came_edge = [in_group(sent_edge, "band", 1, 2, 1)]
        keep_node, came_node = add_stage(me, keep_node, came_node, *along_z, [sent_edge])
        keep_edge, came_edge = add_stage(me, keep_edge, came_edge, *along_y, [keep_node])
        edge_new, grad_edges = edge_outputs([keep_edge])
        piece_node = last_sum(keep_node, came_node, [in_hbm(edge_new)] + came_edge)
        keep_edge, came_edge = add_stage(me, keep_edge, came_edge, *along_z, [piece_node])
        piece_edge = last_sum(keep_edge, came_edge, [])
        grad_nodes = node_output([piece_edge])
        grad_n1, grad_n2 = gathered_from_all(piece_node, node_sizes, [in_hbm(grad_nodes)])
        grad_e1, grad_e2 = gathered_from_all(piece_edge, edge_sizes, [in_hbm(grad_n2)])
    else:
        whole = lax.psum(node_weights[0], "band").astype(bf16)
        grad_n1, grad_n2 = whole[: 2 * width], whole[2 * width :]
        whole = lax.psum(edge_weights[0], "band").astype(bf16)
        grad_e1, grad_e2 = whole[: 3 * width], whole[3 * width :]
        edge_new, grad_edges = edge_outputs([])
        grad_nodes = node_output([])
    return (
        node_new,
        edge_new[None],
        grad_nodes,
        grad_edges[None],
        grad_e1,
        grad_e2,
        grad_n1,
        grad_n2,
    )


def solution(mesh):
    return jax.shard_map(
        local,
        mesh=mesh,
        in_specs=(
            P(("groups", "band"), None),
            P(("groups", "band"), None, None, None),
            P(("groups", "band"), None, None),
            P(("groups", "band"), None, None),
            P(("groups", "band"), None),
            P(),
            P(),
            P(),
            P(),
            P(("groups", "band"), None),
            P(("groups", "band"), None, None, None),
        ),
        out_specs=(
            P(("groups", "band"), None),
            P(("groups", "band"), None, None, None),
            P(("groups", "band"), None),
            P(("groups", "band"), None, None, None),
            P("groups", None),
            P("groups", None),
            P("groups", None),
            P("groups", None),
        ),
        check_vma=False,
    )
```

```python
import functools

import jax
import jax.numpy as jnp
from jax import lax
from jax.experimental import pallas as pl
from jax.experimental.pallas import tpu as pltpu
from jax.sharding import PartitionSpec as P

band_offsets = (0, 1, -1, 2, -2, 4, -4, 8, -8, 16, -16)
norm_eps = 1e-05
near_sets = 7
bf16 = jnp.bfloat16
f32 = jnp.float32
vmem_limit = 20 * 1024 * 1024


def passed_along(block, axis, distance):
    devices = range(lax.axis_size(axis))
    route = [((i - distance) % len(devices), i) for i in devices]
    return lax.ppermute(block, axis, route)


def layer_norm(inputs):
    average = jnp.mean(inputs, axis=-1, keepdims=True)
    centred = inputs - average
    inverse = lax.rsqrt(jnp.mean(centred * centred, axis=-1, keepdims=True) + norm_eps)
    return (centred * inverse, inverse)


def norm_back(normed, inverse, upstream):
    return inverse * (
        upstream
        - jnp.mean(upstream, axis=-1, keepdims=True)
        - normed * jnp.mean(upstream * normed, axis=-1, keepdims=True)
    )


def slope_of(inputs, squashed):
    return squashed * (1.0 + inputs * (1.0 - squashed))


def dot(left_side, right_side):
    return jnp.dot(left_side, right_side, preferred_element_type=f32)


def dot_rt(left_side, right_side):
    return lax.dot_general(
        left_side, right_side, (((1,), (1,)), ((), ())), preferred_element_type=f32
    )


def dot_lt(left_side, right_side):
    return lax.dot_general(
        left_side, right_side, (((0,), (0,)), ((), ())), preferred_element_type=f32
    )


def pick_table(ids, nodes):
    cap = ids.shape[1]
    down = jnp.transpose(jnp.broadcast_to(ids, (cap, cap)))
    parts = []
    for first in range(0, nodes, cap):
        wide = min(cap, nodes - first)
        lanes = lax.broadcasted_iota(jnp.int32, (cap, wide), 1) + first
        parts.append(jnp.where(down[:, :wide] == lanes, 1.0, 0.0).astype(bf16))
    return jnp.concatenate(parts, axis=1)


def sum_table(ids, nodes):
    down = lax.broadcasted_iota(jnp.int32, (nodes, ids.shape[1]), 0)
    return jnp.where(down == ids, 1.0, 0.0).astype(bf16)


def live_rows(count, cap):
    return (lax.broadcasted_iota(jnp.int32, (cap, 128), 0) < count).astype(f32)


def call(body, outs, scratch, *args, smem=(), after=(), last=()):
    spaces, given = [], []
    for i, arg in enumerate(args):
        spaces.append(pl.BlockSpec(memory_space=pltpu.SMEM if i in smem else pltpu.VMEM))
        given.append(arg if i in smem else pltpu.with_memory_space_constraint(arg, pltpu.VMEM))
    spaces += [pl.BlockSpec(memory_space=pl.ANY)] * len(after)

    def kernel(*refs):
        body(*refs[: len(args)], *refs[len(args) + len(after) :])

    return pl.pallas_call(
        kernel,
        out_shape=[
            (pltpu.HBM if i in last else pltpu.VMEM)(shape, kind)
            for i, (shape, kind) in enumerate(outs)
        ],
        in_specs=spaces,
        out_specs=[pl.BlockSpec(memory_space=pltpu.VMEM)] * len(outs),
        scratch_shapes=[pltpu.VMEM(shape, kind) for shape, kind in scratch],
        compiler_params=pltpu.CompilerParams(vmem_limit_bytes=vmem_limit),
        cost_estimate=pl.CostEstimate(flops=1, bytes_accessed=1, transcendentals=0),
    )(*given, *after)


def in_hbm(array):
    return pltpu.with_memory_space_constraint(array, pltpu.HBM)


def load_kernel(count, *refs):
    sems, refs = refs[-1], refs[1:]
    copies = [
        pltpu.make_async_copy(refs[i], refs[count + i], sems.at[i]) for i in range(count)
    ]
    for copy in copies:
        copy.start()
    for copy in copies:
        copy.wait()


def loaded(me, *args):
    count = len(args)
    return pl.pallas_call(
        functools.partial(load_kernel, count),
        out_shape=[pltpu.VMEM(arg.shape, arg.dtype) for arg in args],
        in_specs=[pl.BlockSpec(memory_space=pltpu.SMEM)]
        + [pl.BlockSpec(memory_space=pltpu.HBM)] * count,
        out_specs=[pl.BlockSpec(memory_space=pltpu.VMEM)] * count,
        scratch_shapes=[pltpu.SemaphoreType.DMA((count,))],
        compiler_params=pltpu.CompilerParams(vmem_limit_bytes=1024 * 1024),
        cost_estimate=pl.CostEstimate(flops=1, bytes_accessed=1, transcendentals=0),
    )(me, *[in_hbm(arg) for arg in args])


def ask_kernel(plan, me_ref, send_ref, out_ref):
    bands = out_ref.shape[0]
    out_ref[...] = jnp.zeros_like(out_ref)
    for step, sets in plan:
        ids = [send_ref[k] for k in sets]
        blank = out_ref.shape[2] - len(sets) * send_ref.shape[2]
        if blank:
            ids.append(jnp.zeros((1, blank), jnp.int32))
        out_ref[lax.rem(me_ref[0] + bands - step, bands)] = jnp.concatenate(ids, axis=1)


def asked(me_ref, id_ref, step, index, cap):
    row = lax.rem(me_ref[0] + step, id_ref.shape[0])
    return id_ref[row][:, index * cap : (index + 1) * cap]


def pick_kernel(plan, me_ref, node_ref, id_ref, *out_refs):
    nodes = node_ref.shape[0]
    for out_ref, (step, sets) in zip(out_refs, plan):
        cap = out_ref.shape[0] // len(sets)
        for i in range(len(sets)):
            hot = pick_table(asked(me_ref, id_ref, step, i, cap), nodes)
            out_ref[i * cap : (i + 1) * cap, :] = dot(hot, node_ref[...]).astype(bf16)


def forward_rows(pre, live, w2, act_ref, slope_ref, normed_ref, inv_ref, msg_ref, rows):
    squashed = jax.nn.sigmoid(pre)
    slope_ref[rows, :] = slope_of(pre, squashed)
    act = (pre * squashed).astype(bf16)
    act_ref[rows, :] = act
    normed, inverse = layer_norm(dot(act, w2))
    normed_ref[rows, :] = normed
    inv_ref[rows, :] = jnp.broadcast_to(inverse, (inverse.shape[0], 128))
    msg_ref[rows, :] = (live * normed).astype(bf16)


def backward_rows(cotan, picked, live, normed, inverse, slope, w2):
    upstream = live * (cotan.astype(f32) + picked)
    goe = norm_back(normed, inverse, upstream).astype(bf16)
    return goe, (dot_rt(goe, w2) * slope).astype(bf16)


def stack_into(out_ref, refs):
    first = 0
    for ref in refs:
        out_ref[first : first + ref.shape[0], :] = ref[...]
        first += ref.shape[0]


def start_kernel(plan, *refs):
    order, local_count = plan
    (
        edge_ref,
        recv_ref,
        send_ref,
        count_ref,
        w1_ref,
        w2_ref,
        node_ref,
        pick_ref,
        hot_ref,
        live_ref,
        part_ref,
        sx_ref,
        act_ref,
        slope_ref,
        normed_ref,
        inv_ref,
        sum_ref,
        x_ref,
        msg_ref,
    ) = refs
    nodes, width = node_ref.shape
    cap = recv_ref.shape[2]
    split = local_count * cap
    for i, k in enumerate(order):
        rows = slice(i * cap, (i + 1) * cap)
        x_ref[rows, :width] = edge_ref[k]
        pick_ref[rows, :] = pick_table(recv_ref[k], nodes)
        hot_ref[:, rows] = sum_table(recv_ref[k], nodes)
        live_ref[rows, :] = live_rows(count_ref[0, k], cap)
        if i < local_count:
            sx_ref[rows, :] = dot(pick_table(send_ref[k], nodes), node_ref[...]).astype(bf16)
    x_ref[:, width:] = dot(pick_ref[...], node_ref[...]).astype(bf16)
    part = dot(x_ref[:split, :width], w1_ref[:width, :])
    part += dot(x_ref[:split, width:], w1_ref[2 * width :, :])
    pre = part + dot(sx_ref[...], w1_ref[width : 2 * width, :])
    rows = slice(0, split)
    live = live_ref[rows, :1]
    forward_rows(pre, live, w2_ref[...], act_ref, slope_ref, normed_ref, inv_ref, msg_ref, rows)
    sum_ref[...] = dot(hot_ref[:, :split], msg_ref[...])
    part = dot(x_ref[split:, :width], w1_ref[:width, :])
    part_ref[...] = part + dot(x_ref[split:, width:], w1_ref[2 * width :, :])


def near_kernel(plan, *refs):
    first, count = plan
    part_ref, live_ref, hot_ref, sum_in_ref, w1_ref, w2_ref = refs[:6]
    sx_refs = refs[6 : 6 + count]
    act_ref, slope_ref, normed_ref, inv_ref, sum_ref, sx_ref, msg_ref = refs[6 + count :]
    total, width = sx_ref.shape
    stack_into(sx_ref, sx_refs)
    for j in range(2):
        rows = slice(j * total // 2, (j + 1) * total // 2)
        pre = part_ref[rows, :] + dot(sx_ref[rows, :], w1_ref[width : 2 * width, :])
        live = live_ref[first + rows.start : first + rows.stop, :1]
        forward_rows(pre, live, w2_ref[...], act_ref, slope_ref, normed_ref, inv_ref, msg_ref, rows)
    sum_ref[...] = sum_in_ref[...] + dot(hot_ref[:, first : first + total], msg_ref[...])


def far_kernel(plan, *refs):
    sets, sizes, first, part_first = plan
    count = len(sizes)
    (
        cotan_ref,
        part_ref,
        live_ref,
        pick_ref,
        hot_ref,
        sum_ref,
        w1_ref,
        w2_ref,
        node_ref,
        ncot_ref,
        n1_ref,
        n2_ref,
    ) = refs[:12]
    sx_refs, refs = refs[12 : 12 + count], refs[12 + count :]
    gpe_refs, refs = refs[:count], refs[count:]
    (
        act_ref,
        goe_ref,
        normed_ref,
        gathered_ref,
        gpn_ref,
        act_node_ref,
        gon_ref,
        gg_ref,
        node_new_ref,
        sx_ref,
        slope_ref,
        inv_ref,
        msg_ref,
        cot_ref,
        gpe_ref,
    ) = refs
    total, width = sx_ref.shape
    cap = cotan_ref.shape[1]
    stack_into(sx_ref, sx_refs)
    for i, k in enumerate(sets):
        cot_ref[i * cap : (i + 1) * cap, :] = cotan_ref[k]
    halves = [slice(j * total // 2, (j + 1) * total // 2) for j in range(2)]
    for rows in halves:
        pre = part_ref[part_first + rows.start : part_first + rows.stop, :]
        pre = pre + dot(sx_ref[rows, :], w1_ref[width : 2 * width, :])
        live = live_ref[first + rows.start : first + rows.stop, :1]
        forward_rows(pre, live, w2_ref[...], act_ref, slope_ref, normed_ref, inv_ref, msg_ref, rows)
    gathered = sum_ref[...] + dot(hot_ref[:, first : first + total], msg_ref[...])
    gathered = gathered.astype(bf16)
    gathered_ref[...] = gathered

    pre = dot(node_ref[...], n1_ref[:width, :]) + dot(gathered, n1_ref[width:, :])
    squashed = jax.nn.sigmoid(pre)
    act_node = (pre * squashed).astype(bf16)
    act_node_ref[...] = act_node
    normed, inverse = layer_norm(dot(act_node, n2_ref[...]))
    node_new_ref[...] = (node_ref[...].astype(f32) + normed).astype(bf16)
    gon = norm_back(normed, inverse, ncot_ref[...].astype(f32)).astype(bf16)
    gon_ref[...] = gon
    gpn = (dot_rt(gon, n2_ref[...]) * slope_of(pre, squashed)).astype(bf16)
    gpn_ref[...] = gpn
    gg_ref[...] = dot_rt(gpn, n1_ref[width:, :]).astype(bf16)

    for rows in halves:
        whole = slice(first + rows.start, first + rows.stop)
        goe, gpe = backward_rows(
            cot_ref[rows, :],
            dot(pick_ref[whole, :], gg_ref[...]),
            live_ref[whole, :1],
            normed_ref[rows, :],
            inv_ref[rows, :1],
            slope_ref[rows, :],
            w2_ref[...],
        )
        goe_ref[rows, :] = goe
        gpe_ref[rows, :] = gpe
    at = 0
    for out_ref, size in zip(gpe_refs, sizes):
        out_ref[...] = gpe_ref[at : at + size, :]
        at += size


def back_kernel(plan, *refs):
    sets, local_count = plan
    cotan_ref, live_ref, pick_ref, gg_ref, w2_ref = refs[:5]
    groups = (refs[5:8], refs[8:11])
    goe_ref, local_ref = refs[11:13]
    gpe_refs, (cot_ref, gpe_ref) = refs[13:-2], refs[-2:]
    cap = cotan_ref.shape[1]
    for i, k in enumerate(sets):
        cot_ref[i * cap : (i + 1) * cap, :] = cotan_ref[k]
    first = 0
    for slope_ref, normed_ref, inv_ref in groups:
        rows = slice(first, first + slope_ref.shape[0])
        goe, gpe = backward_rows(
            cot_ref[rows, :],
            dot(pick_ref[rows, :], gg_ref[...]),
            live_ref[rows, :1],
            normed_ref[...],
            inv_ref[:, :1],
            slope_ref[...],
            w2_ref[...],
        )
        goe_ref[rows, :] = goe
        gpe_ref[rows, :] = gpe
        first = rows.stop
    local_ref[...] = gpe_ref[: local_count * cap, :]
    for j, out_ref in enumerate(gpe_refs):
        i = local_count + j
        out_ref[...] = gpe_ref[i * cap : (i + 1) * cap, :]


def node_weight_kernel(me_ref, node_ref, gathered_ref, gpn_ref, act_node_ref, gon_ref, keep_ref, sent_ref, block_ref):
    put = functools.partial(put_block, me_ref, block_ref, keep_ref, sent_ref)
    put(0, node_ref[...], gpn_ref[...])
    put(1, gathered_ref[...], gpn_ref[...])
    put(2, act_node_ref[...], gon_ref[...])


def put_block(me_ref, block_ref, keep_ref, sent_ref, index, left_side, right_side):
    core = lax.rem(me_ref[0], 2)
    half = block_ref.shape[0] // 2
    block_ref[...] = dot_lt(left_side, right_side)
    keep_ref[index] = block_ref[pl.ds(pl.multiple_of(core * half, half), half), :]
    other = block_ref[pl.ds(pl.multiple_of((1 - core) * half, half), half), :]
    sent_ref[index] = other.astype(bf16)


def weight_kernel(plan, *refs):
    order, sx_count, gpe_count, act_count, goe_count = plan
    edge_ref, hot_ref, me_ref, node_ref = refs[:4]
    refs = refs[4:]
    sx_refs, refs = refs[:sx_count], refs[sx_count:]
    gpe_refs, refs = refs[:gpe_count], refs[gpe_count:]
    act_refs, refs = refs[:act_count], refs[act_count:]
    goe_refs, refs = refs[:goe_count], refs[goe_count:]
    keep_ref, sent_ref, rsum_ref, x_ref, sx_ref, gpe_ref, act_ref, goe_ref, block_ref = refs
    cap = edge_ref.shape[1]
    for i, k in enumerate(order):
        x_ref[i * cap : (i + 1) * cap, :] = edge_ref[k]
    stack_into(sx_ref, sx_refs)
    stack_into(gpe_ref, gpe_refs)
    stack_into(act_ref, act_refs)
    stack_into(goe_ref, goe_refs)
    recv_sum = dot(hot_ref[...], gpe_ref[...]).astype(bf16)
    rsum_ref[...] = recv_sum
    put = functools.partial(put_block, me_ref, block_ref, keep_ref, sent_ref)
    put(0, x_ref[...], gpe_ref[...])
    put(1, sx_ref[...], gpe_ref[...])
    put(2, node_ref[...], recv_sum)
    put(3, act_ref[...], goe_ref[...])


def base_kernel(ncot_ref, gpn_ref, rsum_ref, w1_ref, n1_ref, base_ref):
    width = w1_ref.shape[1]
    base_ref[...] = (
        ncot_ref[...].astype(f32)
        + dot_rt(gpn_ref[...], n1_ref[:width, :])
        + dot_rt(rsum_ref[...], w1_ref[2 * width :, :])
    )


def edge_kernel(plan, *refs):
    order, normed_count, gpe_count = plan
    edge_ref, cotan_ref, w1_ref, live_ref = refs[:4]
    refs = refs[4:]
    normed_refs, refs = refs[:normed_count], refs[normed_count:]
    gpe_refs, refs = refs[:gpe_count], refs[gpe_count:]
    new_ref, gedge_ref, gpe_ref = refs
    width = w1_ref.shape[1]
    cap = edge_ref.shape[1]
    stack_into(gpe_ref, gpe_refs)
    places = [(ref, at) for ref in normed_refs for at in range(0, ref.shape[0], cap)]
    for i, (k, (normed_ref, at)) in enumerate(zip(order, places)):
        rows = slice(i * cap, (i + 1) * cap)
        grad = cotan_ref[k].astype(f32) + dot_rt(gpe_ref[rows, :], w1_ref[:width, :])
        gedge_ref[k] = grad.astype(bf16)
        message = live_ref[rows, :1] * normed_ref[at : at + cap, :]
        new_ref[k] = (edge_ref[k].astype(f32) + message).astype(bf16)


def final_kernel(plan, *refs):
    local_sets, remote = plan
    me_ref, base_ref, w1_ref, send_ref, id_ref = refs[:5]
    row_refs, (out_ref, hot_ref, rows_ref) = refs[5:-3], refs[-3:]
    nodes, width = base_ref.shape
    cap = send_ref.shape[2]
    ids = [send_ref[k] for k in local_sets]
    ids += [
        asked(me_ref, id_ref, step, i, cap) for step, sets in remote for i in range(len(sets))
    ]
    for i, one in enumerate(ids):
        hot_ref[:, i * cap : (i + 1) * cap] = sum_table(one, nodes)
    stack_into(rows_ref, row_refs)
    send_sum = dot(hot_ref[...], rows_ref[...]).astype(bf16)
    grad = base_ref[...] + dot_rt(send_sum, w1_ref[width : 2 * width, :])
    out_ref[...] = grad.astype(bf16)


def place(me_ref, stride, members):
    return lax.rem(lax.div(me_ref[0], stride), members)


def add_kernel(plan, *refs):
    came, stride, members = plan
    me_ref, keep_ref = refs[:2]
    arr_refs, out_refs = refs[2 : 2 + came], refs[2 + came :]
    size = keep_ref.shape[1] // members
    here = place(me_ref, stride, members)
    for j, out_ref in enumerate(out_refs):
        at = lax.rem(here + j, members) * size
        rows = pl.ds(pl.multiple_of(at, size), size)
        piece = keep_ref[:, rows, :]
        for arr_ref in arr_refs:
            piece += arr_ref[:, rows, :].astype(f32)
        out_ref[...] = piece.astype(out_ref.dtype)


def gather_kernel(plan, *refs):
    stride, members = plan
    me_ref, piece_refs, out_ref = refs[0], refs[1:-1], refs[-1]
    size = piece_refs[0].shape[1]
    here = place(me_ref, stride, members)
    for j, piece_ref in enumerate(piece_refs):
        at = lax.rem(here + members - j, members) * size
        out_ref[:, pl.ds(pl.multiple_of(at, size), size), :] = piece_ref[...]


def join_kernel(plan, *refs):
    members, blocks = plan
    me_ref = refs[0]
    piece_refs, other_refs = refs[1 : 1 + members], refs[1 + members : 1 + 2 * members]
    out_refs = refs[1 + 2 * members :]
    size = piece_refs[0].shape[1]
    core = lax.rem(me_ref[0], 2)
    here = place(me_ref, 2, members)
    for index, (which, block) in enumerate(blocks):
        first = 2 * block * members * size
        for side, side_refs in ((core, piece_refs), (1 - core, other_refs)):
            for j, piece_ref in enumerate(side_refs):
                at = first + (side * members + lax.rem(here + members - j, members)) * size
                rows = pl.ds(pl.multiple_of(at, size), size)
                out_refs[which][rows, :] = piece_ref[index]


def in_group(block, axis, stride, members, step):
    route = []
    for i in range(lax.axis_size(axis)):
        at = (i // stride) % members
        route.append((i, i + ((at + step) % members - at) * stride))
    return lax.ppermute(block, axis, route)


def add_stage(me, keep, arrived, stride, after, members=2, kind=f32):
    count, rows, width = keep.shape
    shape = (count, rows // members, width)
    outs = call(
        functools.partial(add_kernel, (len(arrived), stride, members)),
        [(shape, kind)] + [(shape, bf16)] * (members - 1),
        [],
        me,
        keep,
        *arrived,
        smem=(0,),
        after=after,
    )
    return outs[0], [in_group(out, "band", stride, members, j + 1) for j, out in enumerate(outs[1:])]


def held_until(array, after):
    return pl.pallas_call(
        lambda *refs: None,
        out_shape=pltpu.VMEM(array.shape, array.dtype),
        in_specs=[pl.BlockSpec(memory_space=pltpu.VMEM)]
        + [pl.BlockSpec(memory_space=pl.ANY)] * len(after),
        out_specs=pl.BlockSpec(memory_space=pltpu.VMEM),
        input_output_aliases={0: 0},
        compiler_params=pltpu.CompilerParams(vmem_limit_bytes=1024 * 1024),
        cost_estimate=pl.CostEstimate(flops=1, bytes_accessed=1, transcendentals=0),
    )(pltpu.with_memory_space_constraint(array, pltpu.VMEM), *after)


def gather_stage(me, piece, came, stride, after):
    count, rows, width = piece.shape
    members, pieces = 2, [piece, came]
    (mine,) = call(
        functools.partial(gather_kernel, (stride, members)),
        [((count, rows * members, width), bf16)],
        [],
        me,
        *pieces,
        smem=(0,),
        after=after,
    )
    return mine


def join_stage(me, mine, members, blocks, shapes, swap_after, after):
    pieces = [in_group(mine, "band", 2, members, j) for j in range(1, members)]
    pieces = [mine] + [held_until(piece, swap_after) if swap_after else piece for piece in pieces]
    others = [in_group(one, "band", 1, 2, 1) for one in pieces]
    return call(
        functools.partial(join_kernel, (members, blocks)),
        [(shape, bf16) for shape in shapes],
        [],
        me,
        *pieces,
        *others,
        smem=(0,),
        after=after,
        last=range(len(shapes)),
    )


def reduce_whole(keep, sent):
    bands = lax.axis_size("band")
    chips = [[i for i in range(bands) if i % 2 == c] for c in range(2)]
    total = keep + in_group(sent, "band", 1, 2, 1).astype(f32)
    total = lax.psum(total.astype(bf16), "band", axis_index_groups=chips)
    other = in_group(total, "band", 1, 2, 1)
    core = lax.axis_index("band") % 2
    low, high = jnp.where(core == 0, total, other), jnp.where(core == 0, other, total)
    return jnp.concatenate([low, high], axis=1)


def local(
    node_latent,
    edge_latent,
    recv_slot,
    send_slot,
    edge_count,
    edge_first,
    edge_second,
    node_first,
    node_second,
    node_cotan,
    edge_cotan,
):
    bands = lax.axis_size("band")
    nodes, width = node_latent.shape
    sets, cap = edge_latent.shape[1:3]
    send_ids = send_slot.reshape(sets, 1, cap)
    me = lax.axis_index("band").astype(jnp.int32).reshape(1)

    def step_of(k):
        return band_offsets[k] % bands

    def reach(k):
        return min(step_of(k), bands - step_of(k))

    ordered = sorted(range(sets), key=lambda k: (reach(k), step_of(k)))
    near, far = tuple(ordered[:near_sets]), tuple(ordered[near_sets:])
    local_count = sum(step_of(k) == 0 for k in near)
    near_steps = [step_of(k) for k in near[local_count:]]
    far_steps = list(dict.fromkeys(step_of(k) for k in far))
    steps = near_steps + far_steps
    near_plan = tuple((k,) for k in near[local_count:])
    far_plan = tuple(tuple(k for k in far if step_of(k) == d) for d in far_steps)
    far = sum(far_plan, ())

    order = near + far

    (
        node_latent,
        send_ids,
        recv_ids,
        edges,
        edge_first,
        edge_second,
        node_first,
        node_second,
        node_cotan,
        cotan,
    ) = loaded(
        me,
        node_latent,
        send_ids,
        recv_slot.reshape(sets, 1, cap),
        edge_latent[0],
        edge_first,
        edge_second,
        node_first,
        node_second,
        node_cotan,
        edge_cotan[0],
    )
    remote_plan = tuple(zip(steps, near_plan + far_plan))
    widest = max(len(piece) for piece in near_plan + far_plan)
    (ids,) = call(
        functools.partial(ask_kernel, remote_plan),
        [((bands, 1, widest * cap), jnp.int32)],
        [],
        me,
        send_ids,
        smem=(0,),
    )
    ids = lax.all_to_all(ids, "band", 0, 0, tiled=True)
    picked = call(
        functools.partial(pick_kernel, remote_plan),
        [((len(piece) * cap, width), bf16) for piece in near_plan + far_plan],
        [],
        me,
        node_latent,
        ids,
        smem=(0,),
    )
    sx = [passed_along(block, "band", d) for block, d in zip(picked, steps)]
    sx_near, sx_far = sx[: len(near_plan)], sx[len(near_plan) :]

    local_rows, near_rows, far_rows = local_count * cap, len(near_plan) * cap, len(far) * cap
    total = sets * cap

    def forward_outs(rows):
        return [
            ((rows, width), bf16),
            ((rows, width), f32),
            ((rows, width), f32),
            ((rows, 128), f32),
            ((nodes, width), f32),
        ]

    pick, hot, live, part, sx_local, act_local, slope_local, normed_local, inv_local, node_sum = call(
        functools.partial(start_kernel, (order, local_count)),
        [
            ((total, nodes), bf16),
            ((nodes, total), bf16),
            ((total, 128), f32),
            ((near_rows + far_rows, width), f32),
            ((local_rows, width), bf16),
        ]
        + forward_outs(local_rows),
        [((total, 2 * width), bf16), ((local_rows, width), bf16)],
        edges,
        recv_ids,
        send_ids,
        in_hbm(edge_count),
        edge_first,
        edge_second,
        node_latent,
        smem=(3,),
        after=[picked[0]],
    )
    act_near, slope_near, normed_near, inv_near, node_sum = call(
        functools.partial(near_kernel, (local_rows, len(near_plan))),
        forward_outs(near_rows),
        [((near_rows, width), bf16), ((near_rows, width), bf16)],
        part,
        live,
        hot,
        node_sum,
        edge_first,
        edge_second,
        *sx_near,
    )
    sizes = [len(piece) * cap for piece in far_plan]
    outs = call(
        functools.partial(far_kernel, (far, sizes, local_rows + near_rows, near_rows)),
        [((size, width), bf16) for size in sizes]
        + [((far_rows, width), bf16), ((far_rows, width), bf16), ((far_rows, width), f32)]
        + [((nodes, width), bf16)] * 6,
        [
            ((far_rows, width), bf16),
            ((far_rows, width), f32),
            ((far_rows, 128), f32),
            ((far_rows, width), bf16),
            ((far_rows, width), bf16),
            ((far_rows, width), bf16),
        ],
        cotan,
        part,
        live,
        pick,
        hot,
        node_sum,
        edge_first,
        edge_second,
        node_latent,
        node_cotan,
        node_first,
        node_second,
        *sx_far,
        last=(len(sizes) + 8,),
    )
    gpe_far, outs = list(outs[: len(far_plan)]), outs[len(far_plan) :]
    act_far, goe_far, normed_far, gathered, gpn, act_node, gon, gg, node_new = outs
    back_far = [passed_along(block, "band", -d) for block, d in zip(gpe_far, far_steps)]

    half = (width // 2, width)
    outs = call(
        functools.partial(back_kernel, (near, local_count)),
        [((local_rows + near_rows, width), bf16), ((local_rows, width), bf16)]
        + [((cap, width), bf16)] * len(near_steps),
        [((local_rows + near_rows, width), bf16)] * 2,
        cotan,
        live,
        pick,
        gg,
        edge_second,
        slope_local,
        normed_local,
        inv_local,
        slope_near,
        normed_near,
        inv_near,
    )
    goe_near, gpe_local = outs[:2]
    gpe_near = list(outs[2:])
    back_near = [passed_along(block, "band", -d) for block, d in zip(gpe_near, near_steps)]

    gpe = [gpe_local] + gpe_near + gpe_far
    sx_all = [sx_local] + sx_near + sx_far
    keep_edge, sent_edge, recv_sum = call(
        functools.partial(weight_kernel, (order, len(sx_all), len(gpe), 3, 2)),
        [((4, *half), f32), ((4, *half), bf16), ((nodes, width), bf16)],
        [((total, width), bf16)] * 5 + [((width, width), f32)],
        edges,
        hot,
        me,
        node_latent,
        *sx_all,
        *gpe,
        act_local,
        act_near,
        act_far,
        goe_near,
        goe_far,
        smem=(2,),
    )

    def edge_outputs(after):
        return call(
            functools.partial(edge_kernel, (order, 3, len(gpe))),
            [((sets, cap, width), bf16), ((sets, cap, width), bf16)],
            [((total, width), bf16)],
            edges,
            cotan,
            edge_first,
            live,
            normed_local,
            normed_near,
            normed_far,
            *gpe,
            after=after,
            last=(0, 1),
        )

    def node_output(after):
        (base,) = call(
            base_kernel,
            [((nodes, width), f32)],
            [],
            node_cotan,
            gpn,
            recv_sum,
            edge_first,
            node_first,
            after=after,
        )
        (grad_nodes,) = call(
            functools.partial(final_kernel, (near[:local_count], remote_plan)),
            [((nodes, width), bf16)],
            [((nodes, total), bf16), ((total, width), bf16)],
            me,
            base,
            edge_first,
            send_ids,
            ids,
            gpe_local,
            *back_near,
            *back_far,
            smem=(0,),
            last=(0,),
        )
        return grad_nodes

    def node_weights(after):
        return call(
            node_weight_kernel,
            [((3, *half), f32), ((3, *half), bf16)],
            [((width, width), f32)],
            me,
            node_latent,
            gathered,
            gpn,
            act_node,
            gon,
            smem=(0,),
            after=after,
        )

    first = 2
    node_blocks, node_shapes = ((0, 0), (0, 1), (1, 0)), [(2 * width, width), (width, width)]
    edge_blocks = ((0, 0), (0, 1), (0, 2), (1, 0))
    edge_shapes = [(3 * width, width), (width, width)]
    if bands == 16 and width % 512 == 0:
        def over(block, stride):
            return in_group(block, "band", stride, 2, 1)

        keep_node, sent_node = node_weights([])
        keep_node, came_node = add_stage(me, keep_node, [over(sent_node, 1)], 2, [])
        sent_edge = held_until(sent_edge, back_far + came_node)
        came_edge = [over(sent_edge, 1)]
        keep_node, came_node = add_stage(me, keep_node, came_node, 4, [sent_edge])
        keep_edge, came_edge = add_stage(me, keep_edge, came_edge, 2, [keep_node])
        edge_new, grad_edges = edge_outputs([keep_edge])
        keep_node, came_node = add_stage(me, keep_node, came_node, 8, [in_hbm(edge_new)])
        piece_node, _ = add_stage(me, keep_node, came_node, 1, [], 1, bf16)
        keep_edge, came_edge = add_stage(me, keep_edge, came_edge, 4, [piece_node])
        piece_node = gather_stage(me, piece_node, over(piece_node, 8), 8, [keep_edge])
        keep_edge, came_edge = add_stage(me, keep_edge, came_edge, 8, [piece_node])
        piece_node = gather_stage(me, piece_node, over(piece_node, 4), 4, [keep_edge])
        piece_edge, _ = add_stage(me, keep_edge, came_edge, 1, [piece_node], 1, bf16)
        some, rest = back_near[: len(back_near) // 2], back_near[len(back_near) // 2 :]
        piece_edge = gather_stage(me, piece_edge, over(piece_edge, 8), 8, some)
        grad_n1, grad_n2 = join_stage(
            me, piece_node, first, node_blocks, node_shapes, [], [piece_edge]
        )
        piece_edge = gather_stage(me, piece_edge, over(piece_edge, 4), 4, rest + [in_hbm(grad_n2)])
        grad_nodes = node_output([piece_edge])
        grad_e1, grad_e2 = join_stage(
            me, piece_edge, first, edge_blocks, edge_shapes, [in_hbm(grad_nodes)], []
        )
    else:
        whole = reduce_whole(*node_weights([]))
        grad_n1, grad_n2 = whole[:2].reshape(2 * width, width), whole[2]
        whole = reduce_whole(keep_edge, sent_edge)
        grad_e1, grad_e2 = whole[:3].reshape(3 * width, width), whole[3]
        edge_new, grad_edges = edge_outputs([])
        grad_nodes = node_output([])
    return (
        node_new,
        edge_new[None],
        grad_nodes,
        grad_edges[None],
        grad_e1,
        grad_e2,
        grad_n1,
        grad_n2,
    )


def solution(mesh):
    return jax.shard_map(
        local,
        mesh=mesh,
        in_specs=(
            P(("groups", "band"), None),
            P(("groups", "band"), None, None, None),
            P(("groups", "band"), None, None),
            P(("groups", "band"), None, None),
            P(("groups", "band"), None),
            P(),
            P(),
            P(),
            P(),
            P(("groups", "band"), None),
            P(("groups", "band"), None, None, None),
        ),
        out_specs=(
            P(("groups", "band"), None),
            P(("groups", "band"), None, None, None),
            P(("groups", "band"), None),
            P(("groups", "band"), None, None, None),
            P("groups", None),
            P("groups", None),
            P("groups", None),
            P("groups", None),
        ),
        check_vma=False,
    )
```

```python
import functools

import jax
import jax.numpy as jnp
from jax import lax
from jax.experimental import pallas as pl
from jax.experimental.pallas import tpu as pltpu
from jax.sharding import PartitionSpec as P

band_offsets = (0, 1, -1, 2, -2, 4, -4, 8, -8, 16, -16)
norm_eps = 1e-05
near_sets = 7
edge_work = 20_000_000_000
bf16 = jnp.bfloat16
f32 = jnp.float32
vmem_limit = 20 * 1024 * 1024


def passed_along(block, axis, distance):
    devices = range(lax.axis_size(axis))
    route = [((i - distance) % len(devices), i) for i in devices]
    return lax.ppermute(block, axis, route)


def layer_norm(inputs):
    average = jnp.mean(inputs, axis=-1, keepdims=True)
    centred = inputs - average
    inverse = lax.rsqrt(jnp.mean(centred * centred, axis=-1, keepdims=True) + norm_eps)
    return (centred * inverse, inverse)


def norm_back(normed, inverse, upstream):
    return inverse * (
        upstream
        - jnp.mean(upstream, axis=-1, keepdims=True)
        - normed * jnp.mean(upstream * normed, axis=-1, keepdims=True)
    )


def slope_of(inputs, squashed):
    return squashed * (1.0 + inputs * (1.0 - squashed))


def dot(left_side, right_side):
    return jnp.dot(left_side, right_side, preferred_element_type=f32)


def dot_rt(left_side, right_side):
    return lax.dot_general(
        left_side, right_side, (((1,), (1,)), ((), ())), preferred_element_type=f32
    )


def dot_lt(left_side, right_side):
    return lax.dot_general(
        left_side, right_side, (((0,), (0,)), ((), ())), preferred_element_type=f32
    )


def pick_table(ids, nodes):
    cap = ids.shape[1]
    down = jnp.transpose(jnp.broadcast_to(ids, (cap, cap)))
    parts = []
    for first in range(0, nodes, cap):
        wide = min(cap, nodes - first)
        lanes = lax.broadcasted_iota(jnp.int32, (cap, wide), 1) + first
        parts.append(jnp.where(down[:, :wide] == lanes, 1.0, 0.0).astype(bf16))
    return jnp.concatenate(parts, axis=1)


def sum_table(ids, nodes):
    down = lax.broadcasted_iota(jnp.int32, (nodes, ids.shape[1]), 0)
    return jnp.where(down == ids, 1.0, 0.0).astype(bf16)


def live_rows(count, cap):
    return (lax.broadcasted_iota(jnp.int32, (cap, 128), 0) < count).astype(f32)


def call(body, outs, scratch, *args, smem=(), after=(), last=(), work=1):
    spaces, given = [], []
    for i, arg in enumerate(args):
        spaces.append(pl.BlockSpec(memory_space=pltpu.SMEM if i in smem else pltpu.VMEM))
        given.append(arg if i in smem else pltpu.with_memory_space_constraint(arg, pltpu.VMEM))
    spaces += [pl.BlockSpec(memory_space=pl.ANY)] * len(after)

    def kernel(*refs):
        body(*refs[: len(args)], *refs[len(args) + len(after) :])

    return pl.pallas_call(
        kernel,
        out_shape=[
            (pltpu.HBM if i in last else pltpu.VMEM)(shape, kind)
            for i, (shape, kind) in enumerate(outs)
        ],
        in_specs=spaces,
        out_specs=[pl.BlockSpec(memory_space=pltpu.VMEM)] * len(outs),
        scratch_shapes=[pltpu.VMEM(shape, kind) for shape, kind in scratch],
        compiler_params=pltpu.CompilerParams(vmem_limit_bytes=vmem_limit),
        cost_estimate=pl.CostEstimate(flops=work, bytes_accessed=1, transcendentals=0),
    )(*given, *after)


def in_hbm(array):
    return pltpu.with_memory_space_constraint(array, pltpu.HBM)


def load_kernel(count, *refs):
    sems, refs = refs[-1], refs[1:]
    copies = [
        pltpu.make_async_copy(refs[i], refs[count + i], sems.at[i]) for i in range(count)
    ]
    for copy in copies:
        copy.start()
    for copy in copies:
        copy.wait()


def loaded(me, *args):
    count = len(args)
    return pl.pallas_call(
        functools.partial(load_kernel, count),
        out_shape=[pltpu.VMEM(arg.shape, arg.dtype) for arg in args],
        in_specs=[pl.BlockSpec(memory_space=pltpu.SMEM)]
        + [pl.BlockSpec(memory_space=pltpu.HBM)] * count,
        out_specs=[pl.BlockSpec(memory_space=pltpu.VMEM)] * count,
        scratch_shapes=[pltpu.SemaphoreType.DMA((count,))],
        compiler_params=pltpu.CompilerParams(vmem_limit_bytes=1024 * 1024),
        cost_estimate=pl.CostEstimate(flops=1, bytes_accessed=1, transcendentals=0),
    )(me, *[in_hbm(arg) for arg in args])


def ask_kernel(plan, me_ref, send_ref, out_ref):
    bands = out_ref.shape[0]
    out_ref[...] = jnp.zeros_like(out_ref)
    for step, sets in plan:
        ids = [send_ref[k] for k in sets]
        blank = out_ref.shape[2] - len(sets) * send_ref.shape[2]
        if blank:
            ids.append(jnp.zeros((1, blank), jnp.int32))
        out_ref[lax.rem(me_ref[0] + bands - step, bands)] = jnp.concatenate(ids, axis=1)


def asked(me_ref, id_ref, step, index, cap):
    row = lax.rem(me_ref[0] + step, id_ref.shape[0])
    return id_ref[row][:, index * cap : (index + 1) * cap]


def pick_kernel(plan, me_ref, node_ref, id_ref, *out_refs):
    nodes = node_ref.shape[0]
    for out_ref, (step, sets) in zip(out_refs, plan):
        cap = out_ref.shape[0] // len(sets)
        for i in range(len(sets)):
            hot = pick_table(asked(me_ref, id_ref, step, i, cap), nodes)
            out_ref[i * cap : (i + 1) * cap, :] = dot(hot, node_ref[...]).astype(bf16)


def forward_rows(pre, live, w2, act_ref, slope_ref, normed_ref, inv_ref, msg_ref, rows):
    squashed = jax.nn.sigmoid(pre)
    slope_ref[rows, :] = slope_of(pre, squashed)
    act = (pre * squashed).astype(bf16)
    act_ref[rows, :] = act
    normed, inverse = layer_norm(dot(act, w2))
    normed_ref[rows, :] = normed
    inv_ref[rows, :] = jnp.broadcast_to(inverse, (inverse.shape[0], 128))
    msg_ref[rows, :] = (live * normed).astype(bf16)


def backward_rows(cotan, picked, live, normed, inverse, slope, w2):
    upstream = live * (cotan.astype(f32) + picked)
    goe = norm_back(normed, inverse, upstream).astype(bf16)
    return goe, (dot_rt(goe, w2) * slope).astype(bf16)


def stack_into(out_ref, refs):
    first = 0
    for ref in refs:
        out_ref[first : first + ref.shape[0], :] = ref[...]
        first += ref.shape[0]


def start_kernel(plan, *refs):
    order, local_count = plan
    (
        edge_ref,
        recv_ref,
        send_ref,
        count_ref,
        w1_ref,
        w2_ref,
        node_ref,
        pick_ref,
        hot_ref,
        live_ref,
        part_ref,
        sx_ref,
        act_ref,
        slope_ref,
        normed_ref,
        inv_ref,
        sum_ref,
        x_ref,
        msg_ref,
    ) = refs
    nodes, width = node_ref.shape
    cap = recv_ref.shape[2]
    split = local_count * cap
    for i, k in enumerate(order):
        rows = slice(i * cap, (i + 1) * cap)
        x_ref[rows, :width] = edge_ref[k]
        pick_ref[rows, :] = pick_table(recv_ref[k], nodes)
        hot_ref[:, rows] = sum_table(recv_ref[k], nodes)
        live_ref[rows, :] = live_rows(count_ref[0, k], cap)
        if i < local_count:
            sx_ref[rows, :] = dot(pick_table(send_ref[k], nodes), node_ref[...]).astype(bf16)
    x_ref[:, width:] = dot(pick_ref[...], node_ref[...]).astype(bf16)
    part = dot(x_ref[:split, :width], w1_ref[:width, :])
    part += dot(x_ref[:split, width:], w1_ref[2 * width :, :])
    pre = part + dot(sx_ref[...], w1_ref[width : 2 * width, :])
    rows = slice(0, split)
    live = live_ref[rows, :1]
    forward_rows(pre, live, w2_ref[...], act_ref, slope_ref, normed_ref, inv_ref, msg_ref, rows)
    sum_ref[...] = dot(hot_ref[:, :split], msg_ref[...])
    part = dot(x_ref[split:, :width], w1_ref[:width, :])
    part_ref[...] = part + dot(x_ref[split:, width:], w1_ref[2 * width :, :])


def near_kernel(plan, *refs):
    first, count = plan
    part_ref, live_ref, hot_ref, sum_in_ref, w1_ref, w2_ref = refs[:6]
    sx_refs = refs[6 : 6 + count]
    act_ref, slope_ref, normed_ref, inv_ref, sum_ref, sx_ref, msg_ref = refs[6 + count :]
    total, width = sx_ref.shape
    stack_into(sx_ref, sx_refs)
    for j in range(2):
        rows = slice(j * total // 2, (j + 1) * total // 2)
        pre = part_ref[rows, :] + dot(sx_ref[rows, :], w1_ref[width : 2 * width, :])
        live = live_ref[first + rows.start : first + rows.stop, :1]
        forward_rows(pre, live, w2_ref[...], act_ref, slope_ref, normed_ref, inv_ref, msg_ref, rows)
    sum_ref[...] = sum_in_ref[...] + dot(hot_ref[:, first : first + total], msg_ref[...])


def far_kernel(plan, *refs):
    sets, sizes, first, part_first = plan
    count = len(sizes)
    (
        cotan_ref,
        part_ref,
        live_ref,
        pick_ref,
        hot_ref,
        sum_ref,
        w1_ref,
        w2_ref,
        node_ref,
        ncot_ref,
        n1_ref,
        n2_ref,
    ) = refs[:12]
    sx_refs, refs = refs[12 : 12 + count], refs[12 + count :]
    gpe_refs, refs = refs[:count], refs[count:]
    (
        act_ref,
        goe_ref,
        normed_ref,
        gathered_ref,
        gpn_ref,
        act_node_ref,
        gon_ref,
        gg_ref,
        node_new_ref,
        sx_ref,
        slope_ref,
        inv_ref,
        msg_ref,
        cot_ref,
        gpe_ref,
    ) = refs
    total, width = sx_ref.shape
    cap = cotan_ref.shape[1]
    stack_into(sx_ref, sx_refs)
    for i, k in enumerate(sets):
        cot_ref[i * cap : (i + 1) * cap, :] = cotan_ref[k]
    halves = [slice(j * total // 2, (j + 1) * total // 2) for j in range(2)]
    for rows in halves:
        pre = part_ref[part_first + rows.start : part_first + rows.stop, :]
        pre = pre + dot(sx_ref[rows, :], w1_ref[width : 2 * width, :])
        live = live_ref[first + rows.start : first + rows.stop, :1]
        forward_rows(pre, live, w2_ref[...], act_ref, slope_ref, normed_ref, inv_ref, msg_ref, rows)
    gathered = sum_ref[...] + dot(hot_ref[:, first : first + total], msg_ref[...])
    gathered = gathered.astype(bf16)
    gathered_ref[...] = gathered

    pre = dot(node_ref[...], n1_ref[:width, :]) + dot(gathered, n1_ref[width:, :])
    squashed = jax.nn.sigmoid(pre)
    act_node = (pre * squashed).astype(bf16)
    act_node_ref[...] = act_node
    normed, inverse = layer_norm(dot(act_node, n2_ref[...]))
    node_new_ref[...] = (node_ref[...].astype(f32) + normed).astype(bf16)
    gon = norm_back(normed, inverse, ncot_ref[...].astype(f32)).astype(bf16)
    gon_ref[...] = gon
    gpn = (dot_rt(gon, n2_ref[...]) * slope_of(pre, squashed)).astype(bf16)
    gpn_ref[...] = gpn
    gg_ref[...] = dot_rt(gpn, n1_ref[width:, :]).astype(bf16)

    for rows in halves:
        whole = slice(first + rows.start, first + rows.stop)
        goe, gpe = backward_rows(
            cot_ref[rows, :],
            dot(pick_ref[whole, :], gg_ref[...]),
            live_ref[whole, :1],
            normed_ref[rows, :],
            inv_ref[rows, :1],
            slope_ref[rows, :],
            w2_ref[...],
        )
        goe_ref[rows, :] = goe
        gpe_ref[rows, :] = gpe
    at = 0
    for out_ref, size in zip(gpe_refs, sizes):
        out_ref[...] = gpe_ref[at : at + size, :]
        at += size


def back_kernel(plan, *refs):
    sets, local_count = plan
    cotan_ref, live_ref, pick_ref, gg_ref, w2_ref = refs[:5]
    groups = (refs[5:8], refs[8:11])
    goe_ref, local_ref = refs[11:13]
    gpe_refs, (cot_ref, gpe_ref) = refs[13:-2], refs[-2:]
    cap = cotan_ref.shape[1]
    for i, k in enumerate(sets):
        cot_ref[i * cap : (i + 1) * cap, :] = cotan_ref[k]
    first = 0
    for slope_ref, normed_ref, inv_ref in groups:
        rows = slice(first, first + slope_ref.shape[0])
        goe, gpe = backward_rows(
            cot_ref[rows, :],
            dot(pick_ref[rows, :], gg_ref[...]),
            live_ref[rows, :1],
            normed_ref[...],
            inv_ref[:, :1],
            slope_ref[...],
            w2_ref[...],
        )
        goe_ref[rows, :] = goe
        gpe_ref[rows, :] = gpe
        first = rows.stop
    local_ref[...] = gpe_ref[: local_count * cap, :]
    for j, out_ref in enumerate(gpe_refs):
        i = local_count + j
        out_ref[...] = gpe_ref[i * cap : (i + 1) * cap, :]


def node_weight_kernel(me_ref, node_ref, gathered_ref, gpn_ref, act_node_ref, gon_ref, keep_ref, sent_ref, block_ref):
    put = functools.partial(put_block, me_ref, block_ref, keep_ref, sent_ref)
    put(0, node_ref[...], gpn_ref[...])
    put(1, gathered_ref[...], gpn_ref[...])
    put(2, act_node_ref[...], gon_ref[...])


def put_block(me_ref, block_ref, keep_ref, sent_ref, index, left_side, right_side):
    core = lax.rem(me_ref[0], 2)
    half = block_ref.shape[0] // 2
    block_ref[...] = dot_lt(left_side, right_side)
    keep_ref[index] = block_ref[pl.ds(pl.multiple_of(core * half, half), half), :]
    other = block_ref[pl.ds(pl.multiple_of((1 - core) * half, half), half), :]
    sent_ref[index] = other.astype(bf16)


def weight_kernel(plan, *refs):
    order, sx_count, gpe_count, act_count, goe_count = plan
    edge_ref, hot_ref, me_ref, node_ref = refs[:4]
    refs = refs[4:]
    sx_refs, refs = refs[:sx_count], refs[sx_count:]
    gpe_refs, refs = refs[:gpe_count], refs[gpe_count:]
    act_refs, refs = refs[:act_count], refs[act_count:]
    goe_refs, refs = refs[:goe_count], refs[goe_count:]
    keep_ref, sent_ref, rsum_ref, x_ref, sx_ref, gpe_ref, act_ref, goe_ref, block_ref = refs
    cap = edge_ref.shape[1]
    for i, k in enumerate(order):
        x_ref[i * cap : (i + 1) * cap, :] = edge_ref[k]
    stack_into(sx_ref, sx_refs)
    stack_into(gpe_ref, gpe_refs)
    stack_into(act_ref, act_refs)
    stack_into(goe_ref, goe_refs)
    recv_sum = dot(hot_ref[...], gpe_ref[...]).astype(bf16)
    rsum_ref[...] = recv_sum
    put = functools.partial(put_block, me_ref, block_ref, keep_ref, sent_ref)
    put(0, x_ref[...], gpe_ref[...])
    put(1, sx_ref[...], gpe_ref[...])
    put(2, node_ref[...], recv_sum)
    put(3, act_ref[...], goe_ref[...])


def base_kernel(ncot_ref, gpn_ref, rsum_ref, w1_ref, n1_ref, base_ref):
    width = w1_ref.shape[1]
    base_ref[...] = (
        ncot_ref[...].astype(f32)
        + dot_rt(gpn_ref[...], n1_ref[:width, :])
        + dot_rt(rsum_ref[...], w1_ref[2 * width :, :])
    )


def edge_kernel(plan, *refs):
    order, normed_count, gpe_count = plan
    edge_ref, cotan_ref, w1_ref, live_ref = refs[:4]
    refs = refs[4:]
    normed_refs, refs = refs[:normed_count], refs[normed_count:]
    gpe_refs, refs = refs[:gpe_count], refs[gpe_count:]
    new_ref, gedge_ref, gpe_ref = refs
    width = w1_ref.shape[1]
    cap = edge_ref.shape[1]
    stack_into(gpe_ref, gpe_refs)
    places = [(ref, at) for ref in normed_refs for at in range(0, ref.shape[0], cap)]
    for i, (k, (normed_ref, at)) in enumerate(zip(order, places)):
        rows = slice(i * cap, (i + 1) * cap)
        grad = cotan_ref[k].astype(f32) + dot_rt(gpe_ref[rows, :], w1_ref[:width, :])
        gedge_ref[k] = grad.astype(bf16)
        message = live_ref[rows, :1] * normed_ref[at : at + cap, :]
        new_ref[k] = (edge_ref[k].astype(f32) + message).astype(bf16)


def final_kernel(plan, *refs):
    local_sets, remote = plan
    me_ref, base_ref, w1_ref, send_ref, id_ref = refs[:5]
    row_refs, (out_ref, hot_ref, rows_ref) = refs[5:-3], refs[-3:]
    nodes, width = base_ref.shape
    cap = send_ref.shape[2]
    ids = [send_ref[k] for k in local_sets]
    ids += [
        asked(me_ref, id_ref, step, i, cap) for step, sets in remote for i in range(len(sets))
    ]
    for i, one in enumerate(ids):
        hot_ref[:, i * cap : (i + 1) * cap] = sum_table(one, nodes)
    stack_into(rows_ref, row_refs)
    send_sum = dot(hot_ref[...], rows_ref[...]).astype(bf16)
    grad = base_ref[...] + dot_rt(send_sum, w1_ref[width : 2 * width, :])
    out_ref[...] = grad.astype(bf16)


def place(me_ref, stride, members):
    return lax.rem(lax.div(me_ref[0], stride), members)


def add_kernel(plan, *refs):
    came, stride, members = plan
    me_ref, keep_ref = refs[:2]
    arr_refs, out_refs = refs[2 : 2 + came], refs[2 + came :]
    size = keep_ref.shape[1] // members
    here = place(me_ref, stride, members)
    for j, out_ref in enumerate(out_refs):
        at = lax.rem(here + j, members) * size
        rows = pl.ds(pl.multiple_of(at, size), size)
        piece = keep_ref[:, rows, :]
        for arr_ref in arr_refs:
            piece += arr_ref[:, rows, :].astype(f32)
        out_ref[...] = piece.astype(out_ref.dtype)


def gather_kernel(plan, *refs):
    stride, members = plan
    me_ref, piece_refs, out_ref = refs[0], refs[1:-1], refs[-1]
    size = piece_refs[0].shape[1]
    here = place(me_ref, stride, members)
    for j, piece_ref in enumerate(piece_refs):
        at = lax.rem(here + members - j, members) * size
        out_ref[:, pl.ds(pl.multiple_of(at, size), size), :] = piece_ref[...]


def join_kernel(plan, *refs):
    members, blocks = plan
    me_ref = refs[0]
    piece_refs, other_refs = refs[1 : 1 + members], refs[1 + members : 1 + 2 * members]
    out_refs = refs[1 + 2 * members :]
    size = piece_refs[0].shape[1]
    core = lax.rem(me_ref[0], 2)
    here = place(me_ref, 2, members)
    for index, (which, block) in enumerate(blocks):
        first = 2 * block * members * size
        for side, side_refs in ((core, piece_refs), (1 - core, other_refs)):
            for j, piece_ref in enumerate(side_refs):
                at = first + (side * members + lax.rem(here + members - j, members)) * size
                rows = pl.ds(pl.multiple_of(at, size), size)
                out_refs[which][rows, :] = piece_ref[index]


def in_group(block, axis, stride, members, step):
    route = []
    for i in range(lax.axis_size(axis)):
        at = (i // stride) % members
        route.append((i, i + ((at + step) % members - at) * stride))
    return lax.ppermute(block, axis, route)


def add_stage(me, keep, arrived, stride, after, members=2, kind=f32):
    count, rows, width = keep.shape
    shape = (count, rows // members, width)
    outs = call(
        functools.partial(add_kernel, (len(arrived), stride, members)),
        [(shape, kind)] + [(shape, bf16)] * (members - 1),
        [],
        me,
        keep,
        *arrived,
        smem=(0,),
        after=after,
    )
    return outs[0], [in_group(out, "band", stride, members, j + 1) for j, out in enumerate(outs[1:])]


def held_until(array, after):
    return pl.pallas_call(
        lambda *refs: None,
        out_shape=pltpu.VMEM(array.shape, array.dtype),
        in_specs=[pl.BlockSpec(memory_space=pltpu.VMEM)]
        + [pl.BlockSpec(memory_space=pl.ANY)] * len(after),
        out_specs=pl.BlockSpec(memory_space=pltpu.VMEM),
        input_output_aliases={0: 0},
        compiler_params=pltpu.CompilerParams(vmem_limit_bytes=1024 * 1024),
        cost_estimate=pl.CostEstimate(flops=1, bytes_accessed=1, transcendentals=0),
    )(pltpu.with_memory_space_constraint(array, pltpu.VMEM), *after)


def gather_stage(me, piece, came, stride, after):
    count, rows, width = piece.shape
    members, pieces = 2, [piece, came]
    (mine,) = call(
        functools.partial(gather_kernel, (stride, members)),
        [((count, rows * members, width), bf16)],
        [],
        me,
        *pieces,
        smem=(0,),
        after=after,
    )
    return mine


def join_stage(me, mine, members, blocks, shapes, swap_after, after):
    pieces = [in_group(mine, "band", 2, members, j) for j in range(1, members)]
    pieces = [mine] + [held_until(piece, swap_after) if swap_after else piece for piece in pieces]
    others = [in_group(one, "band", 1, 2, 1) for one in pieces]
    return call(
        functools.partial(join_kernel, (members, blocks)),
        [(shape, bf16) for shape in shapes],
        [],
        me,
        *pieces,
        *others,
        smem=(0,),
        after=after,
        last=range(len(shapes)),
    )


def reduce_whole(keep, sent):
    bands = lax.axis_size("band")
    chips = [[i for i in range(bands) if i % 2 == c] for c in range(2)]
    total = keep + in_group(sent, "band", 1, 2, 1).astype(f32)
    total = lax.psum(total.astype(bf16), "band", axis_index_groups=chips)
    other = in_group(total, "band", 1, 2, 1)
    core = lax.axis_index("band") % 2
    low, high = jnp.where(core == 0, total, other), jnp.where(core == 0, other, total)
    return jnp.concatenate([low, high], axis=1)


def local(
    node_latent,
    edge_latent,
    recv_slot,
    send_slot,
    edge_count,
    edge_first,
    edge_second,
    node_first,
    node_second,
    node_cotan,
    edge_cotan,
):
    bands = lax.axis_size("band")
    nodes, width = node_latent.shape
    sets, cap = edge_latent.shape[1:3]
    send_ids = send_slot.reshape(sets, 1, cap)
    me = lax.axis_index("band").astype(jnp.int32).reshape(1)

    def step_of(k):
        return band_offsets[k] % bands

    def reach(k):
        return min(step_of(k), bands - step_of(k))

    ordered = sorted(range(sets), key=lambda k: (reach(k), step_of(k)))
    near, far = tuple(ordered[:near_sets]), tuple(ordered[near_sets:])
    local_count = sum(step_of(k) == 0 for k in near)
    near_steps = [step_of(k) for k in near[local_count:]]
    far_steps = list(dict.fromkeys(step_of(k) for k in far))
    steps = near_steps + far_steps
    near_plan = tuple((k,) for k in near[local_count:])
    far_plan = tuple(tuple(k for k in far if step_of(k) == d) for d in far_steps)
    far = sum(far_plan, ())

    order = near + far

    (
        node_latent,
        send_ids,
        recv_ids,
        edges,
        edge_first,
        edge_second,
        node_first,
        node_second,
        node_cotan,
        cotan,
    ) = loaded(
        me,
        node_latent,
        send_ids,
        recv_slot.reshape(sets, 1, cap),
        edge_latent[0],
        edge_first,
        edge_second,
        node_first,
        node_second,
        node_cotan,
        edge_cotan[0],
    )
    remote_plan = tuple(zip(steps, near_plan + far_plan))
    widest = max(len(piece) for piece in near_plan + far_plan)
    (ids,) = call(
        functools.partial(ask_kernel, remote_plan),
        [((bands, 1, widest * cap), jnp.int32)],
        [],
        me,
        send_ids,
        smem=(0,),
    )
    ids = lax.all_to_all(ids, "band", 0, 0, tiled=True)
    picked = call(
        functools.partial(pick_kernel, remote_plan),
        [((len(piece) * cap, width), bf16) for piece in near_plan + far_plan],
        [],
        me,
        node_latent,
        ids,
        smem=(0,),
    )
    sx = [passed_along(block, "band", d) for block, d in zip(picked, steps)]
    sx_near, sx_far = sx[: len(near_plan)], sx[len(near_plan) :]

    local_rows, near_rows, far_rows = local_count * cap, len(near_plan) * cap, len(far) * cap
    total = sets * cap

    def forward_outs(rows):
        return [
            ((rows, width), bf16),
            ((rows, width), f32),
            ((rows, width), f32),
            ((rows, 128), f32),
            ((nodes, width), f32),
        ]

    pick, hot, live, part, sx_local, act_local, slope_local, normed_local, inv_local, node_sum = call(
        functools.partial(start_kernel, (order, local_count)),
        [
            ((total, nodes), bf16),
            ((nodes, total), bf16),
            ((total, 128), f32),
            ((near_rows + far_rows, width), f32),
            ((local_rows, width), bf16),
        ]
        + forward_outs(local_rows),
        [((total, 2 * width), bf16), ((local_rows, width), bf16)],
        edges,
        recv_ids,
        send_ids,
        in_hbm(edge_count),
        edge_first,
        edge_second,
        node_latent,
        smem=(3,),
        after=[picked[0]],
    )
    act_near, slope_near, normed_near, inv_near, node_sum = call(
        functools.partial(near_kernel, (local_rows, len(near_plan))),
        forward_outs(near_rows),
        [((near_rows, width), bf16), ((near_rows, width), bf16)],
        part,
        live,
        hot,
        node_sum,
        edge_first,
        edge_second,
        *sx_near,
    )
    sizes = [len(piece) * cap for piece in far_plan]
    outs = call(
        functools.partial(far_kernel, (far, sizes, local_rows + near_rows, near_rows)),
        [((size, width), bf16) for size in sizes]
        + [((far_rows, width), bf16), ((far_rows, width), bf16), ((far_rows, width), f32)]
        + [((nodes, width), bf16)] * 6,
        [
            ((far_rows, width), bf16),
            ((far_rows, width), f32),
            ((far_rows, 128), f32),
            ((far_rows, width), bf16),
            ((far_rows, width), bf16),
            ((far_rows, width), bf16),
        ],
        cotan,
        part,
        live,
        pick,
        hot,
        node_sum,
        edge_first,
        edge_second,
        node_latent,
        node_cotan,
        node_first,
        node_second,
        *sx_far,
        last=(len(sizes) + 8,),
    )
    gpe_far, outs = list(outs[: len(far_plan)]), outs[len(far_plan) :]
    act_far, goe_far, normed_far, gathered, gpn, act_node, gon, gg, node_new = outs
    back_far = [passed_along(block, "band", -d) for block, d in zip(gpe_far, far_steps)]

    half = (width // 2, width)
    outs = call(
        functools.partial(back_kernel, (near, local_count)),
        [((local_rows + near_rows, width), bf16), ((local_rows, width), bf16)]
        + [((cap, width), bf16)] * len(near_steps),
        [((local_rows + near_rows, width), bf16)] * 2,
        cotan,
        live,
        pick,
        gg,
        edge_second,
        slope_local,
        normed_local,
        inv_local,
        slope_near,
        normed_near,
        inv_near,
    )
    goe_near, gpe_local = outs[:2]
    gpe_near = list(outs[2:])
    back_near = [passed_along(block, "band", -d) for block, d in zip(gpe_near, near_steps)]

    gpe = [gpe_local] + gpe_near + gpe_far
    sx_all = [sx_local] + sx_near + sx_far
    keep_edge, sent_edge, recv_sum = call(
        functools.partial(weight_kernel, (order, len(sx_all), len(gpe), 3, 2)),
        [((4, *half), f32), ((4, *half), bf16), ((nodes, width), bf16)],
        [((total, width), bf16)] * 5 + [((width, width), f32)],
        edges,
        hot,
        me,
        node_latent,
        *sx_all,
        *gpe,
        act_local,
        act_near,
        act_far,
        goe_near,
        goe_far,
        smem=(2,),
    )

    def edge_outputs(after):
        return call(
            functools.partial(edge_kernel, (order, 3, len(gpe))),
            [((sets, cap, width), bf16), ((sets, cap, width), bf16)],
            [((total, width), bf16)],
            edges,
            cotan,
            edge_first,
            live,
            normed_local,
            normed_near,
            normed_far,
            *gpe,
            after=after,
            last=(0, 1),
            work=edge_work,
        )

    def node_output(after):
        (base,) = call(
            base_kernel,
            [((nodes, width), f32)],
            [],
            node_cotan,
            gpn,
            recv_sum,
            edge_first,
            node_first,
            after=after,
        )
        (grad_nodes,) = call(
            functools.partial(final_kernel, (near[:local_count], remote_plan)),
            [((nodes, width), bf16)],
            [((nodes, total), bf16), ((total, width), bf16)],
            me,
            base,
            edge_first,
            send_ids,
            ids,
            gpe_local,
            *back_near,
            *back_far,
            smem=(0,),
            last=(0,),
        )
        return grad_nodes

    def node_weights(after):
        return call(
            node_weight_kernel,
            [((3, *half), f32), ((3, *half), bf16)],
            [((width, width), f32)],
            me,
            node_latent,
            gathered,
            gpn,
            act_node,
            gon,
            smem=(0,),
            after=after,
        )

    first = 2
    node_blocks, node_shapes = ((0, 0), (0, 1), (1, 0)), [(2 * width, width), (width, width)]
    edge_blocks = ((0, 0), (0, 1), (0, 2), (1, 0))
    edge_shapes = [(3 * width, width), (width, width)]
    if bands == 16 and width % 512 == 0:
        def over(block, stride):
            return in_group(block, "band", stride, 2, 1)

        keep_node, sent_node = node_weights([])
        keep_node, came_node = add_stage(me, keep_node, [over(sent_node, 1)], 2, [])
        sent_edge = held_until(sent_edge, back_far + [keep_node])
        came_edge = [over(sent_edge, 1)]
        edge_new, grad_edges = edge_outputs([sent_edge])
        keep_node, came_node = add_stage(me, keep_node, came_node, 4, [in_hbm(edge_new)])
        keep_edge, came_edge = add_stage(me, keep_edge, came_edge, 2, [keep_node])
        keep_node, came_node = add_stage(me, keep_node, came_node, 8, [keep_edge])
        piece_node, _ = add_stage(me, keep_node, came_node, 1, [], 1, bf16)
        keep_edge, came_edge = add_stage(me, keep_edge, came_edge, 4, [piece_node])
        piece_node = gather_stage(me, piece_node, over(piece_node, 8), 8, [keep_edge])
        keep_edge, came_edge = add_stage(me, keep_edge, came_edge, 8, [piece_node])
        piece_edge, _ = add_stage(me, keep_edge, came_edge, 1, back_near, 1, bf16)
        piece_node = gather_stage(me, piece_node, over(piece_node, 4), 4, [piece_edge])
        grad_nodes = node_output([piece_node])
        piece_edge = gather_stage(me, piece_edge, over(piece_edge, 8), 8, [in_hbm(grad_nodes)])
        grad_n1, grad_n2 = join_stage(
            me, piece_node, first, node_blocks, node_shapes, [], [piece_edge]
        )
        piece_edge = gather_stage(me, piece_edge, over(piece_edge, 4), 4, [in_hbm(grad_n2)])
        grad_e1, grad_e2 = join_stage(me, piece_edge, first, edge_blocks, edge_shapes, [], [])
    else:
        whole = reduce_whole(*node_weights([]))
        grad_n1, grad_n2 = whole[:2].reshape(2 * width, width), whole[2]
        whole = reduce_whole(keep_edge, sent_edge)
        grad_e1, grad_e2 = whole[:3].reshape(3 * width, width), whole[3]
        edge_new, grad_edges = edge_outputs([])
        grad_nodes = node_output([])
    return (
        node_new,
        edge_new[None],
        grad_nodes,
        grad_edges[None],
        grad_e1,
        grad_e2,
        grad_n1,
        grad_n2,
    )


def solution(mesh):
    return jax.shard_map(
        local,
        mesh=mesh,
        in_specs=(
            P(("groups", "band"), None),
            P(("groups", "band"), None, None, None),
            P(("groups", "band"), None, None),
            P(("groups", "band"), None, None),
            P(("groups", "band"), None),
            P(),
            P(),
            P(),
            P(),
            P(("groups", "band"), None),
            P(("groups", "band"), None, None, None),
        ),
        out_specs=(
            P(("groups", "band"), None),
            P(("groups", "band"), None, None, None),
            P(("groups", "band"), None),
            P(("groups", "band"), None, None, None),
            P("groups", None),
            P("groups", None),
            P("groups", None),
            P("groups", None),
        ),
        check_vma=False,
    )
```

```python
import functools

import jax
import jax.numpy as jnp
from jax import lax
from jax.experimental import pallas as pl
from jax.experimental.pallas import tpu as pltpu
from jax.sharding import PartitionSpec as P

band_offsets = (0, 1, -1, 2, -2, 4, -4, 8, -8, 16, -16)
norm_eps = 1e-05
near_sets = 7
edge_work = 20_000_000_000
bf16 = jnp.bfloat16
f32 = jnp.float32
vmem_limit = 20 * 1024 * 1024


def passed_along(block, axis, distance):
    devices = range(lax.axis_size(axis))
    route = [((i - distance) % len(devices), i) for i in devices]
    return lax.ppermute(block, axis, route)


def layer_norm(inputs):
    average = jnp.mean(inputs, axis=-1, keepdims=True)
    centred = inputs - average
    inverse = lax.rsqrt(jnp.mean(centred * centred, axis=-1, keepdims=True) + norm_eps)
    return (centred * inverse, inverse)


def norm_back(normed, inverse, upstream):
    return inverse * (
        upstream
        - jnp.mean(upstream, axis=-1, keepdims=True)
        - normed * jnp.mean(upstream * normed, axis=-1, keepdims=True)
    )


def slope_of(inputs, squashed):
    return squashed * (1.0 + inputs * (1.0 - squashed))


def dot(left_side, right_side):
    return jnp.dot(left_side, right_side, preferred_element_type=f32)


def dot_rt(left_side, right_side):
    return lax.dot_general(
        left_side, right_side, (((1,), (1,)), ((), ())), preferred_element_type=f32
    )


def dot_lt(left_side, right_side):
    return lax.dot_general(
        left_side, right_side, (((0,), (0,)), ((), ())), preferred_element_type=f32
    )


def pick_table(ids, nodes):
    cap = ids.shape[1]
    down = jnp.transpose(jnp.broadcast_to(ids, (cap, cap)))
    parts = []
    for first in range(0, nodes, cap):
        wide = min(cap, nodes - first)
        lanes = lax.broadcasted_iota(jnp.int32, (cap, wide), 1) + first
        parts.append(jnp.where(down[:, :wide] == lanes, 1.0, 0.0).astype(bf16))
    return jnp.concatenate(parts, axis=1)


def sum_table(ids, nodes):
    down = lax.broadcasted_iota(jnp.int32, (nodes, ids.shape[1]), 0)
    return jnp.where(down == ids, 1.0, 0.0).astype(bf16)


def live_rows(count, cap):
    return (lax.broadcasted_iota(jnp.int32, (cap, 128), 0) < count).astype(f32)


def call(body, outs, scratch, *args, smem=(), after=(), last=(), work=1):
    spaces, given = [], []
    for i, arg in enumerate(args):
        spaces.append(pl.BlockSpec(memory_space=pltpu.SMEM if i in smem else pltpu.VMEM))
        given.append(arg if i in smem else pltpu.with_memory_space_constraint(arg, pltpu.VMEM))
    spaces += [pl.BlockSpec(memory_space=pl.ANY)] * len(after)

    def kernel(*refs):
        body(*refs[: len(args)], *refs[len(args) + len(after) :])

    return pl.pallas_call(
        kernel,
        out_shape=[
            (pltpu.HBM if i in last else pltpu.VMEM)(shape, kind)
            for i, (shape, kind) in enumerate(outs)
        ],
        in_specs=spaces,
        out_specs=[pl.BlockSpec(memory_space=pltpu.VMEM)] * len(outs),
        scratch_shapes=[pltpu.VMEM(shape, kind) for shape, kind in scratch],
        compiler_params=pltpu.CompilerParams(vmem_limit_bytes=vmem_limit),
        cost_estimate=pl.CostEstimate(flops=work, bytes_accessed=1, transcendentals=0),
    )(*given, *after)


def in_hbm(array):
    return pltpu.with_memory_space_constraint(array, pltpu.HBM)


def load_kernel(count, *refs):
    sems, refs = refs[-1], refs[1:]
    copies = [
        pltpu.make_async_copy(refs[i], refs[count + i], sems.at[i]) for i in range(count)
    ]
    for copy in copies:
        copy.start()
    for copy in copies:
        copy.wait()


def loaded(me, *args):
    count = len(args)
    return pl.pallas_call(
        functools.partial(load_kernel, count),
        out_shape=[pltpu.VMEM(arg.shape, arg.dtype) for arg in args],
        in_specs=[pl.BlockSpec(memory_space=pltpu.SMEM)]
        + [pl.BlockSpec(memory_space=pltpu.HBM)] * count,
        out_specs=[pl.BlockSpec(memory_space=pltpu.VMEM)] * count,
        scratch_shapes=[pltpu.SemaphoreType.DMA((count,))],
        compiler_params=pltpu.CompilerParams(vmem_limit_bytes=1024 * 1024),
        cost_estimate=pl.CostEstimate(flops=1, bytes_accessed=1, transcendentals=0),
    )(me, *[in_hbm(arg) for arg in args])


def ask_kernel(plan, me_ref, send_ref, out_ref):
    bands = out_ref.shape[0]
    out_ref[...] = jnp.zeros_like(out_ref)
    for step, sets in plan:
        ids = [send_ref[k] for k in sets]
        blank = out_ref.shape[2] - len(sets) * send_ref.shape[2]
        if blank:
            ids.append(jnp.zeros((1, blank), jnp.int32))
        out_ref[lax.rem(me_ref[0] + bands - step, bands)] = jnp.concatenate(ids, axis=1)


def asked(me_ref, id_ref, step, index, cap):
    row = lax.rem(me_ref[0] + step, id_ref.shape[0])
    return id_ref[row][:, index * cap : (index + 1) * cap]


def pick_kernel(plan, me_ref, node_ref, id_ref, *out_refs):
    nodes = node_ref.shape[0]
    for out_ref, (step, sets) in zip(out_refs, plan):
        cap = out_ref.shape[0] // len(sets)
        for i in range(len(sets)):
            hot = pick_table(asked(me_ref, id_ref, step, i, cap), nodes)
            out_ref[i * cap : (i + 1) * cap, :] = dot(hot, node_ref[...]).astype(bf16)


def forward_rows(pre, live, w2, act_ref, slope_ref, normed_ref, inv_ref, msg_ref, rows):
    squashed = jax.nn.sigmoid(pre)
    slope_ref[rows, :] = slope_of(pre, squashed)
    act = (pre * squashed).astype(bf16)
    act_ref[rows, :] = act
    normed, inverse = layer_norm(dot(act, w2))
    normed_ref[rows, :] = normed
    inv_ref[rows, :] = jnp.broadcast_to(inverse, (inverse.shape[0], 128))
    msg_ref[rows, :] = (live * normed).astype(bf16)


def backward_rows(cotan, picked, live, normed, inverse, slope, w2):
    upstream = live * (cotan.astype(f32) + picked)
    goe = norm_back(normed, inverse, upstream).astype(bf16)
    return goe, (dot_rt(goe, w2) * slope).astype(bf16)


def stack_into(out_ref, refs):
    first = 0
    for ref in refs:
        out_ref[first : first + ref.shape[0], :] = ref[...]
        first += ref.shape[0]


def start_kernel(plan, *refs):
    order, local_count = plan
    (
        edge_ref,
        recv_ref,
        send_ref,
        count_ref,
        w1_ref,
        w2_ref,
        node_ref,
        pick_ref,
        hot_ref,
        live_ref,
        part_ref,
        sx_ref,
        act_ref,
        slope_ref,
        normed_ref,
        inv_ref,
        sum_ref,
        x_ref,
        msg_ref,
    ) = refs
    nodes, width = node_ref.shape
    cap = recv_ref.shape[2]
    split = local_count * cap
    for i, k in enumerate(order):
        rows = slice(i * cap, (i + 1) * cap)
        x_ref[rows, :width] = edge_ref[k]
        pick_ref[rows, :] = pick_table(recv_ref[k], nodes)
        hot_ref[:, rows] = sum_table(recv_ref[k], nodes)
        live_ref[rows, :] = live_rows(count_ref[0, k], cap)
        if i < local_count:
            sx_ref[rows, :] = dot(pick_table(send_ref[k], nodes), node_ref[...]).astype(bf16)
    x_ref[:, width:] = dot(pick_ref[...], node_ref[...]).astype(bf16)
    part = dot(x_ref[:split, :width], w1_ref[:width, :])
    part += dot(x_ref[:split, width:], w1_ref[2 * width :, :])
    pre = part + dot(sx_ref[...], w1_ref[width : 2 * width, :])
    rows = slice(0, split)
    live = live_ref[rows, :1]
    forward_rows(pre, live, w2_ref[...], act_ref, slope_ref, normed_ref, inv_ref, msg_ref, rows)
    sum_ref[...] = dot(hot_ref[:, :split], msg_ref[...])
    part = dot(x_ref[split:, :width], w1_ref[:width, :])
    part_ref[...] = part + dot(x_ref[split:, width:], w1_ref[2 * width :, :])


def near_kernel(plan, *refs):
    first, count = plan
    part_ref, live_ref, hot_ref, sum_in_ref, w1_ref, w2_ref = refs[:6]
    sx_refs = refs[6 : 6 + count]
    act_ref, slope_ref, normed_ref, inv_ref, sum_ref, sx_ref, msg_ref = refs[6 + count :]
    total, width = sx_ref.shape
    stack_into(sx_ref, sx_refs)
    for j in range(2):
        rows = slice(j * total // 2, (j + 1) * total // 2)
        pre = part_ref[rows, :] + dot(sx_ref[rows, :], w1_ref[width : 2 * width, :])
        live = live_ref[first + rows.start : first + rows.stop, :1]
        forward_rows(pre, live, w2_ref[...], act_ref, slope_ref, normed_ref, inv_ref, msg_ref, rows)
    sum_ref[...] = sum_in_ref[...] + dot(hot_ref[:, first : first + total], msg_ref[...])


def far_kernel(plan, *refs):
    sets, sizes, first, part_first = plan
    count = len(sizes)
    (
        cotan_ref,
        part_ref,
        live_ref,
        pick_ref,
        hot_ref,
        sum_ref,
        w1_ref,
        w2_ref,
        node_ref,
        ncot_ref,
        n1_ref,
        n2_ref,
    ) = refs[:12]
    sx_refs, refs = refs[12 : 12 + count], refs[12 + count :]
    gpe_refs, refs = refs[:count], refs[count:]
    (
        act_ref,
        goe_ref,
        normed_ref,
        gathered_ref,
        gpn_ref,
        act_node_ref,
        gon_ref,
        gg_ref,
        node_new_ref,
        sx_ref,
        slope_ref,
        inv_ref,
        msg_ref,
        cot_ref,
        gpe_ref,
    ) = refs
    total, width = sx_ref.shape
    cap = cotan_ref.shape[1]
    stack_into(sx_ref, sx_refs)
    for i, k in enumerate(sets):
        cot_ref[i * cap : (i + 1) * cap, :] = cotan_ref[k]
    halves = [slice(j * total // 2, (j + 1) * total // 2) for j in range(2)]
    for rows in halves:
        pre = part_ref[part_first + rows.start : part_first + rows.stop, :]
        pre = pre + dot(sx_ref[rows, :], w1_ref[width : 2 * width, :])
        live = live_ref[first + rows.start : first + rows.stop, :1]
        forward_rows(pre, live, w2_ref[...], act_ref, slope_ref, normed_ref, inv_ref, msg_ref, rows)
    gathered = sum_ref[...] + dot(hot_ref[:, first : first + total], msg_ref[...])
    gathered = gathered.astype(bf16)
    gathered_ref[...] = gathered

    pre = dot(node_ref[...], n1_ref[:width, :]) + dot(gathered, n1_ref[width:, :])
    squashed = jax.nn.sigmoid(pre)
    act_node = (pre * squashed).astype(bf16)
    act_node_ref[...] = act_node
    normed, inverse = layer_norm(dot(act_node, n2_ref[...]))
    node_new_ref[...] = (node_ref[...].astype(f32) + normed).astype(bf16)
    gon = norm_back(normed, inverse, ncot_ref[...].astype(f32)).astype(bf16)
    gon_ref[...] = gon
    gpn = (dot_rt(gon, n2_ref[...]) * slope_of(pre, squashed)).astype(bf16)
    gpn_ref[...] = gpn
    gg_ref[...] = dot_rt(gpn, n1_ref[width:, :]).astype(bf16)

    for rows in halves:
        whole = slice(first + rows.start, first + rows.stop)
        goe, gpe = backward_rows(
            cot_ref[rows, :],
            dot(pick_ref[whole, :], gg_ref[...]),
            live_ref[whole, :1],
            normed_ref[rows, :],
            inv_ref[rows, :1],
            slope_ref[rows, :],
            w2_ref[...],
        )
        goe_ref[rows, :] = goe
        gpe_ref[rows, :] = gpe
    at = 0
    for out_ref, size in zip(gpe_refs, sizes):
        out_ref[...] = gpe_ref[at : at + size, :]
        at += size


def back_kernel(plan, *refs):
    sets, local_count = plan
    cotan_ref, live_ref, pick_ref, gg_ref, w2_ref = refs[:5]
    groups = (refs[5:8], refs[8:11])
    goe_ref, local_ref = refs[11:13]
    gpe_refs, (cot_ref, gpe_ref) = refs[13:-2], refs[-2:]
    cap = cotan_ref.shape[1]
    for i, k in enumerate(sets):
        cot_ref[i * cap : (i + 1) * cap, :] = cotan_ref[k]
    first = 0
    for slope_ref, normed_ref, inv_ref in groups:
        rows = slice(first, first + slope_ref.shape[0])
        goe, gpe = backward_rows(
            cot_ref[rows, :],
            dot(pick_ref[rows, :], gg_ref[...]),
            live_ref[rows, :1],
            normed_ref[...],
            inv_ref[:, :1],
            slope_ref[...],
            w2_ref[...],
        )
        goe_ref[rows, :] = goe
        gpe_ref[rows, :] = gpe
        first = rows.stop
    local_ref[...] = gpe_ref[: local_count * cap, :]
    for j, out_ref in enumerate(gpe_refs):
        i = local_count + j
        out_ref[...] = gpe_ref[i * cap : (i + 1) * cap, :]


def node_weight_kernel(me_ref, node_ref, gathered_ref, gpn_ref, act_node_ref, gon_ref, keep_ref, sent_ref, block_ref):
    put = functools.partial(put_block, me_ref, block_ref, keep_ref, sent_ref)
    put(0, node_ref[...], gpn_ref[...])
    put(1, gathered_ref[...], gpn_ref[...])
    put(2, act_node_ref[...], gon_ref[...])


def put_block(me_ref, block_ref, keep_ref, sent_ref, index, left_side, right_side):
    core = lax.rem(me_ref[0], 2)
    half = block_ref.shape[0] // 2
    block_ref[...] = dot_lt(left_side, right_side)
    keep_ref[index] = block_ref[pl.ds(pl.multiple_of(core * half, half), half), :]
    other = block_ref[pl.ds(pl.multiple_of((1 - core) * half, half), half), :]
    sent_ref[index] = other.astype(bf16)


def weight_kernel(plan, *refs):
    order, sx_count, gpe_count, act_count, goe_count = plan
    edge_ref, hot_ref, me_ref, node_ref = refs[:4]
    refs = refs[4:]
    sx_refs, refs = refs[:sx_count], refs[sx_count:]
    gpe_refs, refs = refs[:gpe_count], refs[gpe_count:]
    act_refs, refs = refs[:act_count], refs[act_count:]
    goe_refs, refs = refs[:goe_count], refs[goe_count:]
    keep_ref, sent_ref, rsum_ref, x_ref, sx_ref, gpe_ref, act_ref, goe_ref, block_ref = refs
    cap = edge_ref.shape[1]
    for i, k in enumerate(order):
        x_ref[i * cap : (i + 1) * cap, :] = edge_ref[k]
    stack_into(sx_ref, sx_refs)
    stack_into(gpe_ref, gpe_refs)
    stack_into(act_ref, act_refs)
    stack_into(goe_ref, goe_refs)
    recv_sum = dot(hot_ref[...], gpe_ref[...]).astype(bf16)
    rsum_ref[...] = recv_sum
    put = functools.partial(put_block, me_ref, block_ref, keep_ref, sent_ref)
    put(0, x_ref[...], gpe_ref[...])
    put(1, sx_ref[...], gpe_ref[...])
    put(2, node_ref[...], recv_sum)
    put(3, act_ref[...], goe_ref[...])


def base_kernel(ncot_ref, gpn_ref, rsum_ref, w1_ref, n1_ref, base_ref):
    width = w1_ref.shape[1]
    base_ref[...] = (
        ncot_ref[...].astype(f32)
        + dot_rt(gpn_ref[...], n1_ref[:width, :])
        + dot_rt(rsum_ref[...], w1_ref[2 * width :, :])
    )


def edge_kernel(plan, *refs):
    order, normed_count, gpe_count = plan
    edge_ref, cotan_ref, w1_ref, live_ref = refs[:4]
    refs = refs[4:]
    normed_refs, refs = refs[:normed_count], refs[normed_count:]
    gpe_refs, refs = refs[:gpe_count], refs[gpe_count:]
    new_ref, gedge_ref, gpe_ref = refs
    width = w1_ref.shape[1]
    cap = edge_ref.shape[1]
    stack_into(gpe_ref, gpe_refs)
    places = [(ref, at) for ref in normed_refs for at in range(0, ref.shape[0], cap)]
    for i, (k, (normed_ref, at)) in enumerate(zip(order, places)):
        rows = slice(i * cap, (i + 1) * cap)
        grad = cotan_ref[k].astype(f32) + dot_rt(gpe_ref[rows, :], w1_ref[:width, :])
        gedge_ref[k] = grad.astype(bf16)
        message = live_ref[rows, :1] * normed_ref[at : at + cap, :]
        new_ref[k] = (edge_ref[k].astype(f32) + message).astype(bf16)


def final_kernel(plan, *refs):
    local_sets, remote = plan
    me_ref, base_ref, w1_ref, send_ref, id_ref = refs[:5]
    row_refs, (out_ref, hot_ref, rows_ref) = refs[5:-3], refs[-3:]
    nodes, width = base_ref.shape
    cap = send_ref.shape[2]
    ids = [send_ref[k] for k in local_sets]
    ids += [
        asked(me_ref, id_ref, step, i, cap) for step, sets in remote for i in range(len(sets))
    ]
    for i, one in enumerate(ids):
        hot_ref[:, i * cap : (i + 1) * cap] = sum_table(one, nodes)
    stack_into(rows_ref, row_refs)
    send_sum = dot(hot_ref[...], rows_ref[...]).astype(bf16)
    grad = base_ref[...] + dot_rt(send_sum, w1_ref[width : 2 * width, :])
    out_ref[...] = grad.astype(bf16)


def place(me_ref, stride, members):
    return lax.rem(lax.div(me_ref[0], stride), members)


def add_kernel(plan, *refs):
    came, stride, members = plan
    me_ref, keep_ref = refs[:2]
    arr_refs, out_refs = refs[2 : 2 + came], refs[2 + came :]
    size = keep_ref.shape[1] // members
    here = place(me_ref, stride, members)
    for j, out_ref in enumerate(out_refs):
        at = lax.rem(here + j, members) * size
        rows = pl.ds(pl.multiple_of(at, size), size)
        piece = keep_ref[:, rows, :]
        for arr_ref in arr_refs:
            piece += arr_ref[:, rows, :].astype(f32)
        out_ref[...] = piece.astype(out_ref.dtype)


def gather_kernel(plan, *refs):
    stride, members = plan
    me_ref, piece_refs, out_ref = refs[0], refs[1:-1], refs[-1]
    size = piece_refs[0].shape[1]
    here = place(me_ref, stride, members)
    for j, piece_ref in enumerate(piece_refs):
        at = lax.rem(here + members - j, members) * size
        out_ref[:, pl.ds(pl.multiple_of(at, size), size), :] = piece_ref[...]


def join_kernel(plan, *refs):
    members, blocks = plan
    me_ref = refs[0]
    piece_refs, other_refs = refs[1 : 1 + members], refs[1 + members : 1 + 2 * members]
    out_refs = refs[1 + 2 * members :]
    size = piece_refs[0].shape[1]
    core = lax.rem(me_ref[0], 2)
    here = place(me_ref, 2, members)
    for index, (which, block) in enumerate(blocks):
        first = 2 * block * members * size
        for side, side_refs in ((core, piece_refs), (1 - core, other_refs)):
            for j, piece_ref in enumerate(side_refs):
                at = first + (side * members + lax.rem(here + members - j, members)) * size
                rows = pl.ds(pl.multiple_of(at, size), size)
                out_refs[which][rows, :] = piece_ref[index]


def in_group(block, axis, stride, members, step):
    route = []
    for i in range(lax.axis_size(axis)):
        at = (i // stride) % members
        route.append((i, i + ((at + step) % members - at) * stride))
    return lax.ppermute(block, axis, route)


def add_stage(me, keep, arrived, stride, after, members=2, kind=f32, work=1):
    count, rows, width = keep.shape
    shape = (count, rows // members, width)
    outs = call(
        functools.partial(add_kernel, (len(arrived), stride, members)),
        [(shape, kind)] + [(shape, bf16)] * (members - 1),
        [],
        me,
        keep,
        *arrived,
        smem=(0,),
        after=after,
        work=work,
    )
    return outs[0], [in_group(out, "band", stride, members, j + 1) for j, out in enumerate(outs[1:])]


def held_until(array, after):
    return pl.pallas_call(
        lambda *refs: None,
        out_shape=pltpu.VMEM(array.shape, array.dtype),
        in_specs=[pl.BlockSpec(memory_space=pltpu.VMEM)]
        + [pl.BlockSpec(memory_space=pl.ANY)] * len(after),
        out_specs=pl.BlockSpec(memory_space=pltpu.VMEM),
        input_output_aliases={0: 0},
        compiler_params=pltpu.CompilerParams(vmem_limit_bytes=1024 * 1024),
        cost_estimate=pl.CostEstimate(flops=1, bytes_accessed=1, transcendentals=0),
    )(pltpu.with_memory_space_constraint(array, pltpu.VMEM), *after)


def gather_stage(me, piece, came, stride, after):
    count, rows, width = piece.shape
    members, pieces = 2, [piece, came]
    (mine,) = call(
        functools.partial(gather_kernel, (stride, members)),
        [((count, rows * members, width), bf16)],
        [],
        me,
        *pieces,
        smem=(0,),
        after=after,
    )
    return mine


def join_stage(me, piece, other, members, blocks, shapes):
    pieces = [piece, other]
    others = [in_group(one, "band", 1, 2, 1) for one in pieces]
    return call(
        functools.partial(join_kernel, (members, blocks)),
        [(shape, bf16) for shape in shapes],
        [],
        me,
        *pieces,
        *others,
        smem=(0,),
        last=range(len(shapes)),
    )


def reduce_whole(keep, sent):
    bands = lax.axis_size("band")
    chips = [[i for i in range(bands) if i % 2 == c] for c in range(2)]
    total = keep + in_group(sent, "band", 1, 2, 1).astype(f32)
    total = lax.psum(total.astype(bf16), "band", axis_index_groups=chips)
    other = in_group(total, "band", 1, 2, 1)
    core = lax.axis_index("band") % 2
    low, high = jnp.where(core == 0, total, other), jnp.where(core == 0, other, total)
    return jnp.concatenate([low, high], axis=1)


def local(
    node_latent,
    edge_latent,
    recv_slot,
    send_slot,
    edge_count,
    edge_first,
    edge_second,
    node_first,
    node_second,
    node_cotan,
    edge_cotan,
):
    bands = lax.axis_size("band")
    nodes, width = node_latent.shape
    sets, cap = edge_latent.shape[1:3]
    send_ids = send_slot.reshape(sets, 1, cap)
    me = lax.axis_index("band").astype(jnp.int32).reshape(1)

    def step_of(k):
        return band_offsets[k] % bands

    def reach(k):
        return min(step_of(k), bands - step_of(k))

    ordered = sorted(range(sets), key=lambda k: (reach(k), step_of(k)))
    near, far = tuple(ordered[:near_sets]), tuple(ordered[near_sets:])
    local_count = sum(step_of(k) == 0 for k in near)
    near_steps = [step_of(k) for k in near[local_count:]]
    far_steps = list(dict.fromkeys(step_of(k) for k in far))
    steps = near_steps + far_steps
    near_plan = tuple((k,) for k in near[local_count:])
    far_plan = tuple(tuple(k for k in far if step_of(k) == d) for d in far_steps)
    far = sum(far_plan, ())

    order = near + far

    (
        node_latent,
        send_ids,
        recv_ids,
        edges,
        edge_first,
        edge_second,
        node_first,
        node_second,
        node_cotan,
        cotan,
    ) = loaded(
        me,
        node_latent,
        send_ids,
        recv_slot.reshape(sets, 1, cap),
        edge_latent[0],
        edge_first,
        edge_second,
        node_first,
        node_second,
        node_cotan,
        edge_cotan[0],
    )
    remote_plan = tuple(zip(steps, near_plan + far_plan))
    widest = max(len(piece) for piece in near_plan + far_plan)
    (ids,) = call(
        functools.partial(ask_kernel, remote_plan),
        [((bands, 1, widest * cap), jnp.int32)],
        [],
        me,
        send_ids,
        smem=(0,),
    )
    ids = lax.all_to_all(ids, "band", 0, 0, tiled=True)
    picked = call(
        functools.partial(pick_kernel, remote_plan),
        [((len(piece) * cap, width), bf16) for piece in near_plan + far_plan],
        [],
        me,
        node_latent,
        ids,
        smem=(0,),
    )
    sx = [passed_along(block, "band", d) for block, d in zip(picked, steps)]
    sx_near, sx_far = sx[: len(near_plan)], sx[len(near_plan) :]

    local_rows, near_rows, far_rows = local_count * cap, len(near_plan) * cap, len(far) * cap
    total = sets * cap

    def forward_outs(rows):
        return [
            ((rows, width), bf16),
            ((rows, width), f32),
            ((rows, width), f32),
            ((rows, 128), f32),
            ((nodes, width), f32),
        ]

    pick, hot, live, part, sx_local, act_local, slope_local, normed_local, inv_local, node_sum = call(
        functools.partial(start_kernel, (order, local_count)),
        [
            ((total, nodes), bf16),
            ((nodes, total), bf16),
            ((total, 128), f32),
            ((near_rows + far_rows, width), f32),
            ((local_rows, width), bf16),
        ]
        + forward_outs(local_rows),
        [((total, 2 * width), bf16), ((local_rows, width), bf16)],
        edges,
        recv_ids,
        send_ids,
        in_hbm(edge_count),
        edge_first,
        edge_second,
        node_latent,
        smem=(3,),
        after=[picked[0]],
    )
    act_near, slope_near, normed_near, inv_near, node_sum = call(
        functools.partial(near_kernel, (local_rows, len(near_plan))),
        forward_outs(near_rows),
        [((near_rows, width), bf16), ((near_rows, width), bf16)],
        part,
        live,
        hot,
        node_sum,
        edge_first,
        edge_second,
        *sx_near,
    )
    sizes = [len(piece) * cap for piece in far_plan]
    outs = call(
        functools.partial(far_kernel, (far, sizes, local_rows + near_rows, near_rows)),
        [((size, width), bf16) for size in sizes]
        + [((far_rows, width), bf16), ((far_rows, width), bf16), ((far_rows, width), f32)]
        + [((nodes, width), bf16)] * 6,
        [
            ((far_rows, width), bf16),
            ((far_rows, width), f32),
            ((far_rows, 128), f32),
            ((far_rows, width), bf16),
            ((far_rows, width), bf16),
            ((far_rows, width), bf16),
        ],
        cotan,
        part,
        live,
        pick,
        hot,
        node_sum,
        edge_first,
        edge_second,
        node_latent,
        node_cotan,
        node_first,
        node_second,
        *sx_far,
        last=(len(sizes) + 8,),
    )
    gpe_far, outs = list(outs[: len(far_plan)]), outs[len(far_plan) :]
    act_far, goe_far, normed_far, gathered, gpn, act_node, gon, gg, node_new = outs
    back_far = [passed_along(block, "band", -d) for block, d in zip(gpe_far, far_steps)]

    half = (width // 2, width)
    outs = call(
        functools.partial(back_kernel, (near, local_count)),
        [((local_rows + near_rows, width), bf16), ((local_rows, width), bf16)]
        + [((cap, width), bf16)] * len(near_steps),
        [((local_rows + near_rows, width), bf16)] * 2,
        cotan,
        live,
        pick,
        gg,
        edge_second,
        slope_local,
        normed_local,
        inv_local,
        slope_near,
        normed_near,
        inv_near,
    )
    goe_near, gpe_local = outs[:2]
    gpe_near = list(outs[2:])
    back_near = [passed_along(block, "band", -d) for block, d in zip(gpe_near, near_steps)]

    gpe = [gpe_local] + gpe_near + gpe_far
    sx_all = [sx_local] + sx_near + sx_far
    keep_edge, sent_edge, recv_sum = call(
        functools.partial(weight_kernel, (order, len(sx_all), len(gpe), 3, 2)),
        [((4, *half), f32), ((4, *half), bf16), ((nodes, width), bf16)],
        [((total, width), bf16)] * 5 + [((width, width), f32)],
        edges,
        hot,
        me,
        node_latent,
        *sx_all,
        *gpe,
        act_local,
        act_near,
        act_far,
        goe_near,
        goe_far,
        smem=(2,),
    )

    def edge_outputs(after):
        return call(
            functools.partial(edge_kernel, (order, 3, len(gpe))),
            [((sets, cap, width), bf16), ((sets, cap, width), bf16)],
            [((total, width), bf16)],
            edges,
            cotan,
            edge_first,
            live,
            normed_local,
            normed_near,
            normed_far,
            *gpe,
            after=after,
            last=(0, 1),
            work=edge_work,
        )

    def node_output(after):
        (base,) = call(
            base_kernel,
            [((nodes, width), f32)],
            [],
            node_cotan,
            gpn,
            recv_sum,
            edge_first,
            node_first,
            after=after,
        )
        (grad_nodes,) = call(
            functools.partial(final_kernel, (near[:local_count], remote_plan)),
            [((nodes, width), bf16)],
            [((nodes, total), bf16), ((total, width), bf16)],
            me,
            base,
            edge_first,
            send_ids,
            ids,
            gpe_local,
            *back_near,
            *back_far,
            smem=(0,),
            last=(0,),
        )
        return grad_nodes

    def node_weights(after):
        return call(
            node_weight_kernel,
            [((3, *half), f32), ((3, *half), bf16)],
            [((width, width), f32)],
            me,
            node_latent,
            gathered,
            gpn,
            act_node,
            gon,
            smem=(0,),
            after=after,
        )

    first = 2
    node_blocks, node_shapes = ((0, 0), (0, 1), (1, 0)), [(2 * width, width), (width, width)]
    edge_blocks = ((0, 0), (0, 1), (0, 2), (1, 0))
    edge_shapes = [(3 * width, width), (width, width)]
    if bands == 16 and width % 512 == 0:
        def over(block, stride):
            return in_group(block, "band", stride, 2, 1)

        keep_node, sent_node = node_weights([])
        keep_node, came_node = add_stage(me, keep_node, [over(sent_node, 1)], 2, [])
        sent_edge = held_until(sent_edge, back_far + [keep_node])
        came_edge = [over(sent_edge, 1)]
        edge_new, grad_edges = edge_outputs([sent_edge])
        keep_node, came_node = add_stage(me, keep_node, came_node, 4, [in_hbm(edge_new)])
        keep_edge, came_edge = add_stage(me, keep_edge, came_edge, 2, [keep_node])
        keep_node, came_node = add_stage(me, keep_node, came_node, 8, [keep_edge])
        keep_edge, came_edge = add_stage(me, keep_edge, came_edge, 4, [keep_node])
        piece_node, _ = add_stage(me, keep_node, came_node, 1, [keep_edge], 1, bf16)
        keep_edge, came_edge = add_stage(me, keep_edge, came_edge, 8, [piece_node])
        piece_node = gather_stage(me, piece_node, over(piece_node, 8), 8, [keep_edge])
        piece_edge, _ = add_stage(me, keep_edge, came_edge, 1, [], 1, bf16)
        grad_nodes = node_output([piece_edge])
        piece_edge = gather_stage(me, piece_edge, over(piece_edge, 8), 8, [in_hbm(grad_nodes)])
        piece_node = gather_stage(me, piece_node, over(piece_node, 4), 4, [piece_edge])
        other_node = over(piece_node, 2)
        piece_edge = gather_stage(me, piece_edge, over(piece_edge, 4), 4, [other_node])
        other_node = held_until(other_node, [piece_edge])
        grad_n1, grad_n2 = join_stage(me, piece_node, other_node, first, node_blocks, node_shapes)
        other_edge = held_until(over(piece_edge, 2), [in_hbm(grad_n2)])
        grad_e1, grad_e2 = join_stage(me, piece_edge, other_edge, first, edge_blocks, edge_shapes)
    else:
        whole = reduce_whole(*node_weights([]))
        grad_n1, grad_n2 = whole[:2].reshape(2 * width, width), whole[2]
        whole = reduce_whole(keep_edge, sent_edge)
        grad_e1, grad_e2 = whole[:3].reshape(3 * width, width), whole[3]
        edge_new, grad_edges = edge_outputs([])
        grad_nodes = node_output([])
    return (
        node_new,
        edge_new[None],
        grad_nodes,
        grad_edges[None],
        grad_e1,
        grad_e2,
        grad_n1,
        grad_n2,
    )


def solution(mesh):
    return jax.shard_map(
        local,
        mesh=mesh,
        in_specs=(
            P(("groups", "band"), None),
            P(("groups", "band"), None, None, None),
            P(("groups", "band"), None, None),
            P(("groups", "band"), None, None),
            P(("groups", "band"), None),
            P(),
            P(),
            P(),
            P(),
            P(("groups", "band"), None),
            P(("groups", "band"), None, None, None),
        ),
        out_specs=(
            P(("groups", "band"), None),
            P(("groups", "band"), None, None, None),
            P(("groups", "band"), None),
            P(("groups", "band"), None, None, None),
            P("groups", None),
            P("groups", None),
            P("groups", None),
            P("groups", None),
        ),
        check_vma=False,
    )
```

```python
import functools

import jax
import jax.numpy as jnp
from jax import lax
from jax.experimental import pallas as pl
from jax.experimental.pallas import tpu as pltpu
from jax.sharding import PartitionSpec as P

band_offsets = (0, 1, -1, 2, -2, 4, -4, 8, -8, 16, -16)
norm_eps = 1e-05
near_sets = 7
edge_work = 20_000_000_000
bf16 = jnp.bfloat16
f32 = jnp.float32
vmem_limit = 20 * 1024 * 1024


def passed_along(block, axis, distance):
    devices = range(lax.axis_size(axis))
    route = [((i - distance) % len(devices), i) for i in devices]
    return lax.ppermute(block, axis, route)


def layer_norm(inputs):
    average = jnp.mean(inputs, axis=-1, keepdims=True)
    centred = inputs - average
    inverse = lax.rsqrt(jnp.mean(centred * centred, axis=-1, keepdims=True) + norm_eps)
    return (centred * inverse, inverse)


def norm_back(normed, inverse, upstream):
    return inverse * (
        upstream
        - jnp.mean(upstream, axis=-1, keepdims=True)
        - normed * jnp.mean(upstream * normed, axis=-1, keepdims=True)
    )


def slope_of(inputs, squashed):
    return squashed * (1.0 + inputs * (1.0 - squashed))


def dot(left_side, right_side):
    return jnp.dot(left_side, right_side, preferred_element_type=f32)


def dot_rt(left_side, right_side):
    return lax.dot_general(
        left_side, right_side, (((1,), (1,)), ((), ())), preferred_element_type=f32
    )


def dot_lt(left_side, right_side):
    return lax.dot_general(
        left_side, right_side, (((0,), (0,)), ((), ())), preferred_element_type=f32
    )


def pick_table(ids, nodes):
    cap = ids.shape[1]
    down = jnp.transpose(jnp.broadcast_to(ids, (cap, cap)))
    parts = []
    for first in range(0, nodes, cap):
        wide = min(cap, nodes - first)
        lanes = lax.broadcasted_iota(jnp.int32, (cap, wide), 1) + first
        parts.append(jnp.where(down[:, :wide] == lanes, 1.0, 0.0).astype(bf16))
    return jnp.concatenate(parts, axis=1)


def sum_table(ids, nodes):
    down = lax.broadcasted_iota(jnp.int32, (nodes, ids.shape[1]), 0)
    return jnp.where(down == ids, 1.0, 0.0).astype(bf16)


def live_rows(count, cap):
    return (lax.broadcasted_iota(jnp.int32, (cap, 128), 0) < count).astype(f32)


def call(body, outs, scratch, *args, smem=(), after=(), last=(), work=1):
    spaces, given = [], []
    for i, arg in enumerate(args):
        spaces.append(pl.BlockSpec(memory_space=pltpu.SMEM if i in smem else pltpu.VMEM))
        given.append(arg if i in smem else pltpu.with_memory_space_constraint(arg, pltpu.VMEM))
    spaces += [pl.BlockSpec(memory_space=pl.ANY)] * len(after)

    def kernel(*refs):
        body(*refs[: len(args)], *refs[len(args) + len(after) :])

    return pl.pallas_call(
        kernel,
        out_shape=[
            (pltpu.HBM if i in last else pltpu.VMEM)(shape, kind)
            for i, (shape, kind) in enumerate(outs)
        ],
        in_specs=spaces,
        out_specs=[pl.BlockSpec(memory_space=pltpu.VMEM)] * len(outs),
        scratch_shapes=[pltpu.VMEM(shape, kind) for shape, kind in scratch],
        compiler_params=pltpu.CompilerParams(vmem_limit_bytes=vmem_limit),
        cost_estimate=pl.CostEstimate(flops=work, bytes_accessed=1, transcendentals=0),
    )(*given, *after)


def in_hbm(array):
    return pltpu.with_memory_space_constraint(array, pltpu.HBM)


def load_kernel(count, *refs):
    sems, refs = refs[-1], refs[1:]
    copies = [
        pltpu.make_async_copy(refs[i], refs[count + i], sems.at[i]) for i in range(count)
    ]
    for copy in copies:
        copy.start()
    for copy in copies:
        copy.wait()


def loaded(me, *args):
    count = len(args)
    return pl.pallas_call(
        functools.partial(load_kernel, count),
        out_shape=[pltpu.VMEM(arg.shape, arg.dtype) for arg in args],
        in_specs=[pl.BlockSpec(memory_space=pltpu.SMEM)]
        + [pl.BlockSpec(memory_space=pltpu.HBM)] * count,
        out_specs=[pl.BlockSpec(memory_space=pltpu.VMEM)] * count,
        scratch_shapes=[pltpu.SemaphoreType.DMA((count,))],
        compiler_params=pltpu.CompilerParams(vmem_limit_bytes=1024 * 1024),
        cost_estimate=pl.CostEstimate(flops=1, bytes_accessed=1, transcendentals=0),
    )(me, *[in_hbm(arg) for arg in args])


def ask_kernel(plan, me_ref, send_ref, out_ref):
    bands = out_ref.shape[0]
    out_ref[...] = jnp.zeros_like(out_ref)
    for step, sets in plan:
        ids = [send_ref[k] for k in sets]
        blank = out_ref.shape[2] - len(sets) * send_ref.shape[2]
        if blank:
            ids.append(jnp.zeros((1, blank), jnp.int32))
        out_ref[lax.rem(me_ref[0] + bands - step, bands)] = jnp.concatenate(ids, axis=1)


def asked(me_ref, id_ref, step, index, cap):
    row = lax.rem(me_ref[0] + step, id_ref.shape[0])
    return id_ref[row][:, index * cap : (index + 1) * cap]


def pick_kernel(plan, me_ref, node_ref, id_ref, *out_refs):
    nodes = node_ref.shape[0]
    for out_ref, (step, sets) in zip(out_refs, plan):
        cap = out_ref.shape[0] // len(sets)
        for i in range(len(sets)):
            hot = pick_table(asked(me_ref, id_ref, step, i, cap), nodes)
            out_ref[i * cap : (i + 1) * cap, :] = dot(hot, node_ref[...]).astype(bf16)


def forward_rows(pre, live, w2, act_ref, slope_ref, normed_ref, inv_ref, msg_ref, rows):
    squashed = jax.nn.sigmoid(pre)
    slope_ref[rows, :] = slope_of(pre, squashed)
    act = (pre * squashed).astype(bf16)
    act_ref[rows, :] = act
    normed, inverse = layer_norm(dot(act, w2))
    normed_ref[rows, :] = normed
    inv_ref[rows, :] = jnp.broadcast_to(inverse, (inverse.shape[0], 128))
    msg_ref[rows, :] = (live * normed).astype(bf16)


def backward_rows(cotan, picked, live, normed, inverse, slope, w2):
    upstream = live * (cotan.astype(f32) + picked)
    goe = norm_back(normed, inverse, upstream).astype(bf16)
    return goe, (dot_rt(goe, w2) * slope).astype(bf16)


def stack_into(out_ref, refs):
    first = 0
    for ref in refs:
        out_ref[first : first + ref.shape[0], :] = ref[...]
        first += ref.shape[0]


def start_kernel(plan, *refs):
    order, local_count = plan
    (
        edge_ref,
        recv_ref,
        send_ref,
        count_ref,
        w1_ref,
        w2_ref,
        node_ref,
        pick_ref,
        hot_ref,
        live_ref,
        part_ref,
        sx_ref,
        act_ref,
        slope_ref,
        normed_ref,
        inv_ref,
        sum_ref,
        x_ref,
        msg_ref,
    ) = refs
    nodes, width = node_ref.shape
    cap = recv_ref.shape[2]
    split = local_count * cap
    for i, k in enumerate(order):
        rows = slice(i * cap, (i + 1) * cap)
        x_ref[rows, :width] = edge_ref[k]
        pick_ref[rows, :] = pick_table(recv_ref[k], nodes)
        hot_ref[:, rows] = sum_table(recv_ref[k], nodes)
        live_ref[rows, :] = live_rows(count_ref[0, k], cap)
        if i < local_count:
            sx_ref[rows, :] = dot(pick_table(send_ref[k], nodes), node_ref[...]).astype(bf16)
    x_ref[:, width:] = dot(pick_ref[...], node_ref[...]).astype(bf16)
    part = dot(x_ref[:split, :width], w1_ref[:width, :])
    part += dot(x_ref[:split, width:], w1_ref[2 * width :, :])
    pre = part + dot(sx_ref[...], w1_ref[width : 2 * width, :])
    rows = slice(0, split)
    live = live_ref[rows, :1]
    forward_rows(pre, live, w2_ref[...], act_ref, slope_ref, normed_ref, inv_ref, msg_ref, rows)
    sum_ref[...] = dot(hot_ref[:, :split], msg_ref[...])
    part = dot(x_ref[split:, :width], w1_ref[:width, :])
    part_ref[...] = part + dot(x_ref[split:, width:], w1_ref[2 * width :, :])


def near_kernel(plan, *refs):
    first, count = plan
    part_ref, live_ref, hot_ref, sum_in_ref, w1_ref, w2_ref = refs[:6]
    sx_refs = refs[6 : 6 + count]
    act_ref, slope_ref, normed_ref, inv_ref, sum_ref, sx_ref, msg_ref = refs[6 + count :]
    total, width = sx_ref.shape
    stack_into(sx_ref, sx_refs)
    for j in range(2):
        rows = slice(j * total // 2, (j + 1) * total // 2)
        pre = part_ref[rows, :] + dot(sx_ref[rows, :], w1_ref[width : 2 * width, :])
        live = live_ref[first + rows.start : first + rows.stop, :1]
        forward_rows(pre, live, w2_ref[...], act_ref, slope_ref, normed_ref, inv_ref, msg_ref, rows)
    sum_ref[...] = sum_in_ref[...] + dot(hot_ref[:, first : first + total], msg_ref[...])


def far_kernel(plan, *refs):
    sets, sizes, first, part_first = plan
    count = len(sizes)
    (
        cotan_ref,
        part_ref,
        live_ref,
        pick_ref,
        hot_ref,
        sum_ref,
        w1_ref,
        w2_ref,
        node_ref,
        ncot_ref,
        n1_ref,
        n2_ref,
    ) = refs[:12]
    sx_refs, refs = refs[12 : 12 + count], refs[12 + count :]
    gpe_refs, refs = refs[:count], refs[count:]
    (
        act_ref,
        goe_ref,
        normed_ref,
        gathered_ref,
        gpn_ref,
        act_node_ref,
        gon_ref,
        gg_ref,
        node_new_ref,
        sx_ref,
        slope_ref,
        inv_ref,
        msg_ref,
        cot_ref,
        gpe_ref,
    ) = refs
    total, width = sx_ref.shape
    cap = cotan_ref.shape[1]
    stack_into(sx_ref, sx_refs)
    for i, k in enumerate(sets):
        cot_ref[i * cap : (i + 1) * cap, :] = cotan_ref[k]
    halves = [slice(j * total // 2, (j + 1) * total // 2) for j in range(2)]
    for rows in halves:
        pre = part_ref[part_first + rows.start : part_first + rows.stop, :]
        pre = pre + dot(sx_ref[rows, :], w1_ref[width : 2 * width, :])
        live = live_ref[first + rows.start : first + rows.stop, :1]
        forward_rows(pre, live, w2_ref[...], act_ref, slope_ref, normed_ref, inv_ref, msg_ref, rows)
    gathered = sum_ref[...] + dot(hot_ref[:, first : first + total], msg_ref[...])
    gathered = gathered.astype(bf16)
    gathered_ref[...] = gathered

    pre = dot(node_ref[...], n1_ref[:width, :]) + dot(gathered, n1_ref[width:, :])
    squashed = jax.nn.sigmoid(pre)
    act_node = (pre * squashed).astype(bf16)
    act_node_ref[...] = act_node
    normed, inverse = layer_norm(dot(act_node, n2_ref[...]))
    node_new_ref[...] = (node_ref[...].astype(f32) + normed).astype(bf16)
    gon = norm_back(normed, inverse, ncot_ref[...].astype(f32)).astype(bf16)
    gon_ref[...] = gon
    gpn = (dot_rt(gon, n2_ref[...]) * slope_of(pre, squashed)).astype(bf16)
    gpn_ref[...] = gpn
    gg_ref[...] = dot_rt(gpn, n1_ref[width:, :]).astype(bf16)

    for rows in halves:
        whole = slice(first + rows.start, first + rows.stop)
        goe, gpe = backward_rows(
            cot_ref[rows, :],
            dot(pick_ref[whole, :], gg_ref[...]),
            live_ref[whole, :1],
            normed_ref[rows, :],
            inv_ref[rows, :1],
            slope_ref[rows, :],
            w2_ref[...],
        )
        goe_ref[rows, :] = goe
        gpe_ref[rows, :] = gpe
    at = 0
    for out_ref, size in zip(gpe_refs, sizes):
        out_ref[...] = gpe_ref[at : at + size, :]
        at += size


def back_kernel(plan, *refs):
    sets, local_count = plan
    cotan_ref, live_ref, pick_ref, gg_ref, w2_ref = refs[:5]
    groups = (refs[5:8], refs[8:11])
    goe_ref, local_ref = refs[11:13]
    gpe_refs, (cot_ref, gpe_ref) = refs[13:-2], refs[-2:]
    cap = cotan_ref.shape[1]
    for i, k in enumerate(sets):
        cot_ref[i * cap : (i + 1) * cap, :] = cotan_ref[k]
    first = 0
    for slope_ref, normed_ref, inv_ref in groups:
        rows = slice(first, first + slope_ref.shape[0])
        goe, gpe = backward_rows(
            cot_ref[rows, :],
            dot(pick_ref[rows, :], gg_ref[...]),
            live_ref[rows, :1],
            normed_ref[...],
            inv_ref[:, :1],
            slope_ref[...],
            w2_ref[...],
        )
        goe_ref[rows, :] = goe
        gpe_ref[rows, :] = gpe
        first = rows.stop
    local_ref[...] = gpe_ref[: local_count * cap, :]
    for j, out_ref in enumerate(gpe_refs):
        i = local_count + j
        out_ref[...] = gpe_ref[i * cap : (i + 1) * cap, :]


def node_weight_kernel(me_ref, node_ref, gathered_ref, gpn_ref, act_node_ref, gon_ref, keep_ref, sent_ref, block_ref):
    put = functools.partial(put_block, me_ref, block_ref, keep_ref, sent_ref)
    put(0, node_ref[...], gpn_ref[...])
    put(1, gathered_ref[...], gpn_ref[...])
    put(2, act_node_ref[...], gon_ref[...])


def put_block(me_ref, block_ref, keep_ref, sent_ref, index, left_side, right_side):
    core = lax.rem(me_ref[0], 2)
    half = block_ref.shape[0] // 2
    block_ref[...] = dot_lt(left_side, right_side)
    keep_ref[index] = block_ref[pl.ds(pl.multiple_of(core * half, half), half), :]
    other = block_ref[pl.ds(pl.multiple_of((1 - core) * half, half), half), :]
    sent_ref[index] = other.astype(bf16)


def weight_kernel(plan, *refs):
    order, sx_count, gpe_count, act_count, goe_count = plan
    edge_ref, hot_ref, me_ref, node_ref = refs[:4]
    refs = refs[4:]
    sx_refs, refs = refs[:sx_count], refs[sx_count:]
    gpe_refs, refs = refs[:gpe_count], refs[gpe_count:]
    act_refs, refs = refs[:act_count], refs[act_count:]
    goe_refs, refs = refs[:goe_count], refs[goe_count:]
    keep_ref, sent_ref, rsum_ref, x_ref, sx_ref, gpe_ref, act_ref, goe_ref, block_ref = refs
    cap = edge_ref.shape[1]
    for i, k in enumerate(order):
        x_ref[i * cap : (i + 1) * cap, :] = edge_ref[k]
    stack_into(sx_ref, sx_refs)
    stack_into(gpe_ref, gpe_refs)
    stack_into(act_ref, act_refs)
    stack_into(goe_ref, goe_refs)
    recv_sum = dot(hot_ref[...], gpe_ref[...]).astype(bf16)
    rsum_ref[...] = recv_sum
    put = functools.partial(put_block, me_ref, block_ref, keep_ref, sent_ref)
    put(0, x_ref[...], gpe_ref[...])
    put(1, sx_ref[...], gpe_ref[...])
    put(2, node_ref[...], recv_sum)
    put(3, act_ref[...], goe_ref[...])


def base_kernel(ncot_ref, gpn_ref, rsum_ref, w1_ref, n1_ref, base_ref):
    width = w1_ref.shape[1]
    base_ref[...] = (
        ncot_ref[...].astype(f32)
        + dot_rt(gpn_ref[...], n1_ref[:width, :])
        + dot_rt(rsum_ref[...], w1_ref[2 * width :, :])
    )


def edge_kernel(plan, *refs):
    order, normed_count, gpe_count = plan
    edge_ref, cotan_ref, w1_ref, live_ref = refs[:4]
    refs = refs[4:]
    normed_refs, refs = refs[:normed_count], refs[normed_count:]
    gpe_refs, refs = refs[:gpe_count], refs[gpe_count:]
    new_ref, gedge_ref, gpe_ref = refs
    width = w1_ref.shape[1]
    cap = edge_ref.shape[1]
    stack_into(gpe_ref, gpe_refs)
    places = [(ref, at) for ref in normed_refs for at in range(0, ref.shape[0], cap)]
    for i, (k, (normed_ref, at)) in enumerate(zip(order, places)):
        rows = slice(i * cap, (i + 1) * cap)
        grad = cotan_ref[k].astype(f32) + dot_rt(gpe_ref[rows, :], w1_ref[:width, :])
        gedge_ref[k] = grad.astype(bf16)
        message = live_ref[rows, :1] * normed_ref[at : at + cap, :]
        new_ref[k] = (edge_ref[k].astype(f32) + message).astype(bf16)


def final_kernel(plan, *refs):
    local_sets, remote = plan
    me_ref, base_ref, w1_ref, send_ref, id_ref = refs[:5]
    row_refs, (out_ref, hot_ref, rows_ref) = refs[5:-3], refs[-3:]
    nodes, width = base_ref.shape
    cap = send_ref.shape[2]
    ids = [send_ref[k] for k in local_sets]
    ids += [
        asked(me_ref, id_ref, step, i, cap) for step, sets in remote for i in range(len(sets))
    ]
    for i, one in enumerate(ids):
        hot_ref[:, i * cap : (i + 1) * cap] = sum_table(one, nodes)
    stack_into(rows_ref, row_refs)
    send_sum = dot(hot_ref[...], rows_ref[...]).astype(bf16)
    grad = base_ref[...] + dot_rt(send_sum, w1_ref[width : 2 * width, :])
    out_ref[...] = grad.astype(bf16)


def place(me_ref, stride, members):
    return lax.rem(lax.div(me_ref[0], stride), members)


def add_kernel(plan, *refs):
    came, stride, members = plan
    me_ref, keep_ref = refs[:2]
    arr_refs, out_refs = refs[2 : 2 + came], refs[2 + came :]
    size = keep_ref.shape[1] // members
    here = place(me_ref, stride, members)
    for j, out_ref in enumerate(out_refs):
        at = lax.rem(here + j, members) * size
        rows = pl.ds(pl.multiple_of(at, size), size)
        piece = keep_ref[:, rows, :]
        for arr_ref in arr_refs:
            piece += arr_ref[:, rows, :].astype(f32)
        out_ref[...] = piece.astype(out_ref.dtype)


def gather_kernel(plan, *refs):
    stride, members = plan
    me_ref, piece_refs, out_ref = refs[0], refs[1:-1], refs[-1]
    size = piece_refs[0].shape[1]
    here = place(me_ref, stride, members)
    for j, piece_ref in enumerate(piece_refs):
        at = lax.rem(here + members - j, members) * size
        out_ref[:, pl.ds(pl.multiple_of(at, size), size), :] = piece_ref[...]


def join_kernel(plan, *refs):
    members, blocks = plan
    me_ref = refs[0]
    piece_refs, other_refs = refs[1 : 1 + members], refs[1 + members : 1 + 2 * members]
    out_refs = refs[1 + 2 * members :]
    size = piece_refs[0].shape[1]
    core = lax.rem(me_ref[0], 2)
    here = place(me_ref, 2, members)
    for index, (which, block) in enumerate(blocks):
        first = 2 * block * members * size
        for side, side_refs in ((core, piece_refs), (1 - core, other_refs)):
            for j, piece_ref in enumerate(side_refs):
                at = first + (side * members + lax.rem(here + members - j, members)) * size
                rows = pl.ds(pl.multiple_of(at, size), size)
                out_refs[which][rows, :] = piece_ref[index]


def in_group(block, axis, stride, members, step):
    route = []
    for i in range(lax.axis_size(axis)):
        at = (i // stride) % members
        route.append((i, i + ((at + step) % members - at) * stride))
    return lax.ppermute(block, axis, route)


def add_stage(me, keep, arrived, stride, after, members=2, kind=f32, work=1):
    count, rows, width = keep.shape
    shape = (count, rows // members, width)
    outs = call(
        functools.partial(add_kernel, (len(arrived), stride, members)),
        [(shape, kind)] + [(shape, bf16)] * (members - 1),
        [],
        me,
        keep,
        *arrived,
        smem=(0,),
        after=after,
        work=work,
    )
    return outs[0], [in_group(out, "band", stride, members, j + 1) for j, out in enumerate(outs[1:])]


def held_until(array, after):
    return pl.pallas_call(
        lambda *refs: None,
        out_shape=pltpu.VMEM(array.shape, array.dtype),
        in_specs=[pl.BlockSpec(memory_space=pltpu.VMEM)]
        + [pl.BlockSpec(memory_space=pl.ANY)] * len(after),
        out_specs=pl.BlockSpec(memory_space=pltpu.VMEM),
        input_output_aliases={0: 0},
        compiler_params=pltpu.CompilerParams(vmem_limit_bytes=1024 * 1024),
        cost_estimate=pl.CostEstimate(flops=1, bytes_accessed=1, transcendentals=0),
    )(pltpu.with_memory_space_constraint(array, pltpu.VMEM), *after)


def gather_stage(me, piece, came, stride, after):
    count, rows, width = piece.shape
    members, pieces = 2, [piece, came]
    (mine,) = call(
        functools.partial(gather_kernel, (stride, members)),
        [((count, rows * members, width), bf16)],
        [],
        me,
        *pieces,
        smem=(0,),
        after=after,
    )
    return mine


def join_stage(me, piece, other, members, blocks, shapes):
    pieces = [piece, other]
    others = [in_group(one, "band", 1, 2, 1) for one in pieces]
    return call(
        functools.partial(join_kernel, (members, blocks)),
        [(shape, bf16) for shape in shapes],
        [],
        me,
        *pieces,
        *others,
        smem=(0,),
        last=range(len(shapes)),
    )


def reduce_whole(keep, sent):
    bands = lax.axis_size("band")
    chips = [[i for i in range(bands) if i % 2 == c] for c in range(2)]
    total = keep + in_group(sent, "band", 1, 2, 1).astype(f32)
    total = lax.psum(total.astype(bf16), "band", axis_index_groups=chips)
    other = in_group(total, "band", 1, 2, 1)
    core = lax.axis_index("band") % 2
    low, high = jnp.where(core == 0, total, other), jnp.where(core == 0, other, total)
    return jnp.concatenate([low, high], axis=1)


def local(
    node_latent,
    edge_latent,
    recv_slot,
    send_slot,
    edge_count,
    edge_first,
    edge_second,
    node_first,
    node_second,
    node_cotan,
    edge_cotan,
):
    bands = lax.axis_size("band")
    nodes, width = node_latent.shape
    sets, cap = edge_latent.shape[1:3]
    send_ids = send_slot.reshape(sets, 1, cap)
    me = lax.axis_index("band").astype(jnp.int32).reshape(1)

    def step_of(k):
        return band_offsets[k] % bands

    def reach(k):
        return min(step_of(k), bands - step_of(k))

    ordered = sorted(range(sets), key=lambda k: (reach(k), step_of(k)))
    near, far = tuple(ordered[:near_sets]), tuple(ordered[near_sets:])
    local_count = sum(step_of(k) == 0 for k in near)
    near_steps = [step_of(k) for k in near[local_count:]]
    far_steps = list(dict.fromkeys(step_of(k) for k in far))
    steps = near_steps + far_steps
    near_plan = tuple((k,) for k in near[local_count:])
    far_plan = tuple(tuple(k for k in far if step_of(k) == d) for d in far_steps)
    far = sum(far_plan, ())

    order = near + far

    (
        node_latent,
        send_ids,
        recv_ids,
        edges,
        edge_first,
        edge_second,
        node_first,
        node_second,
        node_cotan,
        cotan,
    ) = loaded(
        me,
        node_latent,
        send_ids,
        recv_slot.reshape(sets, 1, cap),
        edge_latent[0],
        edge_first,
        edge_second,
        node_first,
        node_second,
        node_cotan,
        edge_cotan[0],
    )
    remote_plan = tuple(zip(steps, near_plan + far_plan))
    widest = max(len(piece) for piece in near_plan + far_plan)
    (ids,) = call(
        functools.partial(ask_kernel, remote_plan),
        [((bands, 1, widest * cap), jnp.int32)],
        [],
        me,
        send_ids,
        smem=(0,),
    )
    ids = lax.all_to_all(ids, "band", 0, 0, tiled=True)
    picked = call(
        functools.partial(pick_kernel, remote_plan),
        [((len(piece) * cap, width), bf16) for piece in near_plan + far_plan],
        [],
        me,
        node_latent,
        ids,
        smem=(0,),
    )
    sx = [passed_along(block, "band", d) for block, d in zip(picked, steps)]
    sx_near, sx_far = sx[: len(near_plan)], sx[len(near_plan) :]

    local_rows, near_rows, far_rows = local_count * cap, len(near_plan) * cap, len(far) * cap
    total = sets * cap

    def forward_outs(rows):
        return [
            ((rows, width), bf16),
            ((rows, width), f32),
            ((rows, width), f32),
            ((rows, 128), f32),
            ((nodes, width), f32),
        ]

    pick, hot, live, part, sx_local, act_local, slope_local, normed_local, inv_local, node_sum = call(
        functools.partial(start_kernel, (order, local_count)),
        [
            ((total, nodes), bf16),
            ((nodes, total), bf16),
            ((total, 128), f32),
            ((near_rows + far_rows, width), f32),
            ((local_rows, width), bf16),
        ]
        + forward_outs(local_rows),
        [((total, 2 * width), bf16), ((local_rows, width), bf16)],
        edges,
        recv_ids,
        send_ids,
        in_hbm(edge_count),
        edge_first,
        edge_second,
        node_latent,
        smem=(3,),
        after=[picked[0]],
    )
    act_near, slope_near, normed_near, inv_near, node_sum = call(
        functools.partial(near_kernel, (local_rows, len(near_plan))),
        forward_outs(near_rows),
        [((near_rows, width), bf16), ((near_rows, width), bf16)],
        part,
        live,
        hot,
        node_sum,
        edge_first,
        edge_second,
        *sx_near,
    )
    sizes = [len(piece) * cap for piece in far_plan]
    outs = call(
        functools.partial(far_kernel, (far, sizes, local_rows + near_rows, near_rows)),
        [((size, width), bf16) for size in sizes]
        + [((far_rows, width), bf16), ((far_rows, width), bf16), ((far_rows, width), f32)]
        + [((nodes, width), bf16)] * 6,
        [
            ((far_rows, width), bf16),
            ((far_rows, width), f32),
            ((far_rows, 128), f32),
            ((far_rows, width), bf16),
            ((far_rows, width), bf16),
            ((far_rows, width), bf16),
        ],
        cotan,
        part,
        live,
        pick,
        hot,
        node_sum,
        edge_first,
        edge_second,
        node_latent,
        node_cotan,
        node_first,
        node_second,
        *sx_far,
        last=(len(sizes) + 8,),
    )
    gpe_far, outs = list(outs[: len(far_plan)]), outs[len(far_plan) :]
    act_far, goe_far, normed_far, gathered, gpn, act_node, gon, gg, node_new = outs
    back_far = [passed_along(block, "band", -d) for block, d in zip(gpe_far, far_steps)]

    half = (width // 2, width)
    outs = call(
        functools.partial(back_kernel, (near, local_count)),
        [((local_rows + near_rows, width), bf16), ((local_rows, width), bf16)]
        + [((cap, width), bf16)] * len(near_steps),
        [((local_rows + near_rows, width), bf16)] * 2,
        cotan,
        live,
        pick,
        gg,
        edge_second,
        slope_local,
        normed_local,
        inv_local,
        slope_near,
        normed_near,
        inv_near,
    )
    goe_near, gpe_local = outs[:2]
    gpe_near = list(outs[2:])
    back_near = [passed_along(block, "band", -d) for block, d in zip(gpe_near, near_steps)]

    gpe = [gpe_local] + gpe_near + gpe_far
    sx_all = [sx_local] + sx_near + sx_far
    keep_edge, sent_edge, recv_sum = call(
        functools.partial(weight_kernel, (order, len(sx_all), len(gpe), 3, 2)),
        [((4, *half), f32), ((4, *half), bf16), ((nodes, width), bf16)],
        [((total, width), bf16)] * 5 + [((width, width), f32)],
        edges,
        hot,
        me,
        node_latent,
        *sx_all,
        *gpe,
        act_local,
        act_near,
        act_far,
        goe_near,
        goe_far,
        smem=(2,),
    )

    def edge_outputs(after):
        return call(
            functools.partial(edge_kernel, (order, 3, len(gpe))),
            [((sets, cap, width), bf16), ((sets, cap, width), bf16)],
            [((total, width), bf16)],
            edges,
            cotan,
            edge_first,
            live,
            normed_local,
            normed_near,
            normed_far,
            *gpe,
            after=after,
            last=(0, 1),
            work=edge_work,
        )

    def node_output(after):
        (base,) = call(
            base_kernel,
            [((nodes, width), f32)],
            [],
            node_cotan,
            gpn,
            recv_sum,
            edge_first,
            node_first,
            after=after,
        )
        (grad_nodes,) = call(
            functools.partial(final_kernel, (near[:local_count], remote_plan)),
            [((nodes, width), bf16)],
            [((nodes, total), bf16), ((total, width), bf16)],
            me,
            base,
            edge_first,
            send_ids,
            ids,
            gpe_local,
            *back_near,
            *back_far,
            smem=(0,),
            work=edge_work,
            last=(0,),
        )
        return grad_nodes

    def node_weights(after):
        return call(
            node_weight_kernel,
            [((3, *half), f32), ((3, *half), bf16)],
            [((width, width), f32)],
            me,
            node_latent,
            gathered,
            gpn,
            act_node,
            gon,
            smem=(0,),
            after=after,
        )

    first = 2
    node_blocks, node_shapes = ((0, 0), (0, 1), (1, 0)), [(2 * width, width), (width, width)]
    edge_blocks = ((0, 0), (0, 1), (0, 2), (1, 0))
    edge_shapes = [(3 * width, width), (width, width)]
    if bands == 16 and width % 512 == 0:
        def over(block, stride):
            return in_group(block, "band", stride, 2, 1)

        keep_node, sent_node = node_weights([])
        keep_node, came_node = add_stage(me, keep_node, [over(sent_node, 1)], 2, [])
        sent_edge = held_until(sent_edge, back_far + [keep_node])
        came_edge = [over(sent_edge, 1)]
        edge_new, grad_edges = edge_outputs([sent_edge])
        keep_node, came_node = add_stage(me, keep_node, came_node, 4, [in_hbm(edge_new)])
        keep_edge, came_edge = add_stage(me, keep_edge, came_edge, 2, [keep_node])
        keep_node, came_node = add_stage(me, keep_node, came_node, 8, [keep_edge])
        keep_edge, came_edge = add_stage(me, keep_edge, came_edge, 4, [keep_node])
        keep_edge, came_edge = add_stage(me, keep_edge, came_edge, 8, [])
        piece_node, _ = add_stage(me, keep_node, came_node, 1, [keep_edge], 1, bf16)
        piece_edge, _ = add_stage(me, keep_edge, came_edge, 1, [], 1, bf16)
        piece_node = gather_stage(me, piece_node, over(piece_node, 8), 8, [piece_edge])
        piece_edge = gather_stage(me, piece_edge, over(piece_edge, 8), 8, [])
        grad_nodes = node_output([piece_edge])
        piece_node = gather_stage(me, piece_node, over(piece_node, 4), 4, [piece_edge])
        other_node = over(piece_node, 2)
        piece_edge = gather_stage(
            me, piece_edge, over(piece_edge, 4), 4, [other_node, in_hbm(grad_nodes)]
        )
        other_node = held_until(other_node, [piece_edge])
        grad_n1, grad_n2 = join_stage(me, piece_node, other_node, first, node_blocks, node_shapes)
        other_edge = held_until(over(piece_edge, 2), [in_hbm(grad_n2)])
        grad_e1, grad_e2 = join_stage(me, piece_edge, other_edge, first, edge_blocks, edge_shapes)
    else:
        whole = reduce_whole(*node_weights([]))
        grad_n1, grad_n2 = whole[:2].reshape(2 * width, width), whole[2]
        whole = reduce_whole(keep_edge, sent_edge)
        grad_e1, grad_e2 = whole[:3].reshape(3 * width, width), whole[3]
        edge_new, grad_edges = edge_outputs([])
        grad_nodes = node_output([])
    return (
        node_new,
        edge_new[None],
        grad_nodes,
        grad_edges[None],
        grad_e1,
        grad_e2,
        grad_n1,
        grad_n2,
    )


def solution(mesh):
    return jax.shard_map(
        local,
        mesh=mesh,
        in_specs=(
            P(("groups", "band"), None),
            P(("groups", "band"), None, None, None),
            P(("groups", "band"), None, None),
            P(("groups", "band"), None, None),
            P(("groups", "band"), None),
            P(),
            P(),
            P(),
            P(),
            P(("groups", "band"), None),
            P(("groups", "band"), None, None, None),
        ),
        out_specs=(
            P(("groups", "band"), None),
            P(("groups", "band"), None, None, None),
            P(("groups", "band"), None),
            P(("groups", "band"), None, None, None),
            P("groups", None),
            P("groups", None),
            P("groups", None),
            P("groups", None),
        ),
        check_vma=False,
    )
```

```python
import functools

import jax
import jax.numpy as jnp
from jax import lax
from jax.experimental import pallas as pl
from jax.experimental.pallas import tpu as pltpu
from jax.sharding import PartitionSpec as P

band_offsets = (0, 1, -1, 2, -2, 4, -4, 8, -8, 16, -16)
norm_eps = 1e-05
near_sets = 7
edge_work = 20_000_000_000
bf16 = jnp.bfloat16
f32 = jnp.float32
vmem_limit = 20 * 1024 * 1024


def passed_along(block, axis, distance):
    devices = range(lax.axis_size(axis))
    route = [((i - distance) % len(devices), i) for i in devices]
    return lax.ppermute(block, axis, route)


def layer_norm(inputs):
    average = jnp.mean(inputs, axis=-1, keepdims=True)
    centred = inputs - average
    inverse = lax.rsqrt(jnp.mean(centred * centred, axis=-1, keepdims=True) + norm_eps)
    return (centred * inverse, inverse)


def norm_back(normed, inverse, upstream):
    return inverse * (
        upstream
        - jnp.mean(upstream, axis=-1, keepdims=True)
        - normed * jnp.mean(upstream * normed, axis=-1, keepdims=True)
    )


def slope_of(inputs, squashed):
    return squashed * (1.0 + inputs * (1.0 - squashed))


def dot(left_side, right_side):
    return jnp.dot(left_side, right_side, preferred_element_type=f32)


def dot_rt(left_side, right_side):
    return lax.dot_general(
        left_side, right_side, (((1,), (1,)), ((), ())), preferred_element_type=f32
    )


def dot_lt(left_side, right_side):
    return lax.dot_general(
        left_side, right_side, (((0,), (0,)), ((), ())), preferred_element_type=f32
    )


def pick_table(ids, nodes):
    cap = ids.shape[1]
    down = jnp.transpose(jnp.broadcast_to(ids, (cap, cap)))
    parts = []
    for first in range(0, nodes, cap):
        wide = min(cap, nodes - first)
        lanes = lax.broadcasted_iota(jnp.int32, (cap, wide), 1) + first
        parts.append(jnp.where(down[:, :wide] == lanes, 1.0, 0.0).astype(bf16))
    return jnp.concatenate(parts, axis=1)


def sum_table(ids, nodes):
    down = lax.broadcasted_iota(jnp.int32, (nodes, ids.shape[1]), 0)
    return jnp.where(down == ids, 1.0, 0.0).astype(bf16)


def live_rows(count, cap):
    return (lax.broadcasted_iota(jnp.int32, (cap, 128), 0) < count).astype(f32)


def call(body, outs, scratch, *args, smem=(), after=(), last=(), work=1):
    spaces, given = [], []
    for i, arg in enumerate(args):
        spaces.append(pl.BlockSpec(memory_space=pltpu.SMEM if i in smem else pltpu.VMEM))
        given.append(arg if i in smem else pltpu.with_memory_space_constraint(arg, pltpu.VMEM))
    spaces += [pl.BlockSpec(memory_space=pl.ANY)] * len(after)

    def kernel(*refs):
        body(*refs[: len(args)], *refs[len(args) + len(after) :])

    return pl.pallas_call(
        kernel,
        out_shape=[
            (pltpu.HBM if i in last else pltpu.VMEM)(shape, kind)
            for i, (shape, kind) in enumerate(outs)
        ],
        in_specs=spaces,
        out_specs=[pl.BlockSpec(memory_space=pltpu.VMEM)] * len(outs),
        scratch_shapes=[pltpu.VMEM(shape, kind) for shape, kind in scratch],
        compiler_params=pltpu.CompilerParams(vmem_limit_bytes=vmem_limit),
        cost_estimate=pl.CostEstimate(flops=work, bytes_accessed=1, transcendentals=0),
    )(*given, *after)


def in_hbm(array):
    return pltpu.with_memory_space_constraint(array, pltpu.HBM)


def load_kernel(count, *refs):
    sems, refs = refs[-1], refs[1:]
    copies = [
        pltpu.make_async_copy(refs[i], refs[count + i], sems.at[i]) for i in range(count)
    ]
    for copy in copies:
        copy.start()
    for copy in copies:
        copy.wait()


def loaded(me, *args):
    count = len(args)
    return pl.pallas_call(
        functools.partial(load_kernel, count),
        out_shape=[pltpu.VMEM(arg.shape, arg.dtype) for arg in args],
        in_specs=[pl.BlockSpec(memory_space=pltpu.SMEM)]
        + [pl.BlockSpec(memory_space=pltpu.HBM)] * count,
        out_specs=[pl.BlockSpec(memory_space=pltpu.VMEM)] * count,
        scratch_shapes=[pltpu.SemaphoreType.DMA((count,))],
        compiler_params=pltpu.CompilerParams(vmem_limit_bytes=1024 * 1024),
        cost_estimate=pl.CostEstimate(flops=1, bytes_accessed=1, transcendentals=0),
    )(me, *[in_hbm(arg) for arg in args])


def ask_kernel(plan, me_ref, send_ref, out_ref):
    bands = out_ref.shape[0]
    out_ref[...] = jnp.zeros_like(out_ref)
    for step, sets in plan:
        ids = [send_ref[k] for k in sets]
        blank = out_ref.shape[2] - len(sets) * send_ref.shape[2]
        if blank:
            ids.append(jnp.zeros((1, blank), jnp.int32))
        out_ref[lax.rem(me_ref[0] + bands - step, bands)] = jnp.concatenate(ids, axis=1)


def asked(me_ref, id_ref, step, index, cap):
    row = lax.rem(me_ref[0] + step, id_ref.shape[0])
    return id_ref[row][:, index * cap : (index + 1) * cap]


def pick_kernel(plan, me_ref, node_ref, id_ref, *out_refs):
    nodes = node_ref.shape[0]
    for out_ref, (step, sets) in zip(out_refs, plan):
        cap = out_ref.shape[0] // len(sets)
        for i in range(len(sets)):
            hot = pick_table(asked(me_ref, id_ref, step, i, cap), nodes)
            out_ref[i * cap : (i + 1) * cap, :] = dot(hot, node_ref[...]).astype(bf16)


def forward_rows(pre, live, w2, act_ref, slope_ref, normed_ref, inv_ref, msg_ref, rows):
    squashed = jax.nn.sigmoid(pre)
    slope_ref[rows, :] = slope_of(pre, squashed)
    act = (pre * squashed).astype(bf16)
    act_ref[rows, :] = act
    normed, inverse = layer_norm(dot(act, w2))
    normed_ref[rows, :] = normed
    inv_ref[rows, :] = jnp.broadcast_to(inverse, (inverse.shape[0], 128))
    msg_ref[rows, :] = (live * normed).astype(bf16)


def backward_rows(cotan, picked, live, normed, inverse, slope, w2):
    upstream = live * (cotan.astype(f32) + picked)
    goe = norm_back(normed, inverse, upstream).astype(bf16)
    return goe, (dot_rt(goe, w2) * slope).astype(bf16)


def stack_into(out_ref, refs):
    first = 0
    for ref in refs:
        out_ref[first : first + ref.shape[0], :] = ref[...]
        first += ref.shape[0]


def start_kernel(plan, *refs):
    order, local_count = plan
    (
        edge_ref,
        recv_ref,
        send_ref,
        count_ref,
        w1_ref,
        w2_ref,
        node_ref,
        pick_ref,
        hot_ref,
        live_ref,
        part_ref,
        sx_ref,
        act_ref,
        slope_ref,
        normed_ref,
        inv_ref,
        sum_ref,
        x_ref,
        msg_ref,
    ) = refs
    nodes, width = node_ref.shape
    cap = recv_ref.shape[2]
    split = local_count * cap
    for i, k in enumerate(order):
        rows = slice(i * cap, (i + 1) * cap)
        x_ref[rows, :width] = edge_ref[k]
        pick_ref[rows, :] = pick_table(recv_ref[k], nodes)
        hot_ref[:, rows] = sum_table(recv_ref[k], nodes)
        live_ref[rows, :] = live_rows(count_ref[0, k], cap)
        if i < local_count:
            sx_ref[rows, :] = dot(pick_table(send_ref[k], nodes), node_ref[...]).astype(bf16)
    x_ref[:, width:] = dot(pick_ref[...], node_ref[...]).astype(bf16)
    part = dot(x_ref[:split, :width], w1_ref[:width, :])
    part += dot(x_ref[:split, width:], w1_ref[2 * width :, :])
    pre = part + dot(sx_ref[...], w1_ref[width : 2 * width, :])
    rows = slice(0, split)
    live = live_ref[rows, :1]
    forward_rows(pre, live, w2_ref[...], act_ref, slope_ref, normed_ref, inv_ref, msg_ref, rows)
    sum_ref[...] = dot(hot_ref[:, :split], msg_ref[...])
    part = dot(x_ref[split:, :width], w1_ref[:width, :])
    part_ref[...] = part + dot(x_ref[split:, width:], w1_ref[2 * width :, :])


def near_kernel(plan, *refs):
    first, count = plan
    part_ref, live_ref, hot_ref, sum_in_ref, w1_ref, w2_ref = refs[:6]
    sx_refs = refs[6 : 6 + count]
    act_ref, slope_ref, normed_ref, inv_ref, sum_ref, sx_ref, msg_ref = refs[6 + count :]
    total, width = sx_ref.shape
    stack_into(sx_ref, sx_refs)
    for j in range(2):
        rows = slice(j * total // 2, (j + 1) * total // 2)
        pre = part_ref[rows, :] + dot(sx_ref[rows, :], w1_ref[width : 2 * width, :])
        live = live_ref[first + rows.start : first + rows.stop, :1]
        forward_rows(pre, live, w2_ref[...], act_ref, slope_ref, normed_ref, inv_ref, msg_ref, rows)
    sum_ref[...] = sum_in_ref[...] + dot(hot_ref[:, first : first + total], msg_ref[...])


def far_kernel(plan, *refs):
    sets, sizes, first, part_first = plan
    count = len(sizes)
    (
        cotan_ref,
        part_ref,
        live_ref,
        pick_ref,
        hot_ref,
        sum_ref,
        w1_ref,
        w2_ref,
        node_ref,
        ncot_ref,
        n1_ref,
        n2_ref,
    ) = refs[:12]
    sx_refs, refs = refs[12 : 12 + count], refs[12 + count :]
    gpe_refs, refs = refs[:count], refs[count:]
    (
        act_ref,
        goe_ref,
        normed_ref,
        gathered_ref,
        gpn_ref,
        act_node_ref,
        gon_ref,
        gg_ref,
        node_new_ref,
        sx_ref,
        slope_ref,
        inv_ref,
        msg_ref,
        cot_ref,
        gpe_ref,
    ) = refs
    total, width = sx_ref.shape
    cap = cotan_ref.shape[1]
    stack_into(sx_ref, sx_refs)
    for i, k in enumerate(sets):
        cot_ref[i * cap : (i + 1) * cap, :] = cotan_ref[k]
    halves = [slice(j * total // 2, (j + 1) * total // 2) for j in range(2)]
    for rows in halves:
        pre = part_ref[part_first + rows.start : part_first + rows.stop, :]
        pre = pre + dot(sx_ref[rows, :], w1_ref[width : 2 * width, :])
        live = live_ref[first + rows.start : first + rows.stop, :1]
        forward_rows(pre, live, w2_ref[...], act_ref, slope_ref, normed_ref, inv_ref, msg_ref, rows)
    gathered = sum_ref[...] + dot(hot_ref[:, first : first + total], msg_ref[...])
    gathered = gathered.astype(bf16)
    gathered_ref[...] = gathered

    pre = dot(node_ref[...], n1_ref[:width, :]) + dot(gathered, n1_ref[width:, :])
    squashed = jax.nn.sigmoid(pre)
    act_node = (pre * squashed).astype(bf16)
    act_node_ref[...] = act_node
    normed, inverse = layer_norm(dot(act_node, n2_ref[...]))
    node_new_ref[...] = (node_ref[...].astype(f32) + normed).astype(bf16)
    gon = norm_back(normed, inverse, ncot_ref[...].astype(f32)).astype(bf16)
    gon_ref[...] = gon
    gpn = (dot_rt(gon, n2_ref[...]) * slope_of(pre, squashed)).astype(bf16)
    gpn_ref[...] = gpn
    gg_ref[...] = dot_rt(gpn, n1_ref[width:, :]).astype(bf16)

    for rows in halves:
        whole = slice(first + rows.start, first + rows.stop)
        goe, gpe = backward_rows(
            cot_ref[rows, :],
            dot(pick_ref[whole, :], gg_ref[...]),
            live_ref[whole, :1],
            normed_ref[rows, :],
            inv_ref[rows, :1],
            slope_ref[rows, :],
            w2_ref[...],
        )
        goe_ref[rows, :] = goe
        gpe_ref[rows, :] = gpe
    at = 0
    for out_ref, size in zip(gpe_refs, sizes):
        out_ref[...] = gpe_ref[at : at + size, :]
        at += size


def back_kernel(plan, *refs):
    sets, local_count = plan
    cotan_ref, live_ref, pick_ref, gg_ref, w2_ref = refs[:5]
    groups = (refs[5:8], refs[8:11])
    goe_ref, local_ref = refs[11:13]
    gpe_refs, (cot_ref, gpe_ref) = refs[13:-2], refs[-2:]
    cap = cotan_ref.shape[1]
    for i, k in enumerate(sets):
        cot_ref[i * cap : (i + 1) * cap, :] = cotan_ref[k]
    first = 0
    for slope_ref, normed_ref, inv_ref in groups:
        rows = slice(first, first + slope_ref.shape[0])
        goe, gpe = backward_rows(
            cot_ref[rows, :],
            dot(pick_ref[rows, :], gg_ref[...]),
            live_ref[rows, :1],
            normed_ref[...],
            inv_ref[:, :1],
            slope_ref[...],
            w2_ref[...],
        )
        goe_ref[rows, :] = goe
        gpe_ref[rows, :] = gpe
        first = rows.stop
    local_ref[...] = gpe_ref[: local_count * cap, :]
    for j, out_ref in enumerate(gpe_refs):
        i = local_count + j
        out_ref[...] = gpe_ref[i * cap : (i + 1) * cap, :]


def node_weight_kernel(me_ref, node_ref, gathered_ref, gpn_ref, act_node_ref, gon_ref, keep_ref, sent_ref, block_ref):
    put = functools.partial(put_block, me_ref, block_ref, keep_ref, sent_ref)
    put(0, node_ref[...], gpn_ref[...])
    put(1, gathered_ref[...], gpn_ref[...])
    put(2, act_node_ref[...], gon_ref[...])


def put_block(me_ref, block_ref, keep_ref, sent_ref, index, left_side, right_side):
    core = lax.rem(me_ref[0], 2)
    half = block_ref.shape[0] // 2
    block_ref[...] = dot_lt(left_side, right_side)
    keep_ref[index] = block_ref[pl.ds(pl.multiple_of(core * half, half), half), :]
    other = block_ref[pl.ds(pl.multiple_of((1 - core) * half, half), half), :]
    sent_ref[index] = other.astype(bf16)


def weight_kernel(plan, *refs):
    order, sx_count, gpe_count, act_count, goe_count = plan
    edge_ref, hot_ref, me_ref, node_ref = refs[:4]
    refs = refs[4:]
    sx_refs, refs = refs[:sx_count], refs[sx_count:]
    gpe_refs, refs = refs[:gpe_count], refs[gpe_count:]
    act_refs, refs = refs[:act_count], refs[act_count:]
    goe_refs, refs = refs[:goe_count], refs[goe_count:]
    keep_ref, sent_ref, rsum_ref, x_ref, sx_ref, gpe_ref, act_ref, goe_ref, block_ref = refs
    cap = edge_ref.shape[1]
    for i, k in enumerate(order):
        x_ref[i * cap : (i + 1) * cap, :] = edge_ref[k]
    stack_into(sx_ref, sx_refs)
    stack_into(gpe_ref, gpe_refs)
    stack_into(act_ref, act_refs)
    stack_into(goe_ref, goe_refs)
    recv_sum = dot(hot_ref[...], gpe_ref[...]).astype(bf16)
    rsum_ref[...] = recv_sum
    put = functools.partial(put_block, me_ref, block_ref, keep_ref, sent_ref)
    put(0, x_ref[...], gpe_ref[...])
    put(1, sx_ref[...], gpe_ref[...])
    put(2, node_ref[...], recv_sum)
    put(3, act_ref[...], goe_ref[...])


def base_kernel(ncot_ref, gpn_ref, rsum_ref, w1_ref, n1_ref, base_ref):
    width = w1_ref.shape[1]
    base_ref[...] = (
        ncot_ref[...].astype(f32)
        + dot_rt(gpn_ref[...], n1_ref[:width, :])
        + dot_rt(rsum_ref[...], w1_ref[2 * width :, :])
    )


def edge_kernel(plan, *refs):
    order, normed_count, gpe_count = plan
    edge_ref, cotan_ref, w1_ref, live_ref = refs[:4]
    refs = refs[4:]
    normed_refs, refs = refs[:normed_count], refs[normed_count:]
    gpe_refs, refs = refs[:gpe_count], refs[gpe_count:]
    new_ref, gedge_ref, gpe_ref = refs
    width = w1_ref.shape[1]
    cap = edge_ref.shape[1]
    stack_into(gpe_ref, gpe_refs)
    places = [(ref, at) for ref in normed_refs for at in range(0, ref.shape[0], cap)]
    for i, (k, (normed_ref, at)) in enumerate(zip(order, places)):
        rows = slice(i * cap, (i + 1) * cap)
        grad = cotan_ref[k].astype(f32) + dot_rt(gpe_ref[rows, :], w1_ref[:width, :])
        gedge_ref[k] = grad.astype(bf16)
        message = live_ref[rows, :1] * normed_ref[at : at + cap, :]
        new_ref[k] = (edge_ref[k].astype(f32) + message).astype(bf16)


def final_kernel(plan, *refs):
    local_sets, remote = plan
    me_ref, base_ref, w1_ref, send_ref, id_ref = refs[:5]
    row_refs, (out_ref, hot_ref, rows_ref) = refs[5:-3], refs[-3:]
    nodes, width = base_ref.shape
    cap = send_ref.shape[2]
    ids = [send_ref[k] for k in local_sets]
    ids += [
        asked(me_ref, id_ref, step, i, cap) for step, sets in remote for i in range(len(sets))
    ]
    for i, one in enumerate(ids):
        hot_ref[:, i * cap : (i + 1) * cap] = sum_table(one, nodes)
    stack_into(rows_ref, row_refs)
    send_sum = dot(hot_ref[...], rows_ref[...]).astype(bf16)
    grad = base_ref[...] + dot_rt(send_sum, w1_ref[width : 2 * width, :])
    out_ref[...] = grad.astype(bf16)


def place(me_ref, stride, members):
    return lax.rem(lax.div(me_ref[0], stride), members)


def add_kernel(plan, *refs):
    came, stride, members = plan
    me_ref, keep_ref = refs[:2]
    arr_refs, out_refs = refs[2 : 2 + came], refs[2 + came :]
    size = keep_ref.shape[1] // members
    here = place(me_ref, stride, members)
    for j, out_ref in enumerate(out_refs):
        at = lax.rem(here + j, members) * size
        rows = pl.ds(pl.multiple_of(at, size), size)
        piece = keep_ref[:, rows, :]
        for arr_ref in arr_refs:
            piece += arr_ref[:, rows, :].astype(f32)
        out_ref[...] = piece.astype(out_ref.dtype)


def gather_kernel(plan, *refs):
    stride, members = plan
    me_ref, piece_refs, out_ref = refs[0], refs[1:-1], refs[-1]
    size = piece_refs[0].shape[1]
    here = place(me_ref, stride, members)
    for j, piece_ref in enumerate(piece_refs):
        at = lax.rem(here + members - j, members) * size
        out_ref[:, pl.ds(pl.multiple_of(at, size), size), :] = piece_ref[...]


def join_kernel(plan, *refs):
    members, blocks = plan
    me_ref = refs[0]
    piece_refs, other_refs = refs[1 : 1 + members], refs[1 + members : 1 + 2 * members]
    out_refs = refs[1 + 2 * members :]
    size = piece_refs[0].shape[1]
    core = lax.rem(me_ref[0], 2)
    here = place(me_ref, 2, members)
    for index, (which, block) in enumerate(blocks):
        first = 2 * block * members * size
        for side, side_refs in ((core, piece_refs), (1 - core, other_refs)):
            for j, piece_ref in enumerate(side_refs):
                at = first + (side * members + lax.rem(here + members - j, members)) * size
                rows = pl.ds(pl.multiple_of(at, size), size)
                out_refs[which][rows, :] = piece_ref[index]


def in_group(block, axis, stride, members, step):
    route = []
    for i in range(lax.axis_size(axis)):
        at = (i // stride) % members
        route.append((i, i + ((at + step) % members - at) * stride))
    return lax.ppermute(block, axis, route)


def add_stage(me, keep, arrived, stride, after, members=2, kind=f32, work=1):
    count, rows, width = keep.shape
    shape = (count, rows // members, width)
    outs = call(
        functools.partial(add_kernel, (len(arrived), stride, members)),
        [(shape, kind)] + [(shape, bf16)] * (members - 1),
        [],
        me,
        keep,
        *arrived,
        smem=(0,),
        after=after,
        work=work,
    )
    return outs[0], [in_group(out, "band", stride, members, j + 1) for j, out in enumerate(outs[1:])]


def held_until(array, after):
    return pl.pallas_call(
        lambda *refs: None,
        out_shape=pltpu.VMEM(array.shape, array.dtype),
        in_specs=[pl.BlockSpec(memory_space=pltpu.VMEM)]
        + [pl.BlockSpec(memory_space=pl.ANY)] * len(after),
        out_specs=pl.BlockSpec(memory_space=pltpu.VMEM),
        input_output_aliases={0: 0},
        compiler_params=pltpu.CompilerParams(vmem_limit_bytes=1024 * 1024),
        cost_estimate=pl.CostEstimate(flops=1, bytes_accessed=1, transcendentals=0),
    )(pltpu.with_memory_space_constraint(array, pltpu.VMEM), *after)


def gather_stage(me, piece, came, stride, after):
    count, rows, width = piece.shape
    members, pieces = 2, [piece, came]
    (mine,) = call(
        functools.partial(gather_kernel, (stride, members)),
        [((count, rows * members, width), bf16)],
        [],
        me,
        *pieces,
        smem=(0,),
        after=after,
    )
    return mine


def join_stage(me, piece, other, members, blocks, shapes):
    pieces = [piece, other]
    others = [in_group(one, "band", 1, 2, 1) for one in pieces]
    return call(
        functools.partial(join_kernel, (members, blocks)),
        [(shape, bf16) for shape in shapes],
        [],
        me,
        *pieces,
        *others,
        smem=(0,),
        last=range(len(shapes)),
    )


def reduce_whole(keep, sent):
    bands = lax.axis_size("band")
    chips = [[i for i in range(bands) if i % 2 == c] for c in range(2)]
    total = keep + in_group(sent, "band", 1, 2, 1).astype(f32)
    total = lax.psum(total.astype(bf16), "band", axis_index_groups=chips)
    other = in_group(total, "band", 1, 2, 1)
    core = lax.axis_index("band") % 2
    low, high = jnp.where(core == 0, total, other), jnp.where(core == 0, other, total)
    return jnp.concatenate([low, high], axis=1)


def local(
    node_latent,
    edge_latent,
    recv_slot,
    send_slot,
    edge_count,
    edge_first,
    edge_second,
    node_first,
    node_second,
    node_cotan,
    edge_cotan,
):
    bands = lax.axis_size("band")
    nodes, width = node_latent.shape
    sets, cap = edge_latent.shape[1:3]
    send_ids = send_slot.reshape(sets, 1, cap)
    me = lax.axis_index("band").astype(jnp.int32).reshape(1)

    def step_of(k):
        return band_offsets[k] % bands

    def reach(k):
        return min(step_of(k), bands - step_of(k))

    ordered = sorted(range(sets), key=lambda k: (reach(k), step_of(k)))
    near, far = tuple(ordered[:near_sets]), tuple(ordered[near_sets:])
    local_count = sum(step_of(k) == 0 for k in near)
    near_steps = [step_of(k) for k in near[local_count:]]
    far_steps = list(dict.fromkeys(step_of(k) for k in far))
    steps = near_steps + far_steps
    near_plan = tuple((k,) for k in near[local_count:])
    far_plan = tuple(tuple(k for k in far if step_of(k) == d) for d in far_steps)
    far = sum(far_plan, ())

    order = near + far

    (
        node_latent,
        send_ids,
        recv_ids,
        edges,
        edge_first,
        edge_second,
        node_first,
        node_second,
        node_cotan,
        cotan,
    ) = loaded(
        me,
        node_latent,
        send_ids,
        recv_slot.reshape(sets, 1, cap),
        edge_latent[0],
        edge_first,
        edge_second,
        node_first,
        node_second,
        node_cotan,
        edge_cotan[0],
    )
    remote_plan = tuple(zip(steps, near_plan + far_plan))
    widest = max(len(piece) for piece in near_plan + far_plan)
    (ids,) = call(
        functools.partial(ask_kernel, remote_plan),
        [((bands, 1, widest * cap), jnp.int32)],
        [],
        me,
        send_ids,
        smem=(0,),
    )
    ids = lax.all_to_all(ids, "band", 0, 0, tiled=True)
    picked = call(
        functools.partial(pick_kernel, remote_plan),
        [((len(piece) * cap, width), bf16) for piece in near_plan + far_plan],
        [],
        me,
        node_latent,
        ids,
        smem=(0,),
    )
    sx = [passed_along(block, "band", d) for block, d in zip(picked, steps)]
    sx_near, sx_far = sx[: len(near_plan)], sx[len(near_plan) :]

    local_rows, near_rows, far_rows = local_count * cap, len(near_plan) * cap, len(far) * cap
    total = sets * cap

    def forward_outs(rows):
        return [
            ((rows, width), bf16),
            ((rows, width), f32),
            ((rows, width), f32),
            ((rows, 128), f32),
            ((nodes, width), f32),
        ]

    pick, hot, live, part, sx_local, act_local, slope_local, normed_local, inv_local, node_sum = call(
        functools.partial(start_kernel, (order, local_count)),
        [
            ((total, nodes), bf16),
            ((nodes, total), bf16),
            ((total, 128), f32),
            ((near_rows + far_rows, width), f32),
            ((local_rows, width), bf16),
        ]
        + forward_outs(local_rows),
        [((total, 2 * width), bf16), ((local_rows, width), bf16)],
        edges,
        recv_ids,
        send_ids,
        in_hbm(edge_count),
        edge_first,
        edge_second,
        node_latent,
        smem=(3,),
        after=[picked[0]],
    )
    act_near, slope_near, normed_near, inv_near, node_sum = call(
        functools.partial(near_kernel, (local_rows, len(near_plan))),
        forward_outs(near_rows),
        [((near_rows, width), bf16), ((near_rows, width), bf16)],
        part,
        live,
        hot,
        node_sum,
        edge_first,
        edge_second,
        *sx_near,
    )
    sizes = [len(piece) * cap for piece in far_plan]
    outs = call(
        functools.partial(far_kernel, (far, sizes, local_rows + near_rows, near_rows)),
        [((size, width), bf16) for size in sizes]
        + [((far_rows, width), bf16), ((far_rows, width), bf16), ((far_rows, width), f32)]
        + [((nodes, width), bf16)] * 6,
        [
            ((far_rows, width), bf16),
            ((far_rows, width), f32),
            ((far_rows, 128), f32),
            ((far_rows, width), bf16),
            ((far_rows, width), bf16),
            ((far_rows, width), bf16),
        ],
        cotan,
        part,
        live,
        pick,
        hot,
        node_sum,
        edge_first,
        edge_second,
        node_latent,
        node_cotan,
        node_first,
        node_second,
        *sx_far,
        last=(len(sizes) + 8,),
    )
    gpe_far, outs = list(outs[: len(far_plan)]), outs[len(far_plan) :]
    act_far, goe_far, normed_far, gathered, gpn, act_node, gon, gg, node_new = outs
    back_far = [passed_along(block, "band", -d) for block, d in zip(gpe_far, far_steps)]

    half = (width // 2, width)
    outs = call(
        functools.partial(back_kernel, (near, local_count)),
        [((local_rows + near_rows, width), bf16), ((local_rows, width), bf16)]
        + [((cap, width), bf16)] * len(near_steps),
        [((local_rows + near_rows, width), bf16)] * 2,
        cotan,
        live,
        pick,
        gg,
        edge_second,
        slope_local,
        normed_local,
        inv_local,
        slope_near,
        normed_near,
        inv_near,
    )
    goe_near, gpe_local = outs[:2]
    gpe_near = list(outs[2:])
    back_near = [passed_along(block, "band", -d) for block, d in zip(gpe_near, near_steps)]

    gpe = [gpe_local] + gpe_near + gpe_far
    sx_all = [sx_local] + sx_near + sx_far
    keep_edge, sent_edge, recv_sum = call(
        functools.partial(weight_kernel, (order, len(sx_all), len(gpe), 3, 2)),
        [((4, *half), f32), ((4, *half), bf16), ((nodes, width), bf16)],
        [((total, width), bf16)] * 5 + [((width, width), f32)],
        edges,
        hot,
        me,
        node_latent,
        *sx_all,
        *gpe,
        act_local,
        act_near,
        act_far,
        goe_near,
        goe_far,
        smem=(2,),
    )

    def edge_outputs(after):
        return call(
            functools.partial(edge_kernel, (order, 3, len(gpe))),
            [((sets, cap, width), bf16), ((sets, cap, width), bf16)],
            [((total, width), bf16)],
            edges,
            cotan,
            edge_first,
            live,
            normed_local,
            normed_near,
            normed_far,
            *gpe,
            after=after,
            last=(0, 1),
            work=edge_work,
        )

    def node_output(after):
        (base,) = call(
            base_kernel,
            [((nodes, width), f32)],
            [],
            node_cotan,
            gpn,
            recv_sum,
            edge_first,
            node_first,
            after=after,
        )
        (grad_nodes,) = call(
            functools.partial(final_kernel, (near[:local_count], remote_plan)),
            [((nodes, width), bf16)],
            [((nodes, total), bf16), ((total, width), bf16)],
            me,
            base,
            edge_first,
            send_ids,
            ids,
            gpe_local,
            *back_near,
            *back_far,
            smem=(0,),
            work=edge_work,
            last=(0,),
        )
        return grad_nodes

    def node_weights(after):
        return call(
            node_weight_kernel,
            [((3, *half), f32), ((3, *half), bf16)],
            [((width, width), f32)],
            me,
            node_latent,
            gathered,
            gpn,
            act_node,
            gon,
            smem=(0,),
            after=after,
        )

    first = 2
    node_blocks, node_shapes = ((0, 0), (0, 1), (1, 0)), [(2 * width, width), (width, width)]
    edge_blocks = ((0, 0), (0, 1), (0, 2), (1, 0))
    edge_shapes = [(3 * width, width), (width, width)]
    if bands == 16 and width % 512 == 0:
        def over(block, stride):
            return in_group(block, "band", stride, 2, 1)

        keep_node, sent_node = node_weights([])
        keep_node, came_node = add_stage(me, keep_node, [over(sent_node, 1)], 2, [])
        sent_edge = held_until(sent_edge, back_far + [keep_node])
        came_edge = [over(sent_edge, 1)]
        edge_new, grad_edges = edge_outputs([sent_edge])
        keep_node, came_node = add_stage(me, keep_node, came_node, 4, [in_hbm(edge_new)])
        keep_edge, came_edge = add_stage(me, keep_edge, came_edge, 2, [keep_node])
        keep_node, came_node = add_stage(me, keep_node, came_node, 8, [keep_edge])
        keep_edge, came_edge = add_stage(me, keep_edge, came_edge, 4, [keep_node])
        keep_edge, came_edge = add_stage(me, keep_edge, came_edge, 8, [])
        piece_node, _ = add_stage(me, keep_node, came_node, 1, [keep_edge], 1, bf16)
        piece_edge, _ = add_stage(me, keep_edge, came_edge, 1, [], 1, bf16)
        piece_node = gather_stage(me, piece_node, over(piece_node, 8), 8, [piece_edge])
        piece_edge = gather_stage(me, piece_edge, over(piece_edge, 8), 8, [])
        grad_nodes = node_output([piece_edge])
        piece_node = gather_stage(me, piece_node, over(piece_node, 4), 4, [piece_edge])
        other_node = over(piece_node, 2)
        piece_edge = gather_stage(me, piece_edge, over(piece_edge, 4), 4, [in_hbm(grad_nodes)])
        other_node = held_until(other_node, [piece_edge])
        grad_n1, grad_n2 = join_stage(me, piece_node, other_node, first, node_blocks, node_shapes)
        other_edge = held_until(over(piece_edge, 2), [in_hbm(grad_n2)])
        grad_e1, grad_e2 = join_stage(me, piece_edge, other_edge, first, edge_blocks, edge_shapes)
    else:
        whole = reduce_whole(*node_weights([]))
        grad_n1, grad_n2 = whole[:2].reshape(2 * width, width), whole[2]
        whole = reduce_whole(keep_edge, sent_edge)
        grad_e1, grad_e2 = whole[:3].reshape(3 * width, width), whole[3]
        edge_new, grad_edges = edge_outputs([])
        grad_nodes = node_output([])
    return (
        node_new,
        edge_new[None],
        grad_nodes,
        grad_edges[None],
        grad_e1,
        grad_e2,
        grad_n1,
        grad_n2,
    )


def solution(mesh):
    return jax.shard_map(
        local,
        mesh=mesh,
        in_specs=(
            P(("groups", "band"), None),
            P(("groups", "band"), None, None, None),
            P(("groups", "band"), None, None),
            P(("groups", "band"), None, None),
            P(("groups", "band"), None),
            P(),
            P(),
            P(),
            P(),
            P(("groups", "band"), None),
            P(("groups", "band"), None, None, None),
        ),
        out_specs=(
            P(("groups", "band"), None),
            P(("groups", "band"), None, None, None),
            P(("groups", "band"), None),
            P(("groups", "band"), None, None, None),
            P("groups", None),
            P("groups", None),
            P("groups", None),
            P("groups", None),
        ),
        check_vma=False,
    )
```

```python
import functools

import jax
import jax.numpy as jnp
from jax import lax
from jax.experimental import pallas as pl
from jax.experimental.pallas import tpu as pltpu
from jax.sharding import PartitionSpec as P

band_offsets = (0, 1, -1, 2, -2, 4, -4, 8, -8, 16, -16)
norm_eps = 1e-05
near_sets = 7
edge_work = 20_000_000_000
bf16 = jnp.bfloat16
f32 = jnp.float32
vmem_limit = 20 * 1024 * 1024


def passed_along(block, axis, distance):
    devices = range(lax.axis_size(axis))
    route = [((i - distance) % len(devices), i) for i in devices]
    return lax.ppermute(block, axis, route)


def layer_norm(inputs):
    average = jnp.mean(inputs, axis=-1, keepdims=True)
    centred = inputs - average
    inverse = lax.rsqrt(jnp.mean(centred * centred, axis=-1, keepdims=True) + norm_eps)
    return (centred * inverse, inverse)


def norm_back(normed, inverse, upstream):
    return inverse * (
        upstream
        - jnp.mean(upstream, axis=-1, keepdims=True)
        - normed * jnp.mean(upstream * normed, axis=-1, keepdims=True)
    )


def slope_of(inputs, squashed):
    return squashed * (1.0 + inputs * (1.0 - squashed))


def dot(left_side, right_side):
    return jnp.dot(left_side, right_side, preferred_element_type=f32)


def dot_rt(left_side, right_side):
    return lax.dot_general(
        left_side, right_side, (((1,), (1,)), ((), ())), preferred_element_type=f32
    )


def dot_lt(left_side, right_side):
    return lax.dot_general(
        left_side, right_side, (((0,), (0,)), ((), ())), preferred_element_type=f32
    )


def pick_table(ids, nodes):
    cap = ids.shape[1]
    down = jnp.transpose(jnp.broadcast_to(ids, (cap, cap)))
    parts = []
    for first in range(0, nodes, cap):
        wide = min(cap, nodes - first)
        lanes = lax.broadcasted_iota(jnp.int32, (cap, wide), 1) + first
        parts.append(jnp.where(down[:, :wide] == lanes, 1.0, 0.0).astype(bf16))
    return jnp.concatenate(parts, axis=1)


def sum_table(ids, nodes):
    down = lax.broadcasted_iota(jnp.int32, (nodes, ids.shape[1]), 0)
    return jnp.where(down == ids, 1.0, 0.0).astype(bf16)


def live_rows(count, cap):
    return (lax.broadcasted_iota(jnp.int32, (cap, 128), 0) < count).astype(f32)


def call(body, outs, scratch, *args, smem=(), after=(), last=(), work=1):
    spaces, given = [], []
    for i, arg in enumerate(args):
        spaces.append(pl.BlockSpec(memory_space=pltpu.SMEM if i in smem else pltpu.VMEM))
        given.append(arg if i in smem else pltpu.with_memory_space_constraint(arg, pltpu.VMEM))
    spaces += [pl.BlockSpec(memory_space=pl.ANY)] * len(after)

    def kernel(*refs):
        body(*refs[: len(args)], *refs[len(args) + len(after) :])

    return pl.pallas_call(
        kernel,
        out_shape=[
            (pltpu.HBM if i in last else pltpu.VMEM)(shape, kind)
            for i, (shape, kind) in enumerate(outs)
        ],
        in_specs=spaces,
        out_specs=[pl.BlockSpec(memory_space=pltpu.VMEM)] * len(outs),
        scratch_shapes=[pltpu.VMEM(shape, kind) for shape, kind in scratch],
        compiler_params=pltpu.CompilerParams(vmem_limit_bytes=vmem_limit),
        cost_estimate=pl.CostEstimate(flops=work, bytes_accessed=1, transcendentals=0),
    )(*given, *after)


def in_hbm(array):
    return pltpu.with_memory_space_constraint(array, pltpu.HBM)


def load_kernel(count, *refs):
    sems, refs = refs[-1], refs[1:]
    copies = [
        pltpu.make_async_copy(refs[i], refs[count + i], sems.at[i]) for i in range(count)
    ]
    for copy in copies:
        copy.start()
    for copy in copies:
        copy.wait()


def loaded(me, *args):
    count = len(args)
    return pl.pallas_call(
        functools.partial(load_kernel, count),
        out_shape=[pltpu.VMEM(arg.shape, arg.dtype) for arg in args],
        in_specs=[pl.BlockSpec(memory_space=pltpu.SMEM)]
        + [pl.BlockSpec(memory_space=pltpu.HBM)] * count,
        out_specs=[pl.BlockSpec(memory_space=pltpu.VMEM)] * count,
        scratch_shapes=[pltpu.SemaphoreType.DMA((count,))],
        compiler_params=pltpu.CompilerParams(vmem_limit_bytes=1024 * 1024),
        cost_estimate=pl.CostEstimate(flops=1, bytes_accessed=1, transcendentals=0),
    )(me, *[in_hbm(arg) for arg in args])


def ask_kernel(plan, me_ref, send_ref, out_ref):
    bands = out_ref.shape[0]
    out_ref[...] = jnp.zeros_like(out_ref)
    for step, sets in plan:
        ids = [send_ref[k] for k in sets]
        blank = out_ref.shape[2] - len(sets) * send_ref.shape[2]
        if blank:
            ids.append(jnp.zeros((1, blank), jnp.int32))
        out_ref[lax.rem(me_ref[0] + bands - step, bands)] = jnp.concatenate(ids, axis=1)


def asked(me_ref, id_ref, step, index, cap):
    row = lax.rem(me_ref[0] + step, id_ref.shape[0])
    return id_ref[row][:, index * cap : (index + 1) * cap]


def pick_kernel(plan, me_ref, node_ref, id_ref, *out_refs):
    nodes = node_ref.shape[0]
    for out_ref, (step, sets) in zip(out_refs, plan):
        cap = out_ref.shape[0] // len(sets)
        for i in range(len(sets)):
            hot = pick_table(asked(me_ref, id_ref, step, i, cap), nodes)
            out_ref[i * cap : (i + 1) * cap, :] = dot(hot, node_ref[...]).astype(bf16)


def forward_rows(pre, live, w2, act_ref, slope_ref, normed_ref, inv_ref, msg_ref, rows):
    squashed = jax.nn.sigmoid(pre)
    slope_ref[rows, :] = slope_of(pre, squashed)
    act = (pre * squashed).astype(bf16)
    act_ref[rows, :] = act
    normed, inverse = layer_norm(dot(act, w2))
    normed_ref[rows, :] = normed
    inv_ref[rows, :] = jnp.broadcast_to(inverse, (inverse.shape[0], 128))
    msg_ref[rows, :] = (live * normed).astype(bf16)


def backward_rows(cotan, picked, live, normed, inverse, slope, w2):
    upstream = live * (cotan.astype(f32) + picked)
    goe = norm_back(normed, inverse, upstream).astype(bf16)
    return goe, (dot_rt(goe, w2) * slope).astype(bf16)


def stack_into(out_ref, refs):
    first = 0
    for ref in refs:
        out_ref[first : first + ref.shape[0], :] = ref[...]
        first += ref.shape[0]


def start_kernel(plan, *refs):
    order, local_count = plan
    (
        edge_ref,
        recv_ref,
        send_ref,
        count_ref,
        w1_ref,
        w2_ref,
        node_ref,
        pick_ref,
        hot_ref,
        live_ref,
        part_ref,
        sx_ref,
        act_ref,
        slope_ref,
        normed_ref,
        inv_ref,
        sum_ref,
        x_ref,
        msg_ref,
    ) = refs
    nodes, width = node_ref.shape
    cap = recv_ref.shape[2]
    split = local_count * cap
    for i, k in enumerate(order):
        rows = slice(i * cap, (i + 1) * cap)
        x_ref[rows, :width] = edge_ref[k]
        pick_ref[rows, :] = pick_table(recv_ref[k], nodes)
        hot_ref[:, rows] = sum_table(recv_ref[k], nodes)
        live_ref[rows, :] = live_rows(count_ref[0, k], cap)
        if i < local_count:
            sx_ref[rows, :] = dot(pick_table(send_ref[k], nodes), node_ref[...]).astype(bf16)
    x_ref[:, width:] = dot(pick_ref[...], node_ref[...]).astype(bf16)
    part = dot(x_ref[:split, :width], w1_ref[:width, :])
    part += dot(x_ref[:split, width:], w1_ref[2 * width :, :])
    pre = part + dot(sx_ref[...], w1_ref[width : 2 * width, :])
    rows = slice(0, split)
    live = live_ref[rows, :1]
    forward_rows(pre, live, w2_ref[...], act_ref, slope_ref, normed_ref, inv_ref, msg_ref, rows)
    sum_ref[...] = dot(hot_ref[:, :split], msg_ref[...])
    part = dot(x_ref[split:, :width], w1_ref[:width, :])
    part_ref[...] = part + dot(x_ref[split:, width:], w1_ref[2 * width :, :])


def near_kernel(plan, *refs):
    first, count = plan
    part_ref, live_ref, hot_ref, sum_in_ref, w1_ref, w2_ref = refs[:6]
    sx_refs = refs[6 : 6 + count]
    act_ref, slope_ref, normed_ref, inv_ref, sum_ref, sx_ref, msg_ref = refs[6 + count :]
    total, width = sx_ref.shape
    stack_into(sx_ref, sx_refs)
    for j in range(2):
        rows = slice(j * total // 2, (j + 1) * total // 2)
        pre = part_ref[rows, :] + dot(sx_ref[rows, :], w1_ref[width : 2 * width, :])
        live = live_ref[first + rows.start : first + rows.stop, :1]
        forward_rows(pre, live, w2_ref[...], act_ref, slope_ref, normed_ref, inv_ref, msg_ref, rows)
    sum_ref[...] = sum_in_ref[...] + dot(hot_ref[:, first : first + total], msg_ref[...])


def far_kernel(plan, *refs):
    sets, sizes, first, part_first = plan
    count = len(sizes)
    (
        cotan_ref,
        part_ref,
        live_ref,
        pick_ref,
        hot_ref,
        sum_ref,
        w1_ref,
        w2_ref,
        node_ref,
        ncot_ref,
        n1_ref,
        n2_ref,
    ) = refs[:12]
    sx_refs, refs = refs[12 : 12 + count], refs[12 + count :]
    gpe_refs, refs = refs[:count], refs[count:]
    (
        act_ref,
        goe_ref,
        normed_ref,
        gathered_ref,
        gpn_ref,
        act_node_ref,
        gon_ref,
        gg_ref,
        node_new_ref,
        sx_ref,
        slope_ref,
        inv_ref,
        msg_ref,
        cot_ref,
        gpe_ref,
    ) = refs
    total, width = sx_ref.shape
    cap = cotan_ref.shape[1]
    stack_into(sx_ref, sx_refs)
    for i, k in enumerate(sets):
        cot_ref[i * cap : (i + 1) * cap, :] = cotan_ref[k]
    halves = [slice(j * total // 2, (j + 1) * total // 2) for j in range(2)]
    for rows in halves:
        pre = part_ref[part_first + rows.start : part_first + rows.stop, :]
        pre = pre + dot(sx_ref[rows, :], w1_ref[width : 2 * width, :])
        live = live_ref[first + rows.start : first + rows.stop, :1]
        forward_rows(pre, live, w2_ref[...], act_ref, slope_ref, normed_ref, inv_ref, msg_ref, rows)
    gathered = sum_ref[...] + dot(hot_ref[:, first : first + total], msg_ref[...])
    gathered = gathered.astype(bf16)
    gathered_ref[...] = gathered

    pre = dot(node_ref[...], n1_ref[:width, :]) + dot(gathered, n1_ref[width:, :])
    squashed = jax.nn.sigmoid(pre)
    act_node = (pre * squashed).astype(bf16)
    act_node_ref[...] = act_node
    normed, inverse = layer_norm(dot(act_node, n2_ref[...]))
    node_new_ref[...] = (node_ref[...].astype(f32) + normed).astype(bf16)
    gon = norm_back(normed, inverse, ncot_ref[...].astype(f32)).astype(bf16)
    gon_ref[...] = gon
    gpn = (dot_rt(gon, n2_ref[...]) * slope_of(pre, squashed)).astype(bf16)
    gpn_ref[...] = gpn
    gg_ref[...] = dot_rt(gpn, n1_ref[width:, :]).astype(bf16)

    for rows in halves:
        whole = slice(first + rows.start, first + rows.stop)
        goe, gpe = backward_rows(
            cot_ref[rows, :],
            dot(pick_ref[whole, :], gg_ref[...]),
            live_ref[whole, :1],
            normed_ref[rows, :],
            inv_ref[rows, :1],
            slope_ref[rows, :],
            w2_ref[...],
        )
        goe_ref[rows, :] = goe
        gpe_ref[rows, :] = gpe
    at = 0
    for out_ref, size in zip(gpe_refs, sizes):
        out_ref[...] = gpe_ref[at : at + size, :]
        at += size


def back_kernel(plan, *refs):
    sets, local_count = plan
    cotan_ref, live_ref, pick_ref, gg_ref, w2_ref = refs[:5]
    groups = (refs[5:8], refs[8:11])
    goe_ref, local_ref = refs[11:13]
    gpe_refs, (cot_ref, gpe_ref) = refs[13:-2], refs[-2:]
    cap = cotan_ref.shape[1]
    for i, k in enumerate(sets):
        cot_ref[i * cap : (i + 1) * cap, :] = cotan_ref[k]
    first = 0
    for slope_ref, normed_ref, inv_ref in groups:
        rows = slice(first, first + slope_ref.shape[0])
        goe, gpe = backward_rows(
            cot_ref[rows, :],
            dot(pick_ref[rows, :], gg_ref[...]),
            live_ref[rows, :1],
            normed_ref[...],
            inv_ref[:, :1],
            slope_ref[...],
            w2_ref[...],
        )
        goe_ref[rows, :] = goe
        gpe_ref[rows, :] = gpe
        first = rows.stop
    local_ref[...] = gpe_ref[: local_count * cap, :]
    for j, out_ref in enumerate(gpe_refs):
        i = local_count + j
        out_ref[...] = gpe_ref[i * cap : (i + 1) * cap, :]


def node_weight_kernel(me_ref, node_ref, gathered_ref, gpn_ref, act_node_ref, gon_ref, keep_ref, sent_ref, block_ref):
    put = functools.partial(put_block, me_ref, block_ref, keep_ref, sent_ref)
    put(0, node_ref[...], gpn_ref[...])
    put(1, gathered_ref[...], gpn_ref[...])
    put(2, act_node_ref[...], gon_ref[...])


def put_block(me_ref, block_ref, keep_ref, sent_ref, index, left_side, right_side):
    core = lax.rem(me_ref[0], 2)
    half = block_ref.shape[0] // 2
    block_ref[...] = dot_lt(left_side, right_side)
    keep_ref[index] = block_ref[pl.ds(pl.multiple_of(core * half, half), half), :]
    other = block_ref[pl.ds(pl.multiple_of((1 - core) * half, half), half), :]
    sent_ref[index] = other.astype(bf16)


def weight_kernel(plan, *refs):
    order, sx_count, gpe_count, act_count, goe_count = plan
    edge_ref, hot_ref, me_ref, node_ref = refs[:4]
    refs = refs[4:]
    sx_refs, refs = refs[:sx_count], refs[sx_count:]
    gpe_refs, refs = refs[:gpe_count], refs[gpe_count:]
    act_refs, refs = refs[:act_count], refs[act_count:]
    goe_refs, refs = refs[:goe_count], refs[goe_count:]
    keep_ref, sent_ref, rsum_ref, x_ref, sx_ref, gpe_ref, act_ref, goe_ref, block_ref = refs
    cap = edge_ref.shape[1]
    for i, k in enumerate(order):
        x_ref[i * cap : (i + 1) * cap, :] = edge_ref[k]
    stack_into(sx_ref, sx_refs)
    stack_into(gpe_ref, gpe_refs)
    stack_into(act_ref, act_refs)
    stack_into(goe_ref, goe_refs)
    recv_sum = dot(hot_ref[...], gpe_ref[...]).astype(bf16)
    rsum_ref[...] = recv_sum
    put = functools.partial(put_block, me_ref, block_ref, keep_ref, sent_ref)
    put(0, x_ref[...], gpe_ref[...])
    put(1, sx_ref[...], gpe_ref[...])
    put(2, node_ref[...], recv_sum)
    put(3, act_ref[...], goe_ref[...])


def base_kernel(ncot_ref, gpn_ref, rsum_ref, w1_ref, n1_ref, base_ref):
    width = w1_ref.shape[1]
    base_ref[...] = (
        ncot_ref[...].astype(f32)
        + dot_rt(gpn_ref[...], n1_ref[:width, :])
        + dot_rt(rsum_ref[...], w1_ref[2 * width :, :])
    )


def edge_kernel(plan, *refs):
    order, normed_count, gpe_count = plan
    edge_ref, cotan_ref, w1_ref, live_ref = refs[:4]
    refs = refs[4:]
    normed_refs, refs = refs[:normed_count], refs[normed_count:]
    gpe_refs, refs = refs[:gpe_count], refs[gpe_count:]
    new_ref, gedge_ref, gpe_ref = refs
    width = w1_ref.shape[1]
    cap = edge_ref.shape[1]
    stack_into(gpe_ref, gpe_refs)
    places = [(ref, at) for ref in normed_refs for at in range(0, ref.shape[0], cap)]
    for i, (k, (normed_ref, at)) in enumerate(zip(order, places)):
        rows = slice(i * cap, (i + 1) * cap)
        grad = cotan_ref[k].astype(f32) + dot_rt(gpe_ref[rows, :], w1_ref[:width, :])
        gedge_ref[k] = grad.astype(bf16)
        message = live_ref[rows, :1] * normed_ref[at : at + cap, :]
        new_ref[k] = (edge_ref[k].astype(f32) + message).astype(bf16)


def final_kernel(plan, *refs):
    local_sets, remote = plan
    me_ref, base_ref, w1_ref, send_ref, id_ref = refs[:5]
    row_refs, (out_ref, hot_ref, rows_ref) = refs[5:-3], refs[-3:]
    nodes, width = base_ref.shape
    cap = send_ref.shape[2]
    ids = [send_ref[k] for k in local_sets]
    ids += [
        asked(me_ref, id_ref, step, i, cap) for step, sets in remote for i in range(len(sets))
    ]
    for i, one in enumerate(ids):
        hot_ref[:, i * cap : (i + 1) * cap] = sum_table(one, nodes)
    stack_into(rows_ref, row_refs)
    send_sum = dot(hot_ref[...], rows_ref[...]).astype(bf16)
    grad = base_ref[...] + dot_rt(send_sum, w1_ref[width : 2 * width, :])
    out_ref[...] = grad.astype(bf16)


def place(me_ref, stride, members):
    return lax.rem(lax.div(me_ref[0], stride), members)


def add_kernel(plan, *refs):
    came, stride, members = plan
    me_ref, keep_ref = refs[:2]
    arr_refs, out_refs = refs[2 : 2 + came], refs[2 + came :]
    size = keep_ref.shape[1] // members
    here = place(me_ref, stride, members)
    for j, out_ref in enumerate(out_refs):
        at = lax.rem(here + j, members) * size
        rows = pl.ds(pl.multiple_of(at, size), size)
        piece = keep_ref[:, rows, :]
        for arr_ref in arr_refs:
            piece += arr_ref[:, rows, :].astype(f32)
        out_ref[...] = piece.astype(out_ref.dtype)


def gather_kernel(plan, *refs):
    stride, members = plan
    me_ref, piece_refs, out_ref = refs[0], refs[1:-1], refs[-1]
    size = piece_refs[0].shape[1]
    here = place(me_ref, stride, members)
    for j, piece_ref in enumerate(piece_refs):
        at = lax.rem(here + members - j, members) * size
        out_ref[:, pl.ds(pl.multiple_of(at, size), size), :] = piece_ref[...]


def join_kernel(plan, *refs):
    members, blocks = plan
    me_ref = refs[0]
    piece_refs, other_refs = refs[1 : 1 + members], refs[1 + members : 1 + 2 * members]
    out_refs = refs[1 + 2 * members :]
    size = piece_refs[0].shape[1]
    core = lax.rem(me_ref[0], 2)
    here = place(me_ref, 2, members)
    for index, (which, block) in enumerate(blocks):
        first = 2 * block * members * size
        for side, side_refs in ((core, piece_refs), (1 - core, other_refs)):
            for j, piece_ref in enumerate(side_refs):
                at = first + (side * members + lax.rem(here + members - j, members)) * size
                rows = pl.ds(pl.multiple_of(at, size), size)
                out_refs[which][rows, :] = piece_ref[index]


def in_group(block, axis, stride, members, step):
    route = []
    for i in range(lax.axis_size(axis)):
        at = (i // stride) % members
        route.append((i, i + ((at + step) % members - at) * stride))
    return lax.ppermute(block, axis, route)


def add_stage(me, keep, arrived, stride, after, members=2, kind=f32, work=1):
    count, rows, width = keep.shape
    shape = (count, rows // members, width)
    outs = call(
        functools.partial(add_kernel, (len(arrived), stride, members)),
        [(shape, kind)] + [(shape, bf16)] * (members - 1),
        [],
        me,
        keep,
        *arrived,
        smem=(0,),
        after=after,
        work=work,
    )
    return outs[0], [in_group(out, "band", stride, members, j + 1) for j, out in enumerate(outs[1:])]


def held_until(array, after):
    return pl.pallas_call(
        lambda *refs: None,
        out_shape=pltpu.VMEM(array.shape, array.dtype),
        in_specs=[pl.BlockSpec(memory_space=pltpu.VMEM)]
        + [pl.BlockSpec(memory_space=pl.ANY)] * len(after),
        out_specs=pl.BlockSpec(memory_space=pltpu.VMEM),
        input_output_aliases={0: 0},
        compiler_params=pltpu.CompilerParams(vmem_limit_bytes=1024 * 1024),
        cost_estimate=pl.CostEstimate(flops=1, bytes_accessed=1, transcendentals=0),
    )(pltpu.with_memory_space_constraint(array, pltpu.VMEM), *after)


def gather_stage(me, piece, came, stride, after):
    count, rows, width = piece.shape
    members, pieces = 2, [piece, came]
    (mine,) = call(
        functools.partial(gather_kernel, (stride, members)),
        [((count, rows * members, width), bf16)],
        [],
        me,
        *pieces,
        smem=(0,),
        after=after,
    )
    return mine


def join_stage(me, piece, other, members, blocks, shapes):
    pieces = [piece, other]
    others = [in_group(one, "band", 1, 2, 1) for one in pieces]
    return call(
        functools.partial(join_kernel, (members, blocks)),
        [(shape, bf16) for shape in shapes],
        [],
        me,
        *pieces,
        *others,
        smem=(0,),
        last=range(len(shapes)),
    )


def reduce_whole(keep, sent):
    bands = lax.axis_size("band")
    chips = [[i for i in range(bands) if i % 2 == c] for c in range(2)]
    total = keep + in_group(sent, "band", 1, 2, 1).astype(f32)
    total = lax.psum(total.astype(bf16), "band", axis_index_groups=chips)
    other = in_group(total, "band", 1, 2, 1)
    core = lax.axis_index("band") % 2
    low, high = jnp.where(core == 0, total, other), jnp.where(core == 0, other, total)
    return jnp.concatenate([low, high], axis=1)


def local(
    node_latent,
    edge_latent,
    recv_slot,
    send_slot,
    edge_count,
    edge_first,
    edge_second,
    node_first,
    node_second,
    node_cotan,
    edge_cotan,
):
    bands = lax.axis_size("band")
    nodes, width = node_latent.shape
    sets, cap = edge_latent.shape[1:3]
    send_ids = send_slot.reshape(sets, 1, cap)
    me = lax.axis_index("band").astype(jnp.int32).reshape(1)

    def step_of(k):
        return band_offsets[k] % bands

    def reach(k):
        return min(step_of(k), bands - step_of(k))

    ordered = sorted(range(sets), key=lambda k: (reach(k), step_of(k)))
    near, far = tuple(ordered[:near_sets]), tuple(ordered[near_sets:])
    local_count = sum(step_of(k) == 0 for k in near)
    near_steps = [step_of(k) for k in near[local_count:]]
    far_steps = list(dict.fromkeys(step_of(k) for k in far))
    steps = near_steps + far_steps
    near_plan = tuple((k,) for k in near[local_count:])
    far_plan = tuple(tuple(k for k in far if step_of(k) == d) for d in far_steps)
    far = sum(far_plan, ())

    order = near + far

    (
        node_latent,
        send_ids,
        recv_ids,
        edges,
        edge_first,
        edge_second,
        node_first,
        node_second,
        node_cotan,
        cotan,
    ) = loaded(
        me,
        node_latent,
        send_ids,
        recv_slot.reshape(sets, 1, cap),
        edge_latent[0],
        edge_first,
        edge_second,
        node_first,
        node_second,
        node_cotan,
        edge_cotan[0],
    )
    remote_plan = tuple(zip(steps, near_plan + far_plan))
    widest = max(len(piece) for piece in near_plan + far_plan)
    (ids,) = call(
        functools.partial(ask_kernel, remote_plan),
        [((bands, 1, widest * cap), jnp.int32)],
        [],
        me,
        send_ids,
        smem=(0,),
    )
    ids = lax.all_to_all(ids, "band", 0, 0, tiled=True)
    picked = call(
        functools.partial(pick_kernel, remote_plan),
        [((len(piece) * cap, width), bf16) for piece in near_plan + far_plan],
        [],
        me,
        node_latent,
        ids,
        smem=(0,),
    )
    sx = [passed_along(block, "band", d) for block, d in zip(picked, steps)]
    sx_near, sx_far = sx[: len(near_plan)], sx[len(near_plan) :]

    local_rows, near_rows, far_rows = local_count * cap, len(near_plan) * cap, len(far) * cap
    total = sets * cap

    def forward_outs(rows):
        return [
            ((rows, width), bf16),
            ((rows, width), f32),
            ((rows, width), f32),
            ((rows, 128), f32),
            ((nodes, width), f32),
        ]

    pick, hot, live, part, sx_local, act_local, slope_local, normed_local, inv_local, node_sum = call(
        functools.partial(start_kernel, (order, local_count)),
        [
            ((total, nodes), bf16),
            ((nodes, total), bf16),
            ((total, 128), f32),
            ((near_rows + far_rows, width), f32),
            ((local_rows, width), bf16),
        ]
        + forward_outs(local_rows),
        [((total, 2 * width), bf16), ((local_rows, width), bf16)],
        edges,
        recv_ids,
        send_ids,
        in_hbm(edge_count),
        edge_first,
        edge_second,
        node_latent,
        smem=(3,),
        after=[picked[0]],
    )
    act_near, slope_near, normed_near, inv_near, node_sum = call(
        functools.partial(near_kernel, (local_rows, len(near_plan))),
        forward_outs(near_rows),
        [((near_rows, width), bf16), ((near_rows, width), bf16)],
        part,
        live,
        hot,
        node_sum,
        edge_first,
        edge_second,
        *sx_near,
    )
    sizes = [len(piece) * cap for piece in far_plan]
    outs = call(
        functools.partial(far_kernel, (far, sizes, local_rows + near_rows, near_rows)),
        [((size, width), bf16) for size in sizes]
        + [((far_rows, width), bf16), ((far_rows, width), bf16), ((far_rows, width), f32)]
        + [((nodes, width), bf16)] * 6,
        [
            ((far_rows, width), bf16),
            ((far_rows, width), f32),
            ((far_rows, 128), f32),
            ((far_rows, width), bf16),
            ((far_rows, width), bf16),
            ((far_rows, width), bf16),
        ],
        cotan,
        part,
        live,
        pick,
        hot,
        node_sum,
        edge_first,
        edge_second,
        node_latent,
        node_cotan,
        node_first,
        node_second,
        *sx_far,
        last=(len(sizes) + 8,),
    )
    gpe_far, outs = list(outs[: len(far_plan)]), outs[len(far_plan) :]
    act_far, goe_far, normed_far, gathered, gpn, act_node, gon, gg, node_new = outs
    back_far = [passed_along(block, "band", -d) for block, d in zip(gpe_far, far_steps)]

    half = (width // 2, width)
    outs = call(
        functools.partial(back_kernel, (near, local_count)),
        [((local_rows + near_rows, width), bf16), ((local_rows, width), bf16)]
        + [((cap, width), bf16)] * len(near_steps),
        [((local_rows + near_rows, width), bf16)] * 2,
        cotan,
        live,
        pick,
        gg,
        edge_second,
        slope_local,
        normed_local,
        inv_local,
        slope_near,
        normed_near,
        inv_near,
    )
    goe_near, gpe_local = outs[:2]
    gpe_near = list(outs[2:])
    back_near = [passed_along(block, "band", -d) for block, d in zip(gpe_near, near_steps)]

    gpe = [gpe_local] + gpe_near + gpe_far
    sx_all = [sx_local] + sx_near + sx_far
    keep_edge, sent_edge, recv_sum = call(
        functools.partial(weight_kernel, (order, len(sx_all), len(gpe), 3, 2)),
        [((4, *half), f32), ((4, *half), bf16), ((nodes, width), bf16)],
        [((total, width), bf16)] * 5 + [((width, width), f32)],
        edges,
        hot,
        me,
        node_latent,
        *sx_all,
        *gpe,
        act_local,
        act_near,
        act_far,
        goe_near,
        goe_far,
        smem=(2,),
    )

    def edge_outputs(after):
        return call(
            functools.partial(edge_kernel, (order, 3, len(gpe))),
            [((sets, cap, width), bf16), ((sets, cap, width), bf16)],
            [((total, width), bf16)],
            edges,
            cotan,
            edge_first,
            live,
            normed_local,
            normed_near,
            normed_far,
            *gpe,
            after=after,
            last=(0, 1),
            work=edge_work,
        )

    def node_output(after):
        (base,) = call(
            base_kernel,
            [((nodes, width), f32)],
            [],
            node_cotan,
            gpn,
            recv_sum,
            edge_first,
            node_first,
            after=after,
        )
        (grad_nodes,) = call(
            functools.partial(final_kernel, (near[:local_count], remote_plan)),
            [((nodes, width), bf16)],
            [((nodes, total), bf16), ((total, width), bf16)],
            me,
            base,
            edge_first,
            send_ids,
            ids,
            gpe_local,
            *back_near,
            *back_far,
            smem=(0,),
            work=edge_work,
            last=(0,),
        )
        return grad_nodes

    def node_weights(after):
        return call(
            node_weight_kernel,
            [((3, *half), f32), ((3, *half), bf16)],
            [((width, width), f32)],
            me,
            node_latent,
            gathered,
            gpn,
            act_node,
            gon,
            smem=(0,),
            after=after,
        )

    first = 2
    node_blocks, node_shapes = ((0, 0), (0, 1), (1, 0)), [(2 * width, width), (width, width)]
    edge_blocks = ((0, 0), (0, 1), (0, 2), (1, 0))
    edge_shapes = [(3 * width, width), (width, width)]
    if bands == 16 and width % 512 == 0:
        def over(block, stride):
            return in_group(block, "band", stride, 2, 1)

        keep_node, sent_node = node_weights([])
        keep_node, came_node = add_stage(me, keep_node, [over(sent_node, 1)], 2, [])
        sent_edge = held_until(sent_edge, back_far + [keep_node])
        came_edge = [over(sent_edge, 1)]
        edge_new, grad_edges = edge_outputs([sent_edge])
        keep_node, came_node = add_stage(me, keep_node, came_node, 4, [in_hbm(edge_new)])
        keep_edge, came_edge = add_stage(me, keep_edge, came_edge, 2, [keep_node])
        keep_node, came_node = add_stage(me, keep_node, came_node, 8, [keep_edge])
        keep_edge, came_edge = add_stage(me, keep_edge, came_edge, 4, [keep_node])
        keep_edge, came_edge = add_stage(me, keep_edge, came_edge, 8, [])
        piece_node, _ = add_stage(me, keep_node, came_node, 1, [keep_edge], 1, bf16)
        piece_edge, _ = add_stage(me, keep_edge, came_edge, 1, [], 1, bf16)
        piece_node = gather_stage(me, piece_node, over(piece_node, 8), 8, [piece_edge])
        piece_edge = gather_stage(me, piece_edge, over(piece_edge, 8), 8, [])
        grad_nodes = node_output([piece_edge])
        piece_node = gather_stage(me, piece_node, over(piece_node, 4), 4, [piece_edge])
        other_node = over(piece_node, 2)
        piece_edge = gather_stage(me, piece_edge, over(piece_edge, 4), 4, [])
        other_node = held_until(other_node, [piece_edge])
        grad_n1, grad_n2 = join_stage(me, piece_node, other_node, first, node_blocks, node_shapes)
        other_edge = held_until(over(piece_edge, 2), [in_hbm(grad_n2), in_hbm(grad_nodes)])
        grad_e1, grad_e2 = join_stage(me, piece_edge, other_edge, first, edge_blocks, edge_shapes)
    else:
        whole = reduce_whole(*node_weights([]))
        grad_n1, grad_n2 = whole[:2].reshape(2 * width, width), whole[2]
        whole = reduce_whole(keep_edge, sent_edge)
        grad_e1, grad_e2 = whole[:3].reshape(3 * width, width), whole[3]
        edge_new, grad_edges = edge_outputs([])
        grad_nodes = node_output([])
    return (
        node_new,
        edge_new[None],
        grad_nodes,
        grad_edges[None],
        grad_e1,
        grad_e2,
        grad_n1,
        grad_n2,
    )


def solution(mesh):
    return jax.shard_map(
        local,
        mesh=mesh,
        in_specs=(
            P(("groups", "band"), None),
            P(("groups", "band"), None, None, None),
            P(("groups", "band"), None, None),
            P(("groups", "band"), None, None),
            P(("groups", "band"), None),
            P(),
            P(),
            P(),
            P(),
            P(("groups", "band"), None),
            P(("groups", "band"), None, None, None),
        ),
        out_specs=(
            P(("groups", "band"), None),
            P(("groups", "band"), None, None, None),
            P(("groups", "band"), None),
            P(("groups", "band"), None, None, None),
            P("groups", None),
            P("groups", None),
            P("groups", None),
            P("groups", None),
        ),
        check_vma=False,
    )
```
